32 devices in a mesh: rep: 16 (over z, y, core), inner: 2 (over x).
Axes of the slice: x: 2, y: 2, z: 4, core: 2. Of those that a mesh axis runs over, the one named last changes fastest.
Arguments:
- hidden: bfloat16 [16, 2048, 768], P('rep', 'inner'), may hold values from -6 to 6
- frames: bfloat16 [16, 1500, 768], P('rep', None, 'inner'), may hold values from -6 to 6
- segment: int32 [16, 2048], P('rep'), may hold values from 0 to 8, as said below
- cotangent: bfloat16 [16, 2048, 768], P('rep', 'inner'), may hold values from -8.4 to 8.4
- norm_gain: float32 [4, 768], P(None, 'inner'), may hold values from 0.5 to 1.5
- norm_bias: float32 [4, 768], P(None, 'inner'), may hold values from -1.2 to 1.2
- self_qkv: float32 [768, 2304], P('inner'), may hold values from -0.21875 to 0.21875
- self_out: float32 [768, 768], P('inner'), may hold values from -1.5 to 1.5
- cross_q: float32 [768, 768], P('inner'), may hold values from -0.21875 to 0.21875
- cross_kv: float32 [768, 1536], P(None, 'inner'), may hold values from -0.21875 to 0.21875
- cross_out: float32 [768, 768], P('inner'), may hold values from -1.5 to 1.5
- fc1: float32 [768, 3072], P('inner'), may hold values from -0.21875 to 0.21875
- fc2: float32 [3072, 768], P('inner'), may hold values from -0.109375 to 0.109375
- proj_bias: float32 [7, 768], P(None, 'inner'), may hold values from -1.2 to 1.2
- fc1_bias: float32 [3072], P('inner'), may hold values from -1.2 to 1.2
Outputs:
- output: bfloat16 [16, 2048, 768], P('rep', 'inner')
- grad_hidden: bfloat16 [16, 2048, 768], P('rep', 'inner')
- grad_frames: bfloat16 [16, 1500, 768], P('rep', None, 'inner')
- grad_norm_gain: float32 [4, 768], P(None, 'inner')
- grad_norm_bias: float32 [4, 768], P(None, 'inner')
- grad_self_qkv: float32 [768, 2304], P('inner')
- grad_self_out: float32 [768, 768], P('inner')
- grad_cross_q: float32 [768, 768], P('inner')
- grad_cross_kv: float32 [768, 1536], P(None, 'inner')
- grad_cross_out: float32 [768, 768], P('inner')
- grad_fc1: float32 [768, 3072], P('inner')
- grad_fc2: float32 [3072, 768], P('inner')
- grad_proj_bias: float32 [7, 768], P(None, 'inner')
- grad_fc1_bias: float32 [3072], P('inner')
The draws below stay inside these ranges and needn't reach their ends.
Inputs may be any that keep to these rules, and one draw needn't show every extreme that they name: `segment`: in every group the first 1024 tokens have id 0; the other 1024 tokens hold continuations 1 to 8 in order, ids never falling; each continuation has 64 to 192 tokens, and in every group one has exactly 192.
All inputs are finite; a program needn't handle non-finite values.
Results may differ from the reference program's by a relative error of at most 0.017.
The reference program's roundings to bfloat16 on the way count: a program that leaves them out, or rounds other values in their place, can miss the bound.
Values may be sent and summed in bfloat16 or wider, within the bound.
No kernel may reach another device: no remote copies, remote signals or barrier semaphores. Data moves between devices by JAX's collectives and lax.ppermute only.
A program may use at most 320 MiB of HBM per device.

```python
import jax
import jax.numpy as jnp
from jax import lax

D = 768
HEADS = 12
HDIM = 64
FF = 3072
FRAMES = 1500
PROMPT = 1024
CONT = 128
NCONT = 8
GROUP_TOKENS = 2048
GROUPS = 16


def draw_segment(key, part):
    tail_tokens = NCONT * CONT
    pair_count = NCONT // 2
    spread = CONT // 2
    group_keys = jax.random.split(key, GROUPS)

    def one_group(group_key):
        shift_key, order_key = jax.random.split(group_key)
        offsets = jax.random.randint(shift_key, (pair_count,), 0, spread + 1).astype(jnp.int32)
        offsets = offsets.at[0].set(spread)
        paired = jnp.stack([CONT + offsets, CONT - offsets], axis=1).reshape(NCONT).astype(jnp.int32)
        lengths = jax.random.permutation(order_key, paired).astype(jnp.int32)
        ends = jnp.cumsum(lengths)[:NCONT - 1].astype(jnp.int32)
        positions = jnp.arange(tail_tokens, dtype=jnp.int32)
        labels = 1 + jnp.sum((ends[None, :] <= positions[:, None]).astype(jnp.int32), axis=1)
        return jnp.concatenate([jnp.zeros((PROMPT,), jnp.int32), labels.astype(jnp.int32)])
    return jax.vmap(one_group)(group_keys)


def draw_cotangent(key, part):
    key = jax.random.fold_in(key, 7)
    token_key, group_key = jax.random.split(key)
    token_part = jnp.clip(jax.random.normal(token_key, (GROUPS, GROUP_TOKENS, D), jnp.float32), -6.0, 6.0)
    group_part = jnp.clip(jax.random.normal(group_key, (GROUPS, 1, D), jnp.float32), -6.0, 6.0) * 0.4
    return (token_part + group_part).astype(jnp.bfloat16)


def block_levels(stream_key, extent, shards, low, largest):
    def one(axis_at, blocks):
        draws = jax.random.uniform(jax.random.fold_in(jax.random.fold_in(stream_key, 6), axis_at), (blocks,), jnp.float32, low / len(shards), largest / len(shards))
        return jnp.repeat(jnp.exp(draws), extent[axis_at] // blocks).reshape((-1,) + (1,) * (len(extent) - axis_at - 1))

    factor_of = one(*shards[0])
    for cut in shards[1:]:
        factor_of = factor_of * one(*cut)
    return factor_of


def scatter_about(own_key, extent, deviation, limit, cuts=(), kind=jnp.bfloat16):
    loudness = block_levels(own_key, extent, cuts, -0.22, 0.18) if cuts else 1.0
    drawn = jax.random.normal(own_key, extent, jnp.float32) * deviation * loudness
    return jnp.minimum(jnp.maximum(drawn, -limit), limit).astype(kind)


def setup_inputs(seed: int = 0) -> dict:
    key_list = jax.random.split(jax.random.key(seed), 16)
    hidden = scatter_about(key_list[0], (GROUPS, GROUP_TOKENS, D), 1.0, 6.0, ((0, 16), (1, 2)))
    frames = scatter_about(key_list[1], (GROUPS, FRAMES, D), 1.0, 6.0, ((0, 16), (2, 2)))
    segment = draw_segment(jax.random.fold_in(key_list[15], 71), 0)
    cotangent = draw_cotangent(jax.random.fold_in(key_list[15], 71), 0)
    norm_gain = jnp.clip(1.0 + 0.1 * jax.random.normal(key_list[4], (4, D), jnp.float32), 0.5, 1.5)
    norm_bias = scatter_about(key_list[5], (4, D), 0.2, 1.2, ((1, 2),), jnp.float32)
    self_qkv = scatter_about(key_list[6], (D, 3 * D), D ** -0.5, 0.21875, ((0, 2),), jnp.float32)
    self_out = scatter_about(key_list[7], (D, D), (max(D // 48, 8)) ** -0.5, 1.5, ((0, 2),), jnp.float32)
    cross_q = scatter_about(key_list[8], (D, D), D ** -0.5, 0.21875, ((0, 2),), jnp.float32)
    cross_kv = scatter_about(key_list[9], (D, 2 * D), D ** -0.5, 0.21875, ((1, 2),), jnp.float32)
    cross_out = scatter_about(key_list[10], (D, D), (max(D // 48, 8)) ** -0.5, 1.5, ((0, 2),), jnp.float32)
    fc1 = scatter_about(key_list[11], (D, FF), D ** -0.5, 0.21875, ((0, 2),), jnp.float32)
    fc2 = scatter_about(key_list[12], (FF, D), FF ** -0.5, 0.109375, ((0, 2),), jnp.float32)
    proj_bias = scatter_about(key_list[13], (7, D), 0.2, 1.2, ((1, 2),), jnp.float32)
    fc1_bias = scatter_about(key_list[14], (FF,), 0.2, 1.2, ((0, 2),), jnp.float32)
    return {"hidden": hidden, "frames": frames, "segment": segment, "cotangent": cotangent, "norm_gain": norm_gain, "norm_bias": norm_bias, "self_qkv": self_qkv, "self_out": self_out, "cross_q": cross_q, "cross_kv": cross_kv, "cross_out": cross_out, "fc1": fc1, "fc2": fc2, "proj_bias": proj_bias, "fc1_bias": fc1_bias}


EPSILON = 1e-05
NEGATIVE = -1e+30
HIGHEST = lax.Precision.HIGHEST

@jax.custom_vjp
def low(v):
    return lax.optimization_barrier(v.astype(jnp.bfloat16)).astype(jnp.float32)

@jax.custom_vjp
def low_back(v):
    return v

def low_keep(v):
    return (low(v), None)

def low_pass(kept, grad):
    return (grad,)

def back_keep(v):
    return (v, None)

def back_low(kept, grad):
    return (low(grad),)
low.defvjp(low_keep, low_pass)
low_back.defvjp(back_keep, back_low)

def both_ways(values):
    return low(low_back(values))

def matmul(first_matrix, second_matrix):
    return jnp.dot(first_matrix, second_matrix, precision=HIGHEST)

def layer_norm(hidden_rows, gain_row, shift_row):
    centered = hidden_rows - lax.optimization_barrier(jnp.mean(hidden_rows, axis=-1, keepdims=True))
    variance = lax.optimization_barrier(jnp.mean(centered * centered, axis=-1, keepdims=True))
    return centered * lax.rsqrt(variance + EPSILON) * gain_row + shift_row

def attention(queries, key_rows, value_rows, segment_ids, causal):
    query_count = queries.shape[0]
    key_count = key_rows.shape[0]
    block_rows = min(512, query_count)
    blocks = query_count // block_rows
    query_blocks = queries.reshape(blocks, block_rows, HEADS, HDIM)
    key_heads = key_rows.reshape(key_count, HEADS, HDIM)
    value_heads = value_rows.reshape(key_count, HEADS, HDIM)
    starts = jnp.arange(blocks, dtype=jnp.int32) * block_rows

    def one_block(block_pair):
        query_block, start_row = block_pair
        scores = jnp.einsum('qhd,khd->hqk', query_block, key_heads, precision=HIGHEST) * HDIM ** (-0.5)
        scores = low_back(scores)
        if causal:
            query_pos = start_row + jnp.arange(block_rows, dtype=jnp.int32)
            key_pos = jnp.arange(key_count, dtype=jnp.int32)
            query_seg = lax.dynamic_slice_in_dim(segment_ids, start_row, block_rows)
            allowed = (key_pos[None, :] <= query_pos[:, None]) & ((segment_ids[None, :] == query_seg[:, None]) | (segment_ids[None, :] == 0))
            scores = jnp.where(allowed[None], scores, NEGATIVE)
        soft_weights = low(jax.nn.softmax(scores, axis=-1))
        mixed_heads = jnp.einsum('hqk,khd->qhd', soft_weights, value_heads, precision=HIGHEST)
        return mixed_heads.reshape(block_rows, HEADS * HDIM)
    result = lax.map(jax.checkpoint(one_block), (query_blocks, starts))
    return result.reshape(query_count, HEADS * HDIM)

def group_forward(hidden_rows, frame_rows, segment_ids, params):
    norm_gain, norm_bias, self_qkv, self_out, cross_q, cross_kv, cross_out, fc1, fc2, proj_bias, fc1_bias = params
    gain_rows = low(norm_gain)
    shifts = low(norm_bias)
    biases = low(proj_bias)
    model_width = gain_rows.shape[1]
    zeros_row = jnp.zeros((model_width,), jnp.float32)
    normed = layer_norm(hidden_rows, gain_rows[0], shifts[0])
    qkv_bias = jnp.concatenate([biases[0], zeros_row, biases[1]])
    projected = both_ways(matmul(low(normed), low(self_qkv)) + qkv_bias)
    context = attention(projected[:, :model_width], projected[:, model_width:2 * model_width], projected[:, 2 * model_width:], segment_ids, True)
    context = low(low_back(context))
    after_self = hidden_rows + low_back(matmul(context, low(self_out)) + biases[2])
    normed = layer_norm(after_self, gain_rows[1], shifts[1])
    cross_query = both_ways(matmul(low(normed), low(cross_q)) + biases[3])
    frame_kv = both_ways(matmul(low(frame_rows), low(cross_kv)) + jnp.concatenate([zeros_row, biases[4]]))
    context = attention(cross_query, frame_kv[:, :model_width], frame_kv[:, model_width:], segment_ids, False)
    context = low(low_back(context))
    after_cross = after_self + low_back(matmul(context, low(cross_out)) + biases[5])
    normed = layer_norm(after_cross, gain_rows[2], shifts[2])
    hidden_units = both_ways(matmul(low(normed), low(fc1)) + low(fc1_bias))
    activated = low(jax.nn.gelu(hidden_units, approximate=False))
    after_mlp = after_cross + low_back(matmul(activated, low(fc2)) + biases[6])
    return layer_norm(after_mlp, gain_rows[3], shifts[3])

def reference(hidden, frames, segment, cotangent, norm_gain, norm_bias, self_qkv, self_out, cross_q, cross_kv, cross_out, fc1, fc2, proj_bias, fc1_bias):
    params = (norm_gain, norm_bias, self_qkv, self_out, cross_q, cross_kv, cross_out, fc1, fc2, proj_bias, fc1_bias)

    def one_group(totals, group_data):
        hidden_rows, frame_rows, segment_ids, cot_rows = group_data

        def forward(rows_value, frames_value, weights):
            return group_forward(rows_value, frames_value, segment_ids, weights)
        result, pullback = jax.vjp(forward, hidden_rows.astype(jnp.float32), frame_rows.astype(jnp.float32), params)
        grad_rows, grad_frame_rows, grad_params = pullback(cot_rows.astype(jnp.float32))
        totals = jax.tree.map(lambda first_tree, second_tree: first_tree + second_tree, totals, grad_params)
        return (totals, (result.astype(jnp.bfloat16), grad_rows.astype(jnp.bfloat16), grad_frame_rows.astype(jnp.bfloat16)))
    initial = jax.tree.map(jnp.zeros_like, params)
    totals, (outputs, grad_hidden, grad_frames) = lax.scan(one_group, initial, (hidden, frames, segment, cotangent))
    return (outputs, grad_hidden, grad_frames, totals[0], totals[1], totals[2], totals[3], totals[4], totals[5], totals[6], totals[7], totals[8], totals[9], totals[10])
```

```python
import jax
import jax.numpy as jnp
import numpy as np
from jax import lax
from jax.experimental import pallas as pl
from jax.experimental.pallas import tpu as pltpu
from jax.sharding import Mesh
from jax.sharding import PartitionSpec as P

HEADS = 12
HD = 64
EPSILON = 1e-05
NEG = -1e30
PROMPT = 1024
REACH = 256
bf16 = jnp.bfloat16
f32 = jnp.float32

def _nt(a,b): return lax.dot_general(a,b,(((1,),(1,)),((),())),preferred_element_type=f32)
def _nn(a,b): return lax.dot_general(a,b,(((1,),(0,)),((),())),preferred_element_type=f32)

def cross_fwd(q,k,v,valid,qb=1024):
    tq,width=q.shape; tk=k.shape[0]; pairs=width//128
    qb=min(qb,tq)
    def kern(q_ref,k_ref,v_ref,o_ref,l_ref,ks,vts):
        @pl.when(pl.program_id(1)==0)
        def _():
            low=lax.broadcasted_iota(jnp.int32,(tk,128),1)
            row=lax.broadcasted_iota(jnp.int32,(tk,128),0)
            kk=k_ref[...]
            bias=jnp.where(row>=valid,NEG,0.0).astype(bf16)
            ks[0]=jnp.where(low<HD,kk,bias)
            ks[1]=jnp.where(low>=HD,kk,bias)
            vv=v_ref[...]
            one=jnp.ones((tk,128),bf16)
            vts[0]=jnp.where(low<HD,vv,one).T
            vts[1]=jnp.where(low>=HD,vv,one).T
        lane=lax.broadcasted_iota(jnp.int32,(qb,128),1)
        qq=q_ref[...]*bf16(0.125)
        outs=[]
        scores=[]
        for h in range(2):
            mine=(lane<HD) if h==0 else (lane>=HD)
            inj=(lane==HD) if h==0 else (lane==0)
            qh=jnp.where(mine,qq,jnp.where(inj,1.0,0.0).astype(bf16))
            scores.append(_nt(ks[h],qh))
        for h,s in enumerate(scores):
            m=jnp.max(s,axis=0,keepdims=True)
            p=jnp.exp(s-m).astype(bf16)
            o=_nn(vts[h],p)
            tot=o[HD:HD+1] if h==0 else o[0:1]
            outs.append(o*(1.0/tot))
            l_ref[0,h:h+1,:]=m+jnp.log(tot)
        sub=lax.broadcasted_iota(jnp.int32,(128,qb),0)
        o_ref[...]=jnp.where(sub<HD,outs[0],outs[1]).T.astype(bf16)
    return pl.pallas_call(kern,grid=(pairs,tq//qb),
        in_specs=[pl.BlockSpec((qb,128),lambda p,i:(i,p)),pl.BlockSpec((tk,128),lambda p,i:(0,p)),pl.BlockSpec((tk,128),lambda p,i:(0,p))],
        out_specs=[pl.BlockSpec((qb,128),lambda p,i:(i,p)),pl.BlockSpec((1,8,qb),lambda p,i:(p,0,i))],
        out_shape=[jax.ShapeDtypeStruct((tq,width),bf16),jax.ShapeDtypeStruct((pairs,8,tq),f32)],
        scratch_shapes=[pltpu.VMEM((2,tk,128),bf16),pltpu.VMEM((2,128,tk),bf16)],
        compiler_params=pltpu.CompilerParams(vmem_limit_bytes=58*2**20))(q,k,v)

def delta_of(do,o,rows):
    x=do.astype(f32)*o.astype(f32)
    hi=x.astype(bf16); lo=(x-hi.astype(f32)).astype(bf16)
    r=lax.broadcasted_iota(jnp.int32,(8,128),0); c=lax.broadcasted_iota(jnp.int32,(8,128),1)
    pick=jnp.where((c//HD)==r,1.0,0.0).astype(bf16)
    return _nt(pick,hi)+_nt(pick,lo)

def cross_bwd(q,k,v,o,do,lse,valid,qb=1024):
    tq,width=q.shape; tk=k.shape[0]; pairs=width//128
    qb=min(qb,tq); nq=tq//qb
    def kern(q_ref,k_ref,v_ref,o_ref,do_ref,l_ref,dq_ref,dk_ref,dv_ref,ks,kts,dka,dva):
        i=pl.program_id(1)
        @pl.when(i==0)
        def _():
            low=lax.broadcasted_iota(jnp.int32,(tk,128),1)
            row=lax.broadcasted_iota(jnp.int32,(tk,128),0)
            kk=k_ref[...]
            bias=jnp.where(row>=valid,NEG,0.0).astype(bf16)
            ks[0]=jnp.where(low<HD,kk,bias)
            ks[1]=jnp.where(low>=HD,kk,bias)
            zero=jnp.zeros((tk,128),bf16)
            kts[0]=jnp.where(low<HD,kk,zero).T
            kts[1]=jnp.where(low>=HD,kk,zero).T
            dka[...]=jnp.zeros((tk,128),f32)
            dva[...]=jnp.zeros((tk,128),f32)
        lane=lax.broadcasted_iota(jnp.int32,(qb,128),1)
        qq=q_ref[...]*bf16(0.125)
        dd=do_ref[...]
        delta=delta_of(dd,o_ref[...],8)
        dqt=None; dk=dka[...]; dv=dva[...]
        for h in range(2):
            mine=(lane<HD) if h==0 else (lane>=HD)
            inj=(lane==HD) if h==0 else (lane==0)
            zero=jnp.zeros((qb,128),bf16)
            qc=jnp.where(mine,qq,zero)
            qs=jnp.where(inj,jnp.ones((qb,128),bf16),qc)
            dh=jnp.where(mine,dd,zero)
            s=_nt(ks[h],qs)
            p=jnp.exp(s-l_ref[0,h:h+1,:])
            dp=_nt(v_ref[...],dh)
            ds=(p*(dp-delta[h:h+1])).astype(bf16)
            dv=dv+_nn(p.astype(bf16),dh)
            dk=dk+_nn(ds,qc)
            t=_nn(kts[h],ds)
            dqt=t if dqt is None else dqt+t
        dka[...]=dk; dva[...]=dv
        dq_ref[...]=(dqt*0.125).T.astype(bf16)
        @pl.when(i==nq-1)
        def _():
            dk_ref[...]=dka[...].astype(bf16); dv_ref[...]=dva[...].astype(bf16)
    qs=pl.BlockSpec((qb,128),lambda p,i:(i,p)); kspec=pl.BlockSpec((tk,128),lambda p,i:(0,p))
    return pl.pallas_call(kern,grid=(pairs,nq),
        in_specs=[qs,kspec,kspec,qs,qs,pl.BlockSpec((1,8,qb),lambda p,i:(p,0,i))],
        out_specs=[qs,kspec,kspec],
        out_shape=[jax.ShapeDtypeStruct((tq,width),bf16),jax.ShapeDtypeStruct((tk,width),bf16),jax.ShapeDtypeStruct((tk,width),bf16)],
        scratch_shapes=[pltpu.VMEM((2,tk,128),bf16),pltpu.VMEM((2,128,tk),bf16),pltpu.VMEM((tk,128),f32),pltpu.VMEM((tk,128),f32)],
        compiler_params=pltpu.CompilerParams(vmem_limit_bytes=58*2**20))(q,k,v,o,do,lse)

def spans(r0,qb,prompt,reach):
    if r0<prompt: out=[(0,r0)] if r0 else []
    else:
        left=max(prompt,r0-reach)
        out=[(0,r0)] if left==prompt and r0>prompt else [(0,prompt)]
        if left>prompt: out.append((left,r0))
    return out,(r0,r0+qb)

def seg_marks(seg):
    lane=lax.broadcasted_iota(jnp.int32,(seg.shape[0],128),1)%HD
    same=lane==seg[:,None]
    kmark=jnp.where(same,1.0,0.0).astype(bf16)
    qmark=jnp.where(same|(lane==0)|(lane>8),0.0,NEG).astype(bf16)
    return kmark,qmark

def part_specs(t):
    return [pl.BlockSpec((1,t,128),lambda p,j=j:(j,0,p)) for j in range(3)]

def self_fwd(qkv,kmark,qmark,prompt=PROMPT,reach=REACH,qb=512):
    _,t,width=qkv.shape; pairs=width//128
    blocks=[spans(r0,qb,prompt,reach)+(r0,) for r0 in range(0,t,qb)]
    def kern(q_ref,k_ref,v_ref,km_ref,qm_ref,o_ref,l_ref,ks,vts):
        low=lax.broadcasted_iota(jnp.int32,(t,128),1)
        kk=k_ref[0]; vv=v_ref[0]; km=km_ref[...]
        one=jnp.ones((t,128),bf16)
        ks[0]=jnp.where(low<HD,kk,km); ks[1]=jnp.where(low>=HD,kk,km)
        vts[0]=jnp.where(low<HD,vv,one).T; vts[1]=jnp.where(low>=HD,vv,one).T
        lane=lax.broadcasted_iota(jnp.int32,(qb,128),1)
        hide=lax.broadcasted_iota(jnp.int32,(qb,qb),0)>lax.broadcasted_iota(jnp.int32,(qb,qb),1)
        tasks=[(b,h) for b in blocks for h in range(2)]
        def scores(task):
            (before,own,r0),h=task
            mine=(lane<HD) if h==0 else (lane>=HD)
            qs=jnp.where(mine,q_ref[0,pl.ds(r0,qb),:]*bf16(0.125),qm_ref[pl.ds(r0,qb),:])
            out=[_nt(ks[h,pl.ds(a,b-a),:],qs) for a,b in before]
            out.append(jnp.where(hide,NEG,_nt(ks[h,pl.ds(r0,qb),:],qs)))
            return out
        cur=scores(tasks[0]); res=[None,None]
        for i,task in enumerate(tasks):
            nxt=scores(tasks[i+1]) if i+1<len(tasks) else None
            (before,own,r0),h=task
            m=None
            for s in cur:
                x=jnp.max(s,axis=0,keepdims=True); m=x if m is None else jnp.maximum(m,x)
            o=None
            for s,(a,b) in zip(cur,before+[own]):
                y=_nn(vts[h,:,pl.ds(a,b-a)],jnp.exp(s-m).astype(bf16)); o=y if o is None else o+y
            tot=o[HD:HD+1] if h==0 else o[0:1]
            l_ref[0,h:h+1,pl.ds(r0,qb)]=m+jnp.log(tot)
            res[h]=o*(1.0/tot)
            if h==1:
                sub=lax.broadcasted_iota(jnp.int32,(128,qb),0)
                o_ref[pl.ds(r0,qb),:]=jnp.where(sub<HD,res[0],res[1]).T.astype(bf16)
            cur=nxt
    spec=pl.BlockSpec((t,128),lambda p:(0,p)); whole=pl.BlockSpec((t,128),lambda p:(0,0))
    return pl.pallas_call(kern,grid=(pairs,),in_specs=part_specs(t)+[whole,whole],
        out_specs=[spec,pl.BlockSpec((1,8,t),lambda p:(p,0,0))],
        out_shape=[jax.ShapeDtypeStruct((t,width),bf16),jax.ShapeDtypeStruct((pairs,8,t),f32)],
        scratch_shapes=[pltpu.VMEM((2,t,128),bf16),pltpu.VMEM((2,128,t),bf16)],
        compiler_params=pltpu.CompilerParams(vmem_limit_bytes=58*2**20))(qkv,qkv,qkv,kmark,qmark)

def self_bwd(qkv,o,do,lse,kmark,qmark,prompt=PROMPT,reach=REACH,qb=256):
    _,t,width=qkv.shape; pairs=width//128
    blocks=[spans(r0,qb,prompt,reach)+(r0,) for r0 in range(0,t,qb)]
    def kern(q_ref,k_ref,v_ref,o_ref,do_ref,l_ref,km_ref,qm_ref,d_ref,ks,kts,dka,dva):
        low=lax.broadcasted_iota(jnp.int32,(t,128),1)
        kk=k_ref[0]; km=km_ref[...]
        zero=jnp.zeros((t,128),bf16)
        ks[0]=jnp.where(low<HD,kk,km); ks[1]=jnp.where(low>=HD,kk,km)
        kts[0]=jnp.where(low<HD,kk,zero).T; kts[1]=jnp.where(low>=HD,kk,zero).T
        dka[...]=jnp.zeros((t,128),f32); dva[...]=jnp.zeros((t,128),f32)
        lane=lax.broadcasted_iota(jnp.int32,(qb,128),1)
        hide=lax.broadcasted_iota(jnp.int32,(qb,qb),0)>lax.broadcasted_iota(jnp.int32,(qb,qb),1)
        for before,own,r0 in blocks:
            rows=pl.ds(r0,qb)
            qq=q_ref[0,rows,:]*bf16(0.125); dd=do_ref[rows,:]; qm=qm_ref[rows,:]
            delta=delta_of(dd,o_ref[rows,:],8)
            dqt=None
            zq=jnp.zeros((qb,128),bf16)
            for h in range(2):
                mine=(lane<HD) if h==0 else (lane>=HD)
                qc=jnp.where(mine,qq,zq); qs=jnp.where(mine,qq,qm); dh=jnp.where(mine,dd,zq)
                lrow=l_ref[0,h:h+1,pl.ds(r0,qb)]
                for a,b in before+[own]:
                    keys=pl.ds(a,b-a)
                    s=_nt(ks[h,keys,:],qs)
                    if a==r0: s=jnp.where(hide,NEG,s)
                    p=jnp.exp(s-lrow)
                    dp=_nt(v_ref[0,keys,:],dh)
                    ds=(p*(dp-delta[h:h+1])).astype(bf16)
                    dva[keys,:]+=_nn(p.astype(bf16),dh)
                    dka[keys,:]+=_nn(ds,qc)
                    y=_nn(kts[h,:,keys],ds); dqt=y if dqt is None else dqt+y
            d_ref[0,rows,:]=(dqt*0.125).T.astype(bf16)
        d_ref[1]=dka[...].astype(bf16); d_ref[2]=dva[...].astype(bf16)
    spec=pl.BlockSpec((t,128),lambda p:(0,p)); whole=pl.BlockSpec((t,128),lambda p:(0,0))
    return pl.pallas_call(kern,grid=(pairs,),in_specs=part_specs(t)+[spec]*2+[pl.BlockSpec((1,8,t),lambda p:(p,0,0)),whole,whole],
        out_specs=pl.BlockSpec((3,t,128),lambda p:(0,0,p)),out_shape=jax.ShapeDtypeStruct((3,t,width),bf16),
        scratch_shapes=[pltpu.VMEM((2,t,128),bf16),pltpu.VMEM((2,128,t),bf16),pltpu.VMEM((t,128),f32),pltpu.VMEM((t,128),f32)],
        compiler_params=pltpu.CompilerParams(vmem_limit_bytes=58*2**20))(qkv,qkv,qkv,o,do,lse,kmark,qmark)


def norm_stats(rows):
    centered = rows - jnp.mean(rows, axis=-1, keepdims=True)
    inv = lax.rsqrt(jnp.mean(centered * centered, axis=-1, keepdims=True) + EPSILON)
    return centered * inv, inv


def norm(rows, gain, shift):
    return norm_stats(rows)[0] * gain + shift


def norm_back(rows, gain, dy):
    n, inv = norm_stats(rows)
    dn = dy * gain
    dh = inv * (dn - jnp.mean(dn, axis=-1, keepdims=True) - n * jnp.mean(dn * n, axis=-1, keepdims=True))
    return dh, jnp.sum(dy * n, axis=0), jnp.sum(dy, axis=0)


def mm(a, b):
    return jnp.dot(a, b, preferred_element_type=f32)


def mm_t(a, b):
    return lax.dot_general(a, b, (((1,), (1,)), ((), ())), preferred_element_type=f32)


def t_mm(a, b):
    return lax.dot_general(a, b, (((0,), (0,)), ((), ())), preferred_element_type=f32)


def gelu_parts(u):
    phi = jnp.exp(-0.5 * u * u) * 0.3989422804014327
    return 0.5 * lax.erfc(-u * 0.7071067811865476), phi


GROUP = ("core", "ilo")
SHARD = ("ihi", "ilo")
REP = ("rz", "core")
SPREAD = ("ihi", "ilo", "rz", "core")
FLIP = [(0, 1), (1, 0)]


def body(hidden, frames, segment, cotangent, norm_gain, norm_bias, self_qkv, self_out, cross_q, cross_kv, cross_out, fc1, fc2, proj_bias, fc1_bias):
    c = lax.axis_index("core")
    hi = lax.axis_index("ihi")
    n = lax.axis_size("core") * lax.axis_size("ilo")
    reps = lax.axis_size("rz") * lax.axis_size("core")
    rep_at = lax.axis_index(REP)
    width = self_out.shape[1]
    ff = fc1.shape[1]

    def swap(x):
        return lax.ppermute(x, ("core", "ihi"), [(0, 0), (1, 2), (2, 1), (3, 3)])

    def whole(own):
        if n != 2:
            return lax.all_gather(own, SHARD, axis=0, tiled=True)
        half = own.shape[0] // 2
        mine = lax.ppermute(lax.dynamic_slice_in_dim(own, c * half, half), "ihi", FLIP)
        sib = lax.ppermute(mine, "core", FLIP)
        other = jnp.where(c == 0, jnp.concatenate([mine, sib]), jnp.concatenate([sib, mine]))
        return jnp.where(hi == 0, jnp.concatenate([own, other]), jnp.concatenate([other, own]))

    def slices(own):
        rows = own.shape[0] // reps
        return lax.dynamic_slice_in_dim(own, rep_at * rows, rows)

    rows_in = swap(hidden[0])
    qkv_w = whole(self_qkv.astype(bf16))
    small = jnp.concatenate([norm_gain.astype(bf16), norm_bias.astype(bf16), proj_bias.astype(bf16), fc1_bias.astype(bf16).reshape(-1, norm_gain.shape[1]), jnp.zeros((1, norm_gain.shape[1]), bf16)])
    small = lax.all_gather(small, SHARD, axis=1, tiled=False).astype(f32)
    table = small[:15].reshape(15, width)
    gains, shifts, biases = table[:4], table[4:8], table[8:15]
    fc1_shift = small[15:19].transpose(1, 0, 2).reshape(ff)
    seg = swap(segment)[0]
    frames_half = swap(frames[0])
    if n == 2:
        twin = lax.ppermute(frames_half, "core", FLIP)
        frame_rows = jnp.concatenate([jnp.where(c == 0, frames_half, twin), jnp.where(c == 0, twin, frames_half)], axis=1)
    else:
        frame_rows = lax.all_gather(frames_half, GROUP, axis=1, tiled=True)
    selfout_w = whole(self_out.astype(bf16))
    crossq_w = whole(cross_q.astype(bf16))
    kv_w = whole(cross_kv.astype(bf16)) if n == 2 else None
    if n == 2:
        k_w, v_w = kv_w[:width], kv_w[width:]
    else:
        kv_w = lax.all_gather(cross_kv.astype(bf16), SHARD, axis=1, tiled=True)
        k_w, v_w = kv_w[:, :width], kv_w[:, width:]
    crossout_w = whole(cross_out.astype(bf16))
    cot = swap(cotangent[0])
    units = ff // width
    part1 = slices(fc1.astype(bf16))
    part2 = slices(fc2.astype(bf16))
    few = part1.shape[0]
    parts = jnp.concatenate([part1[:, j * width : (j + 1) * width] for j in range(units)] + [part2])
    ffw = lax.all_gather(parts, SPREAD, axis=0, tiled=False)
    fc1_w = jnp.concatenate([ffw[:, j * few : (j + 1) * few].reshape(width, width) for j in range(units)], axis=1)
    fc2_w = ffw[:, units * few :].reshape(ff, width)

    own_rows = rows_in.shape[0]
    hw = -(-HEADS // n)
    padded = hw * n * HD - width

    lanes = hw * HD

    def to_heads(x):
        x = x.reshape(own_rows, -1, width)
        if padded:
            x = jnp.pad(x, ((0, 0), (0, 0), (0, padded)))
        x = x.reshape(own_rows, -1, n, lanes).transpose(1, 2, 0, 3)
        x = lax.all_to_all(x, GROUP, 1, 1, tiled=True)
        return x.reshape(-1, n * own_rows, lanes)

    def to_tokens(x):
        x = lax.all_to_all(x.reshape(-1, n, own_rows, lanes), GROUP, 1, 1, tiled=True)
        return x.transpose(2, 0, 1, 3).reshape(own_rows, -1, n * lanes)[:, :, :width].reshape(own_rows, -1)

    h0 = rows_in.astype(f32)
    a1 = norm(h0, gains[0], shifts[0]).astype(bf16)
    zeros_row = jnp.zeros((width,), f32)
    qkv = (mm(a1, qkv_w) + jnp.concatenate([biases[0], zeros_row, biases[1]])).astype(bf16)
    heads = to_heads(qkv)
    kmark, qmark = seg_marks(seg)
    ctx, self_lse = self_fwd(heads, kmark, qmark)
    c1 = to_tokens(ctx)
    h1 = h0 + mm(c1, selfout_w) + biases[2]
    a2 = norm(h1, gains[1], shifts[1]).astype(bf16)
    qc = (mm(a2, crossq_w) + biases[3]).astype(bf16)
    count = frame_rows.shape[0]
    pad = -count % 256
    frame_pad = jnp.pad(frame_rows, ((0, pad), (0, 0)))
    kc = mm(frame_pad, k_w).astype(bf16)
    live = lax.broadcasted_iota(jnp.int32, (count + pad, 1), 0) < count
    vc = (mm(frame_pad, v_w) + jnp.where(live, biases[4], 0.0)).astype(bf16)
    c2, cross_lse = cross_fwd(qc, kc, vc, count)
    h2 = h1 + mm(c2, crossout_w) + biases[5]
    a3 = norm(h2, gains[2], shifts[2]).astype(bf16)
    u = (mm(a3, fc1_w) + fc1_shift).astype(bf16)
    uf = u.astype(f32)
    cdf, pdf = gelu_parts(uf)
    g = (uf * cdf).astype(bf16)
    slope = (cdf + uf * pdf).astype(f32)
    h3 = h2 + mm(g, fc2_w) + biases[6]
    output = norm(h3, gains[3], shifts[3]).astype(bf16)
    output = swap(output)

    def total(x):
        return jnp.sum(x.astype(f32), axis=0)

    dh3, gain3, shift3 = norm_back(h3, gains[3], cot.astype(f32))
    dm = dh3.astype(bf16)
    g_fc2 = t_mm(g, dm).astype(bf16)
    du = (slope * mm_t(dm, fc2_w)).astype(bf16)
    g_fc1 = t_mm(a3, du).astype(bf16)

    def reduce_rows(parts, extra=None):
        total = n * reps
        cut = [p.reshape(total, -1, width) for p in parts]
        if extra is not None:
            cut.append(extra)
        flat = jnp.concatenate(cut, axis=1)
        mine = lax.psum_scatter(flat, SPREAD, scatter_dimension=0, tiled=False)
        got = lax.all_gather(mine, REP, axis=0, tiled=False)
        out, at = [], 0
        for p in cut:
            out.append(got[:, at : at + p.shape[1]].reshape(-1, width).astype(f32))
            at += p.shape[1]
        return out

    ff_grads = reduce_rows([g_fc1[:, j * width : (j + 1) * width] for j in range(units)] + [g_fc2])
    fc1_grad = jnp.concatenate(ff_grads[:units], axis=1)
    fc2_grad = ff_grads[units]

    da3 = mm_t(du, fc1_w)
    dres, gain2, shift2 = norm_back(h2, gains[2], da3)
    dh2 = dh3 + dres
    d2 = dh2.astype(bf16)
    g_crossout = t_mm(c2, d2).astype(bf16)
    dc2 = mm_t(d2, crossout_w).astype(bf16)
    dqc, dkc, dvc = cross_bwd(qc, kc, vc, c2, dc2, cross_lse, count)
    share = width // n

    def sum_columns(x):
        return lax.psum_scatter(x, GROUP, scatter_dimension=1, tiled=True)

    if n == 2:

        def sum_columns(x):
            give = lax.dynamic_slice_in_dim(x, (1 - c) * share, share, axis=1)
            keep = lax.dynamic_slice_in_dim(x, c * share, share, axis=1)
            return (keep.astype(f32) + lax.ppermute(give, "core", FLIP).astype(f32)).astype(bf16)

    dk_own = sum_columns(dkc)[:count]
    dv_own = sum_columns(dvc)[:count]
    place = lax.axis_index(GROUP) * share
    kw_own = lax.dynamic_slice_in_dim(k_w, place, share, axis=1)
    vw_own = lax.dynamic_slice_in_dim(v_w, place, share, axis=1)
    dframe = (mm_t(dk_own, kw_own) + mm_t(dv_own, vw_own)).astype(bf16)
    grad_frames = swap(sum_columns(dframe))
    g_k = t_mm(frame_rows, dk_own).astype(bf16)
    g_v = t_mm(frame_rows, dv_own).astype(bf16)
    vb_own = jnp.sum(dv_own.astype(f32), axis=0)

    g_crossq = t_mm(a2, dqc).astype(bf16)
    da2 = mm_t(dqc, crossq_w)
    dres, gain1, shift1 = norm_back(h1, gains[1], da2)
    dh1 = dh2 + dres
    d1 = dh1.astype(bf16)
    g_selfout = t_mm(c1, d1).astype(bf16)
    dctx = mm_t(d1, selfout_w).astype(bf16)
    dctx = to_heads(dctx)[0]
    dqkv = to_tokens(self_bwd(heads, ctx, dctx, self_lse, kmark, qmark))
    da1 = mm_t(dqkv, qkv_w)
    g_qkv = t_mm(a1, dqkv).astype(bf16)
    sums = total(dqkv)
    dres, gain0, shift0 = norm_back(h0, gains[0], da1)
    grad_hidden = swap((dh1 + dres).astype(bf16))

    vb = lax.dynamic_update_slice(jnp.zeros((width,), f32), vb_own, (place,))
    vectors = jnp.stack([gain0, gain1, gain2, gain3, shift0, shift1, shift2, shift3, sums[:width], sums[2 * width :], total(d1), total(dqc), vb, total(d2), total(dm)])
    per = width // n
    vectors = vectors.reshape(15, n, per).transpose(1, 0, 2).reshape(n, 15 * per)
    vectors = jnp.concatenate([vectors, total(du).reshape(n, ff // n)], axis=1)
    long = vectors.shape[1]
    seats = -(-long // reps)
    vectors = jnp.pad(vectors, ((0, 0), (0, seats * reps - long))).reshape(n * reps, seats)
    lines = -(-seats // (8 * width)) * 8
    vectors = jnp.pad(vectors, ((0, 0), (0, lines * width - seats))).reshape(n * reps, lines, width)

    def own_columns(x):
        return lax.dynamic_update_slice(jnp.zeros((x.shape[0], width), x.dtype), x, (jnp.int32(0), place))

    cross = [g_crossq, g_crossout]
    if n == 2:
        cross.append(jnp.concatenate([own_columns(g_k), own_columns(g_v)]))
    cross = reduce_rows(cross)
    crossq_grad, crossout_grad = cross[:2]
    if n == 2:
        kv_grad = cross[2]
    else:
        kv_cols = jnp.concatenate([own_columns(g_k), own_columns(g_v)], axis=1)
        kv_cols = lax.psum_scatter(kv_cols, SHARD, scatter_dimension=1, tiled=True)
        kv_grad = lax.psum(kv_cols, REP).astype(f32)
    got = reduce_rows([g_qkv[:, j * width : (j + 1) * width] for j in range(3)] + [g_selfout], vectors.astype(bf16))
    qkv_grad = jnp.concatenate(got[:3], axis=1)
    selfout_grad = got[3]
    vec = got[4].reshape(reps, lines * width)[:, :seats].reshape(-1)[:long]
    table = vec[: 15 * per].reshape(15, per)
    fc1b_grad = vec[15 * per :]
    return (
        output[None], grad_hidden[None], grad_frames[None],
        table[:4], table[4:8], qkv_grad, selfout_grad, crossq_grad, kv_grad, crossout_grad, fc1_grad, fc2_grad, table[8:15], fc1b_grad,
    )


def solution(mesh):
    reps, n = mesh.devices.shape
    work = Mesh(mesh.devices.reshape(reps // 2, 2, 2, n // 2), ("rz", "core", "ihi", "ilo"))
    rep, inner = ("rz", "core"), ("ihi", "ilo")
    rows, cols = P(inner, None), P(None, inner)
    tokens, features = P(rep, inner, None), P(rep, None, inner)
    weights = (cols, cols, rows, rows, rows, cols, rows, rows, rows, cols, P(inner))
    return jax.shard_map(
        body,
        mesh=work,
        in_specs=(tokens, features, P(rep, None), tokens) + weights,
        out_specs=(tokens, tokens, features) + weights,
        check_vma=False,
    )
```

```python
import math

import jax
import jax.numpy as jnp
from jax import lax
from jax.experimental import pallas as pl
from jax.experimental.pallas import tpu as pltpu
from jax.sharding import Mesh
from jax.sharding import PartitionSpec as P

HEADS = 12
HD = 64
EPSILON = 1e-05
NEG = -1e30
PROMPT = 1024
REACH = 256
bf16 = jnp.bfloat16
f32 = jnp.float32
FLIP = [(0, 1), (1, 0)]


def mm(a, b):
    return jnp.dot(a, b, preferred_element_type=f32)


def mm_t(a, b):
    return lax.dot_general(a, b, (((1,), (1,)), ((), ())), preferred_element_type=f32)


def t_mm(a, b):
    return lax.dot_general(a, b, (((0,), (0,)), ((), ())), preferred_element_type=f32)


def call(kernel, scalars, args, grid, in_specs, out_specs, out_shape, scratch=(), cost=None):
    spec = pltpu.PrefetchScalarGridSpec(
        num_scalar_prefetch=1, grid=grid, in_specs=in_specs, out_specs=out_specs, scratch_shapes=list(scratch)
    )
    estimate = None
    if cost is not None:
        estimate = pl.CostEstimate(flops=cost, bytes_accessed=1 << 20, transcendentals=0)
    return pl.pallas_call(
        kernel,
        grid_spec=spec,
        out_shape=out_shape,
        cost_estimate=estimate,
        compiler_params=pltpu.CompilerParams(vmem_limit_bytes=60 * 2**20),
    )(scalars, *args)


def shape(dims, kind=bf16):
    return jax.ShapeDtypeStruct(dims, kind)


def half_of(lane, h):
    return (lane < HD) if h == 0 else (lane >= HD)


def delta_of(do, o):
    x = do.astype(f32) * o.astype(f32)
    hi = x.astype(bf16)
    lo = (x - hi.astype(f32)).astype(bf16)
    r = lax.broadcasted_iota(jnp.int32, (8, 128), 0)
    lane = lax.broadcasted_iota(jnp.int32, (8, 128), 1)
    pick = jnp.where((lane // HD) == r, 1.0, 0.0).astype(bf16)
    return mm_t(pick, hi) + mm_t(pick, lo)


def cross_fwd(base, pairs, q, k, v, valid, block=1024):
    tq, tk = q.shape[0], k.shape[0]
    block = min(block, tq)

    def kernel(s_ref, q_ref, k_ref, v_ref, o_ref, l_ref, ks, vts):
        @pl.when(pl.program_id(1) == 0)
        def _():
            low = lax.broadcasted_iota(jnp.int32, (tk, 128), 1)
            row = lax.broadcasted_iota(jnp.int32, (tk, 128), 0)
            bias = jnp.where(row >= valid, NEG, 0.0).astype(bf16)
            one = jnp.ones((tk, 128), bf16)
            for h in range(2):
                ks[h] = jnp.where(half_of(low, h), k_ref[...], bias)
                vts[h] = jnp.where(half_of(low, h), v_ref[...], one).T

        lane = lax.broadcasted_iota(jnp.int32, (block, 128), 1)
        qq = q_ref[...] * bf16(0.125)
        scores = []
        for h in range(2):
            spare = lane == (HD if h == 0 else 0)
            qh = jnp.where(half_of(lane, h), qq, jnp.where(spare, 1.0, 0.0).astype(bf16))
            scores.append(mm_t(ks[h], qh))
        outs = []
        for h, s in enumerate(scores):
            m = jnp.max(s, axis=0, keepdims=True)
            o = mm(vts[h], jnp.exp(s - m).astype(bf16))
            total = o[HD : HD + 1] if h == 0 else o[0:1]
            outs.append(o * (1.0 / total))
            l_ref[0, h : h + 1, :] = m + jnp.log(total)
        sub = lax.broadcasted_iota(jnp.int32, (128, block), 0)
        o_ref[...] = jnp.where(sub < HD, outs[0], outs[1]).T.astype(bf16)

    qspec = pl.BlockSpec((block, 128), lambda p, i, s: (i, s[0] + p))
    kspec = pl.BlockSpec((tk, 128), lambda p, i, s: (0, s[0] + p))
    return call(
        kernel, jnp.reshape(base, (1,)).astype(jnp.int32), (q, k, v), (pairs, tq // block), [qspec, kspec, kspec],
        [pl.BlockSpec((block, 128), lambda p, i, s: (i, p)), pl.BlockSpec((1, 8, block), lambda p, i, s: (p, 0, i))],
        [shape((tq, pairs * 128)), shape((pairs, 8, tq), f32)],
        [pltpu.VMEM((2, tk, 128), bf16), pltpu.VMEM((2, 128, tk), bf16)],
        4 * tq * tk * 256 * pairs,
    )


def cross_bwd(base, pairs, q, k, v, o, do, lse, valid, block=1024):
    tq, tk = q.shape[0], k.shape[0]
    block = min(block, tq)
    steps = tq // block

    def kernel(s_ref, q_ref, k_ref, v_ref, o_ref, do_ref, l_ref, dq_ref, d_ref, ks, kts, dka, dva):
        @pl.when(pl.program_id(1) == 0)
        def _():
            low = lax.broadcasted_iota(jnp.int32, (tk, 128), 1)
            row = lax.broadcasted_iota(jnp.int32, (tk, 128), 0)
            bias = jnp.where(row >= valid, NEG, 0.0).astype(bf16)
            zero = jnp.zeros((tk, 128), bf16)
            for h in range(2):
                ks[h] = jnp.where(half_of(low, h), k_ref[...], bias)
                kts[h] = jnp.where(half_of(low, h), k_ref[...], zero).T
            dka[...] = jnp.zeros((tk, 128), f32)
            dva[...] = jnp.zeros((tk, 128), f32)

        lane = lax.broadcasted_iota(jnp.int32, (block, 128), 1)
        qq = q_ref[...] * bf16(0.125)
        dd = do_ref[...]
        delta = delta_of(dd, o_ref[...])
        zero = jnp.zeros((block, 128), bf16)
        dqt, dk, dv = None, dka[...], dva[...]
        for h in range(2):
            mine = half_of(lane, h)
            spare = lane == (HD if h == 0 else 0)
            qc = jnp.where(mine, qq, zero)
            qs = jnp.where(spare, jnp.ones((block, 128), bf16), qc)
            dh = jnp.where(mine, dd, zero)
            p = jnp.exp(mm_t(ks[h], qs) - l_ref[0, h : h + 1, :])
            ds = (p * (mm_t(v_ref[...], dh) - delta[h : h + 1])).astype(bf16)
            dv = dv + mm(p.astype(bf16), dh)
            dk = dk + mm(ds, qc)
            part = mm(kts[h], ds)
            dqt = part if dqt is None else dqt + part
        dka[...] = dk
        dva[...] = dv
        dq_ref[...] = (dqt * 0.125).T.astype(bf16)

        @pl.when(pl.program_id(1) == steps - 1)
        def _():
            d_ref[0] = dka[...].astype(bf16)
            d_ref[1] = dva[...].astype(bf16)

    mine = pl.BlockSpec((block, 128), lambda p, i, s: (i, p))
    qspec = pl.BlockSpec((block, 128), lambda p, i, s: (i, s[0] + p))
    kspec = pl.BlockSpec((tk, 128), lambda p, i, s: (0, s[0] + p))
    return call(
        kernel, jnp.reshape(base, (1,)).astype(jnp.int32), (q, k, v, o, do, lse), (pairs, steps),
        [qspec, kspec, kspec, mine, mine, pl.BlockSpec((1, 8, block), lambda p, i, s: (p, 0, i))],
        [mine, pl.BlockSpec((2, tk, 128), lambda p, i, s: (0, 0, p))],
        [shape((tq, pairs * 128)), shape((2, tk, pairs * 128))],
        [pltpu.VMEM((2, tk, 128), bf16), pltpu.VMEM((2, 128, tk), bf16), pltpu.VMEM((tk, 128), f32), pltpu.VMEM((tk, 128), f32)],
        2 * tq * tk * 10 * 256 * pairs,
    )


def spans(r0, block):
    if r0 < PROMPT:
        return ([(0, r0)] if r0 else []) + [(r0, r0 + block)]
    left = max(PROMPT, r0 - REACH)
    before = [(0, r0)] if left == PROMPT else [(0, PROMPT), (left, r0)]
    return before + [(r0, r0 + block)]


def seg_marks(seg):
    lane = lax.broadcasted_iota(jnp.int32, (seg.shape[0], 128), 1) % HD
    same = lane == seg[:, None]
    kmark = jnp.where(same, 1.0, 0.0).astype(bf16)
    qmark = jnp.where(same | (lane == 0) | (lane > 8), 0.0, NEG).astype(bf16)
    return kmark, qmark


def half_specs(rows, first=0):
    return [pl.BlockSpec((3, rows, 128), lambda p, s: (0, 0, first + p))] * 2


def self_fwd(first, pairs, place, keep, recv, kmark, qmark, block=512):
    rows, width = keep.shape[1], pairs * 128
    t = 2 * rows

    def kernel(s_ref, a_ref, b_ref, km_ref, qm_ref, o_ref, give_ref, l_ref, qf, ks, vts):
        mine0 = pl.multiple_of(s_ref[0] * rows, rows)
        other0 = pl.multiple_of((1 - s_ref[0]) * rows, rows)
        low = lax.broadcasted_iota(jnp.int32, (rows, 128), 1)
        one = jnp.ones((rows, 128), bf16)
        for ref, at in ((a_ref, mine0), (b_ref, other0)):
            spot = pl.ds(at, rows)
            qf[spot, :] = ref[0] * bf16(0.125)
            for h in range(2):
                ks[h, spot, :] = jnp.where(half_of(low, h), ref[1], km_ref[spot, :])
                vts[h, :, spot] = jnp.where(half_of(low, h), ref[2], one).T
        lane = lax.broadcasted_iota(jnp.int32, (block, 128), 1)
        hide = lax.broadcasted_iota(jnp.int32, (block, block), 0) > lax.broadcasted_iota(jnp.int32, (block, block), 1)
        tasks = [(r0, h) for r0 in range(0, t, block) for h in range(2)]

        def scores(task):
            r0, h = task
            spot = pl.ds(r0, block)
            qs = jnp.where(half_of(lane, h), qf[spot, :], qm_ref[spot, :])
            out = [mm_t(ks[h, pl.ds(a, b - a), :], qs) for a, b in spans(r0, block)]
            out[-1] = jnp.where(hide, NEG, out[-1])
            return out

        now, outs = scores(tasks[0]), [None, None]
        for i, (r0, h) in enumerate(tasks):
            later = scores(tasks[i + 1]) if i + 1 < len(tasks) else None
            m = None
            for s in now:
                top = jnp.max(s, axis=0, keepdims=True)
                m = top if m is None else jnp.maximum(m, top)
            o = None
            for s, (a, b) in zip(now, spans(r0, block)):
                part = mm(vts[h, :, pl.ds(a, b - a)], jnp.exp(s - m).astype(bf16))
                o = part if o is None else o + part
            total = o[HD : HD + 1] if h == 0 else o[0:1]
            l_ref[0, h : h + 1, pl.ds(r0, block)] = m + jnp.log(total)
            outs[h] = o * (1.0 / total)
            if h == 1:
                sub = lax.broadcasted_iota(jnp.int32, (128, block), 0)
                o_ref[pl.ds(r0, block), :] = jnp.where(sub < HD, outs[0], outs[1]).T.astype(bf16)
            now = later
        give_ref[...] = o_ref[pl.ds(other0, rows), :]

    whole = pl.BlockSpec((t, 128), lambda p, s: (0, 0))
    return call(
        kernel, jnp.reshape(place, (1,)).astype(jnp.int32), (keep, recv, kmark, qmark), (pairs,),
        half_specs(rows, first) + [whole, whole],
        [pl.BlockSpec((t, 128), lambda p, s: (0, p)), pl.BlockSpec((rows, 128), lambda p, s: (0, p)), pl.BlockSpec((1, 8, t), lambda p, s: (p, 0, 0))],
        [shape((t, width)), shape((rows, width)), shape((pairs, 8, t), f32)],
        [pltpu.VMEM((t, 128), bf16), pltpu.VMEM((2, t, 128), bf16), pltpu.VMEM((2, 128, t), bf16)],
        2 * t * t * 4 * width,
    )


def self_bwd(first, pairs, place, keep, recv, o, dkeep, drecv, lse, kmark, qmark, block=256):
    rows, width = keep.shape[1], pairs * 128
    t = 2 * rows

    def kernel(s_ref, a_ref, b_ref, o_ref, da_ref, db_ref, l_ref, km_ref, qm_ref, give_ref, keep_ref, qf, df, vf, ks, kts, dqa, dka, dva):
        mine0 = pl.multiple_of(s_ref[0] * rows, rows)
        other0 = pl.multiple_of((1 - s_ref[0]) * rows, rows)
        low = lax.broadcasted_iota(jnp.int32, (rows, 128), 1)
        zero = jnp.zeros((rows, 128), bf16)
        for ref, dref, at in ((a_ref, da_ref, mine0), (b_ref, db_ref, other0)):
            spot = pl.ds(at, rows)
            qf[spot, :] = ref[0] * bf16(0.125)
            df[spot, :] = dref[...]
            vf[spot, :] = ref[2]
            for h in range(2):
                ks[h, spot, :] = jnp.where(half_of(low, h), ref[1], km_ref[spot, :])
                kts[h, :, spot] = jnp.where(half_of(low, h), ref[1], zero).T
        dka[...] = jnp.zeros((t, 128), f32)
        dva[...] = jnp.zeros((t, 128), f32)
        lane = lax.broadcasted_iota(jnp.int32, (block, 128), 1)
        hide = lax.broadcasted_iota(jnp.int32, (block, block), 0) > lax.broadcasted_iota(jnp.int32, (block, block), 1)
        none = jnp.zeros((block, 128), bf16)
        for r0 in range(0, t, block):
            spot = pl.ds(r0, block)
            dd = df[spot, :]
            delta = delta_of(dd, o_ref[spot, :])
            dqt = None
            for h in range(2):
                mine = half_of(lane, h)
                qc = jnp.where(mine, qf[spot, :], none)
                qs = jnp.where(mine, qf[spot, :], qm_ref[spot, :])
                dh = jnp.where(mine, dd, none)
                log_total = l_ref[0, h : h + 1, spot]
                for a, b in spans(r0, block):
                    keys = pl.ds(a, b - a)
                    s = mm_t(ks[h, keys, :], qs)
                    if a == r0:
                        s = jnp.where(hide, NEG, s)
                    p = jnp.exp(s - log_total)
                    ds = (p * (mm_t(vf[keys, :], dh) - delta[h : h + 1])).astype(bf16)
                    dva[keys, :] += mm(p.astype(bf16), dh)
                    dka[keys, :] += mm(ds, qc)
                    part = mm(kts[h, :, keys], ds)
                    dqt = part if dqt is None else dqt + part
            dqa[spot, :] = (dqt * 0.125).T.astype(bf16)
        for out, at in ((give_ref, other0), (keep_ref, mine0)):
            spot = pl.ds(at, rows)
            out[0] = dqa[spot, :]
            out[1] = dka[spot, :].astype(bf16)
            out[2] = dva[spot, :].astype(bf16)

    whole = pl.BlockSpec((t, 128), lambda p, s: (0, 0))
    half = pl.BlockSpec((rows, 128), lambda p, s: (0, first + p))
    return call(
        kernel, jnp.reshape(place, (1,)).astype(jnp.int32), (keep, recv, o, dkeep, drecv, lse, kmark, qmark), (pairs,),
        half_specs(rows, first) + [pl.BlockSpec((t, 128), lambda p, s: (0, p)), half, half, pl.BlockSpec((1, 8, t), lambda p, s: (p, 0, 0)), whole, whole],
        half_specs(rows),
        [shape((3, rows, width))] * 2,
        [pltpu.VMEM((t, 128), bf16)] * 3 + [pltpu.VMEM((2, t, 128), bf16), pltpu.VMEM((2, 128, t), bf16), pltpu.VMEM((t, 128), bf16)]
        + [pltpu.VMEM((t, 128), f32)] * 2,
        2 * t * t * 8 * width,
    )


def norm_stats(rows):
    centered = rows - jnp.mean(rows, axis=-1, keepdims=True)
    inv = lax.rsqrt(jnp.mean(centered * centered, axis=-1, keepdims=True) + EPSILON)
    return centered * inv, inv


def norm(rows, gain, shift):
    return norm_stats(rows)[0] * gain + shift


def norm_back(rows, gain, dy):
    n, inv = norm_stats(rows)
    dn = dy * gain
    dh = inv * (dn - jnp.mean(dn, axis=-1, keepdims=True) - n * jnp.mean(dn * n, axis=-1, keepdims=True))
    return dh, jnp.sum(dy * n, axis=0, keepdims=True), jnp.sum(dy, axis=0, keepdims=True)


ERFC = (
    0.22567585470008253, 0.22566975083164525, 0.20784161289369674, 0.1685452087610459, 0.14142852065437478,
    -0.005612938524279035, 0.1691005263450779, -0.1829144800497475, 0.05026606972001335,
)


def gelu_parts(u):
    bell = jnp.exp(u * u * -0.5)
    t = 1.0 / (1.0 + jnp.abs(u) * (0.4 * math.sqrt(0.5)))
    poly = jnp.full_like(t, ERFC[-1])
    for value in ERFC[-2::-1]:
        poly = poly * t + value
    tail = bell * t * poly * 0.5
    cdf = jnp.where(u < 0.0, tail, 1.0 - tail)
    return u * cdf, cdf + u * bell * (1.0 / math.sqrt(2.0 * math.pi))


def const(dims):
    return pl.BlockSpec(dims, lambda i, s: (0,) * len(dims))


def once(dims):
    return pl.BlockSpec(dims, lambda i, s: (0,) * len(dims), pipeline_mode=pl.Buffered(1))


def tile(rows, width):
    return pl.BlockSpec((rows, width), lambda i, s: (i, 0))


def fill(full, s, own, mine, sib):
    rows = own.shape[0]
    c, h = s[0], s[1]
    full[pl.ds(pl.multiple_of(h * rows, 128), rows), :] = own[...].astype(bf16)
    start = (1 - h) * rows
    full[pl.ds(pl.multiple_of(start + c * (rows // 2), 64), rows // 2), :] = mine[...]
    full[pl.ds(pl.multiple_of(start + (1 - c) * (rows // 2), 64), rows // 2), :] = sib[...]


def weight_specs(weight):
    own, mine, sib = weight
    return [once(own.shape), once(mine.shape), once(sib.shape)]


def full_shape(weight):
    return (2 * weight[0].shape[0], weight[0].shape[1])


def at_core(c, width):
    return pl.ds(pl.multiple_of(c * width, 128), width)


def norm_qkv(s, x_own, x_in, weight, table, rows=512):
    t, width = x_own.shape
    hw = width // 2

    def kernel(s_ref, xo, xi, own, mine, sib, tab, w, a_ref, keep, give):
        @pl.when(pl.program_id(0) == 0)
        def _():
            fill(w, s_ref, own, mine, sib)

        x = jnp.where(s_ref[2] == 1, xo[...].astype(f32), xi[...].astype(f32))
        a = norm(x, tab[0:1], tab[4:5]).astype(bf16)
        a_ref[...] = a
        for j in range(3):
            y = mm(a, w[:, j * width : (j + 1) * width])
            if j != 1:
                y = y + tab[8 + j // 2 : 9 + j // 2]
            low, high = y[:, :hw].astype(bf16), y[:, hw:].astype(bf16)
            first = s_ref[0] == 0
            keep[j] = jnp.where(first, low, high)
            give[j] = jnp.where(first, high, low)

    third = pl.BlockSpec((3, rows, hw), lambda i, s: (0, i, 0))
    dims = full_shape(weight)
    return call(
        kernel, s, (x_own, x_in, *weight, table), (t // rows,),
        [tile(rows, width)] * 2 + weight_specs(weight) + [const(table.shape)],
        [const(dims), tile(rows, width), third, third],
        [shape(dims), shape((t, width)), shape((3, t, hw)), shape((3, t, hw))],
        cost=2 * t * width * 3 * width,
    )


def beside(refs):
    return jnp.concatenate([ref[...] for ref in refs], axis=1) if len(refs) > 1 else refs[0][...]


def self_project(s, ctx, ctx_in, x_own, x_in, w_out, w_q, table, rows=512):
    t, width = x_own.shape
    hw = width // 2
    steps = t // rows
    n = len(ctx)

    def kernel(s_ref, *refs):
        cks, cis = refs[:n], refs[n : 2 * n]
        xo, xi, o1, o2, o3, q1, q2, q3, tab, wo, wq, h_ref, a_ref, qc_ref = refs[2 * n :]

        @pl.when(pl.program_id(0) == 0)
        def _():
            fill(wo, s_ref, o1, o2, o3)
            fill(wq, s_ref, q1, q2, q3)

        c = s_ref[0]
        x = jnp.where(s_ref[2] == 1, xo[...].astype(f32), xi[...].astype(f32))
        h = x + mm(beside(cks), wo[at_core(c, hw), :]) + mm(beside(cis), wo[at_core(1 - c, hw), :]) + tab[10:11]
        h_ref[...] = h
        a = norm(h, tab[1:2], tab[5:6]).astype(bf16)
        a_ref[...] = a
        qc_ref[...] = (mm(a, wq[...]) + tab[11:12]).astype(bf16)

    dims = full_shape(w_out)
    return call(
        kernel, s, (*ctx, *ctx_in, x_own, x_in, *w_out, *w_q, table), (steps,),
        [pl.BlockSpec((rows, part.shape[1]), lambda i, s: (s[0] * steps + i, 0)) for part in ctx]
        + [tile(rows, part.shape[1]) for part in ctx_in] + [tile(rows, width), tile(rows, width)]
        + weight_specs(w_out) + weight_specs(w_q) + [const(table.shape)],
        [const(dims), const(dims), tile(rows, width), tile(rows, width), tile(rows, width)],
        [shape(dims), shape(dims), shape((t, width), f32), shape((t, width)), shape((t, width))],
        cost=4 * t * width * width,
    )


def frame_kv(s, half, twin, weight, table, rows=512):
    count, hw = half.shape
    width = 2 * hw
    steps = -(-count // rows)

    def kernel(s_ref, fa, fb, own, mine, sib, tab, w, k_ref, v_ref):
        @pl.when(pl.program_id(0) == 0)
        def _():
            fill(w, s_ref, own, mine, sib)

        c = s_ref[0]
        live = lax.broadcasted_iota(jnp.int32, (rows, 1), 0) + pl.program_id(0) * rows < count
        for j, out in enumerate((k_ref, v_ref)):
            mine0 = pl.multiple_of(j * width + c * hw, 128)
            other0 = pl.multiple_of(j * width + (1 - c) * hw, 128)
            y = mm(fa[...], w[pl.ds(mine0, hw), :]) + mm(fb[...], w[pl.ds(other0, hw), :])
            if j == 1:
                y = y + tab[12:13]
            out[...] = jnp.where(live, y, 0.0).astype(bf16)

    dims = full_shape(weight)
    return call(
        kernel, s, (half, twin, *weight, table), (steps,),
        [tile(rows, hw)] * 2 + weight_specs(weight) + [const(table.shape)],
        [const(dims), tile(rows, width), tile(rows, width)],
        [shape(dims), shape((steps * rows, width)), shape((steps * rows, width))],
        cost=4 * count * width * width,
    )


def middle(s, h1, c2_keep, c2_give, cot_own, cot_in, w_out, ffw, table, fc1_shift, rows=256):
    t, width = h1.shape
    units = fc1_shift.shape[1] // width
    hw = width // 2
    piece = ffw.shape[2]

    def kernel(s_ref, h1_ref, ck_ref, cg_ref, co, ci, o1, o2, o3, w1, w2, tab, shift, wo, out, a_ref, g_ref, dm_ref, du_ref, d2_ref, dh_ref, dk_ref, dg_ref, vec):
        @pl.when(pl.program_id(0) == 0)
        def _():
            fill(wo, s_ref, o1, o2, o3)
            vec[...] = jnp.zeros(vec.shape, f32)

        def up(h, j):
            at, many = (h * units + j) * (hw // piece), hw // piece
            return w1[at : at + many, 0].reshape(hw, width)

        def down(j):
            many = width // piece
            return w2[j * many : (j + 1) * many, 0].reshape(width, width)

        c = s_ref[0]
        h2 = h1_ref[...] + mm(ck_ref[...], wo[at_core(c, hw), :]) + mm(cg_ref[...], wo[at_core(1 - c, hw), :]) + tab[13:14]
        n2, inv2 = norm_stats(h2)
        a = (n2 * tab[2:3] + tab[6:7]).astype(bf16)
        a_ref[...] = a
        acc = h2 + tab[14:15]
        slopes = []
        for j in range(units):
            cols = slice(j * width, (j + 1) * width)
            u = mm(a[:, :hw], up(0, j)) + mm(a[:, hw:], up(1, j)) + shift[:, cols]
            g, slope = gelu_parts(u.astype(bf16).astype(f32))
            slopes.append(slope)
            g = g.astype(bf16)
            g_ref[:, cols] = g
            acc = acc + mm(g, down(j))
        n3, inv3 = norm_stats(acc)
        out[...] = (n3 * tab[3:4] + tab[7:8]).astype(bf16)

        def back(n, inv, gain, dy):
            dn = dy * gain
            return inv * (dn - jnp.mean(dn, axis=-1, keepdims=True) - n * jnp.mean(dn * n, axis=-1, keepdims=True))

        def total(x):
            return jnp.sum(x, axis=0, keepdims=True)

        dy = jnp.where(s_ref[2] == 1, co[...].astype(f32), ci[...].astype(f32))
        dh3 = back(n3, inv3, tab[3:4], dy)
        dm = dh3.astype(bf16)
        dm_ref[...] = dm
        halves = [None, None]
        for j in range(units):
            cols = slice(j * width, (j + 1) * width)
            du = (slopes[j] * mm_t(dm, down(j))).astype(bf16)
            du_ref[:, cols] = du
            vec[0:1, cols] += total(du.astype(f32))
            for h in range(2):
                part = mm_t(du, up(h, j))
                halves[h] = part if halves[h] is None else halves[h] + part
        da = jnp.concatenate(halves, axis=1)
        dh2 = dh3 + back(n2, inv2, tab[2:3], da)
        d2 = dh2.astype(bf16)
        d2_ref[...] = d2
        dh_ref[...] = dh2
        dk_ref[...] = mm_t(d2, wo[at_core(c, hw), :]).astype(bf16)
        dg_ref[...] = mm_t(d2, wo[at_core(1 - c, hw), :]).astype(bf16)
        rows_of = [total(dm.astype(f32)), total(d2.astype(f32)), total(dy * n3), total(dy), total(da * n2), total(da)]
        for k, value in enumerate(rows_of):
            line, at = 1 + k // 3, (k % 3) * width
            vec[line : line + 1, at : at + width] += value

    dims = full_shape(w_out)
    ff = units * width
    line = tile(rows, width)
    wide, half = tile(rows, ff), tile(rows, hw)
    gathered = [pl.BlockSpec((32, 1, piece, width), lambda i, s, k=k: (0, k, 0, 0), pipeline_mode=pl.Buffered(1)) for k in range(2)]
    return call(
        kernel, s, (h1, c2_keep, c2_give, cot_own, cot_in, *w_out, ffw, ffw, table, fc1_shift), (t // rows,),
        [line, half, half, line, line] + weight_specs(w_out) + gathered + [const(table.shape), const(fc1_shift.shape)],
        [const(dims), line, line, wide, line, wide, line, line, half, half, const((8, ff))],
        [shape(dims), shape((t, width)), shape((t, width)), shape((t, ff)), shape((t, width)), shape((t, ff)), shape((t, width)),
         shape((t, width), f32), shape((t, hw)), shape((t, hw)), shape((8, ff), f32)],
        cost=8 * t * width * ff + 4 * t * width * width,
    )


def ff_grads(s, a, du, g, dm):
    t, width = a.shape
    hw = width // 2
    ff = du.shape[1]
    units = ff // width
    piece = hw * units // 16

    def kernel(s_ref, a_ref, du_ref, g_ref, dm_ref, out):
        step = pl.program_id(0)

        @pl.when(step < 2 * units)
        def _():
            out[...] = t_mm(a_ref[...], du_ref[...]).astype(bf16).reshape(out.shape)

        @pl.when(step >= 2 * units)
        def _():
            out[...] = t_mm(g_ref[...], dm_ref[...]).astype(bf16).reshape(out.shape)

    n1 = 2 * units
    many = hw // piece
    return call(
        kernel, s, (a, du, g, dm), (2 * n1,),
        [pl.BlockSpec((t, hw), lambda i, s: (0, jnp.minimum(i // units, 1))),
         pl.BlockSpec((t, width), lambda i, s: (0, jnp.where(i < n1, i % units, units - 1))),
         pl.BlockSpec((t, hw), lambda i, s: (0, jnp.maximum(i - n1, 0))),
         pl.BlockSpec((t, width), lambda i, s: (0, 0))],
        pl.BlockSpec((many, 1, piece, width), lambda i, s: (jnp.where(i < n1, i, i - n1), jnp.where(i < n1, 0, 1), 0, 0)),
        shape((32, 2, piece, width)),
        cost=4 * t * width * ff,
    )


def cross_back(s, dq_keep, dq_give, h1, dh2, w_q, w_out, table, rows=512):
    t, width = h1.shape
    hw = width // 2

    def kernel(s_ref, dk_ref, dg_ref, h_ref, dh2_ref, wq, wo, tab, dh_ref, d1_ref, keep, give, vec):
        @pl.when(pl.program_id(0) == 0)
        def _():
            vec[...] = jnp.zeros(vec.shape, f32)

        c = s_ref[0]
        da = mm_t(dk_ref[...], wq[:, at_core(c, hw)]) + mm_t(dg_ref[...], wq[:, at_core(1 - c, hw)])
        dres, dgain, dshift = norm_back(h_ref[...], tab[1:2], da)
        dh1 = dh2_ref[...] + dres
        dh_ref[...] = dh1
        d1 = dh1.astype(bf16)
        d1_ref[...] = d1
        keep[...] = mm_t(d1, wo[at_core(c, hw), :]).astype(bf16)
        give[...] = mm_t(d1, wo[at_core(1 - c, hw), :]).astype(bf16)
        vec[0:1] += dgain
        vec[1:2] += dshift
        vec[2:3] += jnp.sum(d1.astype(f32), axis=0, keepdims=True)
        vec[3:4, at_core(c, hw)] += jnp.sum(dk_ref[...].astype(f32), axis=0, keepdims=True)
        vec[3:4, at_core(1 - c, hw)] += jnp.sum(dg_ref[...].astype(f32), axis=0, keepdims=True)

    line, half = tile(rows, width), tile(rows, hw)
    return call(
        kernel, s, (dq_keep, dq_give, h1, dh2, w_q, w_out, table), (t // rows,),
        [half, half, line, line, once(w_q.shape), once(w_out.shape), const(table.shape)],
        [line, line, half, half, const((8, width))],
        [shape((t, width), f32), shape((t, width)), shape((t, hw)), shape((t, hw)), shape((8, width), f32)],
        cost=4 * t * width * width,
    )


def frame_back(s, keep, recv, half, twin, weight, rows=512):
    count, hw = half.shape
    width = 2 * hw
    steps = -(-count // rows)

    def kernel(s_ref, ka, kb, fa, fb, w, fkeep, fgive, xkeep, xgive, vec, acc):
        @pl.when(pl.program_id(0) == 0)
        def _():
            vec[...] = jnp.zeros(vec.shape, f32)
            acc[...] = jnp.zeros(acc.shape, f32)

        c, h = s_ref[0], s_ref[1]
        live = lax.broadcasted_iota(jnp.int32, (rows, 1), 0) + pl.program_id(0) * rows < count
        zero = jnp.zeros((rows, hw), bf16)
        f_mine = jnp.where(live, fa[...], zero)
        f_other = jnp.where(live, fb[...], zero)
        back = None
        for j in range(2):
            d = (ka[j].astype(f32) + kb[j].astype(f32)).astype(bf16)
            part = mm_t(d, w[j * width : (j + 1) * width, at_core(c, hw)])
            back = part if back is None else back + part
            acc[j, at_core(c, hw), :] += t_mm(f_mine, d)
            acc[j, at_core(1 - c, hw), :] += t_mm(f_other, d)
            if j == 1:
                vec[0:1] += jnp.sum(d.astype(f32), axis=0, keepdims=True)
        low, high = back[:, :hw].astype(bf16), back[:, hw:].astype(bf16)
        fkeep[...] = jnp.where(c == 0, low, high)
        fgive[...] = jnp.where(c == 0, high, low)

        @pl.when(pl.program_id(0) == steps - 1)
        def _():
            xkeep[...] = acc[h].astype(bf16)
            xgive[...] = acc[1 - h].astype(bf16)

    pair = pl.BlockSpec((2, rows, hw), lambda i, s: (0, i, 0))
    strip = tile(rows, hw)
    return call(
        kernel, s, (keep, recv, half, twin, weight), (steps,),
        [pair, pair, strip, strip, once(weight.shape)],
        [strip, strip, const((width, hw)), const((width, hw)), const((8, hw))],
        [shape((count, hw)), shape((count, hw)), shape((width, hw)), shape((width, hw)), shape((8, hw), f32)],
        [pltpu.VMEM((2, width, hw), f32)],
        cost=8 * count * width * width,
    )


def give_grads(s, c2_keep, c2_give, d2, a2, dq_give):
    t, width = d2.shape
    hw = width // 2

    def kernel(s_ref, k_ref, g_ref, d_ref, a_ref, q_ref, out):
        c = s_ref[0]
        out[0, at_core(c, hw), :] = t_mm(k_ref[...], d_ref[...]).astype(bf16)
        out[0, at_core(1 - c, hw), :] = t_mm(g_ref[...], d_ref[...]).astype(bf16)
        out[1] = t_mm(a_ref[...], q_ref[...]).astype(bf16)

    half = const((t, hw))
    return call(
        kernel, s, (c2_keep, c2_give, d2, a2, dq_give), (1,),
        [half, half, pl.BlockSpec((t, hw), lambda i, s: (0, 1 - s[0])), const((t, width)), half],
        const((2, width, hw)), shape((2, width, hw)), cost=4 * t * width * hw,
    )


def give_grad_out(s, ctx, ctx_in, d1):
    t, width = d1.shape
    hw = width // 2
    n = len(ctx)

    def kernel(s_ref, *refs):
        d_ref, out = refs[2 * n :]
        c = s_ref[0]
        out[at_core(c, hw), :] = t_mm(beside(refs[:n]), d_ref[...]).astype(bf16)
        out[at_core(1 - c, hw), :] = t_mm(beside(refs[n : 2 * n]), d_ref[...]).astype(bf16)

    return call(
        kernel, s, (*ctx, *ctx_in, d1), (1,),
        [pl.BlockSpec((t, part.shape[1]), lambda i, s: (s[0], 0)) for part in ctx] + [const(part.shape) for part in ctx_in]
        + [pl.BlockSpec((t, hw), lambda i, s: (0, 1 - s[0]))],
        const((width, hw)), shape((width, hw)), cost=2 * t * width * hw,
    )


def keep_grads(s, c2_keep, c2_give, d2, a2, dq_keep, ctx, ctx_in, d1, pair_in, out_in, kv_keep, kv_give):
    t, width = d2.shape
    hw = width // 2
    n = len(ctx)

    def kernel(s_ref, ck, cg, d2_ref, a_ref, q_ref, *refs):
        d1_ref, p_ref, o_ref, kk, kg, xgive, xkeep = refs[2 * n :]
        c, h = s_ref[0], s_ref[1]
        same = c == h
        for out, shard, kv in ((xgive, 1 - h, kg), (xkeep, h, kk)):
            rows = at_core(shard, hw)
            out[1] = (t_mm(a_ref[:, rows], q_ref[...]) + p_ref[1, rows, :].astype(f32)).astype(bf16)
            out[3] = kv[:hw]
            out[4] = kv[hw:]
        for k, lefts, right, extra in ((0, (ck[...], cg[...]), d2_ref, p_ref.at[0]), (2, (beside(refs[:n]), beside(refs[n : 2 * n])), d1_ref, o_ref)):
            own_rows = t_mm(lefts[0], right[...]) + extra[at_core(c, hw), :].astype(f32)
            far_rows = t_mm(lefts[1], right[...]) + extra[at_core(1 - c, hw), :].astype(f32)
            xkeep[k] = jnp.where(same, own_rows, far_rows).astype(bf16)
            xgive[k] = jnp.where(same, far_rows, own_rows).astype(bf16)

    cols, half = pl.BlockSpec((t, hw), lambda i, s: (0, s[0])), const((t, hw))
    five = (5, hw, hw)
    return call(
        kernel, s, (c2_keep, c2_give, d2, a2, dq_keep, *ctx, *ctx_in, d1, pair_in, out_in, kv_keep, kv_give), (1,),
        [half, half, cols, const((t, width)), half]
        + [pl.BlockSpec((t, part.shape[1]), lambda i, s: (s[0], 0)) for part in ctx] + [const(part.shape) for part in ctx_in]
        + [cols, const((2, width, hw)), const((width, hw)), const((width, hw)), const((width, hw))],
        [const(five), const(five)], [shape(five), shape(five)], cost=6 * t * width * hw,
    )


def split_y(s, keep, got):
    b, rows, cols = keep.shape
    half = rows // 2

    def kernel(s_ref, k_ref, g_ref, give, mine):
        for out, y in ((give, 1 - s_ref[4]), (mine, s_ref[4])):
            at = pl.ds(pl.multiple_of(y * half, 64), half)
            out[...] = (k_ref[:, at, :].astype(f32) + g_ref[:, at, :].astype(f32)).astype(bf16)

    dims = (b, half, cols)
    return call(kernel, s, (keep, got), (1,), [const(keep.shape)] * 2, [const(dims)] * 2, [shape(dims)] * 2)


def split_z(s, keep, got):
    b, rows, cols = keep.shape
    part = rows // 4

    def kernel(s_ref, k_ref, g_ref, *outs):
        for d, out in enumerate(outs):
            at = pl.ds(pl.multiple_of(s_ref[5 + d] * part, 16), part)
            out[...] = (k_ref[:, at, :].astype(f32) + g_ref[:, at, :].astype(f32)).astype(bf16)

    dims = (b, part, cols)
    return call(kernel, s, (keep, got), (1,), [const(keep.shape)] * 2, [const(dims)] * 4, [shape(dims)] * 4)


def sum_four(s, parts, vectors=()):
    b, part, cols = parts[0].shape

    def kernel(s_ref, p0, p1, p2, p3, *refs):
        out = refs[-1]
        total = (p0[...].astype(f32) + p1[...].astype(f32)) + (p2[...].astype(f32) + p3[...].astype(f32))
        out[0:b] = total.astype(bf16)
        if vectors:
            v = refs[0][...] + refs[1][...]
            high = v.astype(bf16).astype(f32)
            out[b] = jnp.concatenate([high, v - high], axis=0).astype(bf16)

    dims = (b + (1 if vectors else 0), part, cols)
    return call(
        kernel, s, (*parts, *vectors), (1,), [const(parts[0].shape)] * 4 + [const(v.shape) for v in vectors], const(dims), shape(dims)
    )


def pack_vectors(s, last, cross, mid, kv):
    width = last.shape[1]
    hw = width // 2
    units = mid.shape[1] // width

    def kernel(s_ref, l_ref, c_ref, m_ref, k_ref, give, mine):
        def line(ref, row, at=0):
            return ref[row : row + 1, at : at + width]

        zero = jnp.zeros((1, hw), f32)
        first = s_ref[0] == 0
        kv_row = jnp.concatenate([jnp.where(first, k_ref[0:1], zero), jnp.where(first, zero, k_ref[0:1])], axis=1)
        rows = [
            line(l_ref, 0), line(c_ref, 0), line(m_ref, 2, width), line(m_ref, 1, 2 * width),
            line(l_ref, 1), line(c_ref, 1), line(m_ref, 2, 2 * width), line(m_ref, 2),
            line(l_ref, 2), line(l_ref, 3), line(c_ref, 2), line(c_ref, 3), kv_row, line(m_ref, 1, width), line(m_ref, 1),
        ]
        halves = []
        for h in range(2):
            own = [row[:, h * hw : (h + 1) * hw] for row in rows]
            own += [m_ref[0:1, (h * units + j) * hw : (h * units + j + 1) * hw] for j in range(units)]
            halves.append(jnp.concatenate(own + [zero] * (24 - len(own)), axis=0))
        give[...] = jnp.where(s_ref[1] == 0, halves[1], halves[0])
        mine[...] = jnp.where(s_ref[1] == 0, halves[0], halves[1])

    return call(
        kernel, s, (last, cross, mid, kv), (1,), [const(x.shape) for x in (last, cross, mid, kv)],
        [const((24, hw))] * 2, [shape((24, hw), f32)] * 2,
    )


def join_z(s, parts):
    b, part, cols = parts[0].shape

    def kernel(s_ref, p0, p1, p2, p3, out):
        for d, ref in enumerate((p0, p1, p2, p3)):
            out[:, pl.ds(pl.multiple_of(s_ref[5 + d] * part, 16), part), :] = ref[...]

    dims = (b, 4 * part, cols)
    return call(kernel, s, parts, (1,), [const(parts[0].shape)] * 4, const(dims), shape(dims))


def spread_out(s, groups, outs, vectors=False):
    hw = 384

    def kernel(s_ref, *refs):
        results = refs[4 * len(groups) :]
        for n, (parts, spots) in enumerate(groups):
            b, half, cols = parts[0].shape
            for k, ref in enumerate(refs[4 * n : 4 * n + 4]):
                y = s_ref[4] if k % 2 == 0 else 1 - s_ref[4]
                core = s_ref[0] if k < 2 else 1 - s_ref[0]
                for block, (which, row, col) in enumerate(spots):
                    at_row = pl.multiple_of(row + y * half, 64)
                    at_col = pl.multiple_of(col + core * hw, 128)
                    results[which][pl.ds(at_row, half), pl.ds(at_col, cols)] = ref[block].astype(f32)
        if vectors:
            total = None
            for ref in refs[:4]:
                rows = ref[ref.shape[0] - 1].astype(f32)
                for z in range(4):
                    part = rows[48 * z : 48 * z + 48]
                    total = part if total is None else total + part
            results[-1][...] = total[0:24] + total[24:48]

    parts = [part for group, _ in groups for part in group]
    return call(kernel, s, parts, (1,), [const(part.shape) for part in parts], [const(d) for d in outs], [shape(d, f32) for d in outs])


def spread_ff(s, got):
    reps, _, per, width = got.shape
    units = 4
    rows = reps // units * per

    def kernel(s_ref, g_ref, one, two):
        one[...] = g_ref[:, 0].reshape(rows, width).astype(f32)
        two[...] = g_ref[:, 1].reshape(rows, width).astype(f32)

    return call(
        kernel, s, (got,), (units,), [pl.BlockSpec((reps // units, 2, per, width), lambda i, s: (i, 0, 0, 0))],
        [pl.BlockSpec((rows, width), lambda i, s: (0, i)), pl.BlockSpec((rows, width), lambda i, s: (i, 0))],
        [shape((rows, units * width), f32), shape((units * rows, width), f32)],
    )


def qkv_grad(s, a_own, a_sib, keep, give):
    t, width = a_own.shape
    hw = width // 2
    n = len(keep)

    def kernel(s_ref, ao, ai, *refs):
        xgive, xkeep = refs[2 * n :]
        k, g = (jnp.concatenate([ref[0] for ref in part], axis=1) for part in (refs[:n], refs[n : 2 * n]))
        for out, shard in ((xgive, 1 - s_ref[1]), (xkeep, s_ref[1])):
            rows = at_core(shard, hw)
            out[0] = (t_mm(ao[:, rows], k) + t_mm(ai[:, rows], g)).astype(bf16)

    out = pl.BlockSpec((1, hw, hw), lambda i, s: (i, 0, 0))
    return call(
        kernel, s, (a_own, a_sib, *keep, *give), (3,),
        [once((t, width)), once((t, width))] + [pl.BlockSpec((1, t, part.shape[2]), lambda i, s: (i, 0, 0)) for part in (*keep, *give)],
        [out, out], [shape((3, hw, hw))] * 2, cost=12 * t * width * hw,
    )


def last_rows(s, keep, recv, x_own, x_in, dh1, weight, table, rows=512):
    t, width = x_own.shape
    hw = width // 2
    n = len(keep)

    def kernel(s_ref, *refs):
        xo, xi, dh, w, tab, out, vec = refs[2 * n :]

        @pl.when(pl.program_id(0) == 0)
        def _():
            vec[...] = jnp.zeros(vec.shape, f32)

        c = s_ref[0]
        da = None
        for j in range(3):
            for parts, core in ((refs[:n], c), (refs[n : 2 * n], 1 - c)):
                d = jnp.concatenate([part[j] for part in parts], axis=1)
                at = pl.multiple_of(j * width + core * hw, 128)
                part = mm_t(d, w[:, pl.ds(at, hw)])
                da = part if da is None else da + part
                if j != 1:
                    line = 2 + j // 2
                    vec[line : line + 1, at_core(core, hw)] += jnp.sum(d.astype(f32), axis=0, keepdims=True)
        x = jnp.where(s_ref[2] == 1, xo[...].astype(f32), xi[...].astype(f32))
        dres, dgain, dshift = norm_back(x, tab[0:1], da)
        out[...] = (dh[...] + dres).astype(bf16)
        vec[0:1] += dgain
        vec[1:2] += dshift

    line = tile(rows, width)
    return call(
        kernel, s, (*keep, *recv, x_own, x_in, dh1, weight, table), (t // rows,),
        [pl.BlockSpec((3, rows, part.shape[2]), lambda i, s: (0, i, 0)) for part in (*keep, *recv)]
        + [line, line, line, once(weight.shape), const(table.shape)],
        [line, const((8, width))], [shape((t, width)), shape((8, width), f32)],
        cost=6 * t * width * width,
    )


EVERY = ("z", "y", "core", "x")
SPREAD2 = ("x", "z", "y", "core")
REP2 = ("z", "y", "core")
SWAP = [(1, 2), (2, 1)]


def tie(*values):
    return lax.optimization_barrier(values)


def across_z(x, d):
    return lax.ppermute(x, "z", [(j, j ^ d) for j in range(4)])


def across(x, axis):
    return lax.ppermute(x, axis, FLIP)


def body_pair(hidden, frames, segment, cotangent, norm_gain, norm_bias, self_qkv, self_out, cross_q, cross_kv, cross_out, fc1, fc2, proj_bias, fc1_bias):
    c, h = lax.axis_index("core"), lax.axis_index("x")
    y_at, z_at = lax.axis_index("y"), lax.axis_index("z")
    stay = c == h
    s = jnp.stack([c, h, stay.astype(jnp.int32), jnp.int32(0), y_at, z_at, z_at ^ 1, z_at ^ 2, z_at ^ 3]).astype(jnp.int32)
    rep_at = lax.axis_index(REP2)
    reps = lax.axis_size(REP2)
    width = self_out.shape[1]
    hw = width // 2
    ff = fc1.shape[1]
    units = ff // width
    pairs = hw // 128

    def swap(x):
        return lax.ppermute(x, ("core", "x"), SWAP)

    def sibling(x):
        return across(x, "core")

    def near(own):
        half = own.shape[0] // 2
        return across(lax.dynamic_slice_in_dim(own, c * half, half).astype(bf16), "x")

    x_own = hidden[0]
    small = jnp.concatenate([norm_gain, norm_bias, proj_bias, fc1_bias.reshape(units, hw), jnp.zeros((1, hw), f32)]).astype(bf16)
    small_in = across(small, "x")
    qkv_near = near(self_qkv)
    x_in = swap(x_own)
    seg = jnp.where(stay, segment, swap(segment))[0]
    per = hw * units // reps
    small = jnp.where(h == 0, jnp.stack([small, small_in]), jnp.stack([small_in, small])).astype(f32)
    table = jnp.concatenate([small[0, :16], small[1, :16]], axis=1)
    fc1_shift = small[:, 15:19].reshape(1, ff)
    kmark, qmark = seg_marks(seg)
    deep = hw // per
    part1 = lax.dynamic_slice(fc1, (rep_at % deep * per, rep_at // deep * width), (per, width))
    part2 = lax.dynamic_slice_in_dim(fc2, rep_at * per, per)
    slot = jnp.concatenate([part1, part2]).astype(bf16)
    x_in, slot, kmark, qmark, frames, cross_kv = tie(x_in, slot, kmark, qmark, frames, cross_kv)
    ffw = lax.all_gather(slot, SPREAD2, axis=0, tiled=False).reshape(2 * reps, 2, per, width)
    f_own = frames[0]
    f_in = swap(f_own)
    kv_near = near(cross_kv)
    w_qkv, a1, keep, give = norm_qkv(s, x_own, x_in, (self_qkv, qkv_near, sibling(qkv_near)), table)
    recv = sibling(give)

    many = pairs - 1
    ctx_a, give_a, lse_a = self_fwd(0, many, c, keep, recv, kmark, qmark)
    give_a, f_in, kv_near, keep, recv = tie(give_a, f_in, kv_near, keep, recv)
    half = jnp.where(stay, f_own, f_in)
    twin = sibling(half)
    kv_sib = sibling(kv_near)
    in_a = sibling(give_a)
    half, self_out, cross_q = tie(half, self_out, cross_q)
    out_near, q_near = near(self_out), near(cross_q)
    out_near, cross_out, cotangent = tie(out_near, cross_out, cotangent)
    co_near = near(cross_out)
    cot_in = swap(cotangent[0])
    ctx_b, give_b, lse_b = self_fwd(many, 1, c, keep, recv, kmark, qmark)
    in_b = sibling(give_b)
    w_kv, kc, vc = frame_kv(s, half, twin, (cross_kv, kv_near, kv_sib), table)
    kc, out_near, q_near = tie(kc, out_near, q_near)
    ctx, ctx_in = (ctx_a, ctx_b), (in_a, in_b)
    w_out, w_q, h1, a2, qc = self_project(
        s, ctx, ctx_in, x_own, x_in, (self_out, out_near, sibling(out_near)), (cross_q, q_near, sibling(q_near)), table
    )
    count = half.shape[0]
    own_pairs, far_pairs = c * pairs, (1 - c) * pairs
    c2_give, cross_lse_give = cross_fwd(far_pairs, pairs, qc, kc, vc, count)
    c2_give, co_near, qc = tie(c2_give, co_near, qc)
    co_sib = sibling(co_near)
    c2_keep, cross_lse_keep = cross_fwd(own_pairs, pairs, qc, kc, vc, count)
    w_co, out, a3, g, dm, du, d2, dh2, dc2_keep, dc2_give, vec_mid = middle(
        s, h1, c2_keep, c2_give, cotangent[0], cot_in, (cross_out, co_near, co_sib), ffw, table, fc1_shift,
    )

    packed = ff_grads(s, a3, du, g, dm)
    dc2_give, packed, out, a1_out = tie(dc2_give, packed, out, a1)
    ff_mine = lax.psum_scatter(packed.reshape(2 * reps, 2 * per, width), SPREAD2, scatter_dimension=0, tiled=False)
    out_in = swap(out)
    a1_sib = sibling(a1_out)
    dq_give, dkv_give = cross_bwd(far_pairs, pairs, qc, kc, vc, c2_give, dc2_give, cross_lse_give, count)
    dkv_give, dq_give = tie(dkv_give, dq_give)
    dkv_in = sibling(dkv_give)
    pair_give = give_grads(s, c2_keep, c2_give, d2, a2, dq_give)
    pair_give, dc2_keep = tie(pair_give, dc2_keep)
    pair_in = sibling(pair_give)
    dq_keep, dkv_keep = cross_bwd(own_pairs, pairs, qc, kc, vc, c2_keep, dc2_keep, cross_lse_keep, count)
    dq_keep, out_in, dkv_in, a1_sib, pair_in = tie(dq_keep, out_in, dkv_in, a1_sib, pair_in)
    dh1, d1, dctx_keep, dctx_give, vec_cross = cross_back(s, dq_keep, dq_give, h1, dh2, w_q, w_out, table)
    dctx_give, d1 = tie(dctx_give, d1)
    dctx_in = sibling(dctx_give)
    so_give = give_grad_out(s, ctx, ctx_in, d1)
    so_give, dkv_keep = tie(so_give, dkv_keep)
    so_in = sibling(so_give)
    fkeep, fgive, kv_xkeep, kv_xgive, vec_kv = frame_back(s, dkv_keep, dkv_in, half, twin, w_kv)
    fgive, kv_xgive = tie(fgive, kv_xgive)
    fr_in = sibling(fgive)
    xgive, xkeep = keep_grads(s, c2_keep, c2_give, d2, a2, dq_keep, ctx, ctx_in, d1, pair_in, so_in, kv_xkeep, kv_xgive)
    xgive, fr_in, fkeep = tie(xgive, fr_in, fkeep)
    got_x = across(xgive, "x")
    fr_own = (fkeep.astype(f32) + fr_in.astype(f32)).astype(bf16)
    fr_own, dctx_keep = tie(fr_own, dctx_keep)
    fr_swapped = swap(fr_own)

    def send_z(pieces):
        return (pieces[0],) + tuple(across_z(pieces[d], d) for d in (1, 2, 3))

    def gather_z(piece):
        return (piece,) + tuple(across_z(piece, d) for d in (1, 2, 3))

    bg_a, bk_a = self_bwd(0, many, c, keep, recv, ctx_a, dctx_keep, dctx_in, lse_a, kmark, qmark)
    bg_a, bk_a, got_x, keep, ff_mine = tie(bg_a, bk_a, got_x, keep, ff_mine)
    ff_got = lax.all_gather(ff_mine, REP2, axis=0, tiled=False)
    bi_a = sibling(bg_a)
    m_ygive, m_ykeep = split_y(s, xkeep, got_x)
    m_ygive, keep = tie(m_ygive, keep)
    m_y = across(m_ygive, "y")
    bg_b, bk_b = self_bwd(many, 1, c, keep, recv, ctx_b, dctx_keep, dctx_in, lse_b, kmark, qmark)
    bg_b, bk_b, m_y, fr_swapped = tie(bg_b, bk_b, m_y, fr_swapped)
    bi_b = sibling(bg_b)
    m_four = split_z(s, m_ykeep, m_y)
    bk_b, *m_four = tie(bk_b, *m_four)
    m_z = send_z(m_four)
    q_xgive, q_xkeep = qkv_grad(s, a1, a1_sib, (bk_a, bk_b), (bg_a, bg_b))
    q_xgive, q_xkeep, dh1 = tie(q_xgive, q_xkeep, dh1)
    q_x = across(q_xgive, "x")
    grad_hidden, vec_last = last_rows(s, (bk_a, bk_b), (bi_a, bi_b), x_own, x_in, dh1, w_qkv, table)
    v_give, v_mine = pack_vectors(s, vec_last, vec_cross, vec_mid, vec_kv)
    v_got = across(v_give, "x")
    v_mine, *m_z = tie(v_mine, *m_z)
    m_all = gather_z(sum_four(s, m_z))
    q_x, *m_all = tie(q_x, *m_all)
    q_ygive, q_ykeep = split_y(s, q_xkeep, q_x)
    q_ygive, grad_hidden, *m_all = tie(q_ygive, grad_hidden, *m_all)
    q_y = across(q_ygive, "y")
    hid_in = swap(grad_hidden)
    m_own = join_z(s, m_all)
    m_own, q_y = tie(m_own, q_y)
    m_far = across(m_own, "y")
    q_four = split_z(s, q_ykeep, q_y)
    q_z = send_z(q_four)
    q_own = join_z(s, gather_z(sum_four(s, q_z, (v_mine, v_got))))
    q_far = across(q_own, "y")

    def quarters(own, far):
        return own, far, sibling(own), sibling(far)

    spots = ((0, 0, 0), (1, 0, 0), (2, 0, 0), (3, 0, 0), (3, hw, 0))
    crossout_grad, crossq_grad, selfout_grad, kv_grad = spread_out(s, ((quarters(m_own, m_far), spots),), ((hw, width),) * 3 + ((width, width),))
    first = tuple((0, 0, j * width) for j in range(3))
    qkv_grad_out, mine = spread_out(s, ((quarters(q_own, q_far), first),), ((hw, 3 * width), (24, hw)), True)
    fc1_grad, fc2_grad = spread_ff(s, ff_got.reshape(reps, 2, per, width))

    output = jnp.where(stay, out, out_in)
    grad_hidden = jnp.where(stay, grad_hidden, hid_in)
    grad_frames = jnp.where(stay, fr_own, fr_swapped)
    return (
        output[None], grad_hidden[None], grad_frames[None], mine[:4], mine[4:8],
        qkv_grad_out, selfout_grad, crossq_grad, kv_grad, crossout_grad, fc1_grad, fc2_grad, mine[8:15], mine[15:19].reshape(-1),
    )


GROUP = ("core", "ilo")
SHARD = ("ihi", "ilo")
REP = ("rz", "core")
SPREAD = ("ihi", "ilo", "rz", "core")


def body_general(hidden, frames, segment, cotangent, norm_gain, norm_bias, self_qkv, self_out, cross_q, cross_kv, cross_out, fc1, fc2, proj_bias, fc1_bias):
    c = lax.axis_index("core")
    hi = lax.axis_index("ihi")
    n = lax.axis_size("core") * lax.axis_size("ilo")
    reps = lax.axis_size("rz") * lax.axis_size("core")
    rep_at = lax.axis_index(REP)
    width = self_out.shape[1]
    ff = fc1.shape[1]

    def swap(x):
        return lax.ppermute(x, ("core", "ihi"), [(0, 0), (1, 2), (2, 1), (3, 3)])

    def whole(own):
        if n != 2:
            return lax.all_gather(own, SHARD, axis=0, tiled=True)
        half = own.shape[0] // 2
        mine = lax.ppermute(lax.dynamic_slice_in_dim(own, c * half, half), "ihi", FLIP)
        sib = lax.ppermute(mine, "core", FLIP)
        other = jnp.where(c == 0, jnp.concatenate([mine, sib]), jnp.concatenate([sib, mine]))
        return jnp.where(hi == 0, jnp.concatenate([own, other]), jnp.concatenate([other, own]))

    def slices(own):
        rows = own.shape[0] // reps
        return lax.dynamic_slice_in_dim(own, rep_at * rows, rows)

    rows_in = swap(hidden[0])
    qkv_w = whole(self_qkv.astype(bf16))
    small = jnp.concatenate([norm_gain.astype(bf16), norm_bias.astype(bf16), proj_bias.astype(bf16), fc1_bias.astype(bf16).reshape(-1, norm_gain.shape[1]), jnp.zeros((1, norm_gain.shape[1]), bf16)])
    small = lax.all_gather(small, SHARD, axis=1, tiled=False).astype(f32)
    table = small[:15].reshape(15, width)
    gains, shifts, biases = table[:4], table[4:8], table[8:15]
    fc1_shift = small[15:19].transpose(1, 0, 2).reshape(ff)
    seg = swap(segment)[0]
    frames_half = swap(frames[0])
    if n == 2:
        twin = lax.ppermute(frames_half, "core", FLIP)
        frame_rows = jnp.concatenate([jnp.where(c == 0, frames_half, twin), jnp.where(c == 0, twin, frames_half)], axis=1)
    else:
        frame_rows = lax.all_gather(frames_half, GROUP, axis=1, tiled=True)
    selfout_w = whole(self_out.astype(bf16))
    crossq_w = whole(cross_q.astype(bf16))
    kv_w = whole(cross_kv.astype(bf16)) if n == 2 else None
    if n == 2:
        k_w, v_w = kv_w[:width], kv_w[width:]
    else:
        kv_w = lax.all_gather(cross_kv.astype(bf16), SHARD, axis=1, tiled=True)
        k_w, v_w = kv_w[:, :width], kv_w[:, width:]
    crossout_w = whole(cross_out.astype(bf16))
    cot = swap(cotangent[0])
    units = ff // width
    part1 = slices(fc1.astype(bf16))
    part2 = slices(fc2.astype(bf16))
    few = part1.shape[0]
    parts = jnp.concatenate([part1[:, j * width : (j + 1) * width] for j in range(units)] + [part2])
    ffw = lax.all_gather(parts, SPREAD, axis=0, tiled=False)
    fc1_w = jnp.concatenate([ffw[:, j * few : (j + 1) * few].reshape(width, width) for j in range(units)], axis=1)
    fc2_w = ffw[:, units * few :].reshape(ff, width)

    own_rows = rows_in.shape[0]
    hw = -(-HEADS // n)
    padded = hw * n * HD - width

    lanes = hw * HD

    def to_heads(x):
        x = x.reshape(own_rows, -1, width)
        if padded:
            x = jnp.pad(x, ((0, 0), (0, 0), (0, padded)))
        x = x.reshape(own_rows, -1, n, lanes).transpose(1, 2, 0, 3)
        x = lax.all_to_all(x, GROUP, 1, 1, tiled=True)
        return x.reshape(-1, n * own_rows, lanes)

    def to_tokens(x):
        x = lax.all_to_all(x.reshape(-1, n, own_rows, lanes), GROUP, 1, 1, tiled=True)
        return x.transpose(2, 0, 1, 3).reshape(own_rows, -1, n * lanes)[:, :, :width].reshape(own_rows, -1)

    h0 = rows_in.astype(f32)
    a1 = norm(h0, gains[0], shifts[0]).astype(bf16)
    zeros_row = jnp.zeros((width,), f32)
    qkv = (mm(a1, qkv_w) + jnp.concatenate([biases[0], zeros_row, biases[1]])).astype(bf16)
    heads = to_heads(qkv)
    kmark, qmark = seg_marks(seg)
    mid = heads.shape[1] // 2
    first = jnp.int32(0)
    ctx, _, self_lse = self_fwd(0, lanes // 128, first, heads[:, :mid], heads[:, mid:], kmark, qmark)
    c1 = to_tokens(ctx)
    h1 = h0 + mm(c1, selfout_w) + biases[2]
    a2 = norm(h1, gains[1], shifts[1]).astype(bf16)
    qc = (mm(a2, crossq_w) + biases[3]).astype(bf16)
    count = frame_rows.shape[0]
    pad = -count % 256
    frame_pad = jnp.pad(frame_rows, ((0, pad), (0, 0)))
    kc = mm(frame_pad, k_w).astype(bf16)
    live = lax.broadcasted_iota(jnp.int32, (count + pad, 1), 0) < count
    vc = (mm(frame_pad, v_w) + jnp.where(live, biases[4], 0.0)).astype(bf16)
    c2, cross_lse = cross_fwd(first, width // 128, qc, kc, vc, count)
    h2 = h1 + mm(c2, crossout_w) + biases[5]
    a3 = norm(h2, gains[2], shifts[2]).astype(bf16)
    u = (mm(a3, fc1_w) + fc1_shift).astype(bf16)
    uf = u.astype(f32)
    g, slope = gelu_parts(uf)
    g = g.astype(bf16)
    h3 = h2 + mm(g, fc2_w) + biases[6]
    output = norm(h3, gains[3], shifts[3]).astype(bf16)
    output = swap(output)

    def total(x):
        return jnp.sum(x.astype(f32), axis=0)

    dh3, gain3, shift3 = norm_back(h3, gains[3], cot.astype(f32))
    dm = dh3.astype(bf16)
    g_fc2 = t_mm(g, dm).astype(bf16)
    du = (slope * mm_t(dm, fc2_w)).astype(bf16)
    g_fc1 = t_mm(a3, du).astype(bf16)

    def reduce_rows(parts, extra=None):
        total = n * reps
        cut = [p.reshape(total, -1, width) for p in parts]
        if extra is not None:
            cut.append(extra)
        flat = jnp.concatenate(cut, axis=1)
        mine = lax.psum_scatter(flat, SPREAD, scatter_dimension=0, tiled=False)
        got = lax.all_gather(mine, REP, axis=0, tiled=False)
        out, at = [], 0
        for p in cut:
            out.append(got[:, at : at + p.shape[1]].reshape(-1, width).astype(f32))
            at += p.shape[1]
        return out

    ff_grads = reduce_rows([g_fc1[:, j * width : (j + 1) * width] for j in range(units)] + [g_fc2])
    fc1_grad = jnp.concatenate(ff_grads[:units], axis=1)
    fc2_grad = ff_grads[units]

    da3 = mm_t(du, fc1_w)
    dres, gain2, shift2 = norm_back(h2, gains[2], da3)
    dh2 = dh3 + dres
    d2 = dh2.astype(bf16)
    g_crossout = t_mm(c2, d2).astype(bf16)
    dc2 = mm_t(d2, crossout_w).astype(bf16)
    dqc, (dkc, dvc) = cross_bwd(first, width // 128, qc, kc, vc, c2, dc2, cross_lse, count)
    share = width // n

    def sum_columns(x):
        return lax.psum_scatter(x, GROUP, scatter_dimension=1, tiled=True)

    if n == 2:

        def sum_columns(x):
            give = lax.dynamic_slice_in_dim(x, (1 - c) * share, share, axis=1)
            keep = lax.dynamic_slice_in_dim(x, c * share, share, axis=1)
            return (keep.astype(f32) + lax.ppermute(give, "core", FLIP).astype(f32)).astype(bf16)

    dk_own = sum_columns(dkc)[:count]
    dv_own = sum_columns(dvc)[:count]
    place = lax.axis_index(GROUP) * share
    kw_own = lax.dynamic_slice_in_dim(k_w, place, share, axis=1)
    vw_own = lax.dynamic_slice_in_dim(v_w, place, share, axis=1)
    dframe = (mm_t(dk_own, kw_own) + mm_t(dv_own, vw_own)).astype(bf16)
    grad_frames = swap(sum_columns(dframe))
    g_k = t_mm(frame_rows, dk_own).astype(bf16)
    g_v = t_mm(frame_rows, dv_own).astype(bf16)
    vb_own = jnp.sum(dv_own.astype(f32), axis=0)

    g_crossq = t_mm(a2, dqc).astype(bf16)
    da2 = mm_t(dqc, crossq_w)
    dres, gain1, shift1 = norm_back(h1, gains[1], da2)
    dh1 = dh2 + dres
    d1 = dh1.astype(bf16)
    g_selfout = t_mm(c1, d1).astype(bf16)
    dctx = mm_t(d1, selfout_w).astype(bf16)
    dctx = to_heads(dctx)[0]
    late, early = self_bwd(0, lanes // 128, first, heads[:, :mid], heads[:, mid:], ctx, dctx[:mid], dctx[mid:], self_lse, kmark, qmark)
    dqkv = to_tokens(jnp.concatenate([early, late], axis=1))
    da1 = mm_t(dqkv, qkv_w)
    g_qkv = t_mm(a1, dqkv).astype(bf16)
    sums = total(dqkv)
    dres, gain0, shift0 = norm_back(h0, gains[0], da1)
    grad_hidden = swap((dh1 + dres).astype(bf16))

    vb = lax.dynamic_update_slice(jnp.zeros((width,), f32), vb_own, (place,))
    vectors = jnp.stack([gain0[0], gain1[0], gain2[0], gain3[0], shift0[0], shift1[0], shift2[0], shift3[0], sums[:width], sums[2 * width :], total(d1), total(dqc), vb, total(d2), total(dm)])
    per = width // n
    vectors = vectors.reshape(15, n, per).transpose(1, 0, 2).reshape(n, 15 * per)
    vectors = jnp.concatenate([vectors, total(du).reshape(n, ff // n)], axis=1)
    long = vectors.shape[1]
    seats = -(-long // reps)
    vectors = jnp.pad(vectors, ((0, 0), (0, seats * reps - long))).reshape(n * reps, seats)
    lines = -(-seats // (8 * width)) * 8
    vectors = jnp.pad(vectors, ((0, 0), (0, lines * width - seats))).reshape(n * reps, lines, width)

    def own_columns(x):
        return lax.dynamic_update_slice(jnp.zeros((x.shape[0], width), x.dtype), x, (jnp.int32(0), place))

    cross = [g_crossq, g_crossout]
    if n == 2:
        cross.append(jnp.concatenate([own_columns(g_k), own_columns(g_v)]))
    cross = reduce_rows(cross)
    crossq_grad, crossout_grad = cross[:2]
    if n == 2:
        kv_grad = cross[2]
    else:
        kv_cols = jnp.concatenate([own_columns(g_k), own_columns(g_v)], axis=1)
        kv_cols = lax.psum_scatter(kv_cols, SHARD, scatter_dimension=1, tiled=True)
        kv_grad = lax.psum(kv_cols, REP).astype(f32)
    got = reduce_rows([g_qkv[:, j * width : (j + 1) * width] for j in range(3)] + [g_selfout], vectors.astype(bf16))
    qkv_grad = jnp.concatenate(got[:3], axis=1)
    selfout_grad = got[3]
    vec = got[4].reshape(reps, lines * width)[:, :seats].reshape(-1)[:long]
    table = vec[: 15 * per].reshape(15, per)
    fc1b_grad = vec[15 * per :]
    return (
        output[None], grad_hidden[None], grad_frames[None],
        table[:4], table[4:8], qkv_grad, selfout_grad, crossq_grad, kv_grad, crossout_grad, fc1_grad, fc2_grad, table[8:15], fc1b_grad,
    )


def solution(mesh):
    reps, n = mesh.devices.shape
    paired = (reps, n) == (16, 2)
    if paired:
        work = Mesh(mesh.devices.reshape(4, 2, 2, 2), EVERY)
        rep, inner = REP2, ("x",)
    else:
        work = Mesh(mesh.devices.reshape(reps // 2, 2, 2, n // 2), ("rz", "core", "ihi", "ilo"))
        rep, inner = REP, SHARD
    rows, cols = P(inner, None), P(None, inner)
    tokens, features = P(rep, inner, None), P(rep, None, inner)
    weights = (cols, cols, rows, rows, rows, cols, rows, rows, rows, cols, P(inner))
    return jax.shard_map(
        body_pair if paired else body_general,
        mesh=work,
        in_specs=(tokens, features, P(rep, None), tokens) + weights,
        out_specs=(tokens, tokens, features) + weights,
        check_vma=False,
    )
```

```python
import math

import jax
import jax.numpy as jnp
from jax import lax
from jax.experimental import pallas as pl
from jax.experimental.pallas import tpu as pltpu
from jax.sharding import Mesh
from jax.sharding import PartitionSpec as P

HEADS = 12
HD = 64
EPSILON = 1e-05
NEG = -1e30
PROMPT = 1024
REACH = 256
bf16 = jnp.bfloat16
f32 = jnp.float32
FLIP = [(0, 1), (1, 0)]


def mm(a, b):
    return jnp.dot(a, b, preferred_element_type=f32)


def mm_t(a, b):
    return lax.dot_general(a, b, (((1,), (1,)), ((), ())), preferred_element_type=f32)


def t_mm(a, b):
    return lax.dot_general(a, b, (((0,), (0,)), ((), ())), preferred_element_type=f32)


def call(kernel, scalars, args, grid, in_specs, out_specs, out_shape, scratch=(), cost=None):
    spec = pltpu.PrefetchScalarGridSpec(
        num_scalar_prefetch=1, grid=grid, in_specs=in_specs, out_specs=out_specs, scratch_shapes=list(scratch)
    )
    estimate = None
    if cost is not None:
        estimate = pl.CostEstimate(flops=cost // 10, bytes_accessed=1 << 20, transcendentals=0)
    return pl.pallas_call(
        kernel,
        grid_spec=spec,
        out_shape=out_shape,
        cost_estimate=estimate,
        compiler_params=pltpu.CompilerParams(vmem_limit_bytes=60 * 2**20),
    )(scalars, *args)


def shape(dims, kind=bf16):
    return jax.ShapeDtypeStruct(dims, kind)


def half_of(lane, h):
    return (lane < HD) if h == 0 else (lane >= HD)


def delta_of(do, o):
    x = do.astype(f32) * o.astype(f32)
    hi = x.astype(bf16)
    lo = (x - hi.astype(f32)).astype(bf16)
    r = lax.broadcasted_iota(jnp.int32, (8, 128), 0)
    lane = lax.broadcasted_iota(jnp.int32, (8, 128), 1)
    pick = jnp.where((lane // HD) == r, 1.0, 0.0).astype(bf16)
    return mm_t(pick, hi) + mm_t(pick, lo)


def cross_fwd(base, pairs, q, k, v, valid, block=1024):
    tq, tk = q.shape[0], k.shape[0]
    block = min(block, tq)

    def kernel(s_ref, q_ref, k_ref, v_ref, o_ref, l_ref, ks, vts):
        @pl.when(pl.program_id(1) == 0)
        def _():
            low = lax.broadcasted_iota(jnp.int32, (tk, 128), 1)
            row = lax.broadcasted_iota(jnp.int32, (tk, 128), 0)
            bias = jnp.where(row >= valid, NEG, 0.0).astype(bf16)
            one = jnp.ones((tk, 128), bf16)
            for h in range(2):
                ks[h] = jnp.where(half_of(low, h), k_ref[...], bias)
                vts[h] = jnp.where(half_of(low, h), v_ref[...], one).T

        lane = lax.broadcasted_iota(jnp.int32, (block, 128), 1)
        qq = q_ref[...] * bf16(0.125)
        scores = []
        for h in range(2):
            spare = lane == (HD if h == 0 else 0)
            qh = jnp.where(half_of(lane, h), qq, jnp.where(spare, 1.0, 0.0).astype(bf16))
            scores.append(mm_t(ks[h], qh))
        outs = []
        for h, s in enumerate(scores):
            m = jnp.max(s, axis=0, keepdims=True)
            o = mm(vts[h], jnp.exp(s - m).astype(bf16))
            total = o[HD : HD + 1] if h == 0 else o[0:1]
            outs.append(o * (1.0 / total))
            l_ref[0, h : h + 1, :] = m + jnp.log(total)
        sub = lax.broadcasted_iota(jnp.int32, (128, block), 0)
        o_ref[...] = jnp.where(sub < HD, outs[0], outs[1]).T.astype(bf16)

    qspec = pl.BlockSpec((block, 128), lambda p, i, s: (i, s[0] + p))
    kspec = pl.BlockSpec((tk, 128), lambda p, i, s: (0, s[0] + p))
    return call(
        kernel, jnp.reshape(base, (1,)).astype(jnp.int32), (q, k, v), (pairs, tq // block), [qspec, kspec, kspec],
        [pl.BlockSpec((block, 128), lambda p, i, s: (i, p)), pl.BlockSpec((1, 8, block), lambda p, i, s: (p, 0, i))],
        [shape((tq, pairs * 128)), shape((pairs, 8, tq), f32)],
        [pltpu.VMEM((2, tk, 128), bf16), pltpu.VMEM((2, 128, tk), bf16)],
        4 * tq * tk * 256 * pairs,
    )


def cross_bwd(base, pairs, q, k, v, o, do, lse, valid, block=1024):
    tq, tk = q.shape[0], k.shape[0]
    block = min(block, tq)
    steps = tq // block

    def kernel(s_ref, q_ref, k_ref, v_ref, o_ref, do_ref, l_ref, dq_ref, d_ref, ks, kts, dka, dva):
        @pl.when(pl.program_id(1) == 0)
        def _():
            low = lax.broadcasted_iota(jnp.int32, (tk, 128), 1)
            row = lax.broadcasted_iota(jnp.int32, (tk, 128), 0)
            bias = jnp.where(row >= valid, NEG, 0.0).astype(bf16)
            zero = jnp.zeros((tk, 128), bf16)
            for h in range(2):
                ks[h] = jnp.where(half_of(low, h), k_ref[...], bias)
                kts[h] = jnp.where(half_of(low, h), k_ref[...], zero).T
            dka[...] = jnp.zeros((tk, 128), f32)
            dva[...] = jnp.zeros((tk, 128), f32)

        lane = lax.broadcasted_iota(jnp.int32, (block, 128), 1)
        qq = q_ref[...] * bf16(0.125)
        dd = do_ref[...]
        delta = delta_of(dd, o_ref[...])
        zero = jnp.zeros((block, 128), bf16)
        dqt, dk, dv = None, dka[...], dva[...]
        for h in range(2):
            mine = half_of(lane, h)
            spare = lane == (HD if h == 0 else 0)
            qc = jnp.where(mine, qq, zero)
            qs = jnp.where(spare, jnp.ones((block, 128), bf16), qc)
            dh = jnp.where(mine, dd, zero)
            p = jnp.exp(mm_t(ks[h], qs) - l_ref[0, h : h + 1, :])
            ds = (p * (mm_t(v_ref[...], dh) - delta[h : h + 1])).astype(bf16)
            dv = dv + mm(p.astype(bf16), dh)
            dk = dk + mm(ds, qc)
            part = mm(kts[h], ds)
            dqt = part if dqt is None else dqt + part
        dka[...] = dk
        dva[...] = dv
        dq_ref[...] = (dqt * 0.125).T.astype(bf16)

        @pl.when(pl.program_id(1) == steps - 1)
        def _():
            d_ref[0] = dka[...].astype(bf16)
            d_ref[1] = dva[...].astype(bf16)

    mine = pl.BlockSpec((block, 128), lambda p, i, s: (i, p))
    qspec = pl.BlockSpec((block, 128), lambda p, i, s: (i, s[0] + p))
    kspec = pl.BlockSpec((tk, 128), lambda p, i, s: (0, s[0] + p))
    return call(
        kernel, jnp.reshape(base, (1,)).astype(jnp.int32), (q, k, v, o, do, lse), (pairs, steps),
        [qspec, kspec, kspec, mine, mine, pl.BlockSpec((1, 8, block), lambda p, i, s: (p, 0, i))],
        [mine, pl.BlockSpec((2, tk, 128), lambda p, i, s: (0, 0, p))],
        [shape((tq, pairs * 128)), shape((2, tk, pairs * 128))],
        [pltpu.VMEM((2, tk, 128), bf16), pltpu.VMEM((2, 128, tk), bf16), pltpu.VMEM((tk, 128), f32), pltpu.VMEM((tk, 128), f32)],
        2 * tq * tk * 10 * 256 * pairs,
    )


def spans(r0, block):
    if r0 < PROMPT:
        return ([(0, r0)] if r0 else []) + [(r0, r0 + block)]
    left = max(PROMPT, r0 - REACH)
    before = [(0, r0)] if left == PROMPT else [(0, PROMPT), (left, r0)]
    return before + [(r0, r0 + block)]


def seg_marks(seg):
    lane = lax.broadcasted_iota(jnp.int32, (seg.shape[0], 128), 1) % HD
    same = lane == seg[:, None]
    kmark = jnp.where(same, 1.0, 0.0).astype(bf16)
    qmark = jnp.where(same | (lane == 0) | (lane > 8), 0.0, NEG).astype(bf16)
    return kmark, qmark


def half_specs(rows, first=0):
    return [pl.BlockSpec((3, rows, 128), lambda p, s: (0, 0, first + p))] * 2


def self_fwd(first, pairs, place, keep, recv, kmark, qmark, block=512):
    rows, width = keep.shape[1], pairs * 128
    t = 2 * rows

    def kernel(s_ref, a_ref, b_ref, km_ref, qm_ref, o_ref, give_ref, l_ref, qf, ks, vts):
        mine0 = pl.multiple_of(s_ref[0] * rows, rows)
        other0 = pl.multiple_of((1 - s_ref[0]) * rows, rows)
        low = lax.broadcasted_iota(jnp.int32, (rows, 128), 1)
        one = jnp.ones((rows, 128), bf16)
        for ref, at in ((a_ref, mine0), (b_ref, other0)):
            spot = pl.ds(at, rows)
            qf[spot, :] = ref[0] * bf16(0.125)
            for h in range(2):
                ks[h, spot, :] = jnp.where(half_of(low, h), ref[1], km_ref[spot, :])
                vts[h, :, spot] = jnp.where(half_of(low, h), ref[2], one).T
        lane = lax.broadcasted_iota(jnp.int32, (block, 128), 1)
        hide = lax.broadcasted_iota(jnp.int32, (block, block), 0) > lax.broadcasted_iota(jnp.int32, (block, block), 1)
        tasks = [(r0, h) for r0 in range(0, t, block) for h in range(2)]

        def scores(task):
            r0, h = task
            spot = pl.ds(r0, block)
            qs = jnp.where(half_of(lane, h), qf[spot, :], qm_ref[spot, :])
            out = [mm_t(ks[h, pl.ds(a, b - a), :], qs) for a, b in spans(r0, block)]
            out[-1] = jnp.where(hide, NEG, out[-1])
            return out

        now, outs = scores(tasks[0]), [None, None]
        for i, (r0, h) in enumerate(tasks):
            later = scores(tasks[i + 1]) if i + 1 < len(tasks) else None
            m = None
            for s in now:
                top = jnp.max(s, axis=0, keepdims=True)
                m = top if m is None else jnp.maximum(m, top)
            o = None
            for s, (a, b) in zip(now, spans(r0, block)):
                part = mm(vts[h, :, pl.ds(a, b - a)], jnp.exp(s - m).astype(bf16))
                o = part if o is None else o + part
            total = o[HD : HD + 1] if h == 0 else o[0:1]
            l_ref[0, h : h + 1, pl.ds(r0, block)] = m + jnp.log(total)
            outs[h] = o * (1.0 / total)
            if h == 1:
                sub = lax.broadcasted_iota(jnp.int32, (128, block), 0)
                o_ref[pl.ds(r0, block), :] = jnp.where(sub < HD, outs[0], outs[1]).T.astype(bf16)
            now = later
        give_ref[...] = o_ref[pl.ds(other0, rows), :]

    whole = pl.BlockSpec((t, 128), lambda p, s: (0, 0))
    return call(
        kernel, jnp.reshape(place, (1,)).astype(jnp.int32), (keep, recv, kmark, qmark), (pairs,),
        half_specs(rows, first) + [whole, whole],
        [pl.BlockSpec((t, 128), lambda p, s: (0, p)), pl.BlockSpec((rows, 128), lambda p, s: (0, p)), pl.BlockSpec((1, 8, t), lambda p, s: (p, 0, 0))],
        [shape((t, width)), shape((rows, width)), shape((pairs, 8, t), f32)],
        [pltpu.VMEM((t, 128), bf16), pltpu.VMEM((2, t, 128), bf16), pltpu.VMEM((2, 128, t), bf16)],
        2 * t * t * 4 * width,
    )


def self_bwd(first, pairs, seat, place, keep, recv, o, dkeep, drecv, lse, kmark, qmark, block=256):
    rows, width = keep.shape[1], pairs * 128
    t = 2 * rows

    def kernel(s_ref, a_ref, b_ref, o_ref, da_ref, db_ref, l_ref, km_ref, qm_ref, give_ref, keep_ref, qf, df, vf, ks, kts, dqa, dka, dva):
        mine0 = pl.multiple_of(s_ref[0] * rows, rows)
        other0 = pl.multiple_of((1 - s_ref[0]) * rows, rows)
        low = lax.broadcasted_iota(jnp.int32, (rows, 128), 1)
        zero = jnp.zeros((rows, 128), bf16)
        for ref, dref, at in ((a_ref, da_ref, mine0), (b_ref, db_ref, other0)):
            spot = pl.ds(at, rows)
            qf[spot, :] = ref[0] * bf16(0.125)
            df[spot, :] = dref[...]
            vf[spot, :] = ref[2]
            for h in range(2):
                ks[h, spot, :] = jnp.where(half_of(low, h), ref[1], km_ref[spot, :])
                kts[h, :, spot] = jnp.where(half_of(low, h), ref[1], zero).T
        dka[...] = jnp.zeros((t, 128), f32)
        dva[...] = jnp.zeros((t, 128), f32)
        lane = lax.broadcasted_iota(jnp.int32, (block, 128), 1)
        hide = lax.broadcasted_iota(jnp.int32, (block, block), 0) > lax.broadcasted_iota(jnp.int32, (block, block), 1)
        none = jnp.zeros((block, 128), bf16)
        for r0 in range(0, t, block):
            spot = pl.ds(r0, block)
            dd = df[spot, :]
            delta = delta_of(dd, o_ref[spot, :])
            dqt = None
            for h in range(2):
                mine = half_of(lane, h)
                qc = jnp.where(mine, qf[spot, :], none)
                qs = jnp.where(mine, qf[spot, :], qm_ref[spot, :])
                dh = jnp.where(mine, dd, none)
                log_total = l_ref[0, h : h + 1, spot]
                for a, b in spans(r0, block):
                    keys = pl.ds(a, b - a)
                    s = mm_t(ks[h, keys, :], qs)
                    if a == r0:
                        s = jnp.where(hide, NEG, s)
                    p = jnp.exp(s - log_total)
                    ds = (p * (mm_t(vf[keys, :], dh) - delta[h : h + 1])).astype(bf16)
                    dva[keys, :] += mm(p.astype(bf16), dh)
                    dka[keys, :] += mm(ds, qc)
                    part = mm(kts[h, :, keys], ds)
                    dqt = part if dqt is None else dqt + part
            dqa[spot, :] = (dqt * 0.125).T.astype(bf16)
        for out, at in ((give_ref, other0), (keep_ref, mine0)):
            spot = pl.ds(at, rows)
            out[0] = dqa[spot, :]
            out[1] = dka[spot, :].astype(bf16)
            out[2] = dva[spot, :].astype(bf16)

    whole = pl.BlockSpec((t, 128), lambda p, s: (0, 0))
    half = pl.BlockSpec((rows, 128), lambda p, s: (0, first + p))
    return call(
        kernel, jnp.reshape(place, (1,)).astype(jnp.int32), (keep, recv, o, dkeep, drecv, lse, kmark, qmark), (pairs,),
        half_specs(rows, first)
        + [pl.BlockSpec((t, 128), lambda p, s: (0, seat + p)), half, half, pl.BlockSpec((1, 8, t), lambda p, s: (seat + p, 0, 0)), whole, whole],
        half_specs(rows),
        [shape((3, rows, width))] * 2,
        [pltpu.VMEM((t, 128), bf16)] * 3 + [pltpu.VMEM((2, t, 128), bf16), pltpu.VMEM((2, 128, t), bf16), pltpu.VMEM((t, 128), bf16)]
        + [pltpu.VMEM((t, 128), f32)] * 2,
        2 * t * t * 8 * width,
    )


def norm_stats(rows):
    centered = rows - jnp.mean(rows, axis=-1, keepdims=True)
    inv = lax.rsqrt(jnp.mean(centered * centered, axis=-1, keepdims=True) + EPSILON)
    return centered * inv, inv


def norm(rows, gain, shift):
    return norm_stats(rows)[0] * gain + shift


def norm_back(rows, gain, dy):
    n, inv = norm_stats(rows)
    dn = dy * gain
    dh = inv * (dn - jnp.mean(dn, axis=-1, keepdims=True) - n * jnp.mean(dn * n, axis=-1, keepdims=True))
    return dh, jnp.sum(dy * n, axis=0, keepdims=True), jnp.sum(dy, axis=0, keepdims=True)


ERFC = (
    0.22567585470008253, 0.22566975083164525, 0.20784161289369674, 0.1685452087610459, 0.14142852065437478,
    -0.005612938524279035, 0.1691005263450779, -0.1829144800497475, 0.05026606972001335,
)


def gelu_parts(u):
    bell = jnp.exp(u * u * -0.5)
    t = 1.0 / (1.0 + jnp.abs(u) * (0.4 * math.sqrt(0.5)))
    poly = jnp.full_like(t, ERFC[-1])
    for value in ERFC[-2::-1]:
        poly = poly * t + value
    tail = bell * t * poly * 0.5
    cdf = jnp.where(u < 0.0, tail, 1.0 - tail)
    return u * cdf, cdf + u * bell * (1.0 / math.sqrt(2.0 * math.pi))


def const(dims):
    return pl.BlockSpec(dims, lambda i, s: (0,) * len(dims))


def once(dims):
    return pl.BlockSpec(dims, lambda i, s: (0,) * len(dims), pipeline_mode=pl.Buffered(1))


def tile(rows, width):
    return pl.BlockSpec((rows, width), lambda i, s: (i, 0))


def fill(full, s, own, mine, sib):
    rows = own.shape[0]
    c, h = s[0], s[1]
    full[pl.ds(pl.multiple_of(h * rows, 128), rows), :] = own[...].astype(bf16)
    start = (1 - h) * rows
    full[pl.ds(pl.multiple_of(start + c * (rows // 2), 64), rows // 2), :] = mine[...]
    full[pl.ds(pl.multiple_of(start + (1 - c) * (rows // 2), 64), rows // 2), :] = sib[...]


def picked(part):
    if not isinstance(part, tuple):
        return once(part.shape)
    stack, which = part
    return pl.BlockSpec((None, *stack.shape[1:]), lambda i, s: (which, 0, 0), pipeline_mode=pl.Buffered(1))


def weight_specs(weight):
    return [picked(part) for part in weight]


def arrays(weight):
    return [part[0] if isinstance(part, tuple) else part for part in weight]


def full_shape(weight):
    return (2 * weight[0].shape[0], weight[0].shape[1])


def at_core(c, width):
    return pl.ds(pl.multiple_of(c * width, 128), width)


def norm_qkv(s, x_own, x_in, weight, table, rows=512):
    t, width = x_own.shape
    hw = width // 2

    def kernel(s_ref, xo, xi, own, mine, sib, tab, w, a_ref, keep, give):
        @pl.when(pl.program_id(0) == 0)
        def _():
            fill(w, s_ref, own, mine, sib)

        x = jnp.where(s_ref[2] == 1, xo[...].astype(f32), xi[...].astype(f32))
        a = norm(x, tab[0:1], tab[4:5]).astype(bf16)
        a_ref[...] = a
        for j in range(3):
            y = mm(a, w[:, j * width : (j + 1) * width])
            if j != 1:
                y = y + tab[8 + j // 2 : 9 + j // 2]
            low, high = y[:, :hw].astype(bf16), y[:, hw:].astype(bf16)
            first = s_ref[0] == 0
            keep[j] = jnp.where(first, low, high)
            give[j] = jnp.where(first, high, low)

    third = pl.BlockSpec((3, rows, hw), lambda i, s: (0, i, 0))
    dims = full_shape(weight)
    return call(
        kernel, s, (x_own, x_in, *weight, table), (t // rows,),
        [tile(rows, width)] * 2 + weight_specs(weight) + [const(table.shape)],
        [const(dims), tile(rows, width), third, third],
        [shape(dims), shape((t, width)), shape((3, t, hw)), shape((3, t, hw))],
        cost=2 * t * width * 3 * width,
    )


def beside(refs):
    return jnp.concatenate([ref[...] for ref in refs], axis=1) if len(refs) > 1 else refs[0][...]


def self_project(s, ctx, ctx_in, x_own, x_in, w_out, w_q, table, rows=512):
    t, width = x_own.shape
    hw = width // 2
    steps = t // rows
    n = len(ctx)

    def kernel(s_ref, *refs):
        cks, cis = refs[:n], refs[n : 2 * n]
        xo, xi, o1, o2, o3, q1, q2, q3, tab, wo, wq, h_ref, a_ref, qc_ref = refs[2 * n :]

        @pl.when(pl.program_id(0) == 0)
        def _():
            fill(wo, s_ref, o1, o2, o3)
            fill(wq, s_ref, q1, q2, q3)

        c = s_ref[0]
        x = jnp.where(s_ref[2] == 1, xo[...].astype(f32), xi[...].astype(f32))
        h = x + mm(beside(cks), wo[at_core(c, hw), :]) + mm(beside(cis), wo[at_core(1 - c, hw), :]) + tab[10:11]
        h_ref[...] = h
        a = norm(h, tab[1:2], tab[5:6]).astype(bf16)
        a_ref[...] = a
        qc_ref[...] = (mm(a, wq[...]) + tab[11:12]).astype(bf16)

    dims = full_shape(w_out)
    return call(
        kernel, s, (*ctx, *ctx_in, x_own, x_in, *arrays(w_out), *arrays(w_q), table), (steps,),
        [pl.BlockSpec((rows, part.shape[1]), lambda i, s: (s[0] * steps + i, 0)) for part in ctx]
        + [tile(rows, part.shape[1]) for part in ctx_in] + [tile(rows, width), tile(rows, width)]
        + weight_specs(w_out) + weight_specs(w_q) + [const(table.shape)],
        [const(dims), const(dims), tile(rows, width), tile(rows, width), tile(rows, width)],
        [shape(dims), shape(dims), shape((t, width), f32), shape((t, width)), shape((t, width))],
        cost=4 * t * width * width,
    )


def frame_kv(s, half, twin, weight, table, rows=512):
    count, hw = half.shape
    width = 2 * hw
    steps = -(-count // rows)

    def kernel(s_ref, fa, fb, own, mine, sib, tab, w, k_ref, v_ref):
        @pl.when(pl.program_id(0) == 0)
        def _():
            fill(w, s_ref, own, mine, sib)

        c = s_ref[0]
        live = lax.broadcasted_iota(jnp.int32, (rows, 1), 0) + pl.program_id(0) * rows < count
        for j, out in enumerate((k_ref, v_ref)):
            mine0 = pl.multiple_of(j * width + c * hw, 128)
            other0 = pl.multiple_of(j * width + (1 - c) * hw, 128)
            y = mm(fa[...], w[pl.ds(mine0, hw), :]) + mm(fb[...], w[pl.ds(other0, hw), :])
            if j == 1:
                y = y + tab[12:13]
            out[...] = jnp.where(live, y, 0.0).astype(bf16)

    dims = full_shape(weight)
    return call(
        kernel, s, (half, twin, *weight, table), (steps,),
        [tile(rows, hw)] * 2 + weight_specs(weight) + [const(table.shape)],
        [const(dims), tile(rows, width), tile(rows, width)],
        [shape(dims), shape((steps * rows, width)), shape((steps * rows, width))],
        cost=4 * count * width * width,
    )


def middle(s, h1, c2_keep, c2_give, cot_own, cot_in, w_out, ff_own, ff_far, table, fc1_shift, rows=256):
    t, width = h1.shape
    units = fc1_shift.shape[1] // width
    hw = width // 2
    pieces, piece = ff_own[0].shape[:2]

    def kernel(s_ref, h1_ref, ck_ref, cg_ref, co, ci, o1, o2, o3, own1, own2, far, tab, shift, wo, out, a_ref, g_ref, dm_ref, du_ref, d2_ref, dh_ref, dk_ref, dg_ref, vec, w1, w2, sems):
        def moves():
            for k, (dst, own) in enumerate(((w1, own1), (w2, own2))):
                yield pltpu.make_async_copy(own, dst.at[pl.ds(s_ref[1] * pieces, pieces)], sems.at[2 * k])
                yield pltpu.make_async_copy(far.at[:, k], dst.at[pl.ds((1 - s_ref[1]) * pieces, pieces)], sems.at[2 * k + 1])

        @pl.when(pl.program_id(0) == 0)
        def _():
            for move in moves():
                move.start()
            fill(wo, s_ref, o1, o2, o3)
            vec[...] = jnp.zeros(vec.shape, f32)
            for move in moves():
                move.wait()

        def up(h, j):
            at, many = (h * units + j) * (hw // piece), hw // piece
            return w1[at : at + many].reshape(hw, width)

        def down(j):
            many = width // piece
            return w2[j * many : (j + 1) * many].reshape(width, width)

        c = s_ref[0]
        h2 = h1_ref[...] + mm(ck_ref[...], wo[at_core(c, hw), :]) + mm(cg_ref[...], wo[at_core(1 - c, hw), :]) + tab[13:14]
        n2, inv2 = norm_stats(h2)
        a = (n2 * tab[2:3] + tab[6:7]).astype(bf16)
        a_ref[...] = a
        acc = h2 + tab[14:15]
        slopes = []

        def climb(j):
            return mm(a[:, :hw], up(0, j)) + mm(a[:, hw:], up(1, j)) + shift[:, j * width : (j + 1) * width]

        u = climb(0)
        for j in range(units):
            u_next = climb(j + 1) if j + 1 < units else None
            g, slope = gelu_parts(u.astype(bf16).astype(f32))
            slopes.append(slope)
            g = g.astype(bf16)
            g_ref[:, j * width : (j + 1) * width] = g
            acc = acc + mm(g, down(j))
            u = u_next
        n3, inv3 = norm_stats(acc)
        out[...] = (n3 * tab[3:4] + tab[7:8]).astype(bf16)

        def back(n, inv, gain, dy):
            dn = dy * gain
            return inv * (dn - jnp.mean(dn, axis=-1, keepdims=True) - n * jnp.mean(dn * n, axis=-1, keepdims=True))

        def total(x):
            return jnp.sum(x, axis=0, keepdims=True)

        dy = jnp.where(s_ref[2] == 1, co[...].astype(f32), ci[...].astype(f32))
        dh3 = back(n3, inv3, tab[3:4], dy)
        dm = dh3.astype(bf16)
        dm_ref[...] = dm
        halves = [None, None]
        dg = mm_t(dm, down(0))
        for j in range(units):
            cols = slice(j * width, (j + 1) * width)
            dg_next = mm_t(dm, down(j + 1)) if j + 1 < units else None
            du = (slopes[j] * dg).astype(bf16)
            dg = dg_next
            du_ref[:, cols] = du
            vec[0:1, cols] += total(du.astype(f32))
            for h in range(2):
                part = mm_t(du, up(h, j))
                halves[h] = part if halves[h] is None else halves[h] + part
        da = jnp.concatenate(halves, axis=1)
        dh2 = dh3 + back(n2, inv2, tab[2:3], da)
        d2 = dh2.astype(bf16)
        d2_ref[...] = d2
        dh_ref[...] = dh2
        dk_ref[...] = mm_t(d2, wo[at_core(c, hw), :]).astype(bf16)
        dg_ref[...] = mm_t(d2, wo[at_core(1 - c, hw), :]).astype(bf16)
        rows_of = [total(dm.astype(f32)), total(d2.astype(f32)), total(dy * n3), total(dy), total(da * n2), total(da)]
        for k, value in enumerate(rows_of):
            line, at = 1 + k // 3, (k % 3) * width
            vec[line : line + 1, at : at + width] += value

    dims = full_shape(w_out)
    ff = units * width
    line = tile(rows, width)
    wide, half = tile(rows, ff), tile(rows, hw)
    away = pl.BlockSpec(memory_space=pl.ANY)
    return call(
        kernel, s, (h1, c2_keep, c2_give, cot_own, cot_in, *arrays(w_out), *ff_own, ff_far, table, fc1_shift), (t // rows,),
        [line, half, half, line, line] + weight_specs(w_out) + [away] * 3 + [const(table.shape), const(fc1_shift.shape)],
        [const(dims), line, line, wide, line, wide, line, line, half, half, const((8, ff))],
        [shape(dims), shape((t, width)), shape((t, width)), shape((t, ff)), shape((t, width)), shape((t, ff)), shape((t, width)),
         shape((t, width), f32), shape((t, hw)), shape((t, hw)), shape((8, ff), f32)],
        [pltpu.VMEM((2 * pieces, piece, width), bf16)] * 2 + [pltpu.SemaphoreType.DMA((4,))],
        cost=8 * t * width * ff + 4 * t * width * width,
    )


def ff_grads(s, a, du, g, dm):
    t, width = a.shape
    hw = width // 2
    ff = du.shape[1]
    units = ff // width
    piece = hw * units // 16
    many = hw // piece

    def kernel(s_ref, a_ref, du_ref, g0, g1, dm_ref, out):
        @pl.when(pl.program_id(0) < units)
        def _():
            for h in range(2):
                out[h] = t_mm(a_ref[:, h * hw : (h + 1) * hw], du_ref[...]).astype(bf16).reshape(out.shape[1:])

        @pl.when(pl.program_id(0) >= units)
        def _():
            for h, ref in enumerate((g0, g1)):
                out[h] = t_mm(ref[...], dm_ref[...]).astype(bf16).reshape(out.shape[1:])

    return call(
        kernel, s, (a, du, g, g, dm), (2 * units,),
        [once((t, width)), pl.BlockSpec((t, width), lambda i, s: (0, jnp.minimum(i, units - 1))),
         pl.BlockSpec((t, hw), lambda i, s: (0, jnp.maximum(i - units, 0))),
         pl.BlockSpec((t, hw), lambda i, s: (0, units + jnp.maximum(i - units, 0))), once((t, width))],
        pl.BlockSpec((2, many, 1, piece, width), lambda i, s: (0, i % units, i // units, 0, 0)),
        shape((2, 16, 2, piece, width)),
        cost=4 * t * width * ff,
    )


def cross_back(s, dq_keep, dq_give, h1, dh2, w_q, w_out, table, rows=512):
    t, width = h1.shape
    hw = width // 2

    def kernel(s_ref, dk_ref, dg_ref, h_ref, dh2_ref, wq, wo, tab, dh_ref, d1_ref, keep, give, vec):
        @pl.when(pl.program_id(0) == 0)
        def _():
            vec[...] = jnp.zeros(vec.shape, f32)

        c = s_ref[0]
        da = mm_t(dk_ref[...], wq[:, at_core(c, hw)]) + mm_t(dg_ref[...], wq[:, at_core(1 - c, hw)])
        dres, dgain, dshift = norm_back(h_ref[...], tab[1:2], da)
        dh1 = dh2_ref[...] + dres
        dh_ref[...] = dh1
        d1 = dh1.astype(bf16)
        d1_ref[...] = d1
        keep[...] = mm_t(d1, wo[at_core(c, hw), :]).astype(bf16)
        give[...] = mm_t(d1, wo[at_core(1 - c, hw), :]).astype(bf16)
        vec[0:1] += dgain
        vec[1:2] += dshift
        vec[2:3] += jnp.sum(d1.astype(f32), axis=0, keepdims=True)
        vec[3:4, at_core(c, hw)] += jnp.sum(dk_ref[...].astype(f32), axis=0, keepdims=True)
        vec[3:4, at_core(1 - c, hw)] += jnp.sum(dg_ref[...].astype(f32), axis=0, keepdims=True)

    line, half = tile(rows, width), tile(rows, hw)
    return call(
        kernel, s, (dq_keep, dq_give, h1, dh2, w_q, w_out, table), (t // rows,),
        [half, half, line, line, once(w_q.shape), once(w_out.shape), const(table.shape)],
        [line, line, half, half, const((8, width))],
        [shape((t, width), f32), shape((t, width)), shape((t, hw)), shape((t, hw)), shape((8, width), f32)],
        cost=4 * t * width * width,
    )


def frame_back(s, keep, recv, half, twin, weight, rows=512):
    count, hw = half.shape
    width = 2 * hw
    steps = -(-count // rows)

    def kernel(s_ref, ka, kb, fa, fb, w, fkeep, fgive, xkeep, xgive, vec, acc):
        @pl.when(pl.program_id(0) == 0)
        def _():
            vec[...] = jnp.zeros(vec.shape, f32)
            acc[...] = jnp.zeros(acc.shape, f32)

        c, h = s_ref[0], s_ref[1]
        live = lax.broadcasted_iota(jnp.int32, (rows, 1), 0) + pl.program_id(0) * rows < count
        zero = jnp.zeros((rows, hw), bf16)
        f_mine = jnp.where(live, fa[...], zero)
        f_other = jnp.where(live, fb[...], zero)
        back = None
        for j in range(2):
            d = (ka[j].astype(f32) + kb[j].astype(f32)).astype(bf16)
            part = mm_t(d, w[j * width : (j + 1) * width, at_core(c, hw)])
            back = part if back is None else back + part
            acc[j, at_core(c, hw), :] += t_mm(f_mine, d)
            acc[j, at_core(1 - c, hw), :] += t_mm(f_other, d)
            if j == 1:
                vec[0:1] += jnp.sum(d.astype(f32), axis=0, keepdims=True)
        low, high = back[:, :hw].astype(bf16), back[:, hw:].astype(bf16)
        fkeep[...] = jnp.where(c == 0, low, high)
        fgive[...] = jnp.where(c == 0, high, low)

        @pl.when(pl.program_id(0) == steps - 1)
        def _():
            xkeep[...] = acc[h].astype(bf16)
            xgive[...] = acc[1 - h].astype(bf16)

    pair = pl.BlockSpec((2, rows, hw), lambda i, s: (0, i, 0))
    strip = tile(rows, hw)
    return call(
        kernel, s, (keep, recv, half, twin, weight), (steps,),
        [pair, pair, strip, strip, once(weight.shape)],
        [strip, strip, const((width, hw)), const((width, hw)), const((8, hw))],
        [shape((count, hw)), shape((count, hw)), shape((width, hw)), shape((width, hw)), shape((8, hw), f32)],
        [pltpu.VMEM((2, width, hw), f32)],
        cost=8 * count * width * width,
    )


def give_grads(s, c2_keep, c2_give, d2, a2, dq_give):
    t, width = d2.shape
    hw = width // 2

    def kernel(s_ref, k_ref, g_ref, d_ref, a_ref, q_ref, out):
        c = s_ref[0]
        out[0, at_core(c, hw), :] = t_mm(k_ref[...], d_ref[...]).astype(bf16)
        out[0, at_core(1 - c, hw), :] = t_mm(g_ref[...], d_ref[...]).astype(bf16)
        out[1] = t_mm(a_ref[...], q_ref[...]).astype(bf16)

    half = const((t, hw))
    return call(
        kernel, s, (c2_keep, c2_give, d2, a2, dq_give), (1,),
        [half, half, pl.BlockSpec((t, hw), lambda i, s: (0, 1 - s[0])), const((t, width)), half],
        const((2, width, hw)), shape((2, width, hw)), cost=4 * t * width * hw,
    )


def give_grad_out(s, ctx, ctx_in, d1):
    t, width = d1.shape
    hw = width // 2
    n = len(ctx)

    def kernel(s_ref, *refs):
        d_ref, out = refs[2 * n :]
        c = s_ref[0]
        out[at_core(c, hw), :] = t_mm(beside(refs[:n]), d_ref[...]).astype(bf16)
        out[at_core(1 - c, hw), :] = t_mm(beside(refs[n : 2 * n]), d_ref[...]).astype(bf16)

    return call(
        kernel, s, (*ctx, *ctx_in, d1), (1,),
        [pl.BlockSpec((t, part.shape[1]), lambda i, s: (s[0], 0)) for part in ctx] + [const(part.shape) for part in ctx_in]
        + [pl.BlockSpec((t, hw), lambda i, s: (0, 1 - s[0]))],
        const((width, hw)), shape((width, hw)), cost=2 * t * width * hw,
    )


def keep_grads(s, c2_keep, c2_give, d2, a2, dq_keep, pair_in, kv_keep, kv_give):
    t, width = d2.shape
    hw = width // 2

    def kernel(s_ref, ck, cg, d2_ref, a_ref, q_ref, p_ref, kk, kg, xgive, xkeep):
        c, h = s_ref[0], s_ref[1]
        for out, shard, kv in ((xgive, 1 - h, kg), (xkeep, h, kk)):
            rows = at_core(shard, hw)
            out[1] = (t_mm(a_ref[:, rows], q_ref[...]) + p_ref[1, rows, :].astype(f32)).astype(bf16)
            out[2] = kv[:hw]
            out[3] = kv[hw:]
        own_rows = t_mm(ck[...], d2_ref[...]) + p_ref[0, at_core(c, hw), :].astype(f32)
        far_rows = t_mm(cg[...], d2_ref[...]) + p_ref[0, at_core(1 - c, hw), :].astype(f32)
        xkeep[0] = jnp.where(c == h, own_rows, far_rows).astype(bf16)
        xgive[0] = jnp.where(c == h, far_rows, own_rows).astype(bf16)

    cols, half = pl.BlockSpec((t, hw), lambda i, s: (0, s[0])), const((t, hw))
    four = (4, hw, hw)
    return call(
        kernel, s, (c2_keep, c2_give, d2, a2, dq_keep, pair_in, kv_keep, kv_give), (1,),
        [half, half, cols, const((t, width)), half, const((2, width, hw)), const((width, hw)), const((width, hw))],
        [const(four), const(four)], [shape(four), shape(four)], cost=4 * t * width * hw,
    )


def keep_grad_out(s, ctx, ctx_in, d1, out_in):
    t, width = d1.shape
    hw = width // 2
    n = len(ctx)

    def kernel(s_ref, *refs):
        d1_ref, o_ref, xgive, xkeep = refs[2 * n :]
        c, h = s_ref[0], s_ref[1]
        own_rows = t_mm(beside(refs[:n]), d1_ref[...]) + o_ref[at_core(c, hw), :].astype(f32)
        far_rows = t_mm(beside(refs[n : 2 * n]), d1_ref[...]) + o_ref[at_core(1 - c, hw), :].astype(f32)
        xkeep[0] = jnp.where(c == h, own_rows, far_rows).astype(bf16)
        xgive[0] = jnp.where(c == h, far_rows, own_rows).astype(bf16)

    one = (1, hw, hw)
    return call(
        kernel, s, (*ctx, *ctx_in, d1, out_in), (1,),
        [pl.BlockSpec((t, part.shape[1]), lambda i, s: (s[0], 0)) for part in ctx] + [const(part.shape) for part in ctx_in]
        + [pl.BlockSpec((t, hw), lambda i, s: (0, s[0])), const((width, hw))],
        [const(one), const(one)], [shape(one), shape(one)], cost=2 * t * width * hw,
    )


def split_y(s, keeps, gots):
    _, rows, cols = keeps[0].shape
    half, n = rows // 2, len(keeps)
    counts = [k.shape[0] for k in keeps]

    def kernel(s_ref, *refs):
        give, mine = refs[2 * n :]
        for out, y in ((give, 1 - s_ref[4]), (mine, s_ref[4])):
            rows_at = pl.ds(pl.multiple_of(y * half, 64), half)
            at = 0
            for k_ref, g_ref, count in zip(refs[:n], refs[n : 2 * n], counts):
                out[at : at + count] = (k_ref[:, rows_at, :].astype(f32) + g_ref[:, rows_at, :].astype(f32)).astype(bf16)
                at += count

    dims = (sum(counts), half, cols)
    return call(kernel, s, (*keeps, *gots), (1,), [const(k.shape) for k in (*keeps, *gots)], [const(dims)] * 2, [shape(dims)] * 2)


def split_z(s, keep, got):
    b, rows, cols = keep.shape
    part = rows // 4

    def kernel(s_ref, k_ref, g_ref, *outs):
        for d, out in enumerate(outs):
            at = pl.ds(pl.multiple_of(s_ref[5 + d] * part, 16), part)
            out[...] = (k_ref[:, at, :].astype(f32) + g_ref[:, at, :].astype(f32)).astype(bf16)

    dims = (b, part, cols)
    return call(kernel, s, (keep, got), (1,), [const(keep.shape)] * 2, [const(dims)] * 4, [shape(dims)] * 4)


def sum_four(s, parts, vectors=()):
    b, part, cols = parts[0].shape

    def kernel(s_ref, p0, p1, p2, p3, *refs):
        out = refs[-1]
        total = (p0[...].astype(f32) + p1[...].astype(f32)) + (p2[...].astype(f32) + p3[...].astype(f32))
        out[0:b] = total.astype(bf16)
        if vectors:
            v = refs[0][...] + refs[1][...]
            high = v.astype(bf16).astype(f32)
            out[b] = jnp.concatenate([high, v - high], axis=0).astype(bf16)

    dims = (b + (1 if vectors else 0), part, cols)
    return call(
        kernel, s, (*parts, *vectors), (1,), [const(parts[0].shape)] * 4 + [const(v.shape) for v in vectors], const(dims), shape(dims)
    )


def pack_vectors(s, last, cross, mid, kv):
    width = last.shape[1]
    hw = width // 2
    units = mid.shape[1] // width

    def kernel(s_ref, l_ref, c_ref, m_ref, k_ref, give, mine):
        def line(ref, row, at=0):
            return ref[row : row + 1, at : at + width]

        zero = jnp.zeros((1, hw), f32)
        first = s_ref[0] == 0
        kv_row = jnp.concatenate([jnp.where(first, k_ref[0:1], zero), jnp.where(first, zero, k_ref[0:1])], axis=1)
        rows = [
            line(l_ref, 0), line(c_ref, 0), line(m_ref, 2, width), line(m_ref, 1, 2 * width),
            line(l_ref, 1), line(c_ref, 1), line(m_ref, 2, 2 * width), line(m_ref, 2),
            line(l_ref, 2), line(l_ref, 3), line(c_ref, 2), line(c_ref, 3), kv_row, line(m_ref, 1, width), line(m_ref, 1),
        ]
        halves = []
        for h in range(2):
            own = [row[:, h * hw : (h + 1) * hw] for row in rows]
            own += [m_ref[0:1, (h * units + j) * hw : (h * units + j + 1) * hw] for j in range(units)]
            halves.append(jnp.concatenate(own + [zero] * (24 - len(own)), axis=0))
        give[...] = jnp.where(s_ref[1] == 0, halves[1], halves[0])
        mine[...] = jnp.where(s_ref[1] == 0, halves[0], halves[1])

    return call(
        kernel, s, (last, cross, mid, kv), (1,), [const(x.shape) for x in (last, cross, mid, kv)],
        [const((24, hw))] * 2, [shape((24, hw), f32)] * 2,
    )


def join_z(s, parts):
    b, part, cols = parts[0].shape

    def kernel(s_ref, p0, p1, p2, p3, out):
        for d, ref in enumerate((p0, p1, p2, p3)):
            out[:, pl.ds(pl.multiple_of(s_ref[5 + d] * part, 16), part), :] = ref[...]

    dims = (b, 4 * part, cols)
    return call(kernel, s, parts, (1,), [const(parts[0].shape)] * 4, const(dims), shape(dims))


def spread_out(s, groups, outs, vectors=False):
    hw = 384

    def kernel(s_ref, *refs):
        results = refs[4 * len(groups) :]
        for n, (parts, spots) in enumerate(groups):
            b, half, cols = parts[0].shape
            for k, ref in enumerate(refs[4 * n : 4 * n + 4]):
                y = s_ref[4] if k % 2 == 0 else 1 - s_ref[4]
                core = s_ref[0] if k < 2 else 1 - s_ref[0]
                for block, (which, row, col) in enumerate(spots):
                    at_row = pl.multiple_of(row + y * half, 64)
                    at_col = pl.multiple_of(col + core * hw, 128)
                    results[which][pl.ds(at_row, half), pl.ds(at_col, cols)] = ref[block].astype(f32)
        if vectors:
            total = None
            for ref in refs[:4]:
                rows = ref[ref.shape[0] - 1].astype(f32)
                for z in range(4):
                    part = rows[48 * z : 48 * z + 48]
                    total = part if total is None else total + part
            results[-1][...] = total[0:24] + total[24:48]

    parts = [part for group, _ in groups for part in group]
    return call(kernel, s, parts, (1,), [const(part.shape) for part in parts], [const(d) for d in outs], [shape(d, f32) for d in outs])


def spread_ff(s, got):
    reps, _, per, width = got.shape
    units = 4
    rows = reps // units * per

    def kernel(s_ref, g_ref, one, two):
        one[...] = g_ref[:, 0].reshape(rows, width).astype(f32)
        two[...] = g_ref[:, 1].reshape(rows, width).astype(f32)

    return call(
        kernel, s, (got,), (units,), [pl.BlockSpec((reps // units, 2, per, width), lambda i, s: (i, 0, 0, 0))],
        [pl.BlockSpec((rows, width), lambda i, s: (0, i)), pl.BlockSpec((rows, width), lambda i, s: (i, 0))],
        [shape((rows, units * width), f32), shape((units * rows, width), f32)],
    )


def qkv_grad(s, a_own, a_sib, keep, give, mine):
    t, width = a_own.shape
    hw = width // 2
    n = len(keep)

    def kernel(s_ref, ao, ai, *refs):
        k, g = (jnp.concatenate([ref[0] for ref in part], axis=1) for part in (refs[:n], refs[n : 2 * n]))
        refs[-1][0] = (t_mm(ao[...], k) + t_mm(ai[...], g)).astype(bf16)

    cols = pl.BlockSpec((t, hw), lambda i, s: (0, s[1] if mine else 1 - s[1]))
    return call(
        kernel, s, (a_own, a_sib, *keep, *give), (3,),
        [cols, cols] + [pl.BlockSpec((1, t, part.shape[2]), lambda i, s: (i, 0, 0)) for part in (*keep, *give)],
        pl.BlockSpec((1, hw, hw), lambda i, s: (i, 0, 0)), shape((3, hw, hw)), cost=6 * t * width * hw,
    )


def last_rows(s, keep, recv, x_own, x_in, dh1, weight, table, rows=512):
    t, width = x_own.shape
    hw = width // 2
    n = len(keep)

    def kernel(s_ref, *refs):
        xo, xi, dh, w, tab, out, vec = refs[2 * n :]

        @pl.when(pl.program_id(0) == 0)
        def _():
            vec[...] = jnp.zeros(vec.shape, f32)

        c = s_ref[0]
        da = None
        for j in range(3):
            for parts, core in ((refs[:n], c), (refs[n : 2 * n], 1 - c)):
                d = jnp.concatenate([part[j] for part in parts], axis=1)
                at = pl.multiple_of(j * width + core * hw, 128)
                part = mm_t(d, w[:, pl.ds(at, hw)])
                da = part if da is None else da + part
                if j != 1:
                    line = 2 + j // 2
                    vec[line : line + 1, at_core(core, hw)] += jnp.sum(d.astype(f32), axis=0, keepdims=True)
        x = jnp.where(s_ref[2] == 1, xo[...].astype(f32), xi[...].astype(f32))
        dres, dgain, dshift = norm_back(x, tab[0:1], da)
        out[...] = (dh[...] + dres).astype(bf16)
        vec[0:1] += dgain
        vec[1:2] += dshift

    line = tile(rows, width)
    return call(
        kernel, s, (*keep, *recv, x_own, x_in, dh1, weight, table), (t // rows,),
        [pl.BlockSpec((3, rows, part.shape[2]), lambda i, s: (0, i, 0)) for part in (*keep, *recv)]
        + [line, line, line, once(weight.shape), const(table.shape)],
        [line, const((8, width))], [shape((t, width)), shape((8, width), f32)],
        cost=6 * t * width * width,
    )


EVERY = ("z", "y", "core", "x")
SPREAD2 = ("x", "z", "y", "core")
REP2 = ("z", "y", "core")
SWAP = [(1, 2), (2, 1)]


def tie(*values):
    return lax.optimization_barrier(values)


def across_z(x, d):
    return lax.ppermute(x, "z", [(j, j ^ d) for j in range(4)])


def across(x, axis):
    return lax.ppermute(x, axis, FLIP)


def body_pair(hidden, frames, segment, cotangent, norm_gain, norm_bias, self_qkv, self_out, cross_q, cross_kv, cross_out, fc1, fc2, proj_bias, fc1_bias):
    c, h = lax.axis_index("core"), lax.axis_index("x")
    y_at, z_at = lax.axis_index("y"), lax.axis_index("z")
    stay = c == h
    s = jnp.stack([c, h, stay.astype(jnp.int32), jnp.int32(0), y_at, z_at, z_at ^ 1, z_at ^ 2, z_at ^ 3]).astype(jnp.int32)
    rep_at = lax.axis_index(REP2)
    reps = lax.axis_size(REP2)
    width = self_out.shape[1]
    hw = width // 2
    ff = fc1.shape[1]
    units = ff // width
    pairs = hw // 128

    def swap(x):
        return lax.ppermute(x, ("core", "x"), SWAP)

    def sibling(x):
        return across(x, "core")

    def near(own):
        half = own.shape[0] // 2
        return across(lax.dynamic_slice_in_dim(own, c * half, half).astype(bf16), "x")

    x_own = hidden[0]
    small = jnp.concatenate([norm_gain, norm_bias, proj_bias, fc1_bias.reshape(units, hw), jnp.zeros((1, hw), f32)]).astype(bf16)
    small_in = across(small, "x")
    qkv_near = near(self_qkv)
    x_in = swap(x_own)
    seg = jnp.where(stay, segment, swap(segment))[0]
    per = hw * units // reps
    small = jnp.where(h == 0, jnp.stack([small, small_in]), jnp.stack([small_in, small])).astype(f32)
    table = jnp.concatenate([small[0, :16], small[1, :16]], axis=1)
    fc1_shift = small[:, 15:19].reshape(1, ff)
    kmark, qmark = seg_marks(seg)
    own1 = jnp.concatenate([fc1[:, j * width : (j + 1) * width] for j in range(units)]).astype(bf16).reshape(reps, per, width)
    own2 = fc2.astype(bf16).reshape(reps, per, width)
    slot = jnp.stack([lax.dynamic_index_in_dim(own1, rep_at, keepdims=False), lax.dynamic_index_in_dim(own2, rep_at, keepdims=False)])
    part = hw // 2
    squares = jnp.stack([lax.dynamic_slice_in_dim(w, c * part, part) for w in (self_out, cross_q, cross_out)]).astype(bf16)
    kv_part = lax.dynamic_slice_in_dim(cross_kv, c * hw, hw).astype(bf16)
    x_in, kmark, qmark, squares, kv_part, frames, own1, own2, slot = tie(x_in, kmark, qmark, squares, kv_part, frames, own1, own2, slot)
    slot = across(slot, "x")
    squares_near = across(squares, "x")
    f_own = frames[0]
    f_in = swap(f_own)
    kv_near = across(kv_part, "x")
    w_qkv, a1, keep, give = norm_qkv(s, x_own, x_in, (self_qkv, qkv_near, sibling(qkv_near)), table)
    give, slot = tie(give, slot)
    recv = sibling(give)
    ff_far = lax.all_gather(slot, REP2, axis=0, tiled=False)

    many = pairs - 1
    ctx_a, give_a, lse_a = self_fwd(0, many, c, keep, recv, kmark, qmark)
    give_a, keep, recv, squares_near, cotangent = tie(give_a, keep, recv, squares_near, cotangent)
    cot_in = swap(cotangent[0])
    squares_sib = sibling(squares_near)
    w_out, w_q, w_co = (
        (w, (squares_near, k), (squares_sib, k)) for k, w in enumerate((self_out, cross_q, cross_out))
    )
    in_a = sibling(give_a)
    ctx_b, give_b, lse_b = self_fwd(many, 1, c, keep, recv, kmark, qmark)
    in_b = sibling(give_b)
    ctx, ctx_in = (ctx_a, ctx_b), (in_a, in_b)
    w_out, w_q, h1, a2, qc = self_project(s, ctx, ctx_in, x_own, x_in, w_out, w_q, table)
    qc, f_in, kv_near = tie(qc, f_in, kv_near)
    half = jnp.where(stay, f_own, f_in)
    twin = sibling(half)
    w_kv, kc, vc = frame_kv(s, half, twin, (cross_kv, kv_near, sibling(kv_near)), table)
    count = half.shape[0]
    own_pairs, far_pairs = c * pairs, (1 - c) * pairs
    c2_give, cross_lse_give = cross_fwd(far_pairs, pairs, qc, kc, vc, count)
    c2_keep, cross_lse_keep = cross_fwd(own_pairs, pairs, qc, kc, vc, count)
    _, out, a3, g, dm, du, d2, dh2, dc2_keep, dc2_give, vec_mid = middle(
        s, h1, c2_keep, c2_give, cotangent[0], cot_in, w_co, (own1, own2), ff_far, table, fc1_shift,
    )

    packed = ff_grads(s, a3, du, g, dm)
    dc2_give, packed, out, a1_out = tie(dc2_give, packed, out, a1)
    ff_mine = lax.psum_scatter(packed.reshape(2 * reps, 2 * per, width), SPREAD2, scatter_dimension=0, tiled=False)
    out_in = swap(out)
    a1_sib = sibling(a1_out)
    dq_give, dkv_give = cross_bwd(far_pairs, pairs, qc, kc, vc, c2_give, dc2_give, cross_lse_give, count)
    dkv_give, dq_give = tie(dkv_give, dq_give)
    dkv_in = sibling(dkv_give)
    pair_give = give_grads(s, c2_keep, c2_give, d2, a2, dq_give)
    pair_give, dc2_keep = tie(pair_give, dc2_keep)
    pair_in = sibling(pair_give)
    dq_keep, dkv_keep = cross_bwd(own_pairs, pairs, qc, kc, vc, c2_keep, dc2_keep, cross_lse_keep, count)
    dq_keep, out_in, dkv_in, a1_sib, pair_in = tie(dq_keep, out_in, dkv_in, a1_sib, pair_in)
    fkeep, fgive, kv_xkeep, kv_xgive, vec_kv = frame_back(s, dkv_keep, dkv_in, half, twin, w_kv)
    fgive, dq_keep = tie(fgive, dq_keep)
    fr_in = sibling(fgive)
    xgive, xkeep = keep_grads(s, c2_keep, c2_give, d2, a2, dq_keep, pair_in, kv_xkeep, kv_xgive)
    xgive, dq_keep = tie(xgive, dq_keep)
    got_x = across(xgive, "x")
    dh1, d1, dctx_keep, dctx_give, vec_cross = cross_back(s, dq_keep, dq_give, h1, dh2, w_q, w_out, table)
    dctx_give, d1 = tie(dctx_give, d1)
    dctx_in = sibling(dctx_give)
    so_give = give_grad_out(s, ctx, ctx_in, d1)
    so_give, fr_in, fkeep = tie(so_give, fr_in, fkeep)
    so_in = sibling(so_give)
    fr_own = (fkeep.astype(f32) + fr_in.astype(f32)).astype(bf16)
    fr_own, dctx_keep = tie(fr_own, dctx_keep)
    fr_swapped = swap(fr_own)
    so_xgive, so_xkeep = keep_grad_out(s, ctx, ctx_in, d1, so_in)
    so_xgive, dctx_keep = tie(so_xgive, dctx_keep)
    so_x = across(so_xgive, "x")

    def send_z(pieces):
        return (pieces[0],) + tuple(across_z(pieces[d], d) for d in (1, 2, 3))

    def gather_z(piece):
        return (piece,) + tuple(across_z(piece, d) for d in (1, 2, 3))

    bg1, bk1 = self_bwd(0, 1, 0, c, keep, recv, ctx_a, dctx_keep, dctx_in, lse_a, kmark, qmark)
    bg1, bk1, keep = tie(bg1, bk1, keep)
    bi1 = sibling(bg1)
    bg2, bk2 = self_bwd(1, 1, 1, c, keep, recv, ctx_a, dctx_keep, dctx_in, lse_a, kmark, qmark)
    bg2, bk2, got_x, so_x, keep, bi1, fr_swapped = tie(bg2, bk2, got_x, so_x, keep, bi1, fr_swapped)
    bi2 = sibling(bg2)
    m_ygive, m_ykeep = split_y(s, (xkeep, so_xkeep), (got_x, so_x))
    m_ygive, keep, ff_mine = tie(m_ygive, keep, ff_mine)
    m_y = across(m_ygive, "y")
    ff_got = lax.all_gather(ff_mine, REP2, axis=0, tiled=False)
    bg3, bk3 = self_bwd(2, 1, 0, c, keep, recv, ctx_b, dctx_keep, dctx_in, lse_b, kmark, qmark)
    bg3, bk3, m_y, bi2 = tie(bg3, bk3, m_y, bi2)
    bi3 = sibling(bg3)
    q_xgive = qkv_grad(s, a1, a1_sib, (bk1, bk2, bk3), (bg1, bg2, bg3), False)
    q_xgive, m_y = tie(q_xgive, m_y)
    q_x = across(q_xgive, "x")
    m_z = split_z(s, m_ykeep, m_y)
    bk3, dh1, *m_z = tie(bk3, dh1, *m_z)
    m_z = send_z(m_z)
    q_xkeep = qkv_grad(s, a1, a1_sib, (bk1, bk2, bk3), (bg1, bg2, bg3), True)
    grad_hidden, vec_last = last_rows(s, (bk1, bk2, bk3), (bi1, bi2, bi3), x_own, x_in, dh1, w_qkv, table)
    vec_last, *m_z = tie(vec_last, *m_z)
    m_all = gather_z(sum_four(s, m_z))
    v_give, v_mine = pack_vectors(s, vec_last, vec_cross, vec_mid, vec_kv)
    v_got = across(v_give, "x")
    v_mine, q_x = tie(v_mine, q_x)
    q_ygive, q_ykeep = split_y(s, (q_xkeep,), (q_x,))
    q_ygive, grad_hidden = tie(q_ygive, grad_hidden)
    q_y = across(q_ygive, "y")
    hid_in = swap(grad_hidden)
    q_four = split_z(s, q_ykeep, q_y)
    *q_four, m_first = tie(*q_four, m_all[0])
    q_z = send_z(q_four)
    m_own = join_z(s, (m_first, *m_all[1:]))
    m_far = across(m_own, "y")
    fc1_grad, fc2_grad = spread_ff(s, ff_got.reshape(reps, 2, per, width))
    m_own_sib = sibling(m_own)
    output = jnp.where(stay, out, out_in)
    fc1_grad, fc2_grad, output, *q_z = tie(fc1_grad, fc2_grad, output, *q_z)
    q_piece = sum_four(s, q_z, (v_mine, v_got))
    q_piece, m_far = tie(q_piece, m_far)
    q_all = gather_z(q_piece)
    spots = ((0, 0, 0), (1, 0, 0), (3, 0, 0), (3, hw, 0), (2, 0, 0))
    crossout_grad, crossq_grad, selfout_grad, kv_grad = spread_out(
        s, (((m_own, m_far, m_own_sib, sibling(m_far)), spots),), ((hw, width),) * 3 + ((width, width),)
    )
    grad_frames = jnp.where(stay, fr_own, fr_swapped)
    grad_hidden = jnp.where(stay, grad_hidden, hid_in)
    crossout_grad, grad_frames, grad_hidden, *q_all = tie(crossout_grad, grad_frames, grad_hidden, *q_all)
    q_own = join_z(s, q_all)
    q_far = across(q_own, "y")
    q_own_sib = sibling(q_own)
    first = tuple((0, 0, j * width) for j in range(3))
    qkv_grad_out, mine = spread_out(s, (((q_own, q_far, q_own_sib, sibling(q_far)), first),), ((hw, 3 * width), (24, hw)), True)

    return (
        output[None], grad_hidden[None], grad_frames[None], mine[:4], mine[4:8],
        qkv_grad_out, selfout_grad, crossq_grad, kv_grad, crossout_grad, fc1_grad, fc2_grad, mine[8:15], mine[15:19].reshape(-1),
    )


GROUP = ("core", "ilo")
SHARD = ("ihi", "ilo")
REP = ("rz", "core")
SPREAD = ("ihi", "ilo", "rz", "core")


def body_general(hidden, frames, segment, cotangent, norm_gain, norm_bias, self_qkv, self_out, cross_q, cross_kv, cross_out, fc1, fc2, proj_bias, fc1_bias):
    c = lax.axis_index("core")
    hi = lax.axis_index("ihi")
    n = lax.axis_size("core") * lax.axis_size("ilo")
    reps = lax.axis_size("rz") * lax.axis_size("core")
    rep_at = lax.axis_index(REP)
    width = self_out.shape[1]
    ff = fc1.shape[1]

    def swap(x):
        return lax.ppermute(x, ("core", "ihi"), [(0, 0), (1, 2), (2, 1), (3, 3)])

    def whole(own):
        if n != 2:
            return lax.all_gather(own, SHARD, axis=0, tiled=True)
        half = own.shape[0] // 2
        mine = lax.ppermute(lax.dynamic_slice_in_dim(own, c * half, half), "ihi", FLIP)
        sib = lax.ppermute(mine, "core", FLIP)
        other = jnp.where(c == 0, jnp.concatenate([mine, sib]), jnp.concatenate([sib, mine]))
        return jnp.where(hi == 0, jnp.concatenate([own, other]), jnp.concatenate([other, own]))

    def slices(own):
        rows = own.shape[0] // reps
        return lax.dynamic_slice_in_dim(own, rep_at * rows, rows)

    rows_in = swap(hidden[0])
    qkv_w = whole(self_qkv.astype(bf16))
    small = jnp.concatenate([norm_gain.astype(bf16), norm_bias.astype(bf16), proj_bias.astype(bf16), fc1_bias.astype(bf16).reshape(-1, norm_gain.shape[1]), jnp.zeros((1, norm_gain.shape[1]), bf16)])
    small = lax.all_gather(small, SHARD, axis=1, tiled=False).astype(f32)
    table = small[:15].reshape(15, width)
    gains, shifts, biases = table[:4], table[4:8], table[8:15]
    fc1_shift = small[15:19].transpose(1, 0, 2).reshape(ff)
    seg = swap(segment)[0]
    frames_half = swap(frames[0])
    if n == 2:
        twin = lax.ppermute(frames_half, "core", FLIP)
        frame_rows = jnp.concatenate([jnp.where(c == 0, frames_half, twin), jnp.where(c == 0, twin, frames_half)], axis=1)
    else:
        frame_rows = lax.all_gather(frames_half, GROUP, axis=1, tiled=True)
    selfout_w = whole(self_out.astype(bf16))
    crossq_w = whole(cross_q.astype(bf16))
    kv_w = whole(cross_kv.astype(bf16)) if n == 2 else None
    if n == 2:
        k_w, v_w = kv_w[:width], kv_w[width:]
    else:
        kv_w = lax.all_gather(cross_kv.astype(bf16), SHARD, axis=1, tiled=True)
        k_w, v_w = kv_w[:, :width], kv_w[:, width:]
    crossout_w = whole(cross_out.astype(bf16))
    cot = swap(cotangent[0])
    units = ff // width
    part1 = slices(fc1.astype(bf16))
    part2 = slices(fc2.astype(bf16))
    few = part1.shape[0]
    parts = jnp.concatenate([part1[:, j * width : (j + 1) * width] for j in range(units)] + [part2])
    ffw = lax.all_gather(parts, SPREAD, axis=0, tiled=False)
    fc1_w = jnp.concatenate([ffw[:, j * few : (j + 1) * few].reshape(width, width) for j in range(units)], axis=1)
    fc2_w = ffw[:, units * few :].reshape(ff, width)

    own_rows = rows_in.shape[0]
    hw = -(-HEADS // n)
    padded = hw * n * HD - width

    lanes = hw * HD

    def to_heads(x):
        x = x.reshape(own_rows, -1, width)
        if padded:
            x = jnp.pad(x, ((0, 0), (0, 0), (0, padded)))
        x = x.reshape(own_rows, -1, n, lanes).transpose(1, 2, 0, 3)
        x = lax.all_to_all(x, GROUP, 1, 1, tiled=True)
        return x.reshape(-1, n * own_rows, lanes)

    def to_tokens(x):
        x = lax.all_to_all(x.reshape(-1, n, own_rows, lanes), GROUP, 1, 1, tiled=True)
        return x.transpose(2, 0, 1, 3).reshape(own_rows, -1, n * lanes)[:, :, :width].reshape(own_rows, -1)

    h0 = rows_in.astype(f32)
    a1 = norm(h0, gains[0], shifts[0]).astype(bf16)
    zeros_row = jnp.zeros((width,), f32)
    qkv = (mm(a1, qkv_w) + jnp.concatenate([biases[0], zeros_row, biases[1]])).astype(bf16)
    heads = to_heads(qkv)
    kmark, qmark = seg_marks(seg)
    mid = heads.shape[1] // 2
    first = jnp.int32(0)
    ctx, _, self_lse = self_fwd(0, lanes // 128, first, heads[:, :mid], heads[:, mid:], kmark, qmark)
    c1 = to_tokens(ctx)
    h1 = h0 + mm(c1, selfout_w) + biases[2]
    a2 = norm(h1, gains[1], shifts[1]).astype(bf16)
    qc = (mm(a2, crossq_w) + biases[3]).astype(bf16)
    count = frame_rows.shape[0]
    pad = -count % 256
    frame_pad = jnp.pad(frame_rows, ((0, pad), (0, 0)))
    kc = mm(frame_pad, k_w).astype(bf16)
    live = lax.broadcasted_iota(jnp.int32, (count + pad, 1), 0) < count
    vc = (mm(frame_pad, v_w) + jnp.where(live, biases[4], 0.0)).astype(bf16)
    c2, cross_lse = cross_fwd(first, width // 128, qc, kc, vc, count)
    h2 = h1 + mm(c2, crossout_w) + biases[5]
    a3 = norm(h2, gains[2], shifts[2]).astype(bf16)
    u = (mm(a3, fc1_w) + fc1_shift).astype(bf16)
    uf = u.astype(f32)
    g, slope = gelu_parts(uf)
    g = g.astype(bf16)
    h3 = h2 + mm(g, fc2_w) + biases[6]
    output = norm(h3, gains[3], shifts[3]).astype(bf16)
    output = swap(output)

    def total(x):
        return jnp.sum(x.astype(f32), axis=0)

    dh3, gain3, shift3 = norm_back(h3, gains[3], cot.astype(f32))
    dm = dh3.astype(bf16)
    g_fc2 = t_mm(g, dm).astype(bf16)
    du = (slope * mm_t(dm, fc2_w)).astype(bf16)
    g_fc1 = t_mm(a3, du).astype(bf16)

    def reduce_rows(parts, extra=None):
        total = n * reps
        cut = [p.reshape(total, -1, width) for p in parts]
        if extra is not None:
            cut.append(extra)
        flat = jnp.concatenate(cut, axis=1)
        mine = lax.psum_scatter(flat, SPREAD, scatter_dimension=0, tiled=False)
        got = lax.all_gather(mine, REP, axis=0, tiled=False)
        out, at = [], 0
        for p in cut:
            out.append(got[:, at : at + p.shape[1]].reshape(-1, width).astype(f32))
            at += p.shape[1]
        return out

    ff_grads = reduce_rows([g_fc1[:, j * width : (j + 1) * width] for j in range(units)] + [g_fc2])
    fc1_grad = jnp.concatenate(ff_grads[:units], axis=1)
    fc2_grad = ff_grads[units]

    da3 = mm_t(du, fc1_w)
    dres, gain2, shift2 = norm_back(h2, gains[2], da3)
    dh2 = dh3 + dres
    d2 = dh2.astype(bf16)
    g_crossout = t_mm(c2, d2).astype(bf16)
    dc2 = mm_t(d2, crossout_w).astype(bf16)
    dqc, (dkc, dvc) = cross_bwd(first, width // 128, qc, kc, vc, c2, dc2, cross_lse, count)
    share = width // n

    def sum_columns(x):
        return lax.psum_scatter(x, GROUP, scatter_dimension=1, tiled=True)

    if n == 2:

        def sum_columns(x):
            give = lax.dynamic_slice_in_dim(x, (1 - c) * share, share, axis=1)
            keep = lax.dynamic_slice_in_dim(x, c * share, share, axis=1)
            return (keep.astype(f32) + lax.ppermute(give, "core", FLIP).astype(f32)).astype(bf16)

    dk_own = sum_columns(dkc)[:count]
    dv_own = sum_columns(dvc)[:count]
    place = lax.axis_index(GROUP) * share
    kw_own = lax.dynamic_slice_in_dim(k_w, place, share, axis=1)
    vw_own = lax.dynamic_slice_in_dim(v_w, place, share, axis=1)
    dframe = (mm_t(dk_own, kw_own) + mm_t(dv_own, vw_own)).astype(bf16)
    grad_frames = swap(sum_columns(dframe))
    g_k = t_mm(frame_rows, dk_own).astype(bf16)
    g_v = t_mm(frame_rows, dv_own).astype(bf16)
    vb_own = jnp.sum(dv_own.astype(f32), axis=0)

    g_crossq = t_mm(a2, dqc).astype(bf16)
    da2 = mm_t(dqc, crossq_w)
    dres, gain1, shift1 = norm_back(h1, gains[1], da2)
    dh1 = dh2 + dres
    d1 = dh1.astype(bf16)
    g_selfout = t_mm(c1, d1).astype(bf16)
    dctx = mm_t(d1, selfout_w).astype(bf16)
    dctx = to_heads(dctx)[0]
    late, early = self_bwd(0, lanes // 128, 0, first, heads[:, :mid], heads[:, mid:], ctx, dctx[:mid], dctx[mid:], self_lse, kmark, qmark)
    dqkv = to_tokens(jnp.concatenate([early, late], axis=1))
    da1 = mm_t(dqkv, qkv_w)
    g_qkv = t_mm(a1, dqkv).astype(bf16)
    sums = total(dqkv)
    dres, gain0, shift0 = norm_back(h0, gains[0], da1)
    grad_hidden = swap((dh1 + dres).astype(bf16))

    vb = lax.dynamic_update_slice(jnp.zeros((width,), f32), vb_own, (place,))
    vectors = jnp.stack([gain0[0], gain1[0], gain2[0], gain3[0], shift0[0], shift1[0], shift2[0], shift3[0], sums[:width], sums[2 * width :], total(d1), total(dqc), vb, total(d2), total(dm)])
    per = width // n
    vectors = vectors.reshape(15, n, per).transpose(1, 0, 2).reshape(n, 15 * per)
    vectors = jnp.concatenate([vectors, total(du).reshape(n, ff // n)], axis=1)
    long = vectors.shape[1]
    seats = -(-long // reps)
    vectors = jnp.pad(vectors, ((0, 0), (0, seats * reps - long))).reshape(n * reps, seats)
    lines = -(-seats // (8 * width)) * 8
    vectors = jnp.pad(vectors, ((0, 0), (0, lines * width - seats))).reshape(n * reps, lines, width)

    def own_columns(x):
        return lax.dynamic_update_slice(jnp.zeros((x.shape[0], width), x.dtype), x, (jnp.int32(0), place))

    cross = [g_crossq, g_crossout]
    if n == 2:
        cross.append(jnp.concatenate([own_columns(g_k), own_columns(g_v)]))
    cross = reduce_rows(cross)
    crossq_grad, crossout_grad = cross[:2]
    if n == 2:
        kv_grad = cross[2]
    else:
        kv_cols = jnp.concatenate([own_columns(g_k), own_columns(g_v)], axis=1)
        kv_cols = lax.psum_scatter(kv_cols, SHARD, scatter_dimension=1, tiled=True)
        kv_grad = lax.psum(kv_cols, REP).astype(f32)
    got = reduce_rows([g_qkv[:, j * width : (j + 1) * width] for j in range(3)] + [g_selfout], vectors.astype(bf16))
    qkv_grad = jnp.concatenate(got[:3], axis=1)
    selfout_grad = got[3]
    vec = got[4].reshape(reps, lines * width)[:, :seats].reshape(-1)[:long]
    table = vec[: 15 * per].reshape(15, per)
    fc1b_grad = vec[15 * per :]
    return (
        output[None], grad_hidden[None], grad_frames[None],
        table[:4], table[4:8], qkv_grad, selfout_grad, crossq_grad, kv_grad, crossout_grad, fc1_grad, fc2_grad, table[8:15], fc1b_grad,
    )


def solution(mesh):
    reps, n = mesh.devices.shape
    paired = (reps, n) == (16, 2)
    if paired:
        work = Mesh(mesh.devices.reshape(4, 2, 2, 2), EVERY)
        rep, inner = REP2, ("x",)
    else:
        work = Mesh(mesh.devices.reshape(reps // 2, 2, 2, n // 2), ("rz", "core", "ihi", "ilo"))
        rep, inner = REP, SHARD
    rows, cols = P(inner, None), P(None, inner)
    tokens, features = P(rep, inner, None), P(rep, None, inner)
    weights = (cols, cols, rows, rows, rows, cols, rows, rows, rows, cols, P(inner))
    return jax.shard_map(
        body_pair if paired else body_general,
        mesh=work,
        in_specs=(tokens, features, P(rep, None), tokens) + weights,
        out_specs=(tokens, tokens, features) + weights,
        check_vma=False,
    )
```

```python
import math

import jax
import jax.numpy as jnp
from jax import lax
from jax.experimental import pallas as pl
from jax.experimental.pallas import tpu as pltpu
from jax.sharding import Mesh
from jax.sharding import PartitionSpec as P

HEADS = 12
HD = 64
EPSILON = 1e-05
NEG = -1e30
PROMPT = 1024
REACH = 256
bf16 = jnp.bfloat16
f32 = jnp.float32
FLIP = [(0, 1), (1, 0)]


def mm(a, b):
    return jnp.dot(a, b, preferred_element_type=f32)


def mm_t(a, b):
    return lax.dot_general(a, b, (((1,), (1,)), ((), ())), preferred_element_type=f32)


def t_mm(a, b):
    return lax.dot_general(a, b, (((0,), (0,)), ((), ())), preferred_element_type=f32)


def call(kernel, scalars, args, grid, in_specs, out_specs, out_shape, scratch=(), cost=None):
    spec = pltpu.PrefetchScalarGridSpec(
        num_scalar_prefetch=1, grid=grid, in_specs=in_specs, out_specs=out_specs, scratch_shapes=list(scratch)
    )
    estimate = None
    if cost is not None:
        estimate = pl.CostEstimate(flops=cost // 10, bytes_accessed=1 << 20, transcendentals=0)
    return pl.pallas_call(
        kernel,
        grid_spec=spec,
        out_shape=out_shape,
        cost_estimate=estimate,
        compiler_params=pltpu.CompilerParams(vmem_limit_bytes=60 * 2**20),
    )(scalars, *args)


def shape(dims, kind=bf16):
    return jax.ShapeDtypeStruct(dims, kind)


def half_of(lane, h):
    return (lane < HD) if h == 0 else (lane >= HD)


def delta_of(do, o):
    x = do.astype(f32) * o.astype(f32)
    hi = x.astype(bf16)
    lo = (x - hi.astype(f32)).astype(bf16)
    r = lax.broadcasted_iota(jnp.int32, (8, 128), 0)
    lane = lax.broadcasted_iota(jnp.int32, (8, 128), 1)
    pick = jnp.where((lane // HD) == r, 1.0, 0.0).astype(bf16)
    return mm_t(pick, hi) + mm_t(pick, lo)


def cross_fwd(base, pairs, q, k, v, valid, block=1024):
    tq, tk = q.shape[0], k.shape[0]
    block = min(block, tq)

    def kernel(s_ref, q_ref, k_ref, v_ref, o_ref, l_ref, ks, vts):
        @pl.when(pl.program_id(1) == 0)
        def _():
            low = lax.broadcasted_iota(jnp.int32, (tk, 128), 1)
            row = lax.broadcasted_iota(jnp.int32, (tk, 128), 0)
            bias = jnp.where(row >= valid, NEG, 0.0).astype(bf16)
            one = jnp.ones((tk, 128), bf16)
            for h in range(2):
                ks[h] = jnp.where(half_of(low, h), k_ref[...], bias)
                vts[h] = jnp.where(half_of(low, h), v_ref[...], one).T

        lane = lax.broadcasted_iota(jnp.int32, (block, 128), 1)
        qq = q_ref[...] * bf16(0.125)
        scores = []
        for h in range(2):
            spare = lane == (HD if h == 0 else 0)
            qh = jnp.where(half_of(lane, h), qq, jnp.where(spare, 1.0, 0.0).astype(bf16))
            scores.append(mm_t(ks[h], qh))
        outs = []
        for h, s in enumerate(scores):
            m = jnp.max(s, axis=0, keepdims=True)
            o = mm(vts[h], jnp.exp(s - m).astype(bf16))
            total = o[HD : HD + 1] if h == 0 else o[0:1]
            outs.append(o * (1.0 / total))
            l_ref[0, h : h + 1, :] = m + jnp.log(total)
        sub = lax.broadcasted_iota(jnp.int32, (128, block), 0)
        o_ref[...] = jnp.where(sub < HD, outs[0], outs[1]).T.astype(bf16)

    qspec = pl.BlockSpec((block, 128), lambda p, i, s: (i, s[0] + p))
    kspec = pl.BlockSpec((tk, 128), lambda p, i, s: (0, s[0] + p))
    return call(
        kernel, jnp.reshape(base, (1,)).astype(jnp.int32), (q, k, v), (pairs, tq // block), [qspec, kspec, kspec],
        [pl.BlockSpec((block, 128), lambda p, i, s: (i, p)), pl.BlockSpec((1, 8, block), lambda p, i, s: (p, 0, i))],
        [shape((tq, pairs * 128)), shape((pairs, 8, tq), f32)],
        [pltpu.VMEM((2, tk, 128), bf16), pltpu.VMEM((2, 128, tk), bf16)],
        4 * tq * tk * 256 * pairs,
    )


def cross_bwd(base, pairs, q, k, v, o, do, lse, valid, block=1024):
    tq, tk = q.shape[0], k.shape[0]
    block = min(block, tq)
    steps = tq // block

    def kernel(s_ref, q_ref, k_ref, v_ref, o_ref, do_ref, l_ref, dq_ref, d_ref, ks, kts, dka, dva):
        @pl.when(pl.program_id(1) == 0)
        def _():
            low = lax.broadcasted_iota(jnp.int32, (tk, 128), 1)
            row = lax.broadcasted_iota(jnp.int32, (tk, 128), 0)
            bias = jnp.where(row >= valid, NEG, 0.0).astype(bf16)
            zero = jnp.zeros((tk, 128), bf16)
            for h in range(2):
                ks[h] = jnp.where(half_of(low, h), k_ref[...], bias)
                kts[h] = jnp.where(half_of(low, h), k_ref[...], zero).T
            dka[...] = jnp.zeros((tk, 128), f32)
            dva[...] = jnp.zeros((tk, 128), f32)

        lane = lax.broadcasted_iota(jnp.int32, (block, 128), 1)
        qq = q_ref[...] * bf16(0.125)
        dd = do_ref[...]
        delta = delta_of(dd, o_ref[...])
        zero = jnp.zeros((block, 128), bf16)
        dqt, dk, dv = None, dka[...], dva[...]

        def products(h):
            mine = half_of(lane, h)
            spare = lane == (HD if h == 0 else 0)
            qc = jnp.where(mine, qq, zero)
            dh = jnp.where(mine, dd, zero)
            return qc, dh, mm_t(ks[h], jnp.where(spare, jnp.ones((block, 128), bf16), qc)), mm_t(v_ref[...], dh)

        now = products(0)
        for h in range(2):
            qc, dh, scores, dp = now
            now = products(1) if h == 0 else None
            p = jnp.exp(scores - l_ref[0, h : h + 1, :])
            ds = (p * (dp - delta[h : h + 1])).astype(bf16)
            dv = dv + mm(p.astype(bf16), dh)
            dk = dk + mm(ds, qc)
            part = mm(kts[h], ds)
            dqt = part if dqt is None else dqt + part
        dka[...] = dk
        dva[...] = dv
        dq_ref[...] = (dqt * 0.125).T.astype(bf16)

        @pl.when(pl.program_id(1) == steps - 1)
        def _():
            d_ref[0] = dka[...].astype(bf16)
            d_ref[1] = dva[...].astype(bf16)

    mine = pl.BlockSpec((block, 128), lambda p, i, s: (i, p))
    qspec = pl.BlockSpec((block, 128), lambda p, i, s: (i, s[0] + p))
    kspec = pl.BlockSpec((tk, 128), lambda p, i, s: (0, s[0] + p))
    return call(
        kernel, jnp.reshape(base, (1,)).astype(jnp.int32), (q, k, v, o, do, lse), (pairs, steps),
        [qspec, kspec, kspec, mine, mine, pl.BlockSpec((1, 8, block), lambda p, i, s: (p, 0, i))],
        [mine, pl.BlockSpec((2, tk, 128), lambda p, i, s: (0, 0, p))],
        [shape((tq, pairs * 128)), shape((2, tk, pairs * 128))],
        [pltpu.VMEM((2, tk, 128), bf16), pltpu.VMEM((2, 128, tk), bf16), pltpu.VMEM((tk, 128), f32), pltpu.VMEM((tk, 128), f32)],
        2 * tq * tk * 10 * 256 * pairs,
    )


def spans(r0, block):
    if r0 < PROMPT:
        return ([(0, r0)] if r0 else []) + [(r0, r0 + block)]
    left = max(PROMPT, r0 - REACH)
    before = [(0, r0)] if left == PROMPT else [(0, PROMPT), (left, r0)]
    return before + [(r0, r0 + block)]


def seg_marks(seg):
    lane = lax.broadcasted_iota(jnp.int32, (seg.shape[0], 128), 1) % HD
    same = lane == seg[:, None]
    kmark = jnp.where(same, 1.0, 0.0).astype(bf16)
    qmark = jnp.where(same | (lane == 0) | (lane > 8), 0.0, NEG).astype(bf16)
    return kmark, qmark


def half_specs(rows, first=0):
    return [pl.BlockSpec((3, rows, 128), lambda p, s: (0, 0, first + p))] * 2


def self_fwd(first, pairs, place, keep, recv, kmark, qmark, block=512):
    rows, width = keep.shape[1], pairs * 128
    t = 2 * rows

    def kernel(s_ref, a_ref, b_ref, km_ref, qm_ref, o_ref, give_ref, l_ref, qf, ks, vts):
        mine0 = pl.multiple_of(s_ref[0] * rows, rows)
        other0 = pl.multiple_of((1 - s_ref[0]) * rows, rows)
        low = lax.broadcasted_iota(jnp.int32, (rows, 128), 1)
        one = jnp.ones((rows, 128), bf16)
        for ref, at in ((a_ref, mine0), (b_ref, other0)):
            spot = pl.ds(at, rows)
            qf[spot, :] = ref[0] * bf16(0.125)
            for h in range(2):
                ks[h, spot, :] = jnp.where(half_of(low, h), ref[1], km_ref[spot, :])
                vts[h, :, spot] = jnp.where(half_of(low, h), ref[2], one).T
        lane = lax.broadcasted_iota(jnp.int32, (block, 128), 1)
        hide = lax.broadcasted_iota(jnp.int32, (block, block), 0) > lax.broadcasted_iota(jnp.int32, (block, block), 1)
        tasks = [(r0, h) for r0 in range(0, t, block) for h in range(2)]

        def scores(task):
            r0, h = task
            spot = pl.ds(r0, block)
            qs = jnp.where(half_of(lane, h), qf[spot, :], qm_ref[spot, :])
            out = [mm_t(ks[h, pl.ds(a, b - a), :], qs) for a, b in spans(r0, block)]
            out[-1] = jnp.where(hide, NEG, out[-1])
            return out

        now, outs = scores(tasks[0]), [None, None]
        for i, (r0, h) in enumerate(tasks):
            later = scores(tasks[i + 1]) if i + 1 < len(tasks) else None
            m = None
            for s in now:
                top = jnp.max(s, axis=0, keepdims=True)
                m = top if m is None else jnp.maximum(m, top)
            o = None
            for s, (a, b) in zip(now, spans(r0, block)):
                part = mm(vts[h, :, pl.ds(a, b - a)], jnp.exp(s - m).astype(bf16))
                o = part if o is None else o + part
            total = o[HD : HD + 1] if h == 0 else o[0:1]
            l_ref[0, h : h + 1, pl.ds(r0, block)] = m + jnp.log(total)
            outs[h] = o * (1.0 / total)
            if h == 1:
                sub = lax.broadcasted_iota(jnp.int32, (128, block), 0)
                o_ref[pl.ds(r0, block), :] = jnp.where(sub < HD, outs[0], outs[1]).T.astype(bf16)
            now = later
        give_ref[...] = o_ref[pl.ds(other0, rows), :]

    whole = pl.BlockSpec((t, 128), lambda p, s: (0, 0))
    return call(
        kernel, jnp.reshape(place, (1,)).astype(jnp.int32), (keep, recv, kmark, qmark), (pairs,),
        half_specs(rows, first) + [whole, whole],
        [pl.BlockSpec((t, 128), lambda p, s: (0, p)), pl.BlockSpec((rows, 128), lambda p, s: (0, p)), pl.BlockSpec((1, 8, t), lambda p, s: (p, 0, 0))],
        [shape((t, width)), shape((rows, width)), shape((pairs, 8, t), f32)],
        [pltpu.VMEM((t, 128), bf16), pltpu.VMEM((2, t, 128), bf16), pltpu.VMEM((2, 128, t), bf16)],
        2 * t * t * 4 * width,
    )


def self_bwd(first, pairs, seat, place, keep, recv, o, dkeep, drecv, lse, kmark, qmark, block=256):
    rows, width = keep.shape[1], pairs * 128
    t = 2 * rows

    def kernel(s_ref, a_ref, b_ref, o_ref, da_ref, db_ref, l_ref, km_ref, qm_ref, give_ref, keep_ref, qf, df, vf, ks, kts, dqa, dka, dva):
        mine0 = pl.multiple_of(s_ref[0] * rows, rows)
        other0 = pl.multiple_of((1 - s_ref[0]) * rows, rows)
        low = lax.broadcasted_iota(jnp.int32, (rows, 128), 1)
        zero = jnp.zeros((rows, 128), bf16)
        for ref, dref, at in ((a_ref, da_ref, mine0), (b_ref, db_ref, other0)):
            spot = pl.ds(at, rows)
            qf[spot, :] = ref[0] * bf16(0.125)
            df[spot, :] = dref[...]
            vf[spot, :] = ref[2]
            for h in range(2):
                ks[h, spot, :] = jnp.where(half_of(low, h), ref[1], km_ref[spot, :])
                kts[h, :, spot] = jnp.where(half_of(low, h), ref[1], zero).T
        dka[...] = jnp.zeros((t, 128), f32)
        dva[...] = jnp.zeros((t, 128), f32)
        lane = lax.broadcasted_iota(jnp.int32, (block, 128), 1)
        hide = lax.broadcasted_iota(jnp.int32, (block, block), 0) > lax.broadcasted_iota(jnp.int32, (block, block), 1)
        none = jnp.zeros((block, 128), bf16)
        for r0 in range(0, t, block):
            spot = pl.ds(r0, block)
            dd = df[spot, :]
            delta = delta_of(dd, o_ref[spot, :])
            dqt = None
            tasks = []
            for h in range(2):
                mine = half_of(lane, h)
                qc = jnp.where(mine, qf[spot, :], none)
                qs = jnp.where(mine, qf[spot, :], qm_ref[spot, :])
                dh = jnp.where(mine, dd, none)
                tasks += [(h, qc, qs, dh, a, b) for a, b in spans(r0, block)]

            def products(task):
                h, qc, qs, dh, a, b = task
                s = mm_t(ks[h, pl.ds(a, b - a), :], qs)
                return jnp.where(hide, NEG, s) if a == r0 else s, mm_t(vf[pl.ds(a, b - a), :], dh)

            now = products(tasks[0])
            for i, (h, qc, qs, dh, a, b) in enumerate(tasks):
                later = products(tasks[i + 1]) if i + 1 < len(tasks) else None
                log_total = l_ref[0, h : h + 1, spot]
                keys = pl.ds(a, b - a)
                s, dp = now
                now = later
                p = jnp.exp(s - log_total)
                ds = (p * (dp - delta[h : h + 1])).astype(bf16)
                dva[keys, :] += mm(p.astype(bf16), dh)
                dka[keys, :] += mm(ds, qc)
                part = mm(kts[h, :, keys], ds)
                dqt = part if dqt is None else dqt + part
            dqa[spot, :] = (dqt * 0.125).T.astype(bf16)
        for out, at in ((give_ref, other0), (keep_ref, mine0)):
            spot = pl.ds(at, rows)
            out[0] = dqa[spot, :]
            out[1] = dka[spot, :].astype(bf16)
            out[2] = dva[spot, :].astype(bf16)

    whole = pl.BlockSpec((t, 128), lambda p, s: (0, 0))
    half = pl.BlockSpec((rows, 128), lambda p, s: (0, first + p))
    return call(
        kernel, jnp.reshape(place, (1,)).astype(jnp.int32), (keep, recv, o, dkeep, drecv, lse, kmark, qmark), (pairs,),
        half_specs(rows, first)
        + [pl.BlockSpec((t, 128), lambda p, s: (0, seat + p)), half, half, pl.BlockSpec((1, 8, t), lambda p, s: (seat + p, 0, 0)), whole, whole],
        half_specs(rows),
        [shape((3, rows, width))] * 2,
        [pltpu.VMEM((t, 128), bf16)] * 3 + [pltpu.VMEM((2, t, 128), bf16), pltpu.VMEM((2, 128, t), bf16), pltpu.VMEM((t, 128), bf16)]
        + [pltpu.VMEM((t, 128), f32)] * 2,
        2 * t * t * 8 * width,
    )


def norm_stats(rows):
    centered = rows - jnp.mean(rows, axis=-1, keepdims=True)
    inv = lax.rsqrt(jnp.mean(centered * centered, axis=-1, keepdims=True) + EPSILON)
    return centered * inv, inv


def norm(rows, gain, shift):
    return norm_stats(rows)[0] * gain + shift


def norm_back(rows, gain, dy):
    n, inv = norm_stats(rows)
    dn = dy * gain
    dh = inv * (dn - jnp.mean(dn, axis=-1, keepdims=True) - n * jnp.mean(dn * n, axis=-1, keepdims=True))
    return dh, jnp.sum(dy * n, axis=0, keepdims=True), jnp.sum(dy, axis=0, keepdims=True)


ERFC = (
    0.22567585470008253, 0.22566975083164525, 0.20784161289369674, 0.1685452087610459, 0.14142852065437478,
    -0.005612938524279035, 0.1691005263450779, -0.1829144800497475, 0.05026606972001335,
)


def gelu_parts(u):
    bell = jnp.exp(u * u * -0.5)
    t = 1.0 / (1.0 + jnp.abs(u) * (0.4 * math.sqrt(0.5)))
    poly = jnp.full_like(t, ERFC[-1])
    for value in ERFC[-2::-1]:
        poly = poly * t + value
    tail = bell * t * poly * 0.5
    cdf = jnp.where(u < 0.0, tail, 1.0 - tail)
    return u * cdf, cdf + u * bell * (1.0 / math.sqrt(2.0 * math.pi))


def const(dims):
    return pl.BlockSpec(dims, lambda i, s: (0,) * len(dims))


def once(dims):
    return pl.BlockSpec(dims, lambda i, s: (0,) * len(dims), pipeline_mode=pl.Buffered(1))


def tile(rows, width):
    return pl.BlockSpec((rows, width), lambda i, s: (i, 0))


def fill(full, s, own, mine, sib):
    rows = own.shape[0]
    c, h = s[0], s[1]
    full[pl.ds(pl.multiple_of(h * rows, 128), rows), :] = own[...].astype(bf16)
    start = (1 - h) * rows
    full[pl.ds(pl.multiple_of(start + c * (rows // 2), 64), rows // 2), :] = mine[...]
    full[pl.ds(pl.multiple_of(start + (1 - c) * (rows // 2), 64), rows // 2), :] = sib[...]


def picked(part):
    if not isinstance(part, tuple):
        return once(part.shape)
    stack, which = part
    return pl.BlockSpec((None, *stack.shape[1:]), lambda i, s: (which, 0, 0), pipeline_mode=pl.Buffered(1))


def weight_specs(weight):
    return [picked(part) for part in weight]


def arrays(weight):
    return [part[0] if isinstance(part, tuple) else part for part in weight]


def full_shape(weight):
    return (2 * weight[0].shape[0], weight[0].shape[1])


def at_core(c, width):
    return pl.ds(pl.multiple_of(c * width, 128), width)


def norm_qkv(s, x_own, x_in, weight, table, rows=512):
    t, width = x_own.shape
    hw = width // 2

    def kernel(s_ref, xo, xi, own, mine, sib, tab, w, a_ref, keep, give):
        @pl.when(pl.program_id(0) == 0)
        def _():
            fill(w, s_ref, own, mine, sib)

        x = jnp.where(s_ref[2] == 1, xo[...].astype(f32), xi[...].astype(f32))
        a = norm(x, tab[0:1], tab[4:5]).astype(bf16)
        a_ref[...] = a
        for j in range(3):
            y = mm(a, w[:, j * width : (j + 1) * width])
            if j != 1:
                y = y + tab[8 + j // 2 : 9 + j // 2]
            low, high = y[:, :hw].astype(bf16), y[:, hw:].astype(bf16)
            first = s_ref[0] == 0
            keep[j] = jnp.where(first, low, high)
            give[j] = jnp.where(first, high, low)

    third = pl.BlockSpec((3, rows, hw), lambda i, s: (0, i, 0))
    dims = full_shape(weight)
    return call(
        kernel, s, (x_own, x_in, *weight, table), (t // rows,),
        [tile(rows, width)] * 2 + weight_specs(weight) + [const(table.shape)],
        [const(dims), tile(rows, width), third, third],
        [shape(dims), shape((t, width)), shape((3, t, hw)), shape((3, t, hw))],
        cost=2 * t * width * 3 * width,
    )


def beside(refs):
    return jnp.concatenate([ref[...] for ref in refs], axis=1) if len(refs) > 1 else refs[0][...]


def self_project(s, ctx, ctx_in, x_own, x_in, w_out, w_q, table, rows=512):
    t, width = x_own.shape
    hw = width // 2
    steps = t // rows
    n = len(ctx)

    def kernel(s_ref, *refs):
        cks, cis = refs[:n], refs[n : 2 * n]
        xo, xi, o1, o2, o3, q1, q2, q3, tab, wo, wq, h_ref, a_ref, qc_ref = refs[2 * n :]

        @pl.when(pl.program_id(0) == 0)
        def _():
            fill(wo, s_ref, o1, o2, o3)
            fill(wq, s_ref, q1, q2, q3)

        c = s_ref[0]
        x = jnp.where(s_ref[2] == 1, xo[...].astype(f32), xi[...].astype(f32))
        h = x + mm(beside(cks), wo[at_core(c, hw), :]) + mm(beside(cis), wo[at_core(1 - c, hw), :]) + tab[10:11]
        h_ref[...] = h
        a = norm(h, tab[1:2], tab[5:6]).astype(bf16)
        a_ref[...] = a
        qc_ref[...] = (mm(a, wq[...]) + tab[11:12]).astype(bf16)

    dims = full_shape(w_out)
    return call(
        kernel, s, (*ctx, *ctx_in, x_own, x_in, *arrays(w_out), *arrays(w_q), table), (steps,),
        [pl.BlockSpec((rows, part.shape[1]), lambda i, s: (s[0] * steps + i, 0)) for part in ctx]
        + [tile(rows, part.shape[1]) for part in ctx_in] + [tile(rows, width), tile(rows, width)]
        + weight_specs(w_out) + weight_specs(w_q) + [const(table.shape)],
        [const(dims), const(dims), tile(rows, width), tile(rows, width), tile(rows, width)],
        [shape(dims), shape(dims), shape((t, width), f32), shape((t, width)), shape((t, width))],
        cost=4 * t * width * width,
    )


def frame_kv(s, half, twin, weight, table, rows=512):
    count, hw = half.shape
    width = 2 * hw
    steps = -(-count // rows)

    def kernel(s_ref, fa, fb, own, mine, sib, tab, w, k_ref, v_ref):
        @pl.when(pl.program_id(0) == 0)
        def _():
            fill(w, s_ref, own, mine, sib)

        c = s_ref[0]
        live = lax.broadcasted_iota(jnp.int32, (rows, 1), 0) + pl.program_id(0) * rows < count
        for j, out in enumerate((k_ref, v_ref)):
            mine0 = pl.multiple_of(j * width + c * hw, 128)
            other0 = pl.multiple_of(j * width + (1 - c) * hw, 128)
            y = mm(fa[...], w[pl.ds(mine0, hw), :]) + mm(fb[...], w[pl.ds(other0, hw), :])
            if j == 1:
                y = y + tab[12:13]
            out[...] = jnp.where(live, y, 0.0).astype(bf16)

    dims = full_shape(weight)
    return call(
        kernel, s, (half, twin, *weight, table), (steps,),
        [tile(rows, hw)] * 2 + weight_specs(weight) + [const(table.shape)],
        [const(dims), tile(rows, width), tile(rows, width)],
        [shape(dims), shape((steps * rows, width)), shape((steps * rows, width))],
        cost=4 * count * width * width,
    )


def middle(s, h1, c2_keep, c2_give, cot_own, cot_in, w_out, ff_own, ff_far, table, fc1_shift, rows=256):
    t, width = h1.shape
    units = fc1_shift.shape[1] // width
    hw = width // 2
    pieces, piece = ff_own[0].shape[:2]

    def kernel(s_ref, h1_ref, ck_ref, cg_ref, co, ci, o1, o2, o3, own1, own2, far, tab, shift, wo, out, a_ref, g_ref, dm_ref, du_ref, d2_ref, dh_ref, dk_ref, dg_ref, vec, w1, w2, sems):
        def moves():
            for k, (dst, own) in enumerate(((w1, own1), (w2, own2))):
                yield pltpu.make_async_copy(own, dst.at[pl.ds(s_ref[1] * pieces, pieces)], sems.at[2 * k])
                yield pltpu.make_async_copy(far.at[:, k], dst.at[pl.ds((1 - s_ref[1]) * pieces, pieces)], sems.at[2 * k + 1])

        @pl.when(pl.program_id(0) == 0)
        def _():
            for move in moves():
                move.start()
            fill(wo, s_ref, o1, o2, o3)
            vec[...] = jnp.zeros(vec.shape, f32)
            for move in moves():
                move.wait()

        def up(h, j):
            at, many = (h * units + j) * (hw // piece), hw // piece
            return w1[at : at + many].reshape(hw, width)

        def down(j):
            many = width // piece
            return w2[j * many : (j + 1) * many].reshape(width, width)

        c = s_ref[0]
        h2 = h1_ref[...] + mm(ck_ref[...], wo[at_core(c, hw), :]) + mm(cg_ref[...], wo[at_core(1 - c, hw), :]) + tab[13:14]
        n2, inv2 = norm_stats(h2)
        a = (n2 * tab[2:3] + tab[6:7]).astype(bf16)
        a_ref[...] = a
        acc = h2 + tab[14:15]
        slopes = []

        def climb(j):
            return mm(a[:, :hw], up(0, j)) + mm(a[:, hw:], up(1, j)) + shift[:, j * width : (j + 1) * width]

        u = climb(0)
        for j in range(units):
            u_next = climb(j + 1) if j + 1 < units else None
            g, slope = gelu_parts(u.astype(bf16).astype(f32))
            slopes.append(slope)
            g = g.astype(bf16)
            g_ref[:, j * width : (j + 1) * width] = g
            acc = acc + mm(g, down(j))
            u = u_next
        n3, inv3 = norm_stats(acc)
        out[...] = (n3 * tab[3:4] + tab[7:8]).astype(bf16)

        def back(n, inv, gain, dy):
            dn = dy * gain
            return inv * (dn - jnp.mean(dn, axis=-1, keepdims=True) - n * jnp.mean(dn * n, axis=-1, keepdims=True))

        def total(x):
            return jnp.sum(x, axis=0, keepdims=True)

        dy = jnp.where(s_ref[2] == 1, co[...].astype(f32), ci[...].astype(f32))
        dh3 = back(n3, inv3, tab[3:4], dy)
        dm = dh3.astype(bf16)
        dm_ref[...] = dm
        halves = [None, None]
        dg = mm_t(dm, down(0))
        for j in range(units):
            cols = slice(j * width, (j + 1) * width)
            dg_next = mm_t(dm, down(j + 1)) if j + 1 < units else None
            du = (slopes[j] * dg).astype(bf16)
            dg = dg_next
            du_ref[:, cols] = du
            vec[0:1, cols] += total(du.astype(f32))
            for h in range(2):
                part = mm_t(du, up(h, j))
                halves[h] = part if halves[h] is None else halves[h] + part
        da = jnp.concatenate(halves, axis=1)
        dh2 = dh3 + back(n2, inv2, tab[2:3], da)
        d2 = dh2.astype(bf16)
        d2_ref[...] = d2
        dh_ref[...] = dh2
        dk_ref[...] = mm_t(d2, wo[at_core(c, hw), :]).astype(bf16)
        dg_ref[...] = mm_t(d2, wo[at_core(1 - c, hw), :]).astype(bf16)
        rows_of = [total(dm.astype(f32)), total(d2.astype(f32)), total(dy * n3), total(dy), total(da * n2), total(da)]
        for k, value in enumerate(rows_of):
            line, at = 1 + k // 3, (k % 3) * width
            vec[line : line + 1, at : at + width] += value

    dims = full_shape(w_out)
    ff = units * width
    line = tile(rows, width)
    wide, half = tile(rows, ff), tile(rows, hw)
    away = pl.BlockSpec(memory_space=pl.ANY)
    return call(
        kernel, s, (h1, c2_keep, c2_give, cot_own, cot_in, *arrays(w_out), *ff_own, ff_far, table, fc1_shift), (t // rows,),
        [line, half, half, line, line] + weight_specs(w_out) + [away] * 3 + [const(table.shape), const(fc1_shift.shape)],
        [const(dims), line, line, wide, line, wide, line, line, half, half, const((8, ff))],
        [shape(dims), shape((t, width)), shape((t, width)), shape((t, ff)), shape((t, width)), shape((t, ff)), shape((t, width)),
         shape((t, width), f32), shape((t, hw)), shape((t, hw)), shape((8, ff), f32)],
        [pltpu.VMEM((2 * pieces, piece, width), bf16)] * 2 + [pltpu.SemaphoreType.DMA((4,))],
        cost=8 * t * width * ff + 4 * t * width * width,
    )


def ff_grads(s, a, du, g, dm):
    t, width = a.shape
    hw = width // 2
    ff = du.shape[1]
    units = ff // width
    piece = hw * units // 16
    many = hw // piece

    def kernel(s_ref, a_ref, du_ref, g0, g1, dm_ref, out):
        @pl.when(pl.program_id(0) < units)
        def _():
            for h in range(2):
                out[h] = t_mm(a_ref[:, h * hw : (h + 1) * hw], du_ref[...]).astype(bf16).reshape(out.shape[1:])

        @pl.when(pl.program_id(0) >= units)
        def _():
            for h, ref in enumerate((g0, g1)):
                out[h] = t_mm(ref[...], dm_ref[...]).astype(bf16).reshape(out.shape[1:])

    return call(
        kernel, s, (a, du, g, g, dm), (2 * units,),
        [once((t, width)), pl.BlockSpec((t, width), lambda i, s: (0, jnp.minimum(i, units - 1))),
         pl.BlockSpec((t, hw), lambda i, s: (0, jnp.maximum(i - units, 0))),
         pl.BlockSpec((t, hw), lambda i, s: (0, units + jnp.maximum(i - units, 0))), once((t, width))],
        pl.BlockSpec((2, many, 1, piece, width), lambda i, s: (0, i % units, i // units, 0, 0)),
        shape((2, 16, 2, piece, width)),
        cost=4 * t * width * ff,
    )


def cross_back(s, dq_keep, dq_give, h1, dh2, w_q, w_out, table, rows=512):
    t, width = h1.shape
    hw = width // 2

    def kernel(s_ref, dk_ref, dg_ref, h_ref, dh2_ref, wq, wo, tab, dh_ref, d1_ref, keep, give, vec):
        @pl.when(pl.program_id(0) == 0)
        def _():
            vec[...] = jnp.zeros(vec.shape, f32)

        c = s_ref[0]
        da = mm_t(dk_ref[...], wq[:, at_core(c, hw)]) + mm_t(dg_ref[...], wq[:, at_core(1 - c, hw)])
        dres, dgain, dshift = norm_back(h_ref[...], tab[1:2], da)
        dh1 = dh2_ref[...] + dres
        dh_ref[...] = dh1
        d1 = dh1.astype(bf16)
        d1_ref[...] = d1
        keep[...] = mm_t(d1, wo[at_core(c, hw), :]).astype(bf16)
        give[...] = mm_t(d1, wo[at_core(1 - c, hw), :]).astype(bf16)
        vec[0:1] += dgain
        vec[1:2] += dshift
        vec[2:3] += jnp.sum(d1.astype(f32), axis=0, keepdims=True)
        vec[3:4, at_core(c, hw)] += jnp.sum(dk_ref[...].astype(f32), axis=0, keepdims=True)
        vec[3:4, at_core(1 - c, hw)] += jnp.sum(dg_ref[...].astype(f32), axis=0, keepdims=True)

    line, half = tile(rows, width), tile(rows, hw)
    return call(
        kernel, s, (dq_keep, dq_give, h1, dh2, w_q, w_out, table), (t // rows,),
        [half, half, line, line, once(w_q.shape), once(w_out.shape), const(table.shape)],
        [line, line, half, half, const((8, width))],
        [shape((t, width), f32), shape((t, width)), shape((t, hw)), shape((t, hw)), shape((8, width), f32)],
        cost=4 * t * width * width,
    )


def frame_back(s, keep, recv, half, twin, weight, rows=512):
    count, hw = half.shape
    width = 2 * hw
    steps = -(-count // rows)

    def kernel(s_ref, ka, kb, fa, fb, w, fkeep, fgive, xkeep, xgive, vec, acc):
        @pl.when(pl.program_id(0) == 0)
        def _():
            vec[...] = jnp.zeros(vec.shape, f32)
            acc[...] = jnp.zeros(acc.shape, f32)

        c, h = s_ref[0], s_ref[1]
        live = lax.broadcasted_iota(jnp.int32, (rows, 1), 0) + pl.program_id(0) * rows < count
        zero = jnp.zeros((rows, hw), bf16)
        f_mine = jnp.where(live, fa[...], zero)
        f_other = jnp.where(live, fb[...], zero)
        back = None
        for j in range(2):
            d = (ka[j].astype(f32) + kb[j].astype(f32)).astype(bf16)
            part = mm_t(d, w[j * width : (j + 1) * width, at_core(c, hw)])
            back = part if back is None else back + part
            acc[j, at_core(c, hw), :] += t_mm(f_mine, d)
            acc[j, at_core(1 - c, hw), :] += t_mm(f_other, d)
            if j == 1:
                vec[0:1] += jnp.sum(d.astype(f32), axis=0, keepdims=True)
        low, high = back[:, :hw].astype(bf16), back[:, hw:].astype(bf16)
        fkeep[...] = jnp.where(c == 0, low, high)
        fgive[...] = jnp.where(c == 0, high, low)

        @pl.when(pl.program_id(0) == steps - 1)
        def _():
            xkeep[...] = acc[h].astype(bf16)
            xgive[...] = acc[1 - h].astype(bf16)

    pair = pl.BlockSpec((2, rows, hw), lambda i, s: (0, i, 0))
    strip = tile(rows, hw)
    return call(
        kernel, s, (keep, recv, half, twin, weight), (steps,),
        [pair, pair, strip, strip, once(weight.shape)],
        [strip, strip, const((width, hw)), const((width, hw)), const((8, hw))],
        [shape((count, hw)), shape((count, hw)), shape((width, hw)), shape((width, hw)), shape((8, hw), f32)],
        [pltpu.VMEM((2, width, hw), f32)],
        cost=8 * count * width * width,
    )


def give_grads(s, c2_keep, c2_give, d2, a2, dq_give):
    t, width = d2.shape
    hw = width // 2

    def kernel(s_ref, k_ref, g_ref, d_ref, a_ref, q_ref, out):
        c = s_ref[0]
        out[0, at_core(c, hw), :] = t_mm(k_ref[...], d_ref[...]).astype(bf16)
        out[0, at_core(1 - c, hw), :] = t_mm(g_ref[...], d_ref[...]).astype(bf16)
        out[1] = t_mm(a_ref[...], q_ref[...]).astype(bf16)

    half = const((t, hw))
    return call(
        kernel, s, (c2_keep, c2_give, d2, a2, dq_give), (1,),
        [half, half, pl.BlockSpec((t, hw), lambda i, s: (0, 1 - s[0])), const((t, width)), half],
        const((2, width, hw)), shape((2, width, hw)), cost=4 * t * width * hw,
    )


def give_grad_out(s, ctx, ctx_in, d1):
    t, width = d1.shape
    hw = width // 2
    n = len(ctx)

    def kernel(s_ref, *refs):
        d_ref, out = refs[2 * n :]
        c = s_ref[0]
        out[at_core(c, hw), :] = t_mm(beside(refs[:n]), d_ref[...]).astype(bf16)
        out[at_core(1 - c, hw), :] = t_mm(beside(refs[n : 2 * n]), d_ref[...]).astype(bf16)

    return call(
        kernel, s, (*ctx, *ctx_in, d1), (1,),
        [pl.BlockSpec((t, part.shape[1]), lambda i, s: (s[0], 0)) for part in ctx] + [const(part.shape) for part in ctx_in]
        + [pl.BlockSpec((t, hw), lambda i, s: (0, 1 - s[0]))],
        const((width, hw)), shape((width, hw)), cost=2 * t * width * hw,
    )


def keep_grads(s, c2_keep, c2_give, d2, a2, dq_keep, pair_in, kv_keep, kv_give):
    t, width = d2.shape
    hw = width // 2

    def kernel(s_ref, ck, cg, d2_ref, a_ref, q_ref, p_ref, kk, kg, xgive, xkeep):
        c, h = s_ref[0], s_ref[1]
        for out, shard, kv in ((xgive, 1 - h, kg), (xkeep, h, kk)):
            rows = at_core(shard, hw)
            out[1] = (t_mm(a_ref[:, rows], q_ref[...]) + p_ref[1, rows, :].astype(f32)).astype(bf16)
            out[2] = kv[:hw]
            out[3] = kv[hw:]
        own_rows = t_mm(ck[...], d2_ref[...]) + p_ref[0, at_core(c, hw), :].astype(f32)
        far_rows = t_mm(cg[...], d2_ref[...]) + p_ref[0, at_core(1 - c, hw), :].astype(f32)
        xkeep[0] = jnp.where(c == h, own_rows, far_rows).astype(bf16)
        xgive[0] = jnp.where(c == h, far_rows, own_rows).astype(bf16)

    cols, half = pl.BlockSpec((t, hw), lambda i, s: (0, s[0])), const((t, hw))
    four = (4, hw, hw)
    return call(
        kernel, s, (c2_keep, c2_give, d2, a2, dq_keep, pair_in, kv_keep, kv_give), (1,),
        [half, half, cols, const((t, width)), half, const((2, width, hw)), const((width, hw)), const((width, hw))],
        [const(four), const(four)], [shape(four), shape(four)], cost=4 * t * width * hw,
    )


def keep_grad_out(s, ctx, ctx_in, d1, out_in):
    t, width = d1.shape
    hw = width // 2
    n = len(ctx)

    def kernel(s_ref, *refs):
        d1_ref, o_ref, xgive, xkeep = refs[2 * n :]
        c, h = s_ref[0], s_ref[1]
        own_rows = t_mm(beside(refs[:n]), d1_ref[...]) + o_ref[at_core(c, hw), :].astype(f32)
        far_rows = t_mm(beside(refs[n : 2 * n]), d1_ref[...]) + o_ref[at_core(1 - c, hw), :].astype(f32)
        xkeep[0] = jnp.where(c == h, own_rows, far_rows).astype(bf16)
        xgive[0] = jnp.where(c == h, far_rows, own_rows).astype(bf16)

    one = (1, hw, hw)
    return call(
        kernel, s, (*ctx, *ctx_in, d1, out_in), (1,),
        [pl.BlockSpec((t, part.shape[1]), lambda i, s: (s[0], 0)) for part in ctx] + [const(part.shape) for part in ctx_in]
        + [pl.BlockSpec((t, hw), lambda i, s: (0, s[0])), const((width, hw))],
        [const(one), const(one)], [shape(one), shape(one)], cost=2 * t * width * hw,
    )


def split_y(s, keeps, gots):
    _, rows, cols = keeps[0].shape
    half, n = rows // 2, len(keeps)
    counts = [k.shape[0] for k in keeps]

    def kernel(s_ref, *refs):
        give, mine = refs[2 * n :]
        for out, y in ((give, 1 - s_ref[4]), (mine, s_ref[4])):
            rows_at = pl.ds(pl.multiple_of(y * half, 64), half)
            at = 0
            for k_ref, g_ref, count in zip(refs[:n], refs[n : 2 * n], counts):
                out[at : at + count] = (k_ref[:, rows_at, :].astype(f32) + g_ref[:, rows_at, :].astype(f32)).astype(bf16)
                at += count

    dims = (sum(counts), half, cols)
    return call(kernel, s, (*keeps, *gots), (1,), [const(k.shape) for k in (*keeps, *gots)], [const(dims)] * 2, [shape(dims)] * 2)


def split_z(s, keep, got):
    b, rows, cols = keep.shape
    part = rows // 4

    def kernel(s_ref, k_ref, g_ref, *outs):
        for d, out in enumerate(outs):
            at = pl.ds(pl.multiple_of(s_ref[5 + d] * part, 16), part)
            out[...] = (k_ref[:, at, :].astype(f32) + g_ref[:, at, :].astype(f32)).astype(bf16)

    dims = (b, part, cols)
    return call(kernel, s, (keep, got), (1,), [const(keep.shape)] * 2, [const(dims)] * 4, [shape(dims)] * 4)


def sum_four(s, parts, vectors=()):
    b, part, cols = parts[0].shape

    def kernel(s_ref, p0, p1, p2, p3, *refs):
        out = refs[-1]
        total = (p0[...].astype(f32) + p1[...].astype(f32)) + (p2[...].astype(f32) + p3[...].astype(f32))
        out[0:b] = total.astype(bf16)
        if vectors:
            v = refs[0][...] + refs[1][...]
            high = v.astype(bf16).astype(f32)
            out[b] = jnp.concatenate([high, v - high], axis=0).astype(bf16)

    dims = (b + (1 if vectors else 0), part, cols)
    return call(
        kernel, s, (*parts, *vectors), (1,), [const(parts[0].shape)] * 4 + [const(v.shape) for v in vectors], const(dims), shape(dims)
    )


def pack_vectors(s, last, cross, mid, kv):
    width = last.shape[1]
    hw = width // 2
    units = mid.shape[1] // width

    def kernel(s_ref, l_ref, c_ref, m_ref, k_ref, give, mine):
        def line(ref, row, at=0):
            return ref[row : row + 1, at : at + width]

        zero = jnp.zeros((1, hw), f32)
        first = s_ref[0] == 0
        kv_row = jnp.concatenate([jnp.where(first, k_ref[0:1], zero), jnp.where(first, zero, k_ref[0:1])], axis=1)
        rows = [
            line(l_ref, 0), line(c_ref, 0), line(m_ref, 2, width), line(m_ref, 1, 2 * width),
            line(l_ref, 1), line(c_ref, 1), line(m_ref, 2, 2 * width), line(m_ref, 2),
            line(l_ref, 2), line(l_ref, 3), line(c_ref, 2), line(c_ref, 3), kv_row, line(m_ref, 1, width), line(m_ref, 1),
        ]
        halves = []
        for h in range(2):
            own = [row[:, h * hw : (h + 1) * hw] for row in rows]
            own += [m_ref[0:1, (h * units + j) * hw : (h * units + j + 1) * hw] for j in range(units)]
            halves.append(jnp.concatenate(own + [zero] * (24 - len(own)), axis=0))
        give[...] = jnp.where(s_ref[1] == 0, halves[1], halves[0])
        mine[...] = jnp.where(s_ref[1] == 0, halves[0], halves[1])

    return call(
        kernel, s, (last, cross, mid, kv), (1,), [const(x.shape) for x in (last, cross, mid, kv)],
        [const((24, hw))] * 2, [shape((24, hw), f32)] * 2,
    )


def join_z(s, parts):
    b, part, cols = parts[0].shape

    def kernel(s_ref, p0, p1, p2, p3, out):
        for d, ref in enumerate((p0, p1, p2, p3)):
            out[:, pl.ds(pl.multiple_of(s_ref[5 + d] * part, 16), part), :] = ref[...]

    dims = (b, 4 * part, cols)
    return call(kernel, s, parts, (1,), [const(parts[0].shape)] * 4, const(dims), shape(dims))


def spread_out(s, groups, outs, vectors=False):
    hw = 384

    def kernel(s_ref, *refs):
        results = refs[4 * len(groups) :]
        for n, (parts, spots) in enumerate(groups):
            b, half, cols = parts[0].shape
            for k, ref in enumerate(refs[4 * n : 4 * n + 4]):
                y = s_ref[4] if k % 2 == 0 else 1 - s_ref[4]
                core = s_ref[0] if k < 2 else 1 - s_ref[0]
                for block, (which, row, col) in enumerate(spots):
                    at_row = pl.multiple_of(row + y * half, 64)
                    at_col = pl.multiple_of(col + core * hw, 128)
                    results[which][pl.ds(at_row, half), pl.ds(at_col, cols)] = ref[block].astype(f32)
        if vectors:
            total = None
            for ref in refs[:4]:
                rows = ref[ref.shape[0] - 1].astype(f32)
                for z in range(4):
                    part = rows[48 * z : 48 * z + 48]
                    total = part if total is None else total + part
            total, at = total[0:24] + total[24:48], 0
            for ref in results[1:]:
                ref[...] = total[at : at + ref.shape[0]]
                at += ref.shape[0]

    parts = [part for group, _ in groups for part in group]
    return call(kernel, s, parts, (1,), [const(part.shape) for part in parts], [const(d) for d in outs], [shape(d, f32) for d in outs])


def spread_gathered(s, got, spots, outs):
    _, _, part, hw = got.shape

    def kernel(s_ref, g_ref, *results):
        for r in range(got.shape[0]):
            z, y, core = r // 4, r // 2 % 2, r % 2
            for block, (which, row, col) in enumerate(spots):
                at_row, at_col = row + (y * 4 + z) * part, col + core * hw
                results[which][at_row : at_row + part, at_col : at_col + hw] = g_ref[r, block].astype(f32)

    return call(kernel, s, (got,), (1,), [const(got.shape)], [const(d) for d in outs], [shape(d, f32) for d in outs])


def spread_ff(s, got):
    reps, _, per, width = got.shape
    units = 4
    rows = reps // units * per

    def kernel(s_ref, g_ref, one, two):
        one[...] = g_ref[:, 0].reshape(rows, width).astype(f32)
        two[...] = g_ref[:, 1].reshape(rows, width).astype(f32)

    return call(
        kernel, s, (got,), (units,), [pl.BlockSpec((reps // units, 2, per, width), lambda i, s: (i, 0, 0, 0))],
        [pl.BlockSpec((rows, width), lambda i, s: (0, i)), pl.BlockSpec((rows, width), lambda i, s: (i, 0))],
        [shape((rows, units * width), f32), shape((units * rows, width), f32)],
    )


def qkv_grad(s, a_own, a_sib, keep, give, mine):
    t, width = a_own.shape
    hw = width // 2
    n = len(keep)

    def kernel(s_ref, ao, ai, *refs):
        k, g = (jnp.concatenate([ref[0] for ref in part], axis=1) for part in (refs[:n], refs[n : 2 * n]))
        refs[-1][0] = (t_mm(ao[...], k) + t_mm(ai[...], g)).astype(bf16)

    cols = pl.BlockSpec((t, hw), lambda i, s: (0, s[1] if mine else 1 - s[1]))
    return call(
        kernel, s, (a_own, a_sib, *keep, *give), (3,),
        [cols, cols] + [pl.BlockSpec((1, t, part.shape[2]), lambda i, s: (i, 0, 0)) for part in (*keep, *give)],
        pl.BlockSpec((1, hw, hw), lambda i, s: (i, 0, 0)), shape((3, hw, hw)), cost=6 * t * width * hw,
    )


def last_rows(s, keep, recv, x_own, x_in, dh1, weight, table, rows=512):
    t, width = x_own.shape
    hw = width // 2
    n = len(keep)

    def kernel(s_ref, *refs):
        xo, xi, dh, w, tab, out, vec = refs[2 * n :]

        @pl.when(pl.program_id(0) == 0)
        def _():
            vec[...] = jnp.zeros(vec.shape, f32)

        c = s_ref[0]
        da = None
        for j in range(3):
            for parts, core in ((refs[:n], c), (refs[n : 2 * n], 1 - c)):
                d = jnp.concatenate([part[j] for part in parts], axis=1)
                at = pl.multiple_of(j * width + core * hw, 128)
                part = mm_t(d, w[:, pl.ds(at, hw)])
                da = part if da is None else da + part
                if j != 1:
                    line = 2 + j // 2
                    vec[line : line + 1, at_core(core, hw)] += jnp.sum(d.astype(f32), axis=0, keepdims=True)
        x = jnp.where(s_ref[2] == 1, xo[...].astype(f32), xi[...].astype(f32))
        dres, dgain, dshift = norm_back(x, tab[0:1], da)
        out[...] = (dh[...] + dres).astype(bf16)
        vec[0:1] += dgain
        vec[1:2] += dshift

    line = tile(rows, width)
    return call(
        kernel, s, (*keep, *recv, x_own, x_in, dh1, weight, table), (t // rows,),
        [pl.BlockSpec((3, rows, part.shape[2]), lambda i, s: (0, i, 0)) for part in (*keep, *recv)]
        + [line, line, line, once(weight.shape), const(table.shape)],
        [line, const((8, width))], [shape((t, width)), shape((8, width), f32)],
        cost=6 * t * width * width,
    )


EVERY = ("z", "y", "core", "x")
SPREAD2 = ("x", "z", "y", "core")
REP2 = ("z", "y", "core")
SWAP = [(1, 2), (2, 1)]


def tie(*values):
    return lax.optimization_barrier(values)


def across_z(x, d):
    return lax.ppermute(x, "z", [(j, j ^ d) for j in range(4)])


def across(x, axis):
    return lax.ppermute(x, axis, FLIP)


def body_pair(hidden, frames, segment, cotangent, norm_gain, norm_bias, self_qkv, self_out, cross_q, cross_kv, cross_out, fc1, fc2, proj_bias, fc1_bias):
    c, h = lax.axis_index("core"), lax.axis_index("x")
    y_at, z_at = lax.axis_index("y"), lax.axis_index("z")
    stay = c == h
    s = jnp.stack([c, h, stay.astype(jnp.int32), jnp.int32(0), y_at, z_at, z_at ^ 1, z_at ^ 2, z_at ^ 3]).astype(jnp.int32)
    rep_at = lax.axis_index(REP2)
    reps = lax.axis_size(REP2)
    width = self_out.shape[1]
    hw = width // 2
    ff = fc1.shape[1]
    units = ff // width
    pairs = hw // 128

    def swap(x):
        return lax.ppermute(x, ("core", "x"), SWAP)

    def sibling(x):
        return across(x, "core")

    def near(own):
        half = own.shape[0] // 2
        return across(lax.dynamic_slice_in_dim(own, c * half, half).astype(bf16), "x")

    x_own = hidden[0]
    small = jnp.concatenate([norm_gain, norm_bias, proj_bias, fc1_bias.reshape(units, hw), jnp.zeros((1, hw), f32)]).astype(bf16)
    small_in = across(small, "x")
    qkv_near = near(self_qkv)
    x_in = swap(x_own)
    seg = jnp.where(stay, segment, swap(segment))[0]
    per = hw * units // reps
    small = jnp.where(h == 0, jnp.stack([small, small_in]), jnp.stack([small_in, small])).astype(f32)
    table = jnp.concatenate([small[0, :16], small[1, :16]], axis=1)
    fc1_shift = small[:, 15:19].reshape(1, ff)
    kmark, qmark = seg_marks(seg)
    own1 = jnp.concatenate([fc1[:, j * width : (j + 1) * width] for j in range(units)]).astype(bf16).reshape(reps, per, width)
    own2 = fc2.astype(bf16).reshape(reps, per, width)
    slot = jnp.stack([lax.dynamic_index_in_dim(own1, rep_at, keepdims=False), lax.dynamic_index_in_dim(own2, rep_at, keepdims=False)])
    part = hw // 2
    squares = jnp.stack([lax.dynamic_slice_in_dim(w, c * part, part) for w in (self_out, cross_q, cross_out)]).astype(bf16)
    kv_part = lax.dynamic_slice_in_dim(cross_kv, c * hw, hw).astype(bf16)
    x_in, kmark, qmark, squares, kv_part, frames, own1, own2, slot = tie(x_in, kmark, qmark, squares, kv_part, frames, own1, own2, slot)
    slot = across(slot, "x")
    squares_near = across(squares, "x")
    f_own = frames[0]
    f_in = swap(f_own)
    kv_near = across(kv_part, "x")
    w_qkv, a1, keep, give = norm_qkv(s, x_own, x_in, (self_qkv, qkv_near, sibling(qkv_near)), table)
    give, slot = tie(give, slot)
    recv = sibling(give)
    ff_far = lax.all_gather(slot, REP2, axis=0, tiled=False)

    many = pairs - 1
    ctx_a, give_a, lse_a = self_fwd(0, many, c, keep, recv, kmark, qmark)
    give_a, keep, recv, squares_near, cotangent = tie(give_a, keep, recv, squares_near, cotangent)
    cot_in = swap(cotangent[0])
    squares_sib = sibling(squares_near)
    w_out, w_q, w_co = (
        (w, (squares_near, k), (squares_sib, k)) for k, w in enumerate((self_out, cross_q, cross_out))
    )
    in_a = sibling(give_a)
    ctx_b, give_b, lse_b = self_fwd(many, 1, c, keep, recv, kmark, qmark)
    in_b = sibling(give_b)
    ctx, ctx_in = (ctx_a, ctx_b), (in_a, in_b)
    w_out, w_q, h1, a2, qc = self_project(s, ctx, ctx_in, x_own, x_in, w_out, w_q, table)
    qc, f_in, kv_near = tie(qc, f_in, kv_near)
    half = jnp.where(stay, f_own, f_in)
    twin = sibling(half)
    w_kv, kc, vc = frame_kv(s, half, twin, (cross_kv, kv_near, sibling(kv_near)), table)
    count = half.shape[0]
    own_pairs, far_pairs = c * pairs, (1 - c) * pairs
    c2_give, cross_lse_give = cross_fwd(far_pairs, pairs, qc, kc, vc, count)
    c2_keep, cross_lse_keep = cross_fwd(own_pairs, pairs, qc, kc, vc, count)
    _, out, a3, g, dm, du, d2, dh2, dc2_keep, dc2_give, vec_mid = middle(
        s, h1, c2_keep, c2_give, cotangent[0], cot_in, w_co, (own1, own2), ff_far, table, fc1_shift,
    )

    packed = ff_grads(s, a3, du, g, dm)
    dc2_give, packed, out, a1_out = tie(dc2_give, packed, out, a1)
    ff_mine = lax.psum_scatter(packed.reshape(2 * reps, 2 * per, width), SPREAD2, scatter_dimension=0, tiled=False)
    out_in = swap(out)
    a1_sib = sibling(a1_out)
    dq_give, dkv_give = cross_bwd(far_pairs, pairs, qc, kc, vc, c2_give, dc2_give, cross_lse_give, count)
    dkv_give, dq_give = tie(dkv_give, dq_give)
    dkv_in = sibling(dkv_give)
    pair_give = give_grads(s, c2_keep, c2_give, d2, a2, dq_give)
    pair_give, dc2_keep = tie(pair_give, dc2_keep)
    pair_in = sibling(pair_give)
    dq_keep, dkv_keep = cross_bwd(own_pairs, pairs, qc, kc, vc, c2_keep, dc2_keep, cross_lse_keep, count)
    dq_keep, out_in, dkv_in, a1_sib, pair_in = tie(dq_keep, out_in, dkv_in, a1_sib, pair_in)
    fkeep, fgive, kv_xkeep, kv_xgive, vec_kv = frame_back(s, dkv_keep, dkv_in, half, twin, w_kv)
    fgive, dq_keep = tie(fgive, dq_keep)
    fr_in = sibling(fgive)
    xgive, xkeep = keep_grads(s, c2_keep, c2_give, d2, a2, dq_keep, pair_in, kv_xkeep, kv_xgive)
    xgive, dq_keep = tie(xgive, dq_keep)
    got_x = across(xgive, "x")
    dh1, d1, dctx_keep, dctx_give, vec_cross = cross_back(s, dq_keep, dq_give, h1, dh2, w_q, w_out, table)
    dctx_give, d1 = tie(dctx_give, d1)
    dctx_in = sibling(dctx_give)
    so_give = give_grad_out(s, ctx, ctx_in, d1)
    so_give, fr_in, fkeep = tie(so_give, fr_in, fkeep)
    so_in = sibling(so_give)
    fr_own = (fkeep.astype(f32) + fr_in.astype(f32)).astype(bf16)
    fr_own, dctx_keep = tie(fr_own, dctx_keep)
    fr_swapped = swap(fr_own)
    so_xgive, so_xkeep = keep_grad_out(s, ctx, ctx_in, d1, so_in)
    so_xgive, dctx_keep = tie(so_xgive, dctx_keep)
    so_x = across(so_xgive, "x")

    def send_z(pieces):
        return (pieces[0],) + tuple(across_z(pieces[d], d) for d in (1, 2, 3))

    def gather_z(piece):
        return (piece,) + tuple(across_z(piece, d) for d in (1, 2, 3))

    bg1, bk1 = self_bwd(0, 1, 0, c, keep, recv, ctx_a, dctx_keep, dctx_in, lse_a, kmark, qmark)
    bg1, bk1, keep = tie(bg1, bk1, keep)
    bi1 = sibling(bg1)
    bg2, bk2 = self_bwd(1, 1, 1, c, keep, recv, ctx_a, dctx_keep, dctx_in, lse_a, kmark, qmark)
    bg2, bk2, got_x, so_x, keep, bi1, fr_swapped = tie(bg2, bk2, got_x, so_x, keep, bi1, fr_swapped)
    bi2 = sibling(bg2)
    m_ygive, m_ykeep = split_y(s, (xkeep, so_xkeep), (got_x, so_x))
    m_ygive, keep, ff_mine = tie(m_ygive, keep, ff_mine)
    m_y = across(m_ygive, "y")
    ff_got = lax.all_gather(ff_mine, REP2, axis=0, tiled=False)
    bg3, bk3 = self_bwd(2, 1, 0, c, keep, recv, ctx_b, dctx_keep, dctx_in, lse_b, kmark, qmark)
    bg3, bk3, bi2 = tie(bg3, bk3, bi2)
    bi3 = sibling(bg3)
    q_xgive = qkv_grad(s, a1, a1_sib, (bk1, bk2, bk3), (bg1, bg2, bg3), False)
    q_xgive, m_y = tie(q_xgive, m_y)
    q_x = across(q_xgive, "x")
    m_z = split_z(s, m_ykeep, m_y)
    bk3, dh1, *m_z = tie(bk3, dh1, *m_z)
    m_z = send_z(m_z)
    q_xkeep = qkv_grad(s, a1, a1_sib, (bk1, bk2, bk3), (bg1, bg2, bg3), True)
    grad_hidden, vec_last = last_rows(s, (bk1, bk2, bk3), (bi1, bi2, bi3), x_own, x_in, dh1, w_qkv, table)
    v_give, v_mine = pack_vectors(s, vec_last, vec_cross, vec_mid, vec_kv)
    v_got = across(v_give, "x")
    v_mine, q_x = tie(v_mine, q_x)
    q_ygive, q_ykeep = split_y(s, (q_xkeep,), (q_x,))
    q_ygive, grad_hidden, *m_z = tie(q_ygive, grad_hidden, *m_z)
    m_piece = sum_four(s, m_z)
    m_got = lax.all_gather(m_piece, REP2, axis=0, tiled=False)
    q_y = across(q_ygive, "y")
    hid_in = swap(grad_hidden)
    q_four = split_z(s, q_ykeep, q_y)
    q_z = send_z(q_four)
    fc1_grad, fc2_grad = spread_ff(s, ff_got.reshape(reps, 2, per, width))
    output = jnp.where(stay, out, out_in)
    fc1_grad, fc2_grad, output, *q_z = tie(fc1_grad, fc2_grad, output, *q_z)
    q_piece = sum_four(s, q_z, (v_mine, v_got))
    q_all = gather_z(q_piece)
    spots = ((0, 0, 0), (1, 0, 0), (3, 0, 0), (3, hw, 0), (2, 0, 0))
    crossout_grad, crossq_grad, selfout_grad, kv_grad = spread_gathered(s, m_got, spots, ((hw, width),) * 3 + ((width, width),))
    grad_frames = jnp.where(stay, fr_own, fr_swapped)
    grad_frames, *q_all = tie(grad_frames, *q_all)
    q_own = join_z(s, q_all)
    q_far = across(q_own, "y")
    q_own_sib = sibling(q_own)
    grad_hidden = jnp.where(stay, grad_hidden, hid_in)
    q_far, crossout_grad, grad_hidden = tie(q_far, crossout_grad, grad_hidden)
    first = tuple((0, 0, j * width) for j in range(3))
    qkv_grad_out, gain_grad, shift_grad, bias_grad, fc1b_grad = spread_out(s, (((q_own, q_far, q_own_sib, sibling(q_far)), first),), ((hw, 3 * width), (4, hw), (4, hw), (7, hw), (units, hw)), True)

    return (
        output[None], grad_hidden[None], grad_frames[None], gain_grad, shift_grad,
        qkv_grad_out, selfout_grad, crossq_grad, kv_grad, crossout_grad, fc1_grad, fc2_grad, bias_grad, fc1b_grad.reshape(-1),
    )


GROUP = ("core", "ilo")
SHARD = ("ihi", "ilo")
REP = ("rz", "core")
SPREAD = ("ihi", "ilo", "rz", "core")


def body_general(hidden, frames, segment, cotangent, norm_gain, norm_bias, self_qkv, self_out, cross_q, cross_kv, cross_out, fc1, fc2, proj_bias, fc1_bias):
    c = lax.axis_index("core")
    hi = lax.axis_index("ihi")
    n = lax.axis_size("core") * lax.axis_size("ilo")
    reps = lax.axis_size("rz") * lax.axis_size("core")
    rep_at = lax.axis_index(REP)
    width = self_out.shape[1]
    ff = fc1.shape[1]

    def swap(x):
        return lax.ppermute(x, ("core", "ihi"), [(0, 0), (1, 2), (2, 1), (3, 3)])

    def whole(own):
        if n != 2:
            return lax.all_gather(own, SHARD, axis=0, tiled=True)
        half = own.shape[0] // 2
        mine = lax.ppermute(lax.dynamic_slice_in_dim(own, c * half, half), "ihi", FLIP)
        sib = lax.ppermute(mine, "core", FLIP)
        other = jnp.where(c == 0, jnp.concatenate([mine, sib]), jnp.concatenate([sib, mine]))
        return jnp.where(hi == 0, jnp.concatenate([own, other]), jnp.concatenate([other, own]))

    def slices(own):
        rows = own.shape[0] // reps
        return lax.dynamic_slice_in_dim(own, rep_at * rows, rows)

    rows_in = swap(hidden[0])
    qkv_w = whole(self_qkv.astype(bf16))
    small = jnp.concatenate([norm_gain.astype(bf16), norm_bias.astype(bf16), proj_bias.astype(bf16), fc1_bias.astype(bf16).reshape(-1, norm_gain.shape[1]), jnp.zeros((1, norm_gain.shape[1]), bf16)])
    small = lax.all_gather(small, SHARD, axis=1, tiled=False).astype(f32)
    table = small[:15].reshape(15, width)
    gains, shifts, biases = table[:4], table[4:8], table[8:15]
    fc1_shift = small[15:19].transpose(1, 0, 2).reshape(ff)
    seg = swap(segment)[0]
    frames_half = swap(frames[0])
    if n == 2:
        twin = lax.ppermute(frames_half, "core", FLIP)
        frame_rows = jnp.concatenate([jnp.where(c == 0, frames_half, twin), jnp.where(c == 0, twin, frames_half)], axis=1)
    else:
        frame_rows = lax.all_gather(frames_half, GROUP, axis=1, tiled=True)
    selfout_w = whole(self_out.astype(bf16))
    crossq_w = whole(cross_q.astype(bf16))
    kv_w = whole(cross_kv.astype(bf16)) if n == 2 else None
    if n == 2:
        k_w, v_w = kv_w[:width], kv_w[width:]
    else:
        kv_w = lax.all_gather(cross_kv.astype(bf16), SHARD, axis=1, tiled=True)
        k_w, v_w = kv_w[:, :width], kv_w[:, width:]
    crossout_w = whole(cross_out.astype(bf16))
    cot = swap(cotangent[0])
    units = ff // width
    part1 = slices(fc1.astype(bf16))
    part2 = slices(fc2.astype(bf16))
    few = part1.shape[0]
    parts = jnp.concatenate([part1[:, j * width : (j + 1) * width] for j in range(units)] + [part2])
    ffw = lax.all_gather(parts, SPREAD, axis=0, tiled=False)
    fc1_w = jnp.concatenate([ffw[:, j * few : (j + 1) * few].reshape(width, width) for j in range(units)], axis=1)
    fc2_w = ffw[:, units * few :].reshape(ff, width)

    own_rows = rows_in.shape[0]
    hw = -(-HEADS // n)
    padded = hw * n * HD - width

    lanes = hw * HD

    def to_heads(x):
        x = x.reshape(own_rows, -1, width)
        if padded:
            x = jnp.pad(x, ((0, 0), (0, 0), (0, padded)))
        x = x.reshape(own_rows, -1, n, lanes).transpose(1, 2, 0, 3)
        x = lax.all_to_all(x, GROUP, 1, 1, tiled=True)
        return x.reshape(-1, n * own_rows, lanes)

    def to_tokens(x):
        x = lax.all_to_all(x.reshape(-1, n, own_rows, lanes), GROUP, 1, 1, tiled=True)
        return x.transpose(2, 0, 1, 3).reshape(own_rows, -1, n * lanes)[:, :, :width].reshape(own_rows, -1)

    h0 = rows_in.astype(f32)
    a1 = norm(h0, gains[0], shifts[0]).astype(bf16)
    zeros_row = jnp.zeros((width,), f32)
    qkv = (mm(a1, qkv_w) + jnp.concatenate([biases[0], zeros_row, biases[1]])).astype(bf16)
    heads = to_heads(qkv)
    kmark, qmark = seg_marks(seg)
    mid = heads.shape[1] // 2
    first = jnp.int32(0)
    ctx, _, self_lse = self_fwd(0, lanes // 128, first, heads[:, :mid], heads[:, mid:], kmark, qmark)
    c1 = to_tokens(ctx)
    h1 = h0 + mm(c1, selfout_w) + biases[2]
    a2 = norm(h1, gains[1], shifts[1]).astype(bf16)
    qc = (mm(a2, crossq_w) + biases[3]).astype(bf16)
    count = frame_rows.shape[0]
    pad = -count % 256
    frame_pad = jnp.pad(frame_rows, ((0, pad), (0, 0)))
    kc = mm(frame_pad, k_w).astype(bf16)
    live = lax.broadcasted_iota(jnp.int32, (count + pad, 1), 0) < count
    vc = (mm(frame_pad, v_w) + jnp.where(live, biases[4], 0.0)).astype(bf16)
    c2, cross_lse = cross_fwd(first, width // 128, qc, kc, vc, count)
    h2 = h1 + mm(c2, crossout_w) + biases[5]
    a3 = norm(h2, gains[2], shifts[2]).astype(bf16)
    u = (mm(a3, fc1_w) + fc1_shift).astype(bf16)
    uf = u.astype(f32)
    g, slope = gelu_parts(uf)
    g = g.astype(bf16)
    h3 = h2 + mm(g, fc2_w) + biases[6]
    output = norm(h3, gains[3], shifts[3]).astype(bf16)
    output = swap(output)

    def total(x):
        return jnp.sum(x.astype(f32), axis=0)

    dh3, gain3, shift3 = norm_back(h3, gains[3], cot.astype(f32))
    dm = dh3.astype(bf16)
    g_fc2 = t_mm(g, dm).astype(bf16)
    du = (slope * mm_t(dm, fc2_w)).astype(bf16)
    g_fc1 = t_mm(a3, du).astype(bf16)

    def reduce_rows(parts, extra=None):
        total = n * reps
        cut = [p.reshape(total, -1, width) for p in parts]
        if extra is not None:
            cut.append(extra)
        flat = jnp.concatenate(cut, axis=1)
        mine = lax.psum_scatter(flat, SPREAD, scatter_dimension=0, tiled=False)
        got = lax.all_gather(mine, REP, axis=0, tiled=False)
        out, at = [], 0
        for p in cut:
            out.append(got[:, at : at + p.shape[1]].reshape(-1, width).astype(f32))
            at += p.shape[1]
        return out

    ff_grads = reduce_rows([g_fc1[:, j * width : (j + 1) * width] for j in range(units)] + [g_fc2])
    fc1_grad = jnp.concatenate(ff_grads[:units], axis=1)
    fc2_grad = ff_grads[units]

    da3 = mm_t(du, fc1_w)
    dres, gain2, shift2 = norm_back(h2, gains[2], da3)
    dh2 = dh3 + dres
    d2 = dh2.astype(bf16)
    g_crossout = t_mm(c2, d2).astype(bf16)
    dc2 = mm_t(d2, crossout_w).astype(bf16)
    dqc, (dkc, dvc) = cross_bwd(first, width // 128, qc, kc, vc, c2, dc2, cross_lse, count)
    share = width // n

    def sum_columns(x):
        return lax.psum_scatter(x, GROUP, scatter_dimension=1, tiled=True)

    if n == 2:

        def sum_columns(x):
            give = lax.dynamic_slice_in_dim(x, (1 - c) * share, share, axis=1)
            keep = lax.dynamic_slice_in_dim(x, c * share, share, axis=1)
            return (keep.astype(f32) + lax.ppermute(give, "core", FLIP).astype(f32)).astype(bf16)

    dk_own = sum_columns(dkc)[:count]
    dv_own = sum_columns(dvc)[:count]
    place = lax.axis_index(GROUP) * share
    kw_own = lax.dynamic_slice_in_dim(k_w, place, share, axis=1)
    vw_own = lax.dynamic_slice_in_dim(v_w, place, share, axis=1)
    dframe = (mm_t(dk_own, kw_own) + mm_t(dv_own, vw_own)).astype(bf16)
    grad_frames = swap(sum_columns(dframe))
    g_k = t_mm(frame_rows, dk_own).astype(bf16)
    g_v = t_mm(frame_rows, dv_own).astype(bf16)
    vb_own = jnp.sum(dv_own.astype(f32), axis=0)

    g_crossq = t_mm(a2, dqc).astype(bf16)
    da2 = mm_t(dqc, crossq_w)
    dres, gain1, shift1 = norm_back(h1, gains[1], da2)
    dh1 = dh2 + dres
    d1 = dh1.astype(bf16)
    g_selfout = t_mm(c1, d1).astype(bf16)
    dctx = mm_t(d1, selfout_w).astype(bf16)
    dctx = to_heads(dctx)[0]
    late, early = self_bwd(0, lanes // 128, 0, first, heads[:, :mid], heads[:, mid:], ctx, dctx[:mid], dctx[mid:], self_lse, kmark, qmark)
    dqkv = to_tokens(jnp.concatenate([early, late], axis=1))
    da1 = mm_t(dqkv, qkv_w)
    g_qkv = t_mm(a1, dqkv).astype(bf16)
    sums = total(dqkv)
    dres, gain0, shift0 = norm_back(h0, gains[0], da1)
    grad_hidden = swap((dh1 + dres).astype(bf16))

    vb = lax.dynamic_update_slice(jnp.zeros((width,), f32), vb_own, (place,))
    vectors = jnp.stack([gain0[0], gain1[0], gain2[0], gain3[0], shift0[0], shift1[0], shift2[0], shift3[0], sums[:width], sums[2 * width :], total(d1), total(dqc), vb, total(d2), total(dm)])
    per = width // n
    vectors = vectors.reshape(15, n, per).transpose(1, 0, 2).reshape(n, 15 * per)
    vectors = jnp.concatenate([vectors, total(du).reshape(n, ff // n)], axis=1)
    long = vectors.shape[1]
    seats = -(-long // reps)
    vectors = jnp.pad(vectors, ((0, 0), (0, seats * reps - long))).reshape(n * reps, seats)
    lines = -(-seats // (8 * width)) * 8
    vectors = jnp.pad(vectors, ((0, 0), (0, lines * width - seats))).reshape(n * reps, lines, width)

    def own_columns(x):
        return lax.dynamic_update_slice(jnp.zeros((x.shape[0], width), x.dtype), x, (jnp.int32(0), place))

    cross = [g_crossq, g_crossout]
    if n == 2:
        cross.append(jnp.concatenate([own_columns(g_k), own_columns(g_v)]))
    cross = reduce_rows(cross)
    crossq_grad, crossout_grad = cross[:2]
    if n == 2:
        kv_grad = cross[2]
    else:
        kv_cols = jnp.concatenate([own_columns(g_k), own_columns(g_v)], axis=1)
        kv_cols = lax.psum_scatter(kv_cols, SHARD, scatter_dimension=1, tiled=True)
        kv_grad = lax.psum(kv_cols, REP).astype(f32)
    got = reduce_rows([g_qkv[:, j * width : (j + 1) * width] for j in range(3)] + [g_selfout], vectors.astype(bf16))
    qkv_grad = jnp.concatenate(got[:3], axis=1)
    selfout_grad = got[3]
    vec = got[4].reshape(reps, lines * width)[:, :seats].reshape(-1)[:long]
    table = vec[: 15 * per].reshape(15, per)
    fc1b_grad = vec[15 * per :]
    return (
        output[None], grad_hidden[None], grad_frames[None],
        table[:4], table[4:8], qkv_grad, selfout_grad, crossq_grad, kv_grad, crossout_grad, fc1_grad, fc2_grad, table[8:15], fc1b_grad,
    )


def solution(mesh):
    reps, n = mesh.devices.shape
    paired = (reps, n) == (16, 2)
    if paired:
        work = Mesh(mesh.devices.reshape(4, 2, 2, 2), EVERY)
        rep, inner = REP2, ("x",)
    else:
        work = Mesh(mesh.devices.reshape(reps // 2, 2, 2, n // 2), ("rz", "core", "ihi", "ilo"))
        rep, inner = REP, SHARD
    rows, cols = P(inner, None), P(None, inner)
    tokens, features = P(rep, inner, None), P(rep, None, inner)
    weights = (cols, cols, rows, rows, rows, cols, rows, rows, rows, cols, P(inner))
    return jax.shard_map(
        body_pair if paired else body_general,
        mesh=work,
        in_specs=(tokens, features, P(rep, None), tokens) + weights,
        out_specs=(tokens, tokens, features) + weights,
        check_vma=False,
    )
```

```python
import math

import jax
import jax.numpy as jnp
from jax import lax
from jax.experimental import pallas as pl
from jax.experimental.pallas import tpu as pltpu
from jax.sharding import Mesh
from jax.sharding import PartitionSpec as P

HEADS = 12
HD = 64
EPSILON = 1e-05
NEG = -1e30
PROMPT = 1024
REACH = 256
bf16 = jnp.bfloat16
f32 = jnp.float32
FLIP = [(0, 1), (1, 0)]


def mm(a, b):
    return jnp.dot(a, b, preferred_element_type=f32)


def mm_t(a, b):
    return lax.dot_general(a, b, (((1,), (1,)), ((), ())), preferred_element_type=f32)


def t_mm(a, b):
    return lax.dot_general(a, b, (((0,), (0,)), ((), ())), preferred_element_type=f32)


def call(kernel, scalars, args, grid, in_specs, out_specs, out_shape, scratch=(), cost=None):
    spec = pltpu.PrefetchScalarGridSpec(
        num_scalar_prefetch=1, grid=grid, in_specs=in_specs, out_specs=out_specs, scratch_shapes=list(scratch)
    )
    estimate = None
    if cost is not None:
        estimate = pl.CostEstimate(flops=cost // 10, bytes_accessed=1 << 20, transcendentals=0)
    return pl.pallas_call(
        kernel,
        grid_spec=spec,
        out_shape=out_shape,
        cost_estimate=estimate,
        compiler_params=pltpu.CompilerParams(vmem_limit_bytes=60 * 2**20),
    )(scalars, *args)


def shape(dims, kind=bf16):
    return jax.ShapeDtypeStruct(dims, kind)


def half_of(lane, h):
    return (lane < HD) if h == 0 else (lane >= HD)


def delta_of(do, o):
    x = do.astype(f32) * o.astype(f32)
    hi = x.astype(bf16)
    lo = (x - hi.astype(f32)).astype(bf16)
    r = lax.broadcasted_iota(jnp.int32, (8, 128), 0)
    lane = lax.broadcasted_iota(jnp.int32, (8, 128), 1)
    pick = jnp.where((lane // HD) == r, 1.0, 0.0).astype(bf16)
    return mm_t(pick, hi) + mm_t(pick, lo)


def cross_fwd(base, pairs, q, k, v, valid, block=1024):
    tq, tk = q.shape[0], k.shape[0]
    block = min(block, tq)

    def kernel(s_ref, q_ref, k_ref, v_ref, o_ref, l_ref, ks, vts):
        @pl.when(pl.program_id(1) == 0)
        def _():
            low = lax.broadcasted_iota(jnp.int32, (tk, 128), 1)
            row = lax.broadcasted_iota(jnp.int32, (tk, 128), 0)
            bias = jnp.where(row >= valid, NEG, 0.0).astype(bf16)
            one = jnp.ones((tk, 128), bf16)
            for h in range(2):
                ks[h] = jnp.where(half_of(low, h), k_ref[...], bias)
                vts[h] = jnp.where(half_of(low, h), v_ref[...], one).T

        lane = lax.broadcasted_iota(jnp.int32, (block, 128), 1)
        qq = q_ref[...] * bf16(0.125)
        scores = []
        for h in range(2):
            spare = lane == (HD if h == 0 else 0)
            qh = jnp.where(half_of(lane, h), qq, jnp.where(spare, 1.0, 0.0).astype(bf16))
            scores.append(mm_t(ks[h], qh))
        outs = []
        for h, s in enumerate(scores):
            m = jnp.max(s, axis=0, keepdims=True)
            o = mm(vts[h], jnp.exp(s - m).astype(bf16))
            total = o[HD : HD + 1] if h == 0 else o[0:1]
            outs.append(o * (1.0 / total))
            l_ref[0, h : h + 1, :] = m + jnp.log(total)
        sub = lax.broadcasted_iota(jnp.int32, (128, block), 0)
        o_ref[...] = jnp.where(sub < HD, outs[0], outs[1]).T.astype(bf16)

    qspec = pl.BlockSpec((block, 128), lambda p, i, s: (i, s[0] + p))
    kspec = pl.BlockSpec((tk, 128), lambda p, i, s: (0, s[0] + p))
    return call(
        kernel, jnp.reshape(base, (1,)).astype(jnp.int32), (q, k, v), (pairs, tq // block), [qspec, kspec, kspec],
        [pl.BlockSpec((block, 128), lambda p, i, s: (i, p)), pl.BlockSpec((1, 8, block), lambda p, i, s: (p, 0, i))],
        [shape((tq, pairs * 128)), shape((pairs, 8, tq), f32)],
        [pltpu.VMEM((2, tk, 128), bf16), pltpu.VMEM((2, 128, tk), bf16)],
        4 * tq * tk * 256 * pairs,
    )


def cross_bwd(base, pairs, q, k, v, o, do, lse, valid, block=1024):
    tq, tk = q.shape[0], k.shape[0]
    block = min(block, tq)
    steps = tq // block

    def kernel(s_ref, q_ref, k_ref, v_ref, o_ref, do_ref, l_ref, dq_ref, d_ref, ks, kts, dka, dva):
        @pl.when(pl.program_id(1) == 0)
        def _():
            low = lax.broadcasted_iota(jnp.int32, (tk, 128), 1)
            row = lax.broadcasted_iota(jnp.int32, (tk, 128), 0)
            bias = jnp.where(row >= valid, NEG, 0.0).astype(bf16)
            zero = jnp.zeros((tk, 128), bf16)
            for h in range(2):
                ks[h] = jnp.where(half_of(low, h), k_ref[...], bias)
                kts[h] = jnp.where(half_of(low, h), k_ref[...], zero).T
            dka[...] = jnp.zeros((tk, 128), f32)
            dva[...] = jnp.zeros((tk, 128), f32)

        lane = lax.broadcasted_iota(jnp.int32, (block, 128), 1)
        qq = q_ref[...] * bf16(0.125)
        dd = do_ref[...]
        delta = delta_of(dd, o_ref[...])
        zero = jnp.zeros((block, 128), bf16)
        dqt, dk, dv = None, dka[...], dva[...]

        def products(h):
            mine = half_of(lane, h)
            spare = lane == (HD if h == 0 else 0)
            qc = jnp.where(mine, qq, zero)
            dh = jnp.where(mine, dd, zero)
            return qc, dh, mm_t(ks[h], jnp.where(spare, jnp.ones((block, 128), bf16), qc)), mm_t(v_ref[...], dh)

        now = products(0)
        for h in range(2):
            qc, dh, scores, dp = now
            now = products(1) if h == 0 else None
            p = jnp.exp(scores - l_ref[0, h : h + 1, :])
            ds = (p * (dp - delta[h : h + 1])).astype(bf16)
            dv = dv + mm(p.astype(bf16), dh)
            dk = dk + mm(ds, qc)
            part = mm(kts[h], ds)
            dqt = part if dqt is None else dqt + part
        dka[...] = dk
        dva[...] = dv
        dq_ref[...] = (dqt * 0.125).T.astype(bf16)

        @pl.when(pl.program_id(1) == steps - 1)
        def _():
            d_ref[0] = dka[...].astype(bf16)
            d_ref[1] = dva[...].astype(bf16)

    mine = pl.BlockSpec((block, 128), lambda p, i, s: (i, p))
    qspec = pl.BlockSpec((block, 128), lambda p, i, s: (i, s[0] + p))
    kspec = pl.BlockSpec((tk, 128), lambda p, i, s: (0, s[0] + p))
    return call(
        kernel, jnp.reshape(base, (1,)).astype(jnp.int32), (q, k, v, o, do, lse), (pairs, steps),
        [qspec, kspec, kspec, mine, mine, pl.BlockSpec((1, 8, block), lambda p, i, s: (p, 0, i))],
        [mine, pl.BlockSpec((2, tk, 128), lambda p, i, s: (0, 0, p))],
        [shape((tq, pairs * 128)), shape((2, tk, pairs * 128))],
        [pltpu.VMEM((2, tk, 128), bf16), pltpu.VMEM((2, 128, tk), bf16), pltpu.VMEM((tk, 128), f32), pltpu.VMEM((tk, 128), f32)],
        2 * tq * tk * 10 * 256 * pairs,
    )


def spans(r0, block):
    if r0 < PROMPT:
        return ([(0, r0)] if r0 else []) + [(r0, r0 + block)]
    left = max(PROMPT, r0 - REACH)
    before = [(0, r0)] if left == PROMPT else [(0, PROMPT), (left, r0)]
    return before + [(r0, r0 + block)]


def seg_marks(seg):
    lane = lax.broadcasted_iota(jnp.int32, (seg.shape[0], 128), 1) % HD
    same = lane == seg[:, None]
    kmark = jnp.where(same, 1.0, 0.0).astype(bf16)
    qmark = jnp.where(same | (lane == 0) | (lane > 8), 0.0, NEG).astype(bf16)
    return kmark, qmark


def half_specs(rows, first=0):
    return [pl.BlockSpec((3, rows, 128), lambda p, s: (0, 0, first + p))] * 2


def self_fwd(first, pairs, place, keep, recv, kmark, qmark, block=512):
    rows, width = keep.shape[1], pairs * 128
    t = 2 * rows

    def kernel(s_ref, a_ref, b_ref, km_ref, qm_ref, o_ref, give_ref, l_ref, qf, ks, vts):
        mine0 = pl.multiple_of(s_ref[0] * rows, rows)
        other0 = pl.multiple_of((1 - s_ref[0]) * rows, rows)
        low = lax.broadcasted_iota(jnp.int32, (rows, 128), 1)
        one = jnp.ones((rows, 128), bf16)
        for ref, at in ((a_ref, mine0), (b_ref, other0)):
            spot = pl.ds(at, rows)
            qf[spot, :] = ref[0] * bf16(0.125)
            for h in range(2):
                ks[h, spot, :] = jnp.where(half_of(low, h), ref[1], km_ref[spot, :])
                vts[h, :, spot] = jnp.where(half_of(low, h), ref[2], one).T
        lane = lax.broadcasted_iota(jnp.int32, (block, 128), 1)
        hide = lax.broadcasted_iota(jnp.int32, (block, block), 0) > lax.broadcasted_iota(jnp.int32, (block, block), 1)
        tasks = [(r0, h) for r0 in range(0, t, block) for h in range(2)]

        def scores(task):
            r0, h = task
            spot = pl.ds(r0, block)
            qs = jnp.where(half_of(lane, h), qf[spot, :], qm_ref[spot, :])
            out = [mm_t(ks[h, pl.ds(a, b - a), :], qs) for a, b in spans(r0, block)]
            out[-1] = jnp.where(hide, NEG, out[-1])
            return out

        now, outs = scores(tasks[0]), [None, None]
        for i, (r0, h) in enumerate(tasks):
            later = scores(tasks[i + 1]) if i + 1 < len(tasks) else None
            m = None
            for s in now:
                top = jnp.max(s, axis=0, keepdims=True)
                m = top if m is None else jnp.maximum(m, top)
            o = None
            for s, (a, b) in zip(now, spans(r0, block)):
                part = mm(vts[h, :, pl.ds(a, b - a)], jnp.exp(s - m).astype(bf16))
                o = part if o is None else o + part
            total = o[HD : HD + 1] if h == 0 else o[0:1]
            l_ref[0, h : h + 1, pl.ds(r0, block)] = m + jnp.log(total)
            outs[h] = o * (1.0 / total)
            if h == 1:
                sub = lax.broadcasted_iota(jnp.int32, (128, block), 0)
                o_ref[pl.ds(r0, block), :] = jnp.where(sub < HD, outs[0], outs[1]).T.astype(bf16)
            now = later
        give_ref[...] = o_ref[pl.ds(other0, rows), :]

    whole = pl.BlockSpec((t, 128), lambda p, s: (0, 0))
    return call(
        kernel, jnp.reshape(place, (1,)).astype(jnp.int32), (keep, recv, kmark, qmark), (pairs,),
        half_specs(rows, first) + [whole, whole],
        [pl.BlockSpec((t, 128), lambda p, s: (0, p)), pl.BlockSpec((rows, 128), lambda p, s: (0, p)), pl.BlockSpec((1, 8, t), lambda p, s: (p, 0, 0))],
        [shape((t, width)), shape((rows, width)), shape((pairs, 8, t), f32)],
        [pltpu.VMEM((t, 128), bf16), pltpu.VMEM((2, t, 128), bf16), pltpu.VMEM((2, 128, t), bf16)],
        2 * t * t * 4 * width,
    )


def self_bwd(first, pairs, seat, place, keep, recv, o, dkeep, drecv, lse, kmark, qmark, block=256):
    rows, width = keep.shape[1], pairs * 128
    t = 2 * rows

    def kernel(s_ref, a_ref, b_ref, o_ref, da_ref, db_ref, l_ref, km_ref, qm_ref, give_ref, keep_ref, qf, df, vf, ks, kts, dqa, dka, dva):
        mine0 = pl.multiple_of(s_ref[0] * rows, rows)
        other0 = pl.multiple_of((1 - s_ref[0]) * rows, rows)
        low = lax.broadcasted_iota(jnp.int32, (rows, 128), 1)
        zero = jnp.zeros((rows, 128), bf16)
        for ref, dref, at in ((a_ref, da_ref, mine0), (b_ref, db_ref, other0)):
            spot = pl.ds(at, rows)
            qf[spot, :] = ref[0] * bf16(0.125)
            df[spot, :] = dref[...]
            vf[spot, :] = ref[2]
            for h in range(2):
                ks[h, spot, :] = jnp.where(half_of(low, h), ref[1], km_ref[spot, :])
                kts[h, :, spot] = jnp.where(half_of(low, h), ref[1], zero).T
        dka[...] = jnp.zeros((t, 128), f32)
        dva[...] = jnp.zeros((t, 128), f32)
        lane = lax.broadcasted_iota(jnp.int32, (block, 128), 1)
        hide = lax.broadcasted_iota(jnp.int32, (block, block), 0) > lax.broadcasted_iota(jnp.int32, (block, block), 1)
        none = jnp.zeros((block, 128), bf16)
        for r0 in range(0, t, block):
            spot = pl.ds(r0, block)
            dd = df[spot, :]
            delta = delta_of(dd, o_ref[spot, :])
            dqt = None
            tasks = []
            for h in range(2):
                mine = half_of(lane, h)
                qc = jnp.where(mine, qf[spot, :], none)
                qs = jnp.where(mine, qf[spot, :], qm_ref[spot, :])
                dh = jnp.where(mine, dd, none)
                tasks += [(h, qc, qs, dh, a, b) for a, b in spans(r0, block)]

            def products(task):
                h, qc, qs, dh, a, b = task
                s = mm_t(ks[h, pl.ds(a, b - a), :], qs)
                return jnp.where(hide, NEG, s) if a == r0 else s, mm_t(vf[pl.ds(a, b - a), :], dh)

            now = products(tasks[0])
            for i, (h, qc, qs, dh, a, b) in enumerate(tasks):
                later = products(tasks[i + 1]) if i + 1 < len(tasks) else None
                log_total = l_ref[0, h : h + 1, spot]
                keys = pl.ds(a, b - a)
                s, dp = now
                now = later
                p = jnp.exp(s - log_total)
                ds = (p * (dp - delta[h : h + 1])).astype(bf16)
                dva[keys, :] += mm(p.astype(bf16), dh)
                dka[keys, :] += mm(ds, qc)
                part = mm(kts[h, :, keys], ds)
                dqt = part if dqt is None else dqt + part
            dqa[spot, :] = (dqt * 0.125).T.astype(bf16)
        for out, at in ((give_ref, other0), (keep_ref, mine0)):
            spot = pl.ds(at, rows)
            out[0] = dqa[spot, :]
            out[1] = dka[spot, :].astype(bf16)
            out[2] = dva[spot, :].astype(bf16)

    whole = pl.BlockSpec((t, 128), lambda p, s: (0, 0))
    half = pl.BlockSpec((rows, 128), lambda p, s: (0, first + p))
    return call(
        kernel, jnp.reshape(place, (1,)).astype(jnp.int32), (keep, recv, o, dkeep, drecv, lse, kmark, qmark), (pairs,),
        half_specs(rows, first)
        + [pl.BlockSpec((t, 128), lambda p, s: (0, seat + p)), half, half, pl.BlockSpec((1, 8, t), lambda p, s: (seat + p, 0, 0)), whole, whole],
        half_specs(rows),
        [shape((3, rows, width))] * 2,
        [pltpu.VMEM((t, 128), bf16)] * 3 + [pltpu.VMEM((2, t, 128), bf16), pltpu.VMEM((2, 128, t), bf16), pltpu.VMEM((t, 128), bf16)]
        + [pltpu.VMEM((t, 128), f32)] * 2,
        2 * t * t * 8 * width,
    )


def norm_stats(rows):
    centered = rows - jnp.mean(rows, axis=-1, keepdims=True)
    inv = lax.rsqrt(jnp.mean(centered * centered, axis=-1, keepdims=True) + EPSILON)
    return centered * inv, inv


def norm(rows, gain, shift):
    return norm_stats(rows)[0] * gain + shift


def norm_back(rows, gain, dy):
    n, inv = norm_stats(rows)
    dn = dy * gain
    dh = inv * (dn - jnp.mean(dn, axis=-1, keepdims=True) - n * jnp.mean(dn * n, axis=-1, keepdims=True))
    return dh, jnp.sum(dy * n, axis=0, keepdims=True), jnp.sum(dy, axis=0, keepdims=True)


ERFC = (
    0.22567585470008253, 0.22566975083164525, 0.20784161289369674, 0.1685452087610459, 0.14142852065437478,
    -0.005612938524279035, 0.1691005263450779, -0.1829144800497475, 0.05026606972001335,
)


def gelu_parts(u):
    bell = jnp.exp(u * u * -0.5)
    t = 1.0 / (1.0 + jnp.abs(u) * (0.4 * math.sqrt(0.5)))
    poly = jnp.full_like(t, ERFC[-1])
    for value in ERFC[-2::-1]:
        poly = poly * t + value
    tail = bell * t * poly * 0.5
    cdf = jnp.where(u < 0.0, tail, 1.0 - tail)
    return u * cdf, cdf + u * bell * (1.0 / math.sqrt(2.0 * math.pi))


def const(dims):
    return pl.BlockSpec(dims, lambda i, s: (0,) * len(dims))


def once(dims):
    return pl.BlockSpec(dims, lambda i, s: (0,) * len(dims), pipeline_mode=pl.Buffered(1))


def tile(rows, width):
    return pl.BlockSpec((rows, width), lambda i, s: (i, 0))


def fill(full, s, own, mine, sib):
    rows = own.shape[0]
    c, h = s[0], s[1]
    full[pl.ds(pl.multiple_of(h * rows, 128), rows), :] = own[...].astype(bf16)
    start = (1 - h) * rows
    full[pl.ds(pl.multiple_of(start + c * (rows // 2), 64), rows // 2), :] = mine[...]
    full[pl.ds(pl.multiple_of(start + (1 - c) * (rows // 2), 64), rows // 2), :] = sib[...]


def picked(part):
    if not isinstance(part, tuple):
        return once(part.shape)
    stack, which = part
    return pl.BlockSpec((None, *stack.shape[1:]), lambda i, s: (which, 0, 0), pipeline_mode=pl.Buffered(1))


def weight_specs(weight):
    return [picked(part) for part in weight]


def arrays(weight):
    return [part[0] if isinstance(part, tuple) else part for part in weight]


def full_shape(weight):
    return (2 * weight[0].shape[0], weight[0].shape[1])


def at_core(c, width):
    return pl.ds(pl.multiple_of(c * width, 128), width)


def norm_qkv(s, x_own, x_in, weight, table, rows=512):
    t, width = x_own.shape
    hw = width // 2

    def kernel(s_ref, xo, xi, own, mine, sib, tab, w, a_ref, keep, give):
        @pl.when(pl.program_id(0) == 0)
        def _():
            fill(w, s_ref, own, mine, sib)

        x = jnp.where(s_ref[2] == 1, xo[...].astype(f32), xi[...].astype(f32))
        a = norm(x, tab[0:1], tab[4:5]).astype(bf16)
        a_ref[...] = a
        for j in range(3):
            y = mm(a, w[:, j * width : (j + 1) * width])
            if j != 1:
                y = y + tab[8 + j // 2 : 9 + j // 2]
            low, high = y[:, :hw].astype(bf16), y[:, hw:].astype(bf16)
            first = s_ref[0] == 0
            keep[j] = jnp.where(first, low, high)
            give[j] = jnp.where(first, high, low)

    third = pl.BlockSpec((3, rows, hw), lambda i, s: (0, i, 0))
    dims = full_shape(weight)
    return call(
        kernel, s, (x_own, x_in, *weight, table), (t // rows,),
        [tile(rows, width)] * 2 + weight_specs(weight) + [const(table.shape)],
        [const(dims), tile(rows, width), third, third],
        [shape(dims), shape((t, width)), shape((3, t, hw)), shape((3, t, hw))],
        cost=2 * t * width * 3 * width,
    )


def beside(refs):
    return jnp.concatenate([ref[...] for ref in refs], axis=1) if len(refs) > 1 else refs[0][...]


def self_project(s, ctx, ctx_in, x_own, x_in, w_out, w_q, table, rows=512):
    t, width = x_own.shape
    hw = width // 2
    steps = t // rows
    n = len(ctx)

    def kernel(s_ref, *refs):
        cks, cis = refs[:n], refs[n : 2 * n]
        xo, xi, o1, o2, o3, q1, q2, q3, tab, wo, wq, h_ref, a_ref, qc_ref = refs[2 * n :]

        @pl.when(pl.program_id(0) == 0)
        def _():
            fill(wo, s_ref, o1, o2, o3)
            fill(wq, s_ref, q1, q2, q3)

        c = s_ref[0]
        x = jnp.where(s_ref[2] == 1, xo[...].astype(f32), xi[...].astype(f32))
        h = x + mm(beside(cks), wo[at_core(c, hw), :]) + mm(beside(cis), wo[at_core(1 - c, hw), :]) + tab[10:11]
        h_ref[...] = h
        a = norm(h, tab[1:2], tab[5:6]).astype(bf16)
        a_ref[...] = a
        qc_ref[...] = (mm(a, wq[...]) + tab[11:12]).astype(bf16)

    dims = full_shape(w_out)
    return call(
        kernel, s, (*ctx, *ctx_in, x_own, x_in, *arrays(w_out), *arrays(w_q), table), (steps,),
        [pl.BlockSpec((rows, part.shape[1]), lambda i, s: (s[0] * steps + i, 0)) for part in ctx]
        + [tile(rows, part.shape[1]) for part in ctx_in] + [tile(rows, width), tile(rows, width)]
        + weight_specs(w_out) + weight_specs(w_q) + [const(table.shape)],
        [const(dims), const(dims), tile(rows, width), tile(rows, width), tile(rows, width)],
        [shape(dims), shape(dims), shape((t, width), f32), shape((t, width)), shape((t, width))],
        cost=4 * t * width * width,
    )


def frame_kv(s, half, twin, weight, table, rows=512):
    count, hw = half.shape
    width = 2 * hw
    steps = -(-count // rows)

    def kernel(s_ref, fa, fb, own, mine, sib, tab, w, k_ref, v_ref):
        @pl.when(pl.program_id(0) == 0)
        def _():
            fill(w, s_ref, own, mine, sib)

        c = s_ref[0]
        live = lax.broadcasted_iota(jnp.int32, (rows, 1), 0) + pl.program_id(0) * rows < count
        for j, out in enumerate((k_ref, v_ref)):
            mine0 = pl.multiple_of(j * width + c * hw, 128)
            other0 = pl.multiple_of(j * width + (1 - c) * hw, 128)
            y = mm(fa[...], w[pl.ds(mine0, hw), :]) + mm(fb[...], w[pl.ds(other0, hw), :])
            if j == 1:
                y = y + tab[12:13]
            out[...] = jnp.where(live, y, 0.0).astype(bf16)

    dims = full_shape(weight)
    return call(
        kernel, s, (half, twin, *weight, table), (steps,),
        [tile(rows, hw)] * 2 + weight_specs(weight) + [const(table.shape)],
        [const(dims), tile(rows, width), tile(rows, width)],
        [shape(dims), shape((steps * rows, width)), shape((steps * rows, width))],
        cost=4 * count * width * width,
    )


def middle(s, h1, c2_keep, c2_give, cot_own, cot_in, w_out, ff_own, ff_far, table, fc1_shift, rows=256):
    t, width = h1.shape
    units = fc1_shift.shape[1] // width
    hw = width // 2
    pieces, piece = ff_own[0].shape[:2]

    def kernel(s_ref, h1_ref, ck_ref, cg_ref, co, ci, o1, o2, o3, own1, own2, far, tab, shift, wo, out, a_ref, g_ref, dm_ref, du_ref, d2_ref, dh_ref, dk_ref, dg_ref, vec, w1, w2, sems):
        def moves():
            for k, (dst, own) in enumerate(((w1, own1), (w2, own2))):
                yield pltpu.make_async_copy(own, dst.at[pl.ds(s_ref[1] * pieces, pieces)], sems.at[2 * k])
                yield pltpu.make_async_copy(far.at[:, k], dst.at[pl.ds((1 - s_ref[1]) * pieces, pieces)], sems.at[2 * k + 1])

        @pl.when(pl.program_id(0) == 0)
        def _():
            for move in moves():
                move.start()
            fill(wo, s_ref, o1, o2, o3)
            vec[...] = jnp.zeros(vec.shape, f32)
            for move in moves():
                move.wait()

        def up(h, j):
            at, many = (h * units + j) * (hw // piece), hw // piece
            return w1[at : at + many].reshape(hw, width)

        def down(j):
            many = width // piece
            return w2[j * many : (j + 1) * many].reshape(width, width)

        c = s_ref[0]
        h2 = h1_ref[...] + mm(ck_ref[...], wo[at_core(c, hw), :]) + mm(cg_ref[...], wo[at_core(1 - c, hw), :]) + tab[13:14]
        n2, inv2 = norm_stats(h2)
        a = (n2 * tab[2:3] + tab[6:7]).astype(bf16)
        a_ref[...] = a
        acc = h2 + tab[14:15]
        slopes = []

        def climb(j):
            return mm(a[:, :hw], up(0, j)) + mm(a[:, hw:], up(1, j)) + shift[:, j * width : (j + 1) * width]

        u = climb(0)
        for j in range(units):
            u_next = climb(j + 1) if j + 1 < units else None
            g, slope = gelu_parts(u.astype(bf16).astype(f32))
            slopes.append(slope)
            g = g.astype(bf16)
            g_ref[:, j * width : (j + 1) * width] = g
            acc = acc + mm(g, down(j))
            u = u_next
        n3, inv3 = norm_stats(acc)
        out[...] = (n3 * tab[3:4] + tab[7:8]).astype(bf16)

        def back(n, inv, gain, dy):
            dn = dy * gain
            return inv * (dn - jnp.mean(dn, axis=-1, keepdims=True) - n * jnp.mean(dn * n, axis=-1, keepdims=True))

        def total(x):
            return jnp.sum(x, axis=0, keepdims=True)

        dy = jnp.where(s_ref[2] == 1, co[...].astype(f32), ci[...].astype(f32))
        dh3 = back(n3, inv3, tab[3:4], dy)
        dm = dh3.astype(bf16)
        dm_ref[...] = dm
        halves = [None, None]
        dg = mm_t(dm, down(0))
        for j in range(units):
            cols = slice(j * width, (j + 1) * width)
            dg_next = mm_t(dm, down(j + 1)) if j + 1 < units else None
            du = (slopes[j] * dg).astype(bf16)
            dg = dg_next
            du_ref[:, cols] = du
            vec[0:1, cols] += total(du.astype(f32))
            for h in range(2):
                part = mm_t(du, up(h, j))
                halves[h] = part if halves[h] is None else halves[h] + part
        da = jnp.concatenate(halves, axis=1)
        dh2 = dh3 + back(n2, inv2, tab[2:3], da)
        d2 = dh2.astype(bf16)
        d2_ref[...] = d2
        dh_ref[...] = dh2
        dk_ref[...] = mm_t(d2, wo[at_core(c, hw), :]).astype(bf16)
        dg_ref[...] = mm_t(d2, wo[at_core(1 - c, hw), :]).astype(bf16)
        rows_of = [total(dm.astype(f32)), total(d2.astype(f32)), total(dy * n3), total(dy), total(da * n2), total(da)]
        for k, value in enumerate(rows_of):
            line, at = 1 + k // 3, (k % 3) * width
            vec[line : line + 1, at : at + width] += value

    dims = full_shape(w_out)
    ff = units * width
    line = tile(rows, width)
    wide, half = tile(rows, ff), tile(rows, hw)
    away = pl.BlockSpec(memory_space=pl.ANY)
    return call(
        kernel, s, (h1, c2_keep, c2_give, cot_own, cot_in, *arrays(w_out), *ff_own, ff_far, table, fc1_shift), (t // rows,),
        [line, half, half, line, line] + weight_specs(w_out) + [away] * 3 + [const(table.shape), const(fc1_shift.shape)],
        [const(dims), line, line, wide, line, wide, line, line, half, half, const((8, ff))],
        [shape(dims), shape((t, width)), shape((t, width)), shape((t, ff)), shape((t, width)), shape((t, ff)), shape((t, width)),
         shape((t, width), f32), shape((t, hw)), shape((t, hw)), shape((8, ff), f32)],
        [pltpu.VMEM((2 * pieces, piece, width), bf16)] * 2 + [pltpu.SemaphoreType.DMA((4,))],
        cost=8 * t * width * ff + 4 * t * width * width,
    )


def ff_grads(s, a, du, g, dm):
    t, width = a.shape
    hw = width // 2
    ff = du.shape[1]
    units = ff // width
    piece = hw * units // 16
    many = hw // piece

    def kernel(s_ref, a_ref, du_ref, g0, g1, dm_ref, out):
        @pl.when(pl.program_id(0) < units)
        def _():
            for h in range(2):
                out[h] = t_mm(a_ref[:, h * hw : (h + 1) * hw], du_ref[...]).astype(bf16).reshape(out.shape[1:])

        @pl.when(pl.program_id(0) >= units)
        def _():
            for h, ref in enumerate((g0, g1)):
                out[h] = t_mm(ref[...], dm_ref[...]).astype(bf16).reshape(out.shape[1:])

    return call(
        kernel, s, (a, du, g, g, dm), (2 * units,),
        [once((t, width)), pl.BlockSpec((t, width), lambda i, s: (0, jnp.minimum(i, units - 1))),
         pl.BlockSpec((t, hw), lambda i, s: (0, jnp.maximum(i - units, 0))),
         pl.BlockSpec((t, hw), lambda i, s: (0, units + jnp.maximum(i - units, 0))), once((t, width))],
        pl.BlockSpec((2, many, 1, piece, width), lambda i, s: (0, i % units, i // units, 0, 0)),
        shape((2, 16, 2, piece, width)),
        cost=4 * t * width * ff,
    )


def cross_back(s, dq_keep, dq_give, h1, dh2, w_q, w_out, table, rows=512):
    t, width = h1.shape
    hw = width // 2

    def kernel(s_ref, dk_ref, dg_ref, h_ref, dh2_ref, wq, wo, tab, dh_ref, d1_ref, keep, give, vec):
        @pl.when(pl.program_id(0) == 0)
        def _():
            vec[...] = jnp.zeros(vec.shape, f32)

        c = s_ref[0]
        da = mm_t(dk_ref[...], wq[:, at_core(c, hw)]) + mm_t(dg_ref[...], wq[:, at_core(1 - c, hw)])
        dres, dgain, dshift = norm_back(h_ref[...], tab[1:2], da)
        dh1 = dh2_ref[...] + dres
        dh_ref[...] = dh1
        d1 = dh1.astype(bf16)
        d1_ref[...] = d1
        keep[...] = mm_t(d1, wo[at_core(c, hw), :]).astype(bf16)
        give[...] = mm_t(d1, wo[at_core(1 - c, hw), :]).astype(bf16)
        vec[0:1] += dgain
        vec[1:2] += dshift
        vec[2:3] += jnp.sum(d1.astype(f32), axis=0, keepdims=True)
        vec[3:4, at_core(c, hw)] += jnp.sum(dk_ref[...].astype(f32), axis=0, keepdims=True)
        vec[3:4, at_core(1 - c, hw)] += jnp.sum(dg_ref[...].astype(f32), axis=0, keepdims=True)

    line, half = tile(rows, width), tile(rows, hw)
    return call(
        kernel, s, (dq_keep, dq_give, h1, dh2, w_q, w_out, table), (t // rows,),
        [half, half, line, line, once(w_q.shape), once(w_out.shape), const(table.shape)],
        [line, line, half, half, const((8, width))],
        [shape((t, width), f32), shape((t, width)), shape((t, hw)), shape((t, hw)), shape((8, width), f32)],
        cost=4 * t * width * width,
    )


def frame_back(s, keep, recv, half, twin, weight, rows=512):
    count, hw = half.shape
    width = 2 * hw
    steps = -(-count // rows)

    def kernel(s_ref, ka, kb, fa, fb, w, fkeep, fgive, xkeep, xgive, vec, acc):
        @pl.when(pl.program_id(0) == 0)
        def _():
            vec[...] = jnp.zeros(vec.shape, f32)
            acc[...] = jnp.zeros(acc.shape, f32)

        c, h = s_ref[0], s_ref[1]
        live = lax.broadcasted_iota(jnp.int32, (rows, 1), 0) + pl.program_id(0) * rows < count
        zero = jnp.zeros((rows, hw), bf16)
        f_mine = jnp.where(live, fa[...], zero)
        f_other = jnp.where(live, fb[...], zero)
        back = None
        for j in range(2):
            d = (ka[j].astype(f32) + kb[j].astype(f32)).astype(bf16)
            part = mm_t(d, w[j * width : (j + 1) * width, at_core(c, hw)])
            back = part if back is None else back + part
            acc[j, at_core(c, hw), :] += t_mm(f_mine, d)
            acc[j, at_core(1 - c, hw), :] += t_mm(f_other, d)
            if j == 1:
                vec[0:1] += jnp.sum(d.astype(f32), axis=0, keepdims=True)
        low, high = back[:, :hw].astype(bf16), back[:, hw:].astype(bf16)
        fkeep[...] = jnp.where(c == 0, low, high)
        fgive[...] = jnp.where(c == 0, high, low)

        @pl.when(pl.program_id(0) == steps - 1)
        def _():
            xkeep[...] = acc[h].astype(bf16)
            xgive[...] = acc[1 - h].astype(bf16)

    pair = pl.BlockSpec((2, rows, hw), lambda i, s: (0, i, 0))
    strip = tile(rows, hw)
    return call(
        kernel, s, (keep, recv, half, twin, weight), (steps,),
        [pair, pair, strip, strip, once(weight.shape)],
        [strip, strip, const((width, hw)), const((width, hw)), const((8, hw))],
        [shape((count, hw)), shape((count, hw)), shape((width, hw)), shape((width, hw)), shape((8, hw), f32)],
        [pltpu.VMEM((2, width, hw), f32)],
        cost=8 * count * width * width,
    )


def give_grads(s, c2_keep, c2_give, d2, a2, dq_give):
    t, width = d2.shape
    hw = width // 2

    def kernel(s_ref, k_ref, g_ref, d_ref, a_ref, q_ref, out):
        c = s_ref[0]
        out[0, at_core(c, hw), :] = t_mm(k_ref[...], d_ref[...]).astype(bf16)
        out[0, at_core(1 - c, hw), :] = t_mm(g_ref[...], d_ref[...]).astype(bf16)
        out[1] = t_mm(a_ref[...], q_ref[...]).astype(bf16)

    half = const((t, hw))
    return call(
        kernel, s, (c2_keep, c2_give, d2, a2, dq_give), (1,),
        [half, half, pl.BlockSpec((t, hw), lambda i, s: (0, 1 - s[0])), const((t, width)), half],
        const((2, width, hw)), shape((2, width, hw)), cost=4 * t * width * hw,
    )


def give_grad_out(s, ctx, ctx_in, d1):
    t, width = d1.shape
    hw = width // 2
    n = len(ctx)

    def kernel(s_ref, *refs):
        d_ref, out = refs[2 * n :]
        c = s_ref[0]
        out[at_core(c, hw), :] = t_mm(beside(refs[:n]), d_ref[...]).astype(bf16)
        out[at_core(1 - c, hw), :] = t_mm(beside(refs[n : 2 * n]), d_ref[...]).astype(bf16)

    return call(
        kernel, s, (*ctx, *ctx_in, d1), (1,),
        [pl.BlockSpec((t, part.shape[1]), lambda i, s: (s[0], 0)) for part in ctx] + [const(part.shape) for part in ctx_in]
        + [pl.BlockSpec((t, hw), lambda i, s: (0, 1 - s[0]))],
        const((width, hw)), shape((width, hw)), cost=2 * t * width * hw,
    )


def keep_grads(s, c2_keep, c2_give, d2, a2, dq_keep, pair_in, kv_keep, kv_give):
    t, width = d2.shape
    hw = width // 2

    def kernel(s_ref, ck, cg, d2_ref, a_ref, q_ref, p_ref, kk, kg, xgive, xkeep):
        c, h = s_ref[0], s_ref[1]
        for out, shard, kv in ((xgive, 1 - h, kg), (xkeep, h, kk)):
            rows = at_core(shard, hw)
            out[1] = (t_mm(a_ref[:, rows], q_ref[...]) + p_ref[1, rows, :].astype(f32)).astype(bf16)
            out[2] = kv[:hw]
            out[3] = kv[hw:]
        own_rows = t_mm(ck[...], d2_ref[...]) + p_ref[0, at_core(c, hw), :].astype(f32)
        far_rows = t_mm(cg[...], d2_ref[...]) + p_ref[0, at_core(1 - c, hw), :].astype(f32)
        xkeep[0] = jnp.where(c == h, own_rows, far_rows).astype(bf16)
        xgive[0] = jnp.where(c == h, far_rows, own_rows).astype(bf16)

    cols, half = pl.BlockSpec((t, hw), lambda i, s: (0, s[0])), const((t, hw))
    four = (4, hw, hw)
    return call(
        kernel, s, (c2_keep, c2_give, d2, a2, dq_keep, pair_in, kv_keep, kv_give), (1,),
        [half, half, cols, const((t, width)), half, const((2, width, hw)), const((width, hw)), const((width, hw))],
        [const(four), const(four)], [shape(four), shape(four)], cost=4 * t * width * hw,
    )


def keep_grad_out(s, ctx, ctx_in, d1, out_in):
    t, width = d1.shape
    hw = width // 2
    n = len(ctx)

    def kernel(s_ref, *refs):
        d1_ref, o_ref, xgive, xkeep = refs[2 * n :]
        c, h = s_ref[0], s_ref[1]
        own_rows = t_mm(beside(refs[:n]), d1_ref[...]) + o_ref[at_core(c, hw), :].astype(f32)
        far_rows = t_mm(beside(refs[n : 2 * n]), d1_ref[...]) + o_ref[at_core(1 - c, hw), :].astype(f32)
        xkeep[0] = jnp.where(c == h, own_rows, far_rows).astype(bf16)
        xgive[0] = jnp.where(c == h, far_rows, own_rows).astype(bf16)

    one = (1, hw, hw)
    return call(
        kernel, s, (*ctx, *ctx_in, d1, out_in), (1,),
        [pl.BlockSpec((t, part.shape[1]), lambda i, s: (s[0], 0)) for part in ctx] + [const(part.shape) for part in ctx_in]
        + [pl.BlockSpec((t, hw), lambda i, s: (0, s[0])), const((width, hw))],
        [const(one), const(one)], [shape(one), shape(one)], cost=2 * t * width * hw,
    )


def split_y(s, keeps, gots):
    _, rows, cols = keeps[0].shape
    half, n = rows // 2, len(keeps)
    counts = [k.shape[0] for k in keeps]

    def kernel(s_ref, *refs):
        give, mine = refs[2 * n :]
        for out, y in ((give, 1 - s_ref[4]), (mine, s_ref[4])):
            rows_at = pl.ds(pl.multiple_of(y * half, 64), half)
            at = 0
            for k_ref, g_ref, count in zip(refs[:n], refs[n : 2 * n], counts):
                out[at : at + count] = (k_ref[:, rows_at, :].astype(f32) + g_ref[:, rows_at, :].astype(f32)).astype(bf16)
                at += count

    dims = (sum(counts), half, cols)
    return call(kernel, s, (*keeps, *gots), (1,), [const(k.shape) for k in (*keeps, *gots)], [const(dims)] * 2, [shape(dims)] * 2)


def split_z(s, keep, got):
    b, rows, cols = keep.shape
    part = rows // 4

    def kernel(s_ref, k_ref, g_ref, *outs):
        for d, out in enumerate(outs):
            at = pl.ds(pl.multiple_of(s_ref[5 + d] * part, 16), part)
            out[...] = (k_ref[:, at, :].astype(f32) + g_ref[:, at, :].astype(f32)).astype(bf16)

    dims = (b, part, cols)
    return call(kernel, s, (keep, got), (1,), [const(keep.shape)] * 2, [const(dims)] * 4, [shape(dims)] * 4)


def sum_four(s, parts, vectors=()):
    b, part, cols = parts[0].shape

    def kernel(s_ref, p0, p1, p2, p3, *refs):
        out = refs[-1]
        total = (p0[...].astype(f32) + p1[...].astype(f32)) + (p2[...].astype(f32) + p3[...].astype(f32))
        out[0:b] = total.astype(bf16)
        if vectors:
            v = refs[0][...] + refs[1][...]
            high = v.astype(bf16).astype(f32)
            out[b] = jnp.concatenate([high, v - high], axis=0).astype(bf16)

    dims = (b + (1 if vectors else 0), part, cols)
    return call(
        kernel, s, (*parts, *vectors), (1,), [const(parts[0].shape)] * 4 + [const(v.shape) for v in vectors], const(dims), shape(dims)
    )


def pack_vectors(s, last, cross, mid, kv):
    width = last.shape[1]
    hw = width // 2
    units = mid.shape[1] // width

    def kernel(s_ref, l_ref, c_ref, m_ref, k_ref, give, mine):
        def line(ref, row, at=0):
            return ref[row : row + 1, at : at + width]

        zero = jnp.zeros((1, hw), f32)
        first = s_ref[0] == 0
        kv_row = jnp.concatenate([jnp.where(first, k_ref[0:1], zero), jnp.where(first, zero, k_ref[0:1])], axis=1)
        rows = [
            line(l_ref, 0), line(c_ref, 0), line(m_ref, 2, width), line(m_ref, 1, 2 * width),
            line(l_ref, 1), line(c_ref, 1), line(m_ref, 2, 2 * width), line(m_ref, 2),
            line(l_ref, 2), line(l_ref, 3), line(c_ref, 2), line(c_ref, 3), kv_row, line(m_ref, 1, width), line(m_ref, 1),
        ]
        halves = []
        for h in range(2):
            own = [row[:, h * hw : (h + 1) * hw] for row in rows]
            own += [m_ref[0:1, (h * units + j) * hw : (h * units + j + 1) * hw] for j in range(units)]
            halves.append(jnp.concatenate(own + [zero] * (24 - len(own)), axis=0))
        give[...] = jnp.where(s_ref[1] == 0, halves[1], halves[0])
        mine[...] = jnp.where(s_ref[1] == 0, halves[0], halves[1])

    return call(
        kernel, s, (last, cross, mid, kv), (1,), [const(x.shape) for x in (last, cross, mid, kv)],
        [const((24, hw))] * 2, [shape((24, hw), f32)] * 2,
    )


def join_z(s, parts):
    b, part, cols = parts[0].shape

    def kernel(s_ref, p0, p1, p2, p3, out):
        for d, ref in enumerate((p0, p1, p2, p3)):
            out[:, pl.ds(pl.multiple_of(s_ref[5 + d] * part, 16), part), :] = ref[...]

    dims = (b, 4 * part, cols)
    return call(kernel, s, parts, (1,), [const(parts[0].shape)] * 4, const(dims), shape(dims))


def spread_out(s, groups, outs, vectors=False):
    hw = 384

    def kernel(s_ref, *refs):
        results = refs[4 * len(groups) :]
        for n, (parts, spots) in enumerate(groups):
            b, half, cols = parts[0].shape
            for k, ref in enumerate(refs[4 * n : 4 * n + 4]):
                y = s_ref[4] if k % 2 == 0 else 1 - s_ref[4]
                core = s_ref[0] if k < 2 else 1 - s_ref[0]
                for block, (which, row, col) in enumerate(spots):
                    at_row = pl.multiple_of(row + y * half, 64)
                    at_col = pl.multiple_of(col + core * hw, 128)
                    results[which][pl.ds(at_row, half), pl.ds(at_col, cols)] = ref[block].astype(f32)
        if vectors:
            total = None
            for ref in refs[:4]:
                rows = ref[ref.shape[0] - 1].astype(f32)
                for z in range(4):
                    part = rows[48 * z : 48 * z + 48]
                    total = part if total is None else total + part
            total, at = total[0:24] + total[24:48], 0
            for ref in results[1:]:
                ref[...] = total[at : at + ref.shape[0]]
                at += ref.shape[0]

    parts = [part for group, _ in groups for part in group]
    return call(kernel, s, parts, (1,), [const(part.shape) for part in parts], [const(d) for d in outs], [shape(d, f32) for d in outs])


def spread_gathered(s, got, spots, outs):
    _, _, part, hw = got.shape

    def kernel(s_ref, g_ref, *results):
        for r in range(got.shape[0]):
            z, y, core = r // 4, r // 2 % 2, r % 2
            for block, (which, row, col) in enumerate(spots):
                at_row, at_col = row + (y * 4 + z) * part, col + core * hw
                results[which][at_row : at_row + part, at_col : at_col + hw] = g_ref[r, block].astype(f32)

    return call(kernel, s, (got,), (1,), [const(got.shape)], [const(d) for d in outs], [shape(d, f32) for d in outs])


def spread_ff(s, got):
    reps, _, per, width = got.shape
    units = 4
    rows = reps // units * per

    def kernel(s_ref, g_ref, one, two):
        one[...] = g_ref[:, 0].reshape(rows, width).astype(f32)
        two[...] = g_ref[:, 1].reshape(rows, width).astype(f32)

    return call(
        kernel, s, (got,), (units,), [pl.BlockSpec((reps // units, 2, per, width), lambda i, s: (i, 0, 0, 0))],
        [pl.BlockSpec((rows, width), lambda i, s: (0, i)), pl.BlockSpec((rows, width), lambda i, s: (i, 0))],
        [shape((rows, units * width), f32), shape((units * rows, width), f32)],
    )


def qkv_grad(s, a_own, a_sib, keep, give, mine):
    t, width = a_own.shape
    hw = width // 2
    n = len(keep)

    def kernel(s_ref, ao, ai, *refs):
        k, g = (jnp.concatenate([ref[0] for ref in part], axis=1) for part in (refs[:n], refs[n : 2 * n]))
        refs[-1][0] = (t_mm(ao[...], k) + t_mm(ai[...], g)).astype(bf16)

    cols = pl.BlockSpec((t, hw), lambda i, s: (0, s[1] if mine else 1 - s[1]))
    return call(
        kernel, s, (a_own, a_sib, *keep, *give), (3,),
        [cols, cols] + [pl.BlockSpec((1, t, part.shape[2]), lambda i, s: (i, 0, 0)) for part in (*keep, *give)],
        pl.BlockSpec((1, hw, hw), lambda i, s: (i, 0, 0)), shape((3, hw, hw)), cost=6 * t * width * hw,
    )


def last_rows(s, keep, recv, x_own, x_in, dh1, weight, table, rows=512):
    t, width = x_own.shape
    hw = width // 2
    n = len(keep)

    def kernel(s_ref, *refs):
        xo, xi, dh, w, tab, out, vec = refs[2 * n :]

        @pl.when(pl.program_id(0) == 0)
        def _():
            vec[...] = jnp.zeros(vec.shape, f32)

        c = s_ref[0]
        da = None
        for j in range(3):
            for parts, core in ((refs[:n], c), (refs[n : 2 * n], 1 - c)):
                d = jnp.concatenate([part[j] for part in parts], axis=1)
                at = pl.multiple_of(j * width + core * hw, 128)
                part = mm_t(d, w[:, pl.ds(at, hw)])
                da = part if da is None else da + part
                if j != 1:
                    line = 2 + j // 2
                    vec[line : line + 1, at_core(core, hw)] += jnp.sum(d.astype(f32), axis=0, keepdims=True)
        x = jnp.where(s_ref[2] == 1, xo[...].astype(f32), xi[...].astype(f32))
        dres, dgain, dshift = norm_back(x, tab[0:1], da)
        out[...] = (dh[...] + dres).astype(bf16)
        vec[0:1] += dgain
        vec[1:2] += dshift

    line = tile(rows, width)
    return call(
        kernel, s, (*keep, *recv, x_own, x_in, dh1, weight, table), (t // rows,),
        [pl.BlockSpec((3, rows, part.shape[2]), lambda i, s: (0, i, 0)) for part in (*keep, *recv)]
        + [line, line, line, once(weight.shape), const(table.shape)],
        [line, const((8, width))], [shape((t, width)), shape((8, width), f32)],
        cost=6 * t * width * width,
    )


EVERY = ("z", "y", "core", "x")
SPREAD2 = ("x", "z", "y", "core")
REP2 = ("z", "y", "core")
SWAP = [(1, 2), (2, 1)]


def tie(*values):
    return lax.optimization_barrier(values)


def across_z(x, d):
    return lax.ppermute(x, "z", [(j, j ^ d) for j in range(4)])


def across(x, axis):
    return lax.ppermute(x, axis, FLIP)


def body_pair(hidden, frames, segment, cotangent, norm_gain, norm_bias, self_qkv, self_out, cross_q, cross_kv, cross_out, fc1, fc2, proj_bias, fc1_bias):
    c, h = lax.axis_index("core"), lax.axis_index("x")
    y_at, z_at = lax.axis_index("y"), lax.axis_index("z")
    stay = c == h
    s = jnp.stack([c, h, stay.astype(jnp.int32), jnp.int32(0), y_at, z_at, z_at ^ 1, z_at ^ 2, z_at ^ 3]).astype(jnp.int32)
    rep_at = lax.axis_index(REP2)
    reps = lax.axis_size(REP2)
    width = self_out.shape[1]
    hw = width // 2
    ff = fc1.shape[1]
    units = ff // width
    pairs = hw // 128

    def swap(x):
        return lax.ppermute(x, ("core", "x"), SWAP)

    def sibling(x):
        return across(x, "core")

    def near(own):
        half = own.shape[0] // 2
        return across(lax.dynamic_slice_in_dim(own, c * half, half).astype(bf16), "x")

    x_own = hidden[0]
    small = jnp.concatenate([norm_gain, norm_bias, proj_bias, fc1_bias.reshape(units, hw), jnp.zeros((1, hw), f32)]).astype(bf16)
    small_in = across(small, "x")
    qkv_near = near(self_qkv)
    x_in = swap(x_own)
    seg = jnp.where(stay, segment, swap(segment))[0]
    per = hw * units // reps
    small = jnp.where(h == 0, jnp.stack([small, small_in]), jnp.stack([small_in, small])).astype(f32)
    table = jnp.concatenate([small[0, :16], small[1, :16]], axis=1)
    fc1_shift = small[:, 15:19].reshape(1, ff)
    kmark, qmark = seg_marks(seg)
    own1 = jnp.concatenate([fc1[:, j * width : (j + 1) * width] for j in range(units)]).astype(bf16).reshape(reps, per, width)
    own2 = fc2.astype(bf16).reshape(reps, per, width)
    slot = jnp.stack([lax.dynamic_index_in_dim(own1, rep_at, keepdims=False), lax.dynamic_index_in_dim(own2, rep_at, keepdims=False)])
    part = hw // 2
    squares = jnp.stack([lax.dynamic_slice_in_dim(w, c * part, part) for w in (self_out, cross_q, cross_out)]).astype(bf16)
    kv_part = lax.dynamic_slice_in_dim(cross_kv, c * hw, hw).astype(bf16)
    x_in, kmark, qmark, squares, kv_part, frames, own1, own2, slot = tie(x_in, kmark, qmark, squares, kv_part, frames, own1, own2, slot)
    slot = across(slot, "x")
    squares_near = across(squares, "x")
    f_own = frames[0]
    f_in = swap(f_own)
    kv_near = across(kv_part, "x")
    w_qkv, a1, keep, give = norm_qkv(s, x_own, x_in, (self_qkv, qkv_near, sibling(qkv_near)), table)
    give, slot = tie(give, slot)
    recv = sibling(give)
    ff_far = lax.all_gather(slot, REP2, axis=0, tiled=False)

    many = pairs - 1
    ctx_a, give_a, lse_a = self_fwd(0, many, c, keep, recv, kmark, qmark)
    give_a, keep, recv, squares_near, cotangent = tie(give_a, keep, recv, squares_near, cotangent)
    cot_in = swap(cotangent[0])
    squares_sib = sibling(squares_near)
    w_out, w_q, w_co = (
        (w, (squares_near, k), (squares_sib, k)) for k, w in enumerate((self_out, cross_q, cross_out))
    )
    in_a = sibling(give_a)
    ctx_b, give_b, lse_b = self_fwd(many, 1, c, keep, recv, kmark, qmark)
    in_b = sibling(give_b)
    ctx, ctx_in = (ctx_a, ctx_b), (in_a, in_b)
    w_out, w_q, h1, a2, qc = self_project(s, ctx, ctx_in, x_own, x_in, w_out, w_q, table)
    qc, f_in, kv_near = tie(qc, f_in, kv_near)
    half = jnp.where(stay, f_own, f_in)
    twin = sibling(half)
    w_kv, kc, vc = frame_kv(s, half, twin, (cross_kv, kv_near, sibling(kv_near)), table)
    count = half.shape[0]
    own_pairs, far_pairs = c * pairs, (1 - c) * pairs
    c2_give, cross_lse_give = cross_fwd(far_pairs, pairs, qc, kc, vc, count)
    c2_keep, cross_lse_keep = cross_fwd(own_pairs, pairs, qc, kc, vc, count)
    _, out, a3, g, dm, du, d2, dh2, dc2_keep, dc2_give, vec_mid = middle(
        s, h1, c2_keep, c2_give, cotangent[0], cot_in, w_co, (own1, own2), ff_far, table, fc1_shift,
    )

    packed = ff_grads(s, a3, du, g, dm)
    dc2_give, packed, out, a1_out = tie(dc2_give, packed, out, a1)
    ff_mine = lax.psum_scatter(packed.reshape(2 * reps, 2 * per, width), SPREAD2, scatter_dimension=0, tiled=False)
    out_in = swap(out)
    a1_sib = sibling(a1_out)
    dq_give, dkv_give = cross_bwd(far_pairs, pairs, qc, kc, vc, c2_give, dc2_give, cross_lse_give, count)
    dkv_give, dq_give = tie(dkv_give, dq_give)
    dkv_in = sibling(dkv_give)
    pair_give = give_grads(s, c2_keep, c2_give, d2, a2, dq_give)
    pair_give, dc2_keep = tie(pair_give, dc2_keep)
    pair_in = sibling(pair_give)
    dq_keep, dkv_keep = cross_bwd(own_pairs, pairs, qc, kc, vc, c2_keep, dc2_keep, cross_lse_keep, count)
    dq_keep, out_in, dkv_in, a1_sib, pair_in = tie(dq_keep, out_in, dkv_in, a1_sib, pair_in)
    fkeep, fgive, kv_xkeep, kv_xgive, vec_kv = frame_back(s, dkv_keep, dkv_in, half, twin, w_kv)
    fgive, dq_keep = tie(fgive, dq_keep)
    fr_in = sibling(fgive)
    xgive, xkeep = keep_grads(s, c2_keep, c2_give, d2, a2, dq_keep, pair_in, kv_xkeep, kv_xgive)
    xgive, dq_keep = tie(xgive, dq_keep)
    got_x = across(xgive, "x")
    dh1, d1, dctx_keep, dctx_give, vec_cross = cross_back(s, dq_keep, dq_give, h1, dh2, w_q, w_out, table)
    dctx_give, d1 = tie(dctx_give, d1)
    dctx_in = sibling(dctx_give)
    so_give = give_grad_out(s, ctx, ctx_in, d1)
    so_give, fr_in, fkeep = tie(so_give, fr_in, fkeep)
    so_in = sibling(so_give)
    fr_own = (fkeep.astype(f32) + fr_in.astype(f32)).astype(bf16)
    so_xgive, so_xkeep = keep_grad_out(s, ctx, ctx_in, d1, so_in)
    so_xgive, dctx_keep = tie(so_xgive, dctx_keep)
    so_x = across(so_xgive, "x")

    def send_z(pieces):
        return (pieces[0],) + tuple(across_z(pieces[d], d) for d in (1, 2, 3))

    def gather_z(piece):
        return (piece,) + tuple(across_z(piece, d) for d in (1, 2, 3))

    bg1, bk1 = self_bwd(0, 1, 0, c, keep, recv, ctx_a, dctx_keep, dctx_in, lse_a, kmark, qmark)
    bg1, bk1, keep = tie(bg1, bk1, keep)
    bi1 = sibling(bg1)
    bg2, bk2 = self_bwd(1, 1, 1, c, keep, recv, ctx_a, dctx_keep, dctx_in, lse_a, kmark, qmark)
    bg2, bk2, got_x, so_x, keep, bi1, fr_own = tie(bg2, bk2, got_x, so_x, keep, bi1, fr_own)
    fr_swapped = swap(fr_own)
    bi2 = sibling(bg2)
    m_ygive, m_ykeep = split_y(s, (xkeep, so_xkeep), (got_x, so_x))
    m_ygive, keep, ff_mine = tie(m_ygive, keep, ff_mine)
    m_y = across(m_ygive, "y")
    ff_got = lax.all_gather(ff_mine, REP2, axis=0, tiled=False)
    bg3, bk3 = self_bwd(2, 1, 0, c, keep, recv, ctx_b, dctx_keep, dctx_in, lse_b, kmark, qmark)
    bg3, bk3, bi2 = tie(bg3, bk3, bi2)
    bi3 = sibling(bg3)
    q_xgive = qkv_grad(s, a1, a1_sib, (bk1, bk2, bk3), (bg1, bg2, bg3), False)
    q_xgive, m_y, fr_swapped = tie(q_xgive, m_y, fr_swapped)
    q_x = across(q_xgive, "x")
    m_z = split_z(s, m_ykeep, m_y)
    bk3, dh1, *m_z = tie(bk3, dh1, *m_z)
    m_z = send_z(m_z)
    q_xkeep = qkv_grad(s, a1, a1_sib, (bk1, bk2, bk3), (bg1, bg2, bg3), True)
    grad_hidden, vec_last = last_rows(s, (bk1, bk2, bk3), (bi1, bi2, bi3), x_own, x_in, dh1, w_qkv, table)
    v_give, v_mine = pack_vectors(s, vec_last, vec_cross, vec_mid, vec_kv)
    v_got = across(v_give, "x")
    v_mine, q_x = tie(v_mine, q_x)
    q_ygive, q_ykeep = split_y(s, (q_xkeep,), (q_x,))
    q_ygive, grad_hidden = tie(q_ygive, grad_hidden)
    q_y = across(q_ygive, "y")
    hid_in = swap(grad_hidden)
    q_four = split_z(s, q_ykeep, q_y)
    q_first, *m_z = tie(q_four[0], *m_z)
    q_four = (q_first, *q_four[1:])
    m_piece = sum_four(s, m_z)
    m_got = lax.all_gather(m_piece, REP2, axis=0, tiled=False)
    q_z = send_z(q_four)
    fc1_grad, fc2_grad = spread_ff(s, ff_got.reshape(reps, 2, per, width))
    output = jnp.where(stay, out, out_in)
    fc1_grad, fc2_grad, output, *q_z = tie(fc1_grad, fc2_grad, output, *q_z)
    q_piece = sum_four(s, q_z, (v_mine, v_got))
    q_all = gather_z(q_piece)
    spots = ((0, 0, 0), (1, 0, 0), (3, 0, 0), (3, hw, 0), (2, 0, 0))
    crossout_grad, crossq_grad, selfout_grad, kv_grad = spread_gathered(s, m_got, spots, ((hw, width),) * 3 + ((width, width),))
    grad_frames = jnp.where(stay, fr_own, fr_swapped)
    grad_frames, *q_all = tie(grad_frames, *q_all)
    q_own = join_z(s, q_all)
    q_far = across(q_own, "y")
    q_own_sib = sibling(q_own)
    grad_hidden = jnp.where(stay, grad_hidden, hid_in)
    q_far, crossout_grad, grad_hidden = tie(q_far, crossout_grad, grad_hidden)
    first = tuple((0, 0, j * width) for j in range(3))
    qkv_grad_out, gain_grad, shift_grad, bias_grad, fc1b_grad = spread_out(s, (((q_own, q_far, q_own_sib, sibling(q_far)), first),), ((hw, 3 * width), (4, hw), (4, hw), (7, hw), (units, hw)), True)

    return (
        output[None], grad_hidden[None], grad_frames[None], gain_grad, shift_grad,
        qkv_grad_out, selfout_grad, crossq_grad, kv_grad, crossout_grad, fc1_grad, fc2_grad, bias_grad, fc1b_grad.reshape(-1),
    )


GROUP = ("core", "ilo")
SHARD = ("ihi", "ilo")
REP = ("rz", "core")
SPREAD = ("ihi", "ilo", "rz", "core")


def body_general(hidden, frames, segment, cotangent, norm_gain, norm_bias, self_qkv, self_out, cross_q, cross_kv, cross_out, fc1, fc2, proj_bias, fc1_bias):
    c = lax.axis_index("core")
    hi = lax.axis_index("ihi")
    n = lax.axis_size("core") * lax.axis_size("ilo")
    reps = lax.axis_size("rz") * lax.axis_size("core")
    rep_at = lax.axis_index(REP)
    width = self_out.shape[1]
    ff = fc1.shape[1]

    def swap(x):
        return lax.ppermute(x, ("core", "ihi"), [(0, 0), (1, 2), (2, 1), (3, 3)])

    def whole(own):
        if n != 2:
            return lax.all_gather(own, SHARD, axis=0, tiled=True)
        half = own.shape[0] // 2
        mine = lax.ppermute(lax.dynamic_slice_in_dim(own, c * half, half), "ihi", FLIP)
        sib = lax.ppermute(mine, "core", FLIP)
        other = jnp.where(c == 0, jnp.concatenate([mine, sib]), jnp.concatenate([sib, mine]))
        return jnp.where(hi == 0, jnp.concatenate([own, other]), jnp.concatenate([other, own]))

    def slices(own):
        rows = own.shape[0] // reps
        return lax.dynamic_slice_in_dim(own, rep_at * rows, rows)

    rows_in = swap(hidden[0])
    qkv_w = whole(self_qkv.astype(bf16))
    small = jnp.concatenate([norm_gain.astype(bf16), norm_bias.astype(bf16), proj_bias.astype(bf16), fc1_bias.astype(bf16).reshape(-1, norm_gain.shape[1]), jnp.zeros((1, norm_gain.shape[1]), bf16)])
    small = lax.all_gather(small, SHARD, axis=1, tiled=False).astype(f32)
    table = small[:15].reshape(15, width)
    gains, shifts, biases = table[:4], table[4:8], table[8:15]
    fc1_shift = small[15:19].transpose(1, 0, 2).reshape(ff)
    seg = swap(segment)[0]
    frames_half = swap(frames[0])
    if n == 2:
        twin = lax.ppermute(frames_half, "core", FLIP)
        frame_rows = jnp.concatenate([jnp.where(c == 0, frames_half, twin), jnp.where(c == 0, twin, frames_half)], axis=1)
    else:
        frame_rows = lax.all_gather(frames_half, GROUP, axis=1, tiled=True)
    selfout_w = whole(self_out.astype(bf16))
    crossq_w = whole(cross_q.astype(bf16))
    kv_w = whole(cross_kv.astype(bf16)) if n == 2 else None
    if n == 2:
        k_w, v_w = kv_w[:width], kv_w[width:]
    else:
        kv_w = lax.all_gather(cross_kv.astype(bf16), SHARD, axis=1, tiled=True)
        k_w, v_w = kv_w[:, :width], kv_w[:, width:]
    crossout_w = whole(cross_out.astype(bf16))
    cot = swap(cotangent[0])
    units = ff // width
    part1 = slices(fc1.astype(bf16))
    part2 = slices(fc2.astype(bf16))
    few = part1.shape[0]
    parts = jnp.concatenate([part1[:, j * width : (j + 1) * width] for j in range(units)] + [part2])
    ffw = lax.all_gather(parts, SPREAD, axis=0, tiled=False)
    fc1_w = jnp.concatenate([ffw[:, j * few : (j + 1) * few].reshape(width, width) for j in range(units)], axis=1)
    fc2_w = ffw[:, units * few :].reshape(ff, width)

    own_rows = rows_in.shape[0]
    hw = -(-HEADS // n)
    padded = hw * n * HD - width

    lanes = hw * HD

    def to_heads(x):
        x = x.reshape(own_rows, -1, width)
        if padded:
            x = jnp.pad(x, ((0, 0), (0, 0), (0, padded)))
        x = x.reshape(own_rows, -1, n, lanes).transpose(1, 2, 0, 3)
        x = lax.all_to_all(x, GROUP, 1, 1, tiled=True)
        return x.reshape(-1, n * own_rows, lanes)

    def to_tokens(x):
        x = lax.all_to_all(x.reshape(-1, n, own_rows, lanes), GROUP, 1, 1, tiled=True)
        return x.transpose(2, 0, 1, 3).reshape(own_rows, -1, n * lanes)[:, :, :width].reshape(own_rows, -1)

    h0 = rows_in.astype(f32)
    a1 = norm(h0, gains[0], shifts[0]).astype(bf16)
    zeros_row = jnp.zeros((width,), f32)
    qkv = (mm(a1, qkv_w) + jnp.concatenate([biases[0], zeros_row, biases[1]])).astype(bf16)
    heads = to_heads(qkv)
    kmark, qmark = seg_marks(seg)
    mid = heads.shape[1] // 2
    first = jnp.int32(0)
    ctx, _, self_lse = self_fwd(0, lanes // 128, first, heads[:, :mid], heads[:, mid:], kmark, qmark)
    c1 = to_tokens(ctx)
    h1 = h0 + mm(c1, selfout_w) + biases[2]
    a2 = norm(h1, gains[1], shifts[1]).astype(bf16)
    qc = (mm(a2, crossq_w) + biases[3]).astype(bf16)
    count = frame_rows.shape[0]
    pad = -count % 256
    frame_pad = jnp.pad(frame_rows, ((0, pad), (0, 0)))
    kc = mm(frame_pad, k_w).astype(bf16)
    live = lax.broadcasted_iota(jnp.int32, (count + pad, 1), 0) < count
    vc = (mm(frame_pad, v_w) + jnp.where(live, biases[4], 0.0)).astype(bf16)
    c2, cross_lse = cross_fwd(first, width // 128, qc, kc, vc, count)
    h2 = h1 + mm(c2, crossout_w) + biases[5]
    a3 = norm(h2, gains[2], shifts[2]).astype(bf16)
    u = (mm(a3, fc1_w) + fc1_shift).astype(bf16)
    uf = u.astype(f32)
    g, slope = gelu_parts(uf)
    g = g.astype(bf16)
    h3 = h2 + mm(g, fc2_w) + biases[6]
    output = norm(h3, gains[3], shifts[3]).astype(bf16)
    output = swap(output)

    def total(x):
        return jnp.sum(x.astype(f32), axis=0)

    dh3, gain3, shift3 = norm_back(h3, gains[3], cot.astype(f32))
    dm = dh3.astype(bf16)
    g_fc2 = t_mm(g, dm).astype(bf16)
    du = (slope * mm_t(dm, fc2_w)).astype(bf16)
    g_fc1 = t_mm(a3, du).astype(bf16)

    def reduce_rows(parts, extra=None):
        total = n * reps
        cut = [p.reshape(total, -1, width) for p in parts]
        if extra is not None:
            cut.append(extra)
        flat = jnp.concatenate(cut, axis=1)
        mine = lax.psum_scatter(flat, SPREAD, scatter_dimension=0, tiled=False)
        got = lax.all_gather(mine, REP, axis=0, tiled=False)
        out, at = [], 0
        for p in cut:
            out.append(got[:, at : at + p.shape[1]].reshape(-1, width).astype(f32))
            at += p.shape[1]
        return out

    ff_grads = reduce_rows([g_fc1[:, j * width : (j + 1) * width] for j in range(units)] + [g_fc2])
    fc1_grad = jnp.concatenate(ff_grads[:units], axis=1)
    fc2_grad = ff_grads[units]

    da3 = mm_t(du, fc1_w)
    dres, gain2, shift2 = norm_back(h2, gains[2], da3)
    dh2 = dh3 + dres
    d2 = dh2.astype(bf16)
    g_crossout = t_mm(c2, d2).astype(bf16)
    dc2 = mm_t(d2, crossout_w).astype(bf16)
    dqc, (dkc, dvc) = cross_bwd(first, width // 128, qc, kc, vc, c2, dc2, cross_lse, count)
    share = width // n

    def sum_columns(x):
        return lax.psum_scatter(x, GROUP, scatter_dimension=1, tiled=True)

    if n == 2:

        def sum_columns(x):
            give = lax.dynamic_slice_in_dim(x, (1 - c) * share, share, axis=1)
            keep = lax.dynamic_slice_in_dim(x, c * share, share, axis=1)
            return (keep.astype(f32) + lax.ppermute(give, "core", FLIP).astype(f32)).astype(bf16)

    dk_own = sum_columns(dkc)[:count]
    dv_own = sum_columns(dvc)[:count]
    place = lax.axis_index(GROUP) * share
    kw_own = lax.dynamic_slice_in_dim(k_w, place, share, axis=1)
    vw_own = lax.dynamic_slice_in_dim(v_w, place, share, axis=1)
    dframe = (mm_t(dk_own, kw_own) + mm_t(dv_own, vw_own)).astype(bf16)
    grad_frames = swap(sum_columns(dframe))
    g_k = t_mm(frame_rows, dk_own).astype(bf16)
    g_v = t_mm(frame_rows, dv_own).astype(bf16)
    vb_own = jnp.sum(dv_own.astype(f32), axis=0)

    g_crossq = t_mm(a2, dqc).astype(bf16)
    da2 = mm_t(dqc, crossq_w)
    dres, gain1, shift1 = norm_back(h1, gains[1], da2)
    dh1 = dh2 + dres
    d1 = dh1.astype(bf16)
    g_selfout = t_mm(c1, d1).astype(bf16)
    dctx = mm_t(d1, selfout_w).astype(bf16)
    dctx = to_heads(dctx)[0]
    late, early = self_bwd(0, lanes // 128, 0, first, heads[:, :mid], heads[:, mid:], ctx, dctx[:mid], dctx[mid:], self_lse, kmark, qmark)
    dqkv = to_tokens(jnp.concatenate([early, late], axis=1))
    da1 = mm_t(dqkv, qkv_w)
    g_qkv = t_mm(a1, dqkv).astype(bf16)
    sums = total(dqkv)
    dres, gain0, shift0 = norm_back(h0, gains[0], da1)
    grad_hidden = swap((dh1 + dres).astype(bf16))

    vb = lax.dynamic_update_slice(jnp.zeros((width,), f32), vb_own, (place,))
    vectors = jnp.stack([gain0[0], gain1[0], gain2[0], gain3[0], shift0[0], shift1[0], shift2[0], shift3[0], sums[:width], sums[2 * width :], total(d1), total(dqc), vb, total(d2), total(dm)])
    per = width // n
    vectors = vectors.reshape(15, n, per).transpose(1, 0, 2).reshape(n, 15 * per)
    vectors = jnp.concatenate([vectors, total(du).reshape(n, ff // n)], axis=1)
    long = vectors.shape[1]
    seats = -(-long // reps)
    vectors = jnp.pad(vectors, ((0, 0), (0, seats * reps - long))).reshape(n * reps, seats)
    lines = -(-seats // (8 * width)) * 8
    vectors = jnp.pad(vectors, ((0, 0), (0, lines * width - seats))).reshape(n * reps, lines, width)

    def own_columns(x):
        return lax.dynamic_update_slice(jnp.zeros((x.shape[0], width), x.dtype), x, (jnp.int32(0), place))

    cross = [g_crossq, g_crossout]
    if n == 2:
        cross.append(jnp.concatenate([own_columns(g_k), own_columns(g_v)]))
    cross = reduce_rows(cross)
    crossq_grad, crossout_grad = cross[:2]
    if n == 2:
        kv_grad = cross[2]
    else:
        kv_cols = jnp.concatenate([own_columns(g_k), own_columns(g_v)], axis=1)
        kv_cols = lax.psum_scatter(kv_cols, SHARD, scatter_dimension=1, tiled=True)
        kv_grad = lax.psum(kv_cols, REP).astype(f32)
    got = reduce_rows([g_qkv[:, j * width : (j + 1) * width] for j in range(3)] + [g_selfout], vectors.astype(bf16))
    qkv_grad = jnp.concatenate(got[:3], axis=1)
    selfout_grad = got[3]
    vec = got[4].reshape(reps, lines * width)[:, :seats].reshape(-1)[:long]
    table = vec[: 15 * per].reshape(15, per)
    fc1b_grad = vec[15 * per :]
    return (
        output[None], grad_hidden[None], grad_frames[None],
        table[:4], table[4:8], qkv_grad, selfout_grad, crossq_grad, kv_grad, crossout_grad, fc1_grad, fc2_grad, table[8:15], fc1b_grad,
    )


def solution(mesh):
    reps, n = mesh.devices.shape
    paired = (reps, n) == (16, 2)
    if paired:
        work = Mesh(mesh.devices.reshape(4, 2, 2, 2), EVERY)
        rep, inner = REP2, ("x",)
    else:
        work = Mesh(mesh.devices.reshape(reps // 2, 2, 2, n // 2), ("rz", "core", "ihi", "ilo"))
        rep, inner = REP, SHARD
    rows, cols = P(inner, None), P(None, inner)
    tokens, features = P(rep, inner, None), P(rep, None, inner)
    weights = (cols, cols, rows, rows, rows, cols, rows, rows, rows, cols, P(inner))
    return jax.shard_map(
        body_pair if paired else body_general,
        mesh=work,
        in_specs=(tokens, features, P(rep, None), tokens) + weights,
        out_specs=(tokens, tokens, features) + weights,
        check_vma=False,
    )
```

```python
import math

import jax
import jax.numpy as jnp
from jax import lax
from jax.experimental import pallas as pl
from jax.experimental.pallas import tpu as pltpu
from jax.sharding import Mesh
from jax.sharding import PartitionSpec as P

HEADS = 12
HD = 64
EPSILON = 1e-05
NEG = -1e30
PROMPT = 1024
REACH = 256
bf16 = jnp.bfloat16
f32 = jnp.float32
FLIP = [(0, 1), (1, 0)]


def mm(a, b):
    return jnp.dot(a, b, preferred_element_type=f32)


def mm_t(a, b):
    return lax.dot_general(a, b, (((1,), (1,)), ((), ())), preferred_element_type=f32)


def t_mm(a, b):
    return lax.dot_general(a, b, (((0,), (0,)), ((), ())), preferred_element_type=f32)


def call(kernel, scalars, args, grid, in_specs, out_specs, out_shape, scratch=(), cost=None):
    spec = pltpu.PrefetchScalarGridSpec(
        num_scalar_prefetch=1, grid=grid, in_specs=in_specs, out_specs=out_specs, scratch_shapes=list(scratch)
    )
    estimate = None
    if cost is not None:
        estimate = pl.CostEstimate(flops=cost // 10, bytes_accessed=1 << 20, transcendentals=0)
    return pl.pallas_call(
        kernel,
        grid_spec=spec,
        out_shape=out_shape,
        cost_estimate=estimate,
        compiler_params=pltpu.CompilerParams(vmem_limit_bytes=60 * 2**20),
    )(scalars, *args)


def shape(dims, kind=bf16):
    return jax.ShapeDtypeStruct(dims, kind)


def half_of(lane, h):
    return (lane < HD) if h == 0 else (lane >= HD)


def delta_of(do, o):
    x = do.astype(f32) * o.astype(f32)
    hi = x.astype(bf16)
    lo = (x - hi.astype(f32)).astype(bf16)
    r = lax.broadcasted_iota(jnp.int32, (8, 128), 0)
    lane = lax.broadcasted_iota(jnp.int32, (8, 128), 1)
    pick = jnp.where((lane // HD) == r, 1.0, 0.0).astype(bf16)
    return mm_t(pick, hi) + mm_t(pick, lo)


def cross_fwd(base, pairs, q, k, v, valid, block=1024):
    tq, tk = q.shape[0], k.shape[0]
    block = min(block, tq)

    def kernel(s_ref, q_ref, k_ref, v_ref, o_ref, l_ref, ks, vts):
        @pl.when(pl.program_id(1) == 0)
        def _():
            low = lax.broadcasted_iota(jnp.int32, (tk, 128), 1)
            row = lax.broadcasted_iota(jnp.int32, (tk, 128), 0)
            bias = jnp.where(row >= valid, NEG, 0.0).astype(bf16)
            one = jnp.ones((tk, 128), bf16)
            for h in range(2):
                ks[h] = jnp.where(half_of(low, h), k_ref[...], bias)
                vts[h] = jnp.where(half_of(low, h), v_ref[...], one).T

        lane = lax.broadcasted_iota(jnp.int32, (block, 128), 1)
        qq = q_ref[...] * bf16(0.125)
        scores = []
        for h in range(2):
            spare = lane == (HD if h == 0 else 0)
            qh = jnp.where(half_of(lane, h), qq, jnp.where(spare, 1.0, 0.0).astype(bf16))
            scores.append(mm_t(ks[h], qh))
        outs = []
        for h, s in enumerate(scores):
            m = jnp.max(s, axis=0, keepdims=True)
            o = mm(vts[h], jnp.exp(s - m).astype(bf16))
            total = o[HD : HD + 1] if h == 0 else o[0:1]
            outs.append(o * (1.0 / total))
            l_ref[0, h : h + 1, :] = m + jnp.log(total)
        sub = lax.broadcasted_iota(jnp.int32, (128, block), 0)
        o_ref[...] = jnp.where(sub < HD, outs[0], outs[1]).T.astype(bf16)

    qspec = pl.BlockSpec((block, 128), lambda p, i, s: (i, s[0] + p))
    kspec = pl.BlockSpec((tk, 128), lambda p, i, s: (0, s[0] + p))
    return call(
        kernel, jnp.reshape(base, (1,)).astype(jnp.int32), (q, k, v), (pairs, tq // block), [qspec, kspec, kspec],
        [pl.BlockSpec((block, 128), lambda p, i, s: (i, p)), pl.BlockSpec((1, 8, block), lambda p, i, s: (p, 0, i))],
        [shape((tq, pairs * 128)), shape((pairs, 8, tq), f32)],
        [pltpu.VMEM((2, tk, 128), bf16), pltpu.VMEM((2, 128, tk), bf16)],
        4 * tq * tk * 256 * pairs,
    )


def cross_bwd(base, pairs, q, k, v, o, do, lse, valid, block=1024):
    tq, tk = q.shape[0], k.shape[0]
    block = min(block, tq)
    steps = tq // block

    def kernel(s_ref, q_ref, k_ref, v_ref, o_ref, do_ref, l_ref, dq_ref, d_ref, ks, kts, dka, dva):
        @pl.when(pl.program_id(1) == 0)
        def _():
            low = lax.broadcasted_iota(jnp.int32, (tk, 128), 1)
            row = lax.broadcasted_iota(jnp.int32, (tk, 128), 0)
            bias = jnp.where(row >= valid, NEG, 0.0).astype(bf16)
            zero = jnp.zeros((tk, 128), bf16)
            for h in range(2):
                ks[h] = jnp.where(half_of(low, h), k_ref[...], bias)
                kts[h] = jnp.where(half_of(low, h), k_ref[...], zero).T
            dka[...] = jnp.zeros((tk, 128), f32)
            dva[...] = jnp.zeros((tk, 128), f32)

        lane = lax.broadcasted_iota(jnp.int32, (block, 128), 1)
        qq = q_ref[...] * bf16(0.125)
        dd = do_ref[...]
        delta = delta_of(dd, o_ref[...])
        zero = jnp.zeros((block, 128), bf16)
        dqt, dk, dv = None, dka[...], dva[...]

        def products(h):
            mine = half_of(lane, h)
            spare = lane == (HD if h == 0 else 0)
            qc = jnp.where(mine, qq, zero)
            dh = jnp.where(mine, dd, zero)
            return qc, dh, mm_t(ks[h], jnp.where(spare, jnp.ones((block, 128), bf16), qc)), mm_t(v_ref[...], dh)

        now = products(0)
        for h in range(2):
            qc, dh, scores, dp = now
            now = products(1) if h == 0 else None
            p = jnp.exp(scores - l_ref[0, h : h + 1, :])
            ds = (p * (dp - delta[h : h + 1])).astype(bf16)
            dv = dv + mm(p.astype(bf16), dh)
            dk = dk + mm(ds, qc)
            part = mm(kts[h], ds)
            dqt = part if dqt is None else dqt + part
        dka[...] = dk
        dva[...] = dv
        dq_ref[...] = (dqt * 0.125).T.astype(bf16)

        @pl.when(pl.program_id(1) == steps - 1)
        def _():
            d_ref[0] = dka[...].astype(bf16)
            d_ref[1] = dva[...].astype(bf16)

    mine = pl.BlockSpec((block, 128), lambda p, i, s: (i, p))
    qspec = pl.BlockSpec((block, 128), lambda p, i, s: (i, s[0] + p))
    kspec = pl.BlockSpec((tk, 128), lambda p, i, s: (0, s[0] + p))
    return call(
        kernel, jnp.reshape(base, (1,)).astype(jnp.int32), (q, k, v, o, do, lse), (pairs, steps),
        [qspec, kspec, kspec, mine, mine, pl.BlockSpec((1, 8, block), lambda p, i, s: (p, 0, i))],
        [mine, pl.BlockSpec((2, tk, 128), lambda p, i, s: (0, 0, p))],
        [shape((tq, pairs * 128)), shape((2, tk, pairs * 128))],
        [pltpu.VMEM((2, tk, 128), bf16), pltpu.VMEM((2, 128, tk), bf16), pltpu.VMEM((tk, 128), f32), pltpu.VMEM((tk, 128), f32)],
        2 * tq * tk * 10 * 256 * pairs,
    )


def spans(r0, block):
    if r0 < PROMPT:
        return ([(0, r0)] if r0 else []) + [(r0, r0 + block)]
    left = max(PROMPT, r0 - REACH)
    before = [(0, r0)] if left == PROMPT else [(0, PROMPT), (left, r0)]
    return before + [(r0, r0 + block)]


def seg_marks(seg):
    lane = lax.broadcasted_iota(jnp.int32, (seg.shape[0], 128), 1) % HD
    same = lane == seg[:, None]
    kmark = jnp.where(same, 1.0, 0.0).astype(bf16)
    qmark = jnp.where(same | (lane == 0) | (lane > 8), 0.0, NEG).astype(bf16)
    return kmark, qmark


def half_specs(rows, first=0):
    return [pl.BlockSpec((3, rows, 128), lambda p, s: (0, 0, first + p))] * 2


def self_fwd(first, pairs, place, keep, recv, kmark, qmark, block=512):
    rows, width = keep.shape[1], pairs * 128
    t = 2 * rows

    def kernel(s_ref, a_ref, b_ref, km_ref, qm_ref, o_ref, give_ref, l_ref, qf, ks, vts):
        mine0 = pl.multiple_of(s_ref[0] * rows, rows)
        other0 = pl.multiple_of((1 - s_ref[0]) * rows, rows)
        low = lax.broadcasted_iota(jnp.int32, (rows, 128), 1)
        one = jnp.ones((rows, 128), bf16)
        for ref, at in ((a_ref, mine0), (b_ref, other0)):
            spot = pl.ds(at, rows)
            qf[spot, :] = ref[0] * bf16(0.125)
            for h in range(2):
                ks[h, spot, :] = jnp.where(half_of(low, h), ref[1], km_ref[spot, :])
                vts[h, :, spot] = jnp.where(half_of(low, h), ref[2], one).T
        lane = lax.broadcasted_iota(jnp.int32, (block, 128), 1)
        hide = lax.broadcasted_iota(jnp.int32, (block, block), 0) > lax.broadcasted_iota(jnp.int32, (block, block), 1)
        tasks = [(r0, h) for r0 in range(0, t, block) for h in range(2)]

        def scores(task):
            r0, h = task
            spot = pl.ds(r0, block)
            qs = jnp.where(half_of(lane, h), qf[spot, :], qm_ref[spot, :])
            out = [mm_t(ks[h, pl.ds(a, b - a), :], qs) for a, b in spans(r0, block)]
            out[-1] = jnp.where(hide, NEG, out[-1])
            return out

        now, outs = scores(tasks[0]), [None, None]
        for i, (r0, h) in enumerate(tasks):
            later = scores(tasks[i + 1]) if i + 1 < len(tasks) else None
            m = None
            for s in now:
                top = jnp.max(s, axis=0, keepdims=True)
                m = top if m is None else jnp.maximum(m, top)
            o = None
            for s, (a, b) in zip(now, spans(r0, block)):
                part = mm(vts[h, :, pl.ds(a, b - a)], jnp.exp(s - m).astype(bf16))
                o = part if o is None else o + part
            total = o[HD : HD + 1] if h == 0 else o[0:1]
            l_ref[0, h : h + 1, pl.ds(r0, block)] = m + jnp.log(total)
            outs[h] = o * (1.0 / total)
            if h == 1:
                sub = lax.broadcasted_iota(jnp.int32, (128, block), 0)
                o_ref[pl.ds(r0, block), :] = jnp.where(sub < HD, outs[0], outs[1]).T.astype(bf16)
            now = later
        give_ref[...] = o_ref[pl.ds(other0, rows), :]

    whole = pl.BlockSpec((t, 128), lambda p, s: (0, 0))
    return call(
        kernel, jnp.reshape(place, (1,)).astype(jnp.int32), (keep, recv, kmark, qmark), (pairs,),
        half_specs(rows, first) + [whole, whole],
        [pl.BlockSpec((t, 128), lambda p, s: (0, p)), pl.BlockSpec((rows, 128), lambda p, s: (0, p)), pl.BlockSpec((1, 8, t), lambda p, s: (p, 0, 0))],
        [shape((t, width)), shape((rows, width)), shape((pairs, 8, t), f32)],
        [pltpu.VMEM((t, 128), bf16), pltpu.VMEM((2, t, 128), bf16), pltpu.VMEM((2, 128, t), bf16)],
        2 * t * t * 4 * width,
    )


def self_bwd(first, pairs, seat, place, keep, recv, o, dkeep, drecv, lse, kmark, qmark, block=256):
    rows, width = keep.shape[1], pairs * 128
    t = 2 * rows

    def kernel(s_ref, a_ref, b_ref, o_ref, da_ref, db_ref, l_ref, km_ref, qm_ref, give_ref, keep_ref, qf, df, vf, ks, kts, dqa, dka, dva):
        mine0 = pl.multiple_of(s_ref[0] * rows, rows)
        other0 = pl.multiple_of((1 - s_ref[0]) * rows, rows)
        low = lax.broadcasted_iota(jnp.int32, (rows, 128), 1)
        zero = jnp.zeros((rows, 128), bf16)
        for ref, dref, at in ((a_ref, da_ref, mine0), (b_ref, db_ref, other0)):
            spot = pl.ds(at, rows)
            qf[spot, :] = ref[0] * bf16(0.125)
            df[spot, :] = dref[...]
            vf[spot, :] = ref[2]
            for h in range(2):
                ks[h, spot, :] = jnp.where(half_of(low, h), ref[1], km_ref[spot, :])
                kts[h, :, spot] = jnp.where(half_of(low, h), ref[1], zero).T
        dka[...] = jnp.zeros((t, 128), f32)
        dva[...] = jnp.zeros((t, 128), f32)
        lane = lax.broadcasted_iota(jnp.int32, (block, 128), 1)
        hide = lax.broadcasted_iota(jnp.int32, (block, block), 0) > lax.broadcasted_iota(jnp.int32, (block, block), 1)
        none = jnp.zeros((block, 128), bf16)
        for r0 in range(0, t, block):
            spot = pl.ds(r0, block)
            dd = df[spot, :]
            delta = delta_of(dd, o_ref[spot, :])
            dqt = None
            tasks = []
            for h in range(2):
                mine = half_of(lane, h)
                qc = jnp.where(mine, qf[spot, :], none)
                qs = jnp.where(mine, qf[spot, :], qm_ref[spot, :])
                dh = jnp.where(mine, dd, none)
                tasks += [(h, qc, qs, dh, a, b) for a, b in spans(r0, block)]

            def products(task):
                h, qc, qs, dh, a, b = task
                s = mm_t(ks[h, pl.ds(a, b - a), :], qs)
                return jnp.where(hide, NEG, s) if a == r0 else s, mm_t(vf[pl.ds(a, b - a), :], dh)

            now = products(tasks[0])
            for i, (h, qc, qs, dh, a, b) in enumerate(tasks):
                later = products(tasks[i + 1]) if i + 1 < len(tasks) else None
                log_total = l_ref[0, h : h + 1, spot]
                keys = pl.ds(a, b - a)
                s, dp = now
                now = later
                p = jnp.exp(s - log_total)
                ds = (p * (dp - delta[h : h + 1])).astype(bf16)
                dva[keys, :] += mm(p.astype(bf16), dh)
                dka[keys, :] += mm(ds, qc)
                part = mm(kts[h, :, keys], ds)
                dqt = part if dqt is None else dqt + part
            dqa[spot, :] = (dqt * 0.125).T.astype(bf16)
        for out, at in ((give_ref, other0), (keep_ref, mine0)):
            spot = pl.ds(at, rows)
            out[0] = dqa[spot, :]
            out[1] = dka[spot, :].astype(bf16)
            out[2] = dva[spot, :].astype(bf16)

    whole = pl.BlockSpec((t, 128), lambda p, s: (0, 0))
    half = pl.BlockSpec((rows, 128), lambda p, s: (0, first + p))
    return call(
        kernel, jnp.reshape(place, (1,)).astype(jnp.int32), (keep, recv, o, dkeep, drecv, lse, kmark, qmark), (pairs,),
        half_specs(rows, first)
        + [pl.BlockSpec((t, 128), lambda p, s: (0, seat + p)), half, half, pl.BlockSpec((1, 8, t), lambda p, s: (seat + p, 0, 0)), whole, whole],
        half_specs(rows),
        [shape((3, rows, width))] * 2,
        [pltpu.VMEM((t, 128), bf16)] * 3 + [pltpu.VMEM((2, t, 128), bf16), pltpu.VMEM((2, 128, t), bf16), pltpu.VMEM((t, 128), bf16)]
        + [pltpu.VMEM((t, 128), f32)] * 2,
        2 * t * t * 8 * width,
    )


def norm_stats(rows):
    centered = rows - jnp.mean(rows, axis=-1, keepdims=True)
    inv = lax.rsqrt(jnp.mean(centered * centered, axis=-1, keepdims=True) + EPSILON)
    return centered * inv, inv


def norm(rows, gain, shift):
    return norm_stats(rows)[0] * gain + shift


def norm_back(rows, gain, dy):
    n, inv = norm_stats(rows)
    dn = dy * gain
    dh = inv * (dn - jnp.mean(dn, axis=-1, keepdims=True) - n * jnp.mean(dn * n, axis=-1, keepdims=True))
    return dh, jnp.sum(dy * n, axis=0, keepdims=True), jnp.sum(dy, axis=0, keepdims=True)


ERFC = (
    0.22567585470008253, 0.22566975083164525, 0.20784161289369674, 0.1685452087610459, 0.14142852065437478,
    -0.005612938524279035, 0.1691005263450779, -0.1829144800497475, 0.05026606972001335,
)


def gelu_parts(u):
    bell = jnp.exp(u * u * -0.5)
    t = 1.0 / (1.0 + jnp.abs(u) * (0.4 * math.sqrt(0.5)))
    poly = jnp.full_like(t, ERFC[-1])
    for value in ERFC[-2::-1]:
        poly = poly * t + value
    tail = bell * t * poly * 0.5
    cdf = jnp.where(u < 0.0, tail, 1.0 - tail)
    return u * cdf, cdf + u * bell * (1.0 / math.sqrt(2.0 * math.pi))


def const(dims):
    return pl.BlockSpec(dims, lambda i, s: (0,) * len(dims))


def once(dims):
    return pl.BlockSpec(dims, lambda i, s: (0,) * len(dims), pipeline_mode=pl.Buffered(1))


def tile(rows, width):
    return pl.BlockSpec((rows, width), lambda i, s: (i, 0))


def fill(full, s, own, mine, sib):
    rows = own.shape[0]
    c, h = s[0], s[1]
    full[pl.ds(pl.multiple_of(h * rows, 128), rows), :] = own[...].astype(bf16)
    start = (1 - h) * rows
    full[pl.ds(pl.multiple_of(start + c * (rows // 2), 64), rows // 2), :] = mine[...]
    full[pl.ds(pl.multiple_of(start + (1 - c) * (rows // 2), 64), rows // 2), :] = sib[...]


def picked(part):
    if not isinstance(part, tuple):
        return once(part.shape)
    stack, which = part
    return pl.BlockSpec((None, *stack.shape[1:]), lambda i, s: (which, 0, 0), pipeline_mode=pl.Buffered(1))


def weight_specs(weight):
    return [picked(part) for part in weight]


def arrays(weight):
    return [part[0] if isinstance(part, tuple) else part for part in weight]


def full_shape(weight):
    return (2 * weight[0].shape[0], weight[0].shape[1])


def at_core(c, width):
    return pl.ds(pl.multiple_of(c * width, 128), width)


def norm_qkv(s, x_own, x_in, weight, table, rows=512):
    t, width = x_own.shape
    hw = width // 2

    def kernel(s_ref, xo, xi, own, mine, sib, tab, w, a_ref, keep, give):
        @pl.when(pl.program_id(0) == 0)
        def _():
            fill(w, s_ref, own, mine, sib)

        x = jnp.where(s_ref[2] == 1, xo[...].astype(f32), xi[...].astype(f32))
        a = norm(x, tab[0:1], tab[4:5]).astype(bf16)
        a_ref[...] = a
        for j in range(3):
            y = mm(a, w[:, j * width : (j + 1) * width])
            if j != 1:
                y = y + tab[8 + j // 2 : 9 + j // 2]
            low, high = y[:, :hw].astype(bf16), y[:, hw:].astype(bf16)
            first = s_ref[0] == 0
            keep[j] = jnp.where(first, low, high)
            give[j] = jnp.where(first, high, low)

    third = pl.BlockSpec((3, rows, hw), lambda i, s: (0, i, 0))
    dims = full_shape(weight)
    return call(
        kernel, s, (x_own, x_in, *weight, table), (t // rows,),
        [tile(rows, width)] * 2 + weight_specs(weight) + [const(table.shape)],
        [const(dims), tile(rows, width), third, third],
        [shape(dims), shape((t, width)), shape((3, t, hw)), shape((3, t, hw))],
        cost=2 * t * width * 3 * width,
    )


def beside(refs):
    return jnp.concatenate([ref[...] for ref in refs], axis=1) if len(refs) > 1 else refs[0][...]


def self_project(s, ctx, ctx_in, x_own, x_in, w_out, w_q, table, rows=512):
    t, width = x_own.shape
    hw = width // 2
    steps = t // rows
    n = len(ctx)

    def kernel(s_ref, *refs):
        cks, cis = refs[:n], refs[n : 2 * n]
        xo, xi, o1, o2, o3, q1, q2, q3, tab, wo, wq, h_ref, a_ref, qc_ref = refs[2 * n :]

        @pl.when(pl.program_id(0) == 0)
        def _():
            fill(wo, s_ref, o1, o2, o3)
            fill(wq, s_ref, q1, q2, q3)

        c = s_ref[0]
        x = jnp.where(s_ref[2] == 1, xo[...].astype(f32), xi[...].astype(f32))
        h = x + mm(beside(cks), wo[at_core(c, hw), :]) + mm(beside(cis), wo[at_core(1 - c, hw), :]) + tab[10:11]
        h_ref[...] = h
        a = norm(h, tab[1:2], tab[5:6]).astype(bf16)
        a_ref[...] = a
        qc_ref[...] = (mm(a, wq[...]) + tab[11:12]).astype(bf16)

    dims = full_shape(w_out)
    return call(
        kernel, s, (*ctx, *ctx_in, x_own, x_in, *arrays(w_out), *arrays(w_q), table), (steps,),
        [pl.BlockSpec((rows, part.shape[1]), lambda i, s: (s[0] * steps + i, 0)) for part in ctx]
        + [tile(rows, part.shape[1]) for part in ctx_in] + [tile(rows, width), tile(rows, width)]
        + weight_specs(w_out) + weight_specs(w_q) + [const(table.shape)],
        [const(dims), const(dims), tile(rows, width), tile(rows, width), tile(rows, width)],
        [shape(dims), shape(dims), shape((t, width), f32), shape((t, width)), shape((t, width))],
        cost=4 * t * width * width,
    )


def frame_kv(s, half, twin, weight, table, rows=512):
    count, hw = half.shape
    width = 2 * hw
    steps = -(-count // rows)

    def kernel(s_ref, fa, fb, own, mine, sib, tab, w, k_ref, v_ref):
        @pl.when(pl.program_id(0) == 0)
        def _():
            fill(w, s_ref, own, mine, sib)

        c = s_ref[0]
        live = lax.broadcasted_iota(jnp.int32, (rows, 1), 0) + pl.program_id(0) * rows < count
        for j, out in enumerate((k_ref, v_ref)):
            mine0 = pl.multiple_of(j * width + c * hw, 128)
            other0 = pl.multiple_of(j * width + (1 - c) * hw, 128)
            y = mm(fa[...], w[pl.ds(mine0, hw), :]) + mm(fb[...], w[pl.ds(other0, hw), :])
            if j == 1:
                y = y + tab[12:13]
            out[...] = jnp.where(live, y, 0.0).astype(bf16)

    dims = full_shape(weight)
    return call(
        kernel, s, (half, twin, *weight, table), (steps,),
        [tile(rows, hw)] * 2 + weight_specs(weight) + [const(table.shape)],
        [const(dims), tile(rows, width), tile(rows, width)],
        [shape(dims), shape((steps * rows, width)), shape((steps * rows, width))],
        cost=4 * count * width * width,
    )


def middle(s, h1, c2_keep, c2_give, cot_own, cot_in, w_out, ff_own, ff_far, table, fc1_shift, rows=256):
    t, width = h1.shape
    units = fc1_shift.shape[1] // width
    hw = width // 2
    pieces, piece = ff_own[0].shape[:2]

    def kernel(s_ref, h1_ref, ck_ref, cg_ref, co, ci, o1, o2, o3, own1, own2, far, tab, shift, wo, out, a_ref, g_ref, dm_ref, du_ref, d2_ref, dh_ref, dk_ref, dg_ref, vec, w1, w2, sems):
        def moves():
            for k, (dst, own) in enumerate(((w1, own1), (w2, own2))):
                yield pltpu.make_async_copy(own, dst.at[pl.ds(s_ref[1] * pieces, pieces)], sems.at[2 * k])
                yield pltpu.make_async_copy(far.at[:, k], dst.at[pl.ds((1 - s_ref[1]) * pieces, pieces)], sems.at[2 * k + 1])

        @pl.when(pl.program_id(0) == 0)
        def _():
            for move in moves():
                move.start()
            fill(wo, s_ref, o1, o2, o3)
            vec[...] = jnp.zeros(vec.shape, f32)
            for move in moves():
                move.wait()

        def up(h, j):
            at, many = (h * units + j) * (hw // piece), hw // piece
            return w1[at : at + many].reshape(hw, width)

        def down(j):
            many = width // piece
            return w2[j * many : (j + 1) * many].reshape(width, width)

        c = s_ref[0]
        h2 = h1_ref[...] + mm(ck_ref[...], wo[at_core(c, hw), :]) + mm(cg_ref[...], wo[at_core(1 - c, hw), :]) + tab[13:14]
        n2, inv2 = norm_stats(h2)
        a = (n2 * tab[2:3] + tab[6:7]).astype(bf16)
        a_ref[...] = a
        acc = h2 + tab[14:15]
        slopes = []

        def climb(j):
            return mm(a[:, :hw], up(0, j)) + mm(a[:, hw:], up(1, j)) + shift[:, j * width : (j + 1) * width]

        u = climb(0)
        for j in range(units):
            u_next = climb(j + 1) if j + 1 < units else None
            g, slope = gelu_parts(u.astype(bf16).astype(f32))
            slopes.append(slope)
            g = g.astype(bf16)
            g_ref[:, j * width : (j + 1) * width] = g
            acc = acc + mm(g, down(j))
            u = u_next
        n3, inv3 = norm_stats(acc)
        out[...] = (n3 * tab[3:4] + tab[7:8]).astype(bf16)

        def back(n, inv, gain, dy):
            dn = dy * gain
            return inv * (dn - jnp.mean(dn, axis=-1, keepdims=True) - n * jnp.mean(dn * n, axis=-1, keepdims=True))

        def total(x):
            return jnp.sum(x, axis=0, keepdims=True)

        dy = jnp.where(s_ref[2] == 1, co[...].astype(f32), ci[...].astype(f32))
        dh3 = back(n3, inv3, tab[3:4], dy)
        dm = dh3.astype(bf16)
        dm_ref[...] = dm
        halves = [None, None]
        dg = mm_t(dm, down(0))
        for j in range(units):
            cols = slice(j * width, (j + 1) * width)
            dg_next = mm_t(dm, down(j + 1)) if j + 1 < units else None
            du = (slopes[j] * dg).astype(bf16)
            dg = dg_next
            du_ref[:, cols] = du
            vec[0:1, cols] += total(du.astype(f32))
            for h in range(2):
                part = mm_t(du, up(h, j))
                halves[h] = part if halves[h] is None else halves[h] + part
        da = jnp.concatenate(halves, axis=1)
        dh2 = dh3 + back(n2, inv2, tab[2:3], da)
        d2 = dh2.astype(bf16)
        d2_ref[...] = d2
        dh_ref[...] = dh2
        dk_ref[...] = mm_t(d2, wo[at_core(c, hw), :]).astype(bf16)
        dg_ref[...] = mm_t(d2, wo[at_core(1 - c, hw), :]).astype(bf16)
        rows_of = [total(dm.astype(f32)), total(d2.astype(f32)), total(dy * n3), total(dy), total(da * n2), total(da)]
        for k, value in enumerate(rows_of):
            line, at = 1 + k // 3, (k % 3) * width
            vec[line : line + 1, at : at + width] += value

    dims = full_shape(w_out)
    ff = units * width
    line = tile(rows, width)
    wide, half = tile(rows, ff), tile(rows, hw)
    away = pl.BlockSpec(memory_space=pl.ANY)
    return call(
        kernel, s, (h1, c2_keep, c2_give, cot_own, cot_in, *arrays(w_out), *ff_own, ff_far, table, fc1_shift), (t // rows,),
        [line, half, half, line, line] + weight_specs(w_out) + [away] * 3 + [const(table.shape), const(fc1_shift.shape)],
        [const(dims), line, line, wide, line, wide, line, line, half, half, const((8, ff))],
        [shape(dims), shape((t, width)), shape((t, width)), shape((t, ff)), shape((t, width)), shape((t, ff)), shape((t, width)),
         shape((t, width), f32), shape((t, hw)), shape((t, hw)), shape((8, ff), f32)],
        [pltpu.VMEM((2 * pieces, piece, width), bf16)] * 2 + [pltpu.SemaphoreType.DMA((4,))],
        cost=8 * t * width * ff + 4 * t * width * width,
    )


def ff_grads(s, a, du, g, dm):
    t, width = a.shape
    hw = width // 2
    ff = du.shape[1]
    units = ff // width
    piece = hw * units // 16
    many = hw // piece

    def kernel(s_ref, a_ref, du_ref, g0, g1, dm_ref, out):
        @pl.when(pl.program_id(0) < units)
        def _():
            for h in range(2):
                out[h] = t_mm(a_ref[:, h * hw : (h + 1) * hw], du_ref[...]).astype(bf16).reshape(out.shape[1:])

        @pl.when(pl.program_id(0) >= units)
        def _():
            for h, ref in enumerate((g0, g1)):
                out[h] = t_mm(ref[...], dm_ref[...]).astype(bf16).reshape(out.shape[1:])

    return call(
        kernel, s, (a, du, g, g, dm), (2 * units,),
        [once((t, width)), pl.BlockSpec((t, width), lambda i, s: (0, jnp.minimum(i, units - 1))),
         pl.BlockSpec((t, hw), lambda i, s: (0, jnp.maximum(i - units, 0))),
         pl.BlockSpec((t, hw), lambda i, s: (0, units + jnp.maximum(i - units, 0))), once((t, width))],
        pl.BlockSpec((2, many, 1, piece, width), lambda i, s: (0, i % units, i // units, 0, 0)),
        shape((2, 16, 2, piece, width)),
        cost=4 * t * width * ff,
    )


def cross_back(s, dq_keep, dq_give, h1, dh2, w_q, w_out, table, rows=512):
    t, width = h1.shape
    hw = width // 2

    def kernel(s_ref, dk_ref, dg_ref, h_ref, dh2_ref, wq, wo, tab, dh_ref, d1_ref, keep, give, vec):
        @pl.when(pl.program_id(0) == 0)
        def _():
            vec[...] = jnp.zeros(vec.shape, f32)

        c = s_ref[0]
        da = mm_t(dk_ref[...], wq[:, at_core(c, hw)]) + mm_t(dg_ref[...], wq[:, at_core(1 - c, hw)])
        dres, dgain, dshift = norm_back(h_ref[...], tab[1:2], da)
        dh1 = dh2_ref[...] + dres
        dh_ref[...] = dh1
        d1 = dh1.astype(bf16)
        d1_ref[...] = d1
        keep[...] = mm_t(d1, wo[at_core(c, hw), :]).astype(bf16)
        give[...] = mm_t(d1, wo[at_core(1 - c, hw), :]).astype(bf16)
        vec[0:1] += dgain
        vec[1:2] += dshift
        vec[2:3] += jnp.sum(d1.astype(f32), axis=0, keepdims=True)
        vec[3:4, at_core(c, hw)] += jnp.sum(dk_ref[...].astype(f32), axis=0, keepdims=True)
        vec[3:4, at_core(1 - c, hw)] += jnp.sum(dg_ref[...].astype(f32), axis=0, keepdims=True)

    line, half = tile(rows, width), tile(rows, hw)
    return call(
        kernel, s, (dq_keep, dq_give, h1, dh2, w_q, w_out, table), (t // rows,),
        [half, half, line, line, once(w_q.shape), once(w_out.shape), const(table.shape)],
        [line, line, half, half, const((8, width))],
        [shape((t, width), f32), shape((t, width)), shape((t, hw)), shape((t, hw)), shape((8, width), f32)],
        cost=4 * t * width * width,
    )


def frame_back(s, keep, recv, half, twin, weight, rows=512):
    count, hw = half.shape
    width = 2 * hw
    steps = -(-count // rows)

    def kernel(s_ref, ka, kb, fa, fb, w, fkeep, fgive, xkeep, xgive, vec, acc):
        @pl.when(pl.program_id(0) == 0)
        def _():
            vec[...] = jnp.zeros(vec.shape, f32)
            acc[...] = jnp.zeros(acc.shape, f32)

        c, h = s_ref[0], s_ref[1]
        live = lax.broadcasted_iota(jnp.int32, (rows, 1), 0) + pl.program_id(0) * rows < count
        zero = jnp.zeros((rows, hw), bf16)
        f_mine = jnp.where(live, fa[...], zero)
        f_other = jnp.where(live, fb[...], zero)
        back = None
        for j in range(2):
            d = (ka[j].astype(f32) + kb[j].astype(f32)).astype(bf16)
            part = mm_t(d, w[j * width : (j + 1) * width, at_core(c, hw)])
            back = part if back is None else back + part
            acc[j, at_core(c, hw), :] += t_mm(f_mine, d)
            acc[j, at_core(1 - c, hw), :] += t_mm(f_other, d)
            if j == 1:
                vec[0:1] += jnp.sum(d.astype(f32), axis=0, keepdims=True)
        low, high = back[:, :hw].astype(bf16), back[:, hw:].astype(bf16)
        fkeep[...] = jnp.where(c == 0, low, high)
        fgive[...] = jnp.where(c == 0, high, low)

        @pl.when(pl.program_id(0) == steps - 1)
        def _():
            xkeep[...] = acc[h].astype(bf16)
            xgive[...] = acc[1 - h].astype(bf16)

    pair = pl.BlockSpec((2, rows, hw), lambda i, s: (0, i, 0))
    strip = tile(rows, hw)
    return call(
        kernel, s, (keep, recv, half, twin, weight), (steps,),
        [pair, pair, strip, strip, once(weight.shape)],
        [strip, strip, const((width, hw)), const((width, hw)), const((8, hw))],
        [shape((count, hw)), shape((count, hw)), shape((width, hw)), shape((width, hw)), shape((8, hw), f32)],
        [pltpu.VMEM((2, width, hw), f32)],
        cost=8 * count * width * width,
    )


def give_grads(s, c2_keep, c2_give, d2, a2, dq_give):
    t, width = d2.shape
    hw = width // 2

    def kernel(s_ref, k_ref, g_ref, d_ref, a_ref, q_ref, out):
        c = s_ref[0]
        out[0, at_core(c, hw), :] = t_mm(k_ref[...], d_ref[...]).astype(bf16)
        out[0, at_core(1 - c, hw), :] = t_mm(g_ref[...], d_ref[...]).astype(bf16)
        out[1] = t_mm(a_ref[...], q_ref[...]).astype(bf16)

    half = const((t, hw))
    return call(
        kernel, s, (c2_keep, c2_give, d2, a2, dq_give), (1,),
        [half, half, pl.BlockSpec((t, hw), lambda i, s: (0, 1 - s[0])), const((t, width)), half],
        const((2, width, hw)), shape((2, width, hw)), cost=4 * t * width * hw,
    )


def give_grad_out(s, ctx, ctx_in, d1):
    t, width = d1.shape
    hw = width // 2
    n = len(ctx)

    def kernel(s_ref, *refs):
        d_ref, out = refs[2 * n :]
        c = s_ref[0]
        out[at_core(c, hw), :] = t_mm(beside(refs[:n]), d_ref[...]).astype(bf16)
        out[at_core(1 - c, hw), :] = t_mm(beside(refs[n : 2 * n]), d_ref[...]).astype(bf16)

    return call(
        kernel, s, (*ctx, *ctx_in, d1), (1,),
        [pl.BlockSpec((t, part.shape[1]), lambda i, s: (s[0], 0)) for part in ctx] + [const(part.shape) for part in ctx_in]
        + [pl.BlockSpec((t, hw), lambda i, s: (0, 1 - s[0]))],
        const((width, hw)), shape((width, hw)), cost=2 * t * width * hw,
    )


def keep_grads(s, c2_keep, c2_give, d2, a2, dq_keep, pair_in, kv_keep, kv_give):
    t, width = d2.shape
    hw = width // 2

    def kernel(s_ref, ck, cg, d2_ref, a_ref, q_ref, p_ref, kk, kg, xgive, xkeep):
        c, h = s_ref[0], s_ref[1]
        for out, shard, kv in ((xgive, 1 - h, kg), (xkeep, h, kk)):
            rows = at_core(shard, hw)
            out[1] = (t_mm(a_ref[:, rows], q_ref[...]) + p_ref[1, rows, :].astype(f32)).astype(bf16)
            out[2] = kv[:hw]
            out[3] = kv[hw:]
        own_rows = t_mm(ck[...], d2_ref[...]) + p_ref[0, at_core(c, hw), :].astype(f32)
        far_rows = t_mm(cg[...], d2_ref[...]) + p_ref[0, at_core(1 - c, hw), :].astype(f32)
        xkeep[0] = jnp.where(c == h, own_rows, far_rows).astype(bf16)
        xgive[0] = jnp.where(c == h, far_rows, own_rows).astype(bf16)

    cols, half = pl.BlockSpec((t, hw), lambda i, s: (0, s[0])), const((t, hw))
    four = (4, hw, hw)
    return call(
        kernel, s, (c2_keep, c2_give, d2, a2, dq_keep, pair_in, kv_keep, kv_give), (1,),
        [half, half, cols, const((t, width)), half, const((2, width, hw)), const((width, hw)), const((width, hw))],
        [const(four), const(four)], [shape(four), shape(four)], cost=4 * t * width * hw,
    )


def keep_grad_out(s, ctx, ctx_in, d1, out_in):
    t, width = d1.shape
    hw = width // 2
    n = len(ctx)

    def kernel(s_ref, *refs):
        d1_ref, o_ref, xgive, xkeep = refs[2 * n :]
        c, h = s_ref[0], s_ref[1]
        own_rows = t_mm(beside(refs[:n]), d1_ref[...]) + o_ref[at_core(c, hw), :].astype(f32)
        far_rows = t_mm(beside(refs[n : 2 * n]), d1_ref[...]) + o_ref[at_core(1 - c, hw), :].astype(f32)
        xkeep[0] = jnp.where(c == h, own_rows, far_rows).astype(bf16)
        xgive[0] = jnp.where(c == h, far_rows, own_rows).astype(bf16)

    one = (1, hw, hw)
    return call(
        kernel, s, (*ctx, *ctx_in, d1, out_in), (1,),
        [pl.BlockSpec((t, part.shape[1]), lambda i, s: (s[0], 0)) for part in ctx] + [const(part.shape) for part in ctx_in]
        + [pl.BlockSpec((t, hw), lambda i, s: (0, s[0])), const((width, hw))],
        [const(one), const(one)], [shape(one), shape(one)], cost=2 * t * width * hw,
    )


def split_y(s, keeps, gots):
    _, rows, cols = keeps[0].shape
    half, n = rows // 2, len(keeps)
    counts = [k.shape[0] for k in keeps]

    def kernel(s_ref, *refs):
        give, mine = refs[2 * n :]
        for out, y in ((give, 1 - s_ref[4]), (mine, s_ref[4])):
            rows_at = pl.ds(pl.multiple_of(y * half, 64), half)
            at = 0
            for k_ref, g_ref, count in zip(refs[:n], refs[n : 2 * n], counts):
                out[at : at + count] = (k_ref[:, rows_at, :].astype(f32) + g_ref[:, rows_at, :].astype(f32)).astype(bf16)
                at += count

    dims = (sum(counts), half, cols)
    return call(kernel, s, (*keeps, *gots), (1,), [const(k.shape) for k in (*keeps, *gots)], [const(dims)] * 2, [shape(dims)] * 2)


def split_z(s, keep, got):
    b, rows, cols = keep.shape
    part = rows // 4

    def kernel(s_ref, k_ref, g_ref, *outs):
        for d, out in enumerate(outs):
            at = pl.ds(pl.multiple_of(s_ref[5 + d] * part, 16), part)
            out[...] = (k_ref[:, at, :].astype(f32) + g_ref[:, at, :].astype(f32)).astype(bf16)

    dims = (b, part, cols)
    return call(kernel, s, (keep, got), (1,), [const(keep.shape)] * 2, [const(dims)] * 4, [shape(dims)] * 4)


def sum_four(s, parts, vectors=()):
    b, part, cols = parts[0].shape

    def kernel(s_ref, p0, p1, p2, p3, *refs):
        out = refs[-1]
        total = (p0[...].astype(f32) + p1[...].astype(f32)) + (p2[...].astype(f32) + p3[...].astype(f32))
        out[0:b] = total.astype(bf16)
        if vectors:
            v = refs[0][...] + refs[1][...]
            high = v.astype(bf16).astype(f32)
            out[b] = jnp.concatenate([high, v - high], axis=0).astype(bf16)

    dims = (b + (1 if vectors else 0), part, cols)
    return call(
        kernel, s, (*parts, *vectors), (1,), [const(parts[0].shape)] * 4 + [const(v.shape) for v in vectors], const(dims), shape(dims)
    )


def pack_vectors(s, last, cross, mid, kv):
    width = last.shape[1]
    hw = width // 2
    units = mid.shape[1] // width

    def kernel(s_ref, l_ref, c_ref, m_ref, k_ref, give, mine):
        def line(ref, row, at=0):
            return ref[row : row + 1, at : at + width]

        zero = jnp.zeros((1, hw), f32)
        first = s_ref[0] == 0
        kv_row = jnp.concatenate([jnp.where(first, k_ref[0:1], zero), jnp.where(first, zero, k_ref[0:1])], axis=1)
        rows = [
            line(l_ref, 0), line(c_ref, 0), line(m_ref, 2, width), line(m_ref, 1, 2 * width),
            line(l_ref, 1), line(c_ref, 1), line(m_ref, 2, 2 * width), line(m_ref, 2),
            line(l_ref, 2), line(l_ref, 3), line(c_ref, 2), line(c_ref, 3), kv_row, line(m_ref, 1, width), line(m_ref, 1),
        ]
        halves = []
        for h in range(2):
            own = [row[:, h * hw : (h + 1) * hw] for row in rows]
            own += [m_ref[0:1, (h * units + j) * hw : (h * units + j + 1) * hw] for j in range(units)]
            halves.append(jnp.concatenate(own + [zero] * (24 - len(own)), axis=0))
        give[...] = jnp.where(s_ref[1] == 0, halves[1], halves[0])
        mine[...] = jnp.where(s_ref[1] == 0, halves[0], halves[1])

    return call(
        kernel, s, (last, cross, mid, kv), (1,), [const(x.shape) for x in (last, cross, mid, kv)],
        [const((24, hw))] * 2, [shape((24, hw), f32)] * 2,
    )


def join_z(s, parts):
    b, part, cols = parts[0].shape

    def kernel(s_ref, p0, p1, p2, p3, out):
        for d, ref in enumerate((p0, p1, p2, p3)):
            out[:, pl.ds(pl.multiple_of(s_ref[5 + d] * part, 16), part), :] = ref[...]

    dims = (b, 4 * part, cols)
    return call(kernel, s, parts, (1,), [const(parts[0].shape)] * 4, const(dims), shape(dims))


def spread_out(s, groups, outs, vectors=False):
    hw = 384

    def kernel(s_ref, *refs):
        results = refs[4 * len(groups) :]
        for n, (parts, spots) in enumerate(groups):
            b, half, cols = parts[0].shape
            for k, ref in enumerate(refs[4 * n : 4 * n + 4]):
                y = s_ref[4] if k % 2 == 0 else 1 - s_ref[4]
                core = s_ref[0] if k < 2 else 1 - s_ref[0]
                for block, (which, row, col) in enumerate(spots):
                    at_row = pl.multiple_of(row + y * half, 64)
                    at_col = pl.multiple_of(col + core * hw, 128)
                    results[which][pl.ds(at_row, half), pl.ds(at_col, cols)] = ref[block].astype(f32)
        if vectors:
            total = None
            for ref in refs[:4]:
                rows = ref[ref.shape[0] - 1].astype(f32)
                for z in range(4):
                    part = rows[48 * z : 48 * z + 48]
                    total = part if total is None else total + part
            total, at = total[0:24] + total[24:48], 0
            for ref in results[1:]:
                ref[...] = total[at : at + ref.shape[0]]
                at += ref.shape[0]

    parts = [part for group, _ in groups for part in group]
    return call(kernel, s, parts, (1,), [const(part.shape) for part in parts], [const(d) for d in outs], [shape(d, f32) for d in outs])


def spread_gathered(s, got, spots, outs):
    _, _, part, hw = got.shape

    def kernel(s_ref, g_ref, *results):
        for r in range(got.shape[0]):
            z, y, core = r // 4, r // 2 % 2, r % 2
            for block, (which, row, col) in enumerate(spots):
                at_row, at_col = row + (y * 4 + z) * part, col + core * hw
                results[which][at_row : at_row + part, at_col : at_col + hw] = g_ref[r, block].astype(f32)

    return call(kernel, s, (got,), (1,), [const(got.shape)], [const(d) for d in outs], [shape(d, f32) for d in outs])


def spread_ff(s, got):
    reps, _, per, width = got.shape
    units = 4
    rows = reps // units * per

    def kernel(s_ref, g_ref, one, two):
        one[...] = g_ref[:, 0].reshape(rows, width).astype(f32)
        two[...] = g_ref[:, 1].reshape(rows, width).astype(f32)

    return call(
        kernel, s, (got,), (units,), [pl.BlockSpec((reps // units, 2, per, width), lambda i, s: (i, 0, 0, 0))],
        [pl.BlockSpec((rows, width), lambda i, s: (0, i)), pl.BlockSpec((rows, width), lambda i, s: (i, 0))],
        [shape((rows, units * width), f32), shape((units * rows, width), f32)],
    )


def qkv_grad(s, a_own, a_sib, keep, give, mine):
    t, width = a_own.shape
    hw = width // 2
    n = len(keep)

    def kernel(s_ref, ao, ai, *refs):
        k, g = (jnp.concatenate([ref[0] for ref in part], axis=1) for part in (refs[:n], refs[n : 2 * n]))
        refs[-1][0] = (t_mm(ao[...], k) + t_mm(ai[...], g)).astype(bf16)

    cols = pl.BlockSpec((t, hw), lambda i, s: (0, s[1] if mine else 1 - s[1]))
    return call(
        kernel, s, (a_own, a_sib, *keep, *give), (3,),
        [cols, cols] + [pl.BlockSpec((1, t, part.shape[2]), lambda i, s: (i, 0, 0)) for part in (*keep, *give)],
        pl.BlockSpec((1, hw, hw), lambda i, s: (i, 0, 0)), shape((3, hw, hw)), cost=6 * t * width * hw,
    )


def last_rows(s, keep, recv, x_own, x_in, dh1, weight, table, rows=512):
    t, width = x_own.shape
    hw = width // 2
    n = len(keep)

    def kernel(s_ref, *refs):
        xo, xi, dh, w, tab, out, vec = refs[2 * n :]

        @pl.when(pl.program_id(0) == 0)
        def _():
            vec[...] = jnp.zeros(vec.shape, f32)

        c = s_ref[0]
        da = None
        for j in range(3):
            for parts, core in ((refs[:n], c), (refs[n : 2 * n], 1 - c)):
                d = jnp.concatenate([part[j] for part in parts], axis=1)
                at = pl.multiple_of(j * width + core * hw, 128)
                part = mm_t(d, w[:, pl.ds(at, hw)])
                da = part if da is None else da + part
                if j != 1:
                    line = 2 + j // 2
                    vec[line : line + 1, at_core(core, hw)] += jnp.sum(d.astype(f32), axis=0, keepdims=True)
        x = jnp.where(s_ref[2] == 1, xo[...].astype(f32), xi[...].astype(f32))
        dres, dgain, dshift = norm_back(x, tab[0:1], da)
        out[...] = (dh[...] + dres).astype(bf16)
        vec[0:1] += dgain
        vec[1:2] += dshift

    line = tile(rows, width)
    return call(
        kernel, s, (*keep, *recv, x_own, x_in, dh1, weight, table), (t // rows,),
        [pl.BlockSpec((3, rows, part.shape[2]), lambda i, s: (0, i, 0)) for part in (*keep, *recv)]
        + [line, line, line, once(weight.shape), const(table.shape)],
        [line, const((8, width))], [shape((t, width)), shape((8, width), f32)],
        cost=6 * t * width * width,
    )


EVERY = ("z", "y", "core", "x")
SPREAD2 = ("x", "z", "y", "core")
REP2 = ("z", "y", "core")
SWAP = [(1, 2), (2, 1)]


def tie(*values):
    return lax.optimization_barrier(values)


def across_z(x, d):
    return lax.ppermute(x, "z", [(j, j ^ d) for j in range(4)])


def across(x, axis):
    return lax.ppermute(x, axis, FLIP)


def body_pair(hidden, frames, segment, cotangent, norm_gain, norm_bias, self_qkv, self_out, cross_q, cross_kv, cross_out, fc1, fc2, proj_bias, fc1_bias):
    c, h = lax.axis_index("core"), lax.axis_index("x")
    y_at, z_at = lax.axis_index("y"), lax.axis_index("z")
    stay = c == h
    s = jnp.stack([c, h, stay.astype(jnp.int32), jnp.int32(0), y_at, z_at, z_at ^ 1, z_at ^ 2, z_at ^ 3]).astype(jnp.int32)
    rep_at = lax.axis_index(REP2)
    reps = lax.axis_size(REP2)
    width = self_out.shape[1]
    hw = width // 2
    ff = fc1.shape[1]
    units = ff // width
    pairs = hw // 128

    def swap(x):
        return lax.ppermute(x, ("core", "x"), SWAP)

    def sibling(x):
        return across(x, "core")

    def near(own):
        half = own.shape[0] // 2
        return across(lax.dynamic_slice_in_dim(own, c * half, half).astype(bf16), "x")

    x_own = hidden[0]
    small = jnp.concatenate([norm_gain, norm_bias, proj_bias, fc1_bias.reshape(units, hw), jnp.zeros((1, hw), f32)]).astype(bf16)
    small_in = across(small, "x")
    qkv_near = near(self_qkv)
    x_in = swap(x_own)
    seg = jnp.where(stay, segment, swap(segment))[0]
    per = hw * units // reps
    small = jnp.where(h == 0, jnp.stack([small, small_in]), jnp.stack([small_in, small])).astype(f32)
    table = jnp.concatenate([small[0, :16], small[1, :16]], axis=1)
    fc1_shift = small[:, 15:19].reshape(1, ff)
    kmark, qmark = seg_marks(seg)
    own1 = jnp.concatenate([fc1[:, j * width : (j + 1) * width] for j in range(units)]).astype(bf16).reshape(reps, per, width)
    own2 = fc2.astype(bf16).reshape(reps, per, width)
    slot = jnp.stack([lax.dynamic_index_in_dim(own1, rep_at, keepdims=False), lax.dynamic_index_in_dim(own2, rep_at, keepdims=False)])
    part = hw // 2
    squares = jnp.stack([lax.dynamic_slice_in_dim(w, c * part, part) for w in (self_out, cross_q, cross_out)]).astype(bf16)
    kv_part = lax.dynamic_slice_in_dim(cross_kv, c * hw, hw).astype(bf16)
    x_in, kmark, qmark, squares, kv_part, frames, own1, own2, slot = tie(x_in, kmark, qmark, squares, kv_part, frames, own1, own2, slot)
    slot = across(slot, "x")
    squares_near = across(squares, "x")
    f_own = frames[0]
    f_in = swap(f_own)
    kv_near = across(kv_part, "x")
    w_qkv, a1, keep, give = norm_qkv(s, x_own, x_in, (self_qkv, qkv_near, sibling(qkv_near)), table)
    give, slot = tie(give, slot)
    recv = sibling(give)
    ff_far = lax.all_gather(slot, REP2, axis=0, tiled=False)

    many = pairs - 1
    ctx_a, give_a, lse_a = self_fwd(0, many, c, keep, recv, kmark, qmark)
    give_a, keep, recv, squares_near, cotangent = tie(give_a, keep, recv, squares_near, cotangent)
    cot_in = swap(cotangent[0])
    squares_sib = sibling(squares_near)
    w_out, w_q, w_co = (
        (w, (squares_near, k), (squares_sib, k)) for k, w in enumerate((self_out, cross_q, cross_out))
    )
    in_a = sibling(give_a)
    ctx_b, give_b, lse_b = self_fwd(many, 1, c, keep, recv, kmark, qmark)
    in_b = sibling(give_b)
    ctx, ctx_in = (ctx_a, ctx_b), (in_a, in_b)
    w_out, w_q, h1, a2, qc = self_project(s, ctx, ctx_in, x_own, x_in, w_out, w_q, table)
    qc, f_in, kv_near = tie(qc, f_in, kv_near)
    half = jnp.where(stay, f_own, f_in)
    twin = sibling(half)
    w_kv, kc, vc = frame_kv(s, half, twin, (cross_kv, kv_near, sibling(kv_near)), table)
    count = half.shape[0]
    own_pairs, far_pairs = c * pairs, (1 - c) * pairs
    c2_give, cross_lse_give = cross_fwd(far_pairs, pairs, qc, kc, vc, count)
    c2_keep, cross_lse_keep = cross_fwd(own_pairs, pairs, qc, kc, vc, count)
    _, out, a3, g, dm, du, d2, dh2, dc2_keep, dc2_give, vec_mid = middle(
        s, h1, c2_keep, c2_give, cotangent[0], cot_in, w_co, (own1, own2), ff_far, table, fc1_shift,
    )

    packed = ff_grads(s, a3, du, g, dm)
    dc2_give, packed, out, a1_out = tie(dc2_give, packed, out, a1)
    ff_mine = lax.psum_scatter(packed.reshape(2 * reps, 2 * per, width), SPREAD2, scatter_dimension=0, tiled=False)
    out_in = swap(out)
    a1_sib = sibling(a1_out)
    dq_give, dkv_give = cross_bwd(far_pairs, pairs, qc, kc, vc, c2_give, dc2_give, cross_lse_give, count)
    dkv_give, dq_give = tie(dkv_give, dq_give)
    dkv_in = sibling(dkv_give)
    pair_give = give_grads(s, c2_keep, c2_give, d2, a2, dq_give)
    pair_give, dc2_keep = tie(pair_give, dc2_keep)
    pair_in = sibling(pair_give)
    dq_keep, dkv_keep = cross_bwd(own_pairs, pairs, qc, kc, vc, c2_keep, dc2_keep, cross_lse_keep, count)
    dq_keep, out_in, dkv_in, a1_sib, pair_in = tie(dq_keep, out_in, dkv_in, a1_sib, pair_in)
    fkeep, fgive, kv_xkeep, kv_xgive, vec_kv = frame_back(s, dkv_keep, dkv_in, half, twin, w_kv)
    fgive, dq_keep = tie(fgive, dq_keep)
    fr_in = sibling(fgive)
    xgive, xkeep = keep_grads(s, c2_keep, c2_give, d2, a2, dq_keep, pair_in, kv_xkeep, kv_xgive)
    xgive, dq_keep = tie(xgive, dq_keep)
    got_x = across(xgive, "x")
    dh1, d1, dctx_keep, dctx_give, vec_cross = cross_back(s, dq_keep, dq_give, h1, dh2, w_q, w_out, table)
    dctx_give, d1 = tie(dctx_give, d1)
    dctx_in = sibling(dctx_give)
    so_give = give_grad_out(s, ctx, ctx_in, d1)
    so_give, fr_in, fkeep = tie(so_give, fr_in, fkeep)
    so_in = sibling(so_give)
    fr_own = (fkeep.astype(f32) + fr_in.astype(f32)).astype(bf16)
    so_xgive, so_xkeep = keep_grad_out(s, ctx, ctx_in, d1, so_in)
    so_xgive, dctx_keep = tie(so_xgive, dctx_keep)
    so_x = across(so_xgive, "x")

    def send_z(pieces):
        return (pieces[0],) + tuple(across_z(pieces[d], d) for d in (1, 2, 3))

    def gather_z(piece):
        return (piece,) + tuple(across_z(piece, d) for d in (1, 2, 3))

    bg1, bk1 = self_bwd(0, 1, 0, c, keep, recv, ctx_a, dctx_keep, dctx_in, lse_a, kmark, qmark)
    bg1, bk1, keep = tie(bg1, bk1, keep)
    bi1 = sibling(bg1)
    bg2, bk2 = self_bwd(1, 1, 1, c, keep, recv, ctx_a, dctx_keep, dctx_in, lse_a, kmark, qmark)
    bg2, bk2, got_x, so_x, keep, bi1, fr_own = tie(bg2, bk2, got_x, so_x, keep, bi1, fr_own)
    fr_swapped = swap(fr_own)
    bi2 = sibling(bg2)
    m_ygive, m_ykeep = split_y(s, (xkeep, so_xkeep), (got_x, so_x))
    m_ygive, keep, ff_mine = tie(m_ygive, keep, ff_mine)
    m_y = across(m_ygive, "y")
    ff_got = lax.all_gather(ff_mine, REP2, axis=0, tiled=False)
    bg3, bk3 = self_bwd(2, 1, 0, c, keep, recv, ctx_b, dctx_keep, dctx_in, lse_b, kmark, qmark)
    bg3, bk3, bi2 = tie(bg3, bk3, bi2)
    bi3 = sibling(bg3)
    q_xgive = qkv_grad(s, a1, a1_sib, (bk1, bk2, bk3), (bg1, bg2, bg3), False)
    q_xgive, m_y, fr_swapped = tie(q_xgive, m_y, fr_swapped)
    q_x = across(q_xgive, "x")
    m_z = split_z(s, m_ykeep, m_y)
    bk3, dh1, *m_z = tie(bk3, dh1, *m_z)
    m_z = send_z(m_z)
    q_xkeep = qkv_grad(s, a1, a1_sib, (bk1, bk2, bk3), (bg1, bg2, bg3), True)
    grad_hidden, vec_last = last_rows(s, (bk1, bk2, bk3), (bi1, bi2, bi3), x_own, x_in, dh1, w_qkv, table)
    vec_last, q_x = tie(vec_last, q_x)
    q_ygive, q_ykeep = split_y(s, (q_xkeep,), (q_x,))
    q_ygive, grad_hidden, vec_last = tie(q_ygive, grad_hidden, vec_last)
    q_y = across(q_ygive, "y")
    hid_in = swap(grad_hidden)
    v_give, v_mine = pack_vectors(s, vec_last, vec_cross, vec_mid, vec_kv)
    v_got = across(v_give, "x")
    q_four = split_z(s, q_ykeep, q_y)
    q_first, *m_z = tie(q_four[0], *m_z)
    q_four = (q_first, *q_four[1:])
    m_piece = sum_four(s, m_z)
    m_got = lax.all_gather(m_piece, REP2, axis=0, tiled=False)
    q_z = send_z(q_four)
    fc1_grad, fc2_grad = spread_ff(s, ff_got.reshape(reps, 2, per, width))
    output = jnp.where(stay, out, out_in)
    fc1_grad, fc2_grad, output, *q_z = tie(fc1_grad, fc2_grad, output, *q_z)
    q_piece = sum_four(s, q_z, (v_mine, v_got))
    q_all = gather_z(q_piece)
    spots = ((0, 0, 0), (1, 0, 0), (3, 0, 0), (3, hw, 0), (2, 0, 0))
    crossout_grad, crossq_grad, selfout_grad, kv_grad = spread_gathered(s, m_got, spots, ((hw, width),) * 3 + ((width, width),))
    grad_frames = jnp.where(stay, fr_own, fr_swapped)
    grad_frames, *q_all = tie(grad_frames, *q_all)
    q_own = join_z(s, q_all)
    q_far = across(q_own, "y")
    q_own_sib = sibling(q_own)
    grad_hidden = jnp.where(stay, grad_hidden, hid_in)
    q_far, crossout_grad, grad_hidden = tie(q_far, crossout_grad, grad_hidden)
    first = tuple((0, 0, j * width) for j in range(3))
    qkv_grad_out, gain_grad, shift_grad, bias_grad, fc1b_grad = spread_out(s, (((q_own, q_far, q_own_sib, sibling(q_far)), first),), ((hw, 3 * width), (4, hw), (4, hw), (7, hw), (units, hw)), True)

    return (
        output[None], grad_hidden[None], grad_frames[None], gain_grad, shift_grad,
        qkv_grad_out, selfout_grad, crossq_grad, kv_grad, crossout_grad, fc1_grad, fc2_grad, bias_grad, fc1b_grad.reshape(-1),
    )


GROUP = ("core", "ilo")
SHARD = ("ihi", "ilo")
REP = ("rz", "core")
SPREAD = ("ihi", "ilo", "rz", "core")


def body_general(hidden, frames, segment, cotangent, norm_gain, norm_bias, self_qkv, self_out, cross_q, cross_kv, cross_out, fc1, fc2, proj_bias, fc1_bias):
    c = lax.axis_index("core")
    hi = lax.axis_index("ihi")
    n = lax.axis_size("core") * lax.axis_size("ilo")
    reps = lax.axis_size("rz") * lax.axis_size("core")
    rep_at = lax.axis_index(REP)
    width = self_out.shape[1]
    ff = fc1.shape[1]

    def swap(x):
        return lax.ppermute(x, ("core", "ihi"), [(0, 0), (1, 2), (2, 1), (3, 3)])

    def whole(own):
        if n != 2:
            return lax.all_gather(own, SHARD, axis=0, tiled=True)
        half = own.shape[0] // 2
        mine = lax.ppermute(lax.dynamic_slice_in_dim(own, c * half, half), "ihi", FLIP)
        sib = lax.ppermute(mine, "core", FLIP)
        other = jnp.where(c == 0, jnp.concatenate([mine, sib]), jnp.concatenate([sib, mine]))
        return jnp.where(hi == 0, jnp.concatenate([own, other]), jnp.concatenate([other, own]))

    def slices(own):
        rows = own.shape[0] // reps
        return lax.dynamic_slice_in_dim(own, rep_at * rows, rows)

    rows_in = swap(hidden[0])
    qkv_w = whole(self_qkv.astype(bf16))
    small = jnp.concatenate([norm_gain.astype(bf16), norm_bias.astype(bf16), proj_bias.astype(bf16), fc1_bias.astype(bf16).reshape(-1, norm_gain.shape[1]), jnp.zeros((1, norm_gain.shape[1]), bf16)])
    small = lax.all_gather(small, SHARD, axis=1, tiled=False).astype(f32)
    table = small[:15].reshape(15, width)
    gains, shifts, biases = table[:4], table[4:8], table[8:15]
    fc1_shift = small[15:19].transpose(1, 0, 2).reshape(ff)
    seg = swap(segment)[0]
    frames_half = swap(frames[0])
    if n == 2:
        twin = lax.ppermute(frames_half, "core", FLIP)
        frame_rows = jnp.concatenate([jnp.where(c == 0, frames_half, twin), jnp.where(c == 0, twin, frames_half)], axis=1)
    else:
        frame_rows = lax.all_gather(frames_half, GROUP, axis=1, tiled=True)
    selfout_w = whole(self_out.astype(bf16))
    crossq_w = whole(cross_q.astype(bf16))
    kv_w = whole(cross_kv.astype(bf16)) if n == 2 else None
    if n == 2:
        k_w, v_w = kv_w[:width], kv_w[width:]
    else:
        kv_w = lax.all_gather(cross_kv.astype(bf16), SHARD, axis=1, tiled=True)
        k_w, v_w = kv_w[:, :width], kv_w[:, width:]
    crossout_w = whole(cross_out.astype(bf16))
    cot = swap(cotangent[0])
    units = ff // width
    part1 = slices(fc1.astype(bf16))
    part2 = slices(fc2.astype(bf16))
    few = part1.shape[0]
    parts = jnp.concatenate([part1[:, j * width : (j + 1) * width] for j in range(units)] + [part2])
    ffw = lax.all_gather(parts, SPREAD, axis=0, tiled=False)
    fc1_w = jnp.concatenate([ffw[:, j * few : (j + 1) * few].reshape(width, width) for j in range(units)], axis=1)
    fc2_w = ffw[:, units * few :].reshape(ff, width)

    own_rows = rows_in.shape[0]
    hw = -(-HEADS // n)
    padded = hw * n * HD - width

    lanes = hw * HD

    def to_heads(x):
        x = x.reshape(own_rows, -1, width)
        if padded:
            x = jnp.pad(x, ((0, 0), (0, 0), (0, padded)))
        x = x.reshape(own_rows, -1, n, lanes).transpose(1, 2, 0, 3)
        x = lax.all_to_all(x, GROUP, 1, 1, tiled=True)
        return x.reshape(-1, n * own_rows, lanes)

    def to_tokens(x):
        x = lax.all_to_all(x.reshape(-1, n, own_rows, lanes), GROUP, 1, 1, tiled=True)
        return x.transpose(2, 0, 1, 3).reshape(own_rows, -1, n * lanes)[:, :, :width].reshape(own_rows, -1)

    h0 = rows_in.astype(f32)
    a1 = norm(h0, gains[0], shifts[0]).astype(bf16)
    zeros_row = jnp.zeros((width,), f32)
    qkv = (mm(a1, qkv_w) + jnp.concatenate([biases[0], zeros_row, biases[1]])).astype(bf16)
    heads = to_heads(qkv)
    kmark, qmark = seg_marks(seg)
    mid = heads.shape[1] // 2
    first = jnp.int32(0)
    ctx, _, self_lse = self_fwd(0, lanes // 128, first, heads[:, :mid], heads[:, mid:], kmark, qmark)
    c1 = to_tokens(ctx)
    h1 = h0 + mm(c1, selfout_w) + biases[2]
    a2 = norm(h1, gains[1], shifts[1]).astype(bf16)
    qc = (mm(a2, crossq_w) + biases[3]).astype(bf16)
    count = frame_rows.shape[0]
    pad = -count % 256
    frame_pad = jnp.pad(frame_rows, ((0, pad), (0, 0)))
    kc = mm(frame_pad, k_w).astype(bf16)
    live = lax.broadcasted_iota(jnp.int32, (count + pad, 1), 0) < count
    vc = (mm(frame_pad, v_w) + jnp.where(live, biases[4], 0.0)).astype(bf16)
    c2, cross_lse = cross_fwd(first, width // 128, qc, kc, vc, count)
    h2 = h1 + mm(c2, crossout_w) + biases[5]
    a3 = norm(h2, gains[2], shifts[2]).astype(bf16)
    u = (mm(a3, fc1_w) + fc1_shift).astype(bf16)
    uf = u.astype(f32)
    g, slope = gelu_parts(uf)
    g = g.astype(bf16)
    h3 = h2 + mm(g, fc2_w) + biases[6]
    output = norm(h3, gains[3], shifts[3]).astype(bf16)
    output = swap(output)

    def total(x):
        return jnp.sum(x.astype(f32), axis=0)

    dh3, gain3, shift3 = norm_back(h3, gains[3], cot.astype(f32))
    dm = dh3.astype(bf16)
    g_fc2 = t_mm(g, dm).astype(bf16)
    du = (slope * mm_t(dm, fc2_w)).astype(bf16)
    g_fc1 = t_mm(a3, du).astype(bf16)

    def reduce_rows(parts, extra=None):
        total = n * reps
        cut = [p.reshape(total, -1, width) for p in parts]
        if extra is not None:
            cut.append(extra)
        flat = jnp.concatenate(cut, axis=1)
        mine = lax.psum_scatter(flat, SPREAD, scatter_dimension=0, tiled=False)
        got = lax.all_gather(mine, REP, axis=0, tiled=False)
        out, at = [], 0
        for p in cut:
            out.append(got[:, at : at + p.shape[1]].reshape(-1, width).astype(f32))
            at += p.shape[1]
        return out

    ff_grads = reduce_rows([g_fc1[:, j * width : (j + 1) * width] for j in range(units)] + [g_fc2])
    fc1_grad = jnp.concatenate(ff_grads[:units], axis=1)
    fc2_grad = ff_grads[units]

    da3 = mm_t(du, fc1_w)
    dres, gain2, shift2 = norm_back(h2, gains[2], da3)
    dh2 = dh3 + dres
    d2 = dh2.astype(bf16)
    g_crossout = t_mm(c2, d2).astype(bf16)
    dc2 = mm_t(d2, crossout_w).astype(bf16)
    dqc, (dkc, dvc) = cross_bwd(first, width // 128, qc, kc, vc, c2, dc2, cross_lse, count)
    share = width // n

    def sum_columns(x):
        return lax.psum_scatter(x, GROUP, scatter_dimension=1, tiled=True)

    if n == 2:

        def sum_columns(x):
            give = lax.dynamic_slice_in_dim(x, (1 - c) * share, share, axis=1)
            keep = lax.dynamic_slice_in_dim(x, c * share, share, axis=1)
            return (keep.astype(f32) + lax.ppermute(give, "core", FLIP).astype(f32)).astype(bf16)

    dk_own = sum_columns(dkc)[:count]
    dv_own = sum_columns(dvc)[:count]
    place = lax.axis_index(GROUP) * share
    kw_own = lax.dynamic_slice_in_dim(k_w, place, share, axis=1)
    vw_own = lax.dynamic_slice_in_dim(v_w, place, share, axis=1)
    dframe = (mm_t(dk_own, kw_own) + mm_t(dv_own, vw_own)).astype(bf16)
    grad_frames = swap(sum_columns(dframe))
    g_k = t_mm(frame_rows, dk_own).astype(bf16)
    g_v = t_mm(frame_rows, dv_own).astype(bf16)
    vb_own = jnp.sum(dv_own.astype(f32), axis=0)

    g_crossq = t_mm(a2, dqc).astype(bf16)
    da2 = mm_t(dqc, crossq_w)
    dres, gain1, shift1 = norm_back(h1, gains[1], da2)
    dh1 = dh2 + dres
    d1 = dh1.astype(bf16)
    g_selfout = t_mm(c1, d1).astype(bf16)
    dctx = mm_t(d1, selfout_w).astype(bf16)
    dctx = to_heads(dctx)[0]
    late, early = self_bwd(0, lanes // 128, 0, first, heads[:, :mid], heads[:, mid:], ctx, dctx[:mid], dctx[mid:], self_lse, kmark, qmark)
    dqkv = to_tokens(jnp.concatenate([early, late], axis=1))
    da1 = mm_t(dqkv, qkv_w)
    g_qkv = t_mm(a1, dqkv).astype(bf16)
    sums = total(dqkv)
    dres, gain0, shift0 = norm_back(h0, gains[0], da1)
    grad_hidden = swap((dh1 + dres).astype(bf16))

    vb = lax.dynamic_update_slice(jnp.zeros((width,), f32), vb_own, (place,))
    vectors = jnp.stack([gain0[0], gain1[0], gain2[0], gain3[0], shift0[0], shift1[0], shift2[0], shift3[0], sums[:width], sums[2 * width :], total(d1), total(dqc), vb, total(d2), total(dm)])
    per = width // n
    vectors = vectors.reshape(15, n, per).transpose(1, 0, 2).reshape(n, 15 * per)
    vectors = jnp.concatenate([vectors, total(du).reshape(n, ff // n)], axis=1)
    long = vectors.shape[1]
    seats = -(-long // reps)
    vectors = jnp.pad(vectors, ((0, 0), (0, seats * reps - long))).reshape(n * reps, seats)
    lines = -(-seats // (8 * width)) * 8
    vectors = jnp.pad(vectors, ((0, 0), (0, lines * width - seats))).reshape(n * reps, lines, width)

    def own_columns(x):
        return lax.dynamic_update_slice(jnp.zeros((x.shape[0], width), x.dtype), x, (jnp.int32(0), place))

    cross = [g_crossq, g_crossout]
    if n == 2:
        cross.append(jnp.concatenate([own_columns(g_k), own_columns(g_v)]))
    cross = reduce_rows(cross)
    crossq_grad, crossout_grad = cross[:2]
    if n == 2:
        kv_grad = cross[2]
    else:
        kv_cols = jnp.concatenate([own_columns(g_k), own_columns(g_v)], axis=1)
        kv_cols = lax.psum_scatter(kv_cols, SHARD, scatter_dimension=1, tiled=True)
        kv_grad = lax.psum(kv_cols, REP).astype(f32)
    got = reduce_rows([g_qkv[:, j * width : (j + 1) * width] for j in range(3)] + [g_selfout], vectors.astype(bf16))
    qkv_grad = jnp.concatenate(got[:3], axis=1)
    selfout_grad = got[3]
    vec = got[4].reshape(reps, lines * width)[:, :seats].reshape(-1)[:long]
    table = vec[: 15 * per].reshape(15, per)
    fc1b_grad = vec[15 * per :]
    return (
        output[None], grad_hidden[None], grad_frames[None],
        table[:4], table[4:8], qkv_grad, selfout_grad, crossq_grad, kv_grad, crossout_grad, fc1_grad, fc2_grad, table[8:15], fc1b_grad,
    )


def solution(mesh):
    reps, n = mesh.devices.shape
    paired = (reps, n) == (16, 2)
    if paired:
        work = Mesh(mesh.devices.reshape(4, 2, 2, 2), EVERY)
        rep, inner = REP2, ("x",)
    else:
        work = Mesh(mesh.devices.reshape(reps // 2, 2, 2, n // 2), ("rz", "core", "ihi", "ilo"))
        rep, inner = REP, SHARD
    rows, cols = P(inner, None), P(None, inner)
    tokens, features = P(rep, inner, None), P(rep, None, inner)
    weights = (cols, cols, rows, rows, rows, cols, rows, rows, rows, cols, P(inner))
    return jax.shard_map(
        body_pair if paired else body_general,
        mesh=work,
        in_specs=(tokens, features, P(rep, None), tokens) + weights,
        out_specs=(tokens, tokens, features) + weights,
        check_vma=False,
    )
```
